32 devices in a mesh: dp: 8 (over z, x), mp: 4 (over y, core).
Axes of the slice: x: 2, y: 2, z: 4, core: 2. Of those that a mesh axis runs over, the one named last changes fastest.
Arguments:
- tokens: bfloat16 [4096, 1024], P('dp'), may hold values from -6 to 6
- memory: bfloat16 [8192, 1024], P('dp'), may hold values from -6 to 6
- segment_ids: int32 [8, 512], P('dp'), may hold values from 0 to 7, never falling along the last dimension, each value on 1 to 256 neighbouring positions
- answer_ids: int32 [8, 512], P('dp'), may hold values from 0 to 50264
- loss_mask: int32 [8, 512], P('dp'), may hold values 0 or 1
- doc_scores: float32 [16, 4], replicated, may hold values from -5 to 5
- slot_place: int32 [64], replicated, may hold values from 0 to 63, each once
- self_query: bfloat16 [1024, 1024], P(None, 'mp'), may hold values from -0.25 to 0.25
- self_key: bfloat16 [1024, 1024], P(None, 'mp'), may hold values from -0.25 to 0.25
- self_value: bfloat16 [1024, 1024], P(None, 'mp'), may hold values from -0.1875 to 0.1875
- self_out: bfloat16 [1024, 1024], P('mp'), may hold values from -0.75 to 0.75
- cross_query: bfloat16 [1024, 1024], P(None, 'mp'), may hold values from -0.25 to 0.25
- cross_key: bfloat16 [1024, 1024], P(None, 'mp'), may hold values from -0.25 to 0.25
- cross_value: bfloat16 [1024, 1024], P(None, 'mp'), may hold values from -0.1875 to 0.1875
- cross_out: bfloat16 [1024, 1024], P('mp'), may hold values from -1 to 1
- feed_up: bfloat16 [1024, 4096], P(None, 'mp'), may hold values from -0.1875 to 0.1875
- feed_down: bfloat16 [4096, 1024], P('mp'), may hold values from -0.09375 to 0.09375
- gain_self: float32 [1024], replicated, may hold values from 0.5 to 1.5
- shift_self: float32 [1024], replicated, may hold values from -1.5 to 1.5
- gain_cross: float32 [1024], replicated, may hold values from 0.5 to 1.5
- shift_cross: float32 [1024], replicated, may hold values from -1.5 to 1.5
- gain_feed: float32 [1024], replicated, may hold values from 0.5 to 1.5
- shift_feed: float32 [1024], replicated, may hold values from -1.5 to 1.5
- embedding: bfloat16 [51200, 1024], P('mp', 'dp'), may hold values from -0.5 to 0.5
Outputs:
- loss: float32 [], replicated
- tokens_grad: float32 [4096, 1024], P('dp', 'mp')
- memory_grad: float32 [8192, 1024], P('dp', 'mp')
- self_query_grad: float32 [1024, 1024], P(None, 'mp')
- self_key_grad: float32 [1024, 1024], P(None, 'mp')
- self_value_grad: float32 [1024, 1024], P(None, 'mp')
- self_out_grad: float32 [1024, 1024], P('mp')
- cross_query_grad: float32 [1024, 1024], P(None, 'mp')
- cross_key_grad: float32 [1024, 1024], P(None, 'mp')
- cross_value_grad: float32 [1024, 1024], P(None, 'mp')
- cross_out_grad: float32 [1024, 1024], P('mp')
- feed_up_grad: float32 [1024, 4096], P(None, 'mp')
- feed_down_grad: float32 [4096, 1024], P('mp')
- gain_self_grad: float32 [1024], replicated
- shift_self_grad: float32 [1024], replicated
- gain_cross_grad: float32 [1024], replicated
- shift_cross_grad: float32 [1024], replicated
- gain_feed_grad: float32 [1024], replicated
- shift_feed_grad: float32 [1024], replicated
- embedding_grad: float32 [51200, 1024], P('mp', 'dp')
- scores_grad: float32 [16, 4], replicated
The draws below stay inside these ranges and needn't reach their ends.
Inputs may be any that keep to these rules, and one draw needn't show every extreme that they name: `segment_ids`: segment numbers never fall along a row and every number of 0 to 7 occurs in every row. `slot_place`: every number of 0 to 63 occurs exactly once; entry q * 4 + k names the global segment r * 8 + s that decodes passage slot k of question q.
All inputs are finite; a program needn't handle non-finite values. No bound on the sum of `loss_mask` on one device may be relied on, other than what follows from the above.
Results may differ from the reference program's by a relative error of at most 0.03.
The reference program's roundings to bfloat16 on the way count: a program that leaves them out, or rounds other values in their place, can miss the bound.
Values may be sent and summed in bfloat16 or wider, within the bound.
A program may use at most 256 MiB of HBM per device.

```python
import math
import jax
import jax.numpy as jnp
import numpy as np
from jax import lax

D = 1024
HEADS = 16
HEAD_DIM = 64
FF = 4096
WORDS = 50265
VOCAB = 51200
L = 512
SEG_ROW = 8
MEM = 128
K = 4
ROWS = 8
TOKENS = 4096
SEGMENTS = 64
MEMROWS = 8192
QUESTIONS = 16


def plant(array, own_key, low, high):
    extent = array.shape
    place = [jax.random.randint(jax.random.fold_in(own_key, axis), (), 0, extent[axis]) for axis in range(len(extent))]
    array = array.at[tuple(place)].set(low)
    longest = extent.index(max(extent))
    place[longest] = (place[longest] + 1) % extent[longest]
    return array.at[tuple(place)].set(high)


def shard_levels(own_key, shape, split, low, top_value):
    level = 1.0
    for position, blocks in split:
        steps = jax.random.uniform(jax.random.fold_in(jax.random.fold_in(own_key, 6), position), (blocks,), jnp.float32, low / len(split), top_value / len(split))
        level = level * jnp.repeat(jnp.exp(steps), shape[position] // blocks).reshape((-1,) + (1,) * (len(shape) - 1 - position))
    return level


def rank_table(number_of, slope):
    portions = [(1 << 20) // math.isqrt(rank ** slope) + 1 for rank in range(1, number_of + 1)]
    width = 1 + sum(portions) // (1 << 30)
    return np.cumsum(np.array([max(1, weight // width) for weight in portions]))


def ranked_ids(rng, shape, amount, slope):
    grid = rank_table(amount, slope)
    pick = jax.random.randint(jax.random.fold_in(rng, 1), shape, 0, int(grid[amount - 1]))
    rank = jnp.searchsorted(jnp.asarray(grid, jnp.int32), pick, side="right")
    return jax.random.permutation(jax.random.fold_in(rng, 2), amount)[rank].astype(jnp.int32)


def split_up(amount, total, most, lean):
    weights = [(1 << 20) // math.isqrt(grade ** lean) + 1 for grade in range(2, amount + 1)]
    spare, given = total - most - (amount - 1), [1] * (amount - 1)
    while spare > 0:
        free = [i for i in range(amount - 1) if given[i] < most]
        whole, left = sum([weights[i] for i in free]), spare
        for i in free:
            more = min(most - given[i], max(1, left * weights[i] // whole), spare)
            given[i] = given[i] + more
            spare = spare - more
    return np.array([most] + given)


def uneven_parts(own_key, number_of, total, most, skew):
    if number_of == 2:
        one = jax.random.randint(own_key, (), max(1, total - most), min(most, total - 1) + 1)
        return jnp.stack([one, total - one])
    sizes = jnp.asarray(split_up(number_of, total, most, skew), jnp.int32)
    pairs = (number_of - 1) // 2
    donor, taker = sizes[1:1 + 2 * pairs:2], sizes[2:2 + 2 * pairs:2]
    slack = jnp.minimum(donor - 1, most - taker)
    passed = jax.random.randint(jax.random.fold_in(own_key, 1), (pairs,), 0, 1 << 20) % (slack + 1)
    sizes = sizes.at[1:1 + 2 * pairs:2].set(donor - passed).at[2:2 + 2 * pairs:2].set(taker + passed)
    return sizes[jax.random.permutation(jax.random.fold_in(own_key, 2), number_of)]


def centred(own_key, shape, deviation, most, pieces=(), kind=jnp.bfloat16):
    factor_of = shard_levels(own_key, shape, pieces, -0.22, 0.18) if pieces else 1.0
    entries = jax.random.normal(own_key, shape, jnp.float32) * deviation * factor_of
    return jnp.minimum(jnp.maximum(entries, -most), most).astype(kind)


def setup_inputs(seed: int = 0) -> dict:
    key_list = jax.random.split(jax.random.key(seed), 25)
    tokens = centred(key_list[0], (TOKENS, D), 1.0, 6.0, ((0, 8),))
    memory = centred(key_list[1], (MEMROWS, D), 1.0, 6.0, ((0, 8),))
    segment_ids = jax.vmap(lambda own: jnp.searchsorted(jnp.cumsum(uneven_parts(own, SEG_ROW, L, L // 2, 1)), jnp.arange(L), side="right"))(jax.random.split(key_list[2], ROWS)).reshape((ROWS, L)).astype(jnp.int32)
    answer_ids = plant(ranked_ids(key_list[3], (ROWS, L), WORDS, 2), jax.random.fold_in(key_list[3], 3), 0, WORDS - 1).astype(jnp.int32)
    loss_mask = plant((jax.random.randint(key_list[4], (ROWS, L), 0, 8) < 7).astype(jnp.int32), jax.random.fold_in(key_list[4], 1), 0, 1)
    doc_scores = centred(key_list[5], (QUESTIONS, K), 1.0, 5.0, (), jnp.float32)
    slot_place = jax.random.permutation(key_list[6], SEGMENTS).astype(jnp.int32)
    self_query = centred(key_list[7], (D, D), (D // 2) ** -0.5, 0.25, ((1, 4),))
    self_key = centred(key_list[8], (D, D), (D // 2) ** -0.5, 0.25, ((1, 4),))
    self_value = centred(key_list[9], (D, D), D ** -0.5, 0.1875, ((1, 4),))
    self_out = centred(key_list[10], (D, D), (D // 16) ** -0.5, 0.75, ((0, 4),))
    cross_query = centred(key_list[11], (D, D), (D // 2) ** -0.5, 0.25, ((1, 4),))
    cross_key = centred(key_list[12], (D, D), (D // 2) ** -0.5, 0.25, ((1, 4),))
    cross_value = centred(key_list[13], (D, D), D ** -0.5, 0.1875, ((1, 4),))
    cross_out = centred(key_list[14], (D, D), (D // 32) ** -0.5, 1.0, ((0, 4),))
    feed_up = centred(key_list[15], (D, FF), D ** -0.5, 0.1875, ((1, 4),))
    feed_down = centred(key_list[16], (FF, D), FF ** -0.5, 0.09375, ((0, 4),))
    gain_self = jnp.clip(1.0 + 0.1 * jax.random.normal(key_list[17], (D,), jnp.float32), 0.5, 1.5)
    shift_self = centred(key_list[18], (D,), 0.3, 1.5, (), jnp.float32)
    gain_cross = jnp.clip(1.0 + 0.1 * jax.random.normal(key_list[19], (D,), jnp.float32), 0.5, 1.5)
    shift_cross = centred(key_list[20], (D,), 0.3, 1.5, (), jnp.float32)
    gain_feed = jnp.clip(1.0 + 0.1 * jax.random.normal(key_list[21], (D,), jnp.float32), 0.5, 1.5)
    shift_feed = centred(key_list[22], (D,), 0.3, 1.5, (), jnp.float32)
    embedding = centred(key_list[23], (VOCAB, D), (D // 9) ** -0.5, 0.5, ((0, 4), (1, 8)))
    return {"tokens": tokens, "memory": memory, "segment_ids": segment_ids, "answer_ids": answer_ids, "loss_mask": loss_mask, "doc_scores": doc_scores, "slot_place": slot_place, "self_query": self_query, "self_key": self_key, "self_value": self_value, "self_out": self_out, "cross_query": cross_query, "cross_key": cross_key, "cross_value": cross_value, "cross_out": cross_out, "feed_up": feed_up, "feed_down": feed_down, "gain_self": gain_self, "shift_self": shift_self, "gain_cross": gain_cross, "shift_cross": shift_cross, "gain_feed": gain_feed, "shift_feed": shift_feed, "embedding": embedding}


@jax.custom_vjp
def low(v):
    return lax.optimization_barrier(v.astype(jnp.bfloat16)).astype(jnp.float32)

@jax.custom_vjp
def low_back(v):
    return v

def low_keep(v):
    return (low(v), None)

def low_pass(kept, grad):
    return (grad,)

def back_keep(v):
    return (v, None)

def back_low(kept, grad):
    return (low(grad),)
low.defvjp(low_keep, low_pass)
low_back.defvjp(back_keep, back_low)
masked_score = -1e+30
norm_eps = 1e-05
highest = lax.Precision.HIGHEST

def rounded(inputs):
    return low(low_back(inputs))

def matmul(left_side, right_side):
    return jnp.dot(left_side, right_side, precision=highest)

def layer_norm(inputs, gain_vec, shift_vec):
    center = inputs - lax.optimization_barrier(jnp.mean(inputs, axis=-1, keepdims=True))
    spread = lax.optimization_barrier(jnp.mean(center * center, axis=-1, keepdims=True))
    return center * lax.rsqrt(spread + norm_eps) * gain_vec + shift_vec

def attend(queries, keys, values, allowed):
    heads_q = queries.reshape(queries.shape[0], HEADS, HEAD_DIM)
    heads_k = keys.reshape(keys.shape[0], HEADS, HEAD_DIM)
    heads_v = values.reshape(values.shape[0], HEADS, HEAD_DIM)
    scores = jnp.einsum('qhd,khd->hqk', heads_q, heads_k, precision=highest) * HEAD_DIM ** (-0.5)
    scores = low_back(jnp.where(allowed[None], scores, masked_score))
    largest = lax.optimization_barrier(jnp.max(scores, axis=-1, keepdims=True))
    weights = jnp.exp(scores - largest)
    probabilities = low(weights / lax.optimization_barrier(jnp.sum(weights, axis=-1, keepdims=True)))
    mixed_out = jnp.einsum('hqk,khd->qhd', probabilities, heads_v, precision=highest)
    return mixed_out.reshape(queries.shape[0], HEADS * HEAD_DIM)

def row_forward(weights, table_f, row_in, row_mem, segment, target, counted):
    self_query, self_key, self_value, self_out, cross_query, cross_key, cross_value, cross_out, feed_up, feed_down, gain_self, shift_self, gain_cross, shift_cross, gain_feed, shift_feed = weights
    places = jnp.arange(L, dtype=jnp.int32)
    self_mask = (segment[:, None] == segment[None, :]) & (places[None, :] <= places[:, None])
    owners = jnp.arange(SEG_ROW * MEM, dtype=jnp.int32) // MEM
    cross_mask = segment[:, None] == owners[None, :]
    attended = rounded(attend(rounded(matmul(row_in, self_query)), rounded(matmul(row_in, self_key)), rounded(matmul(row_in, self_value)), self_mask))
    first_norm = layer_norm(row_in + low_back(matmul(attended, self_out)), gain_self, shift_self)
    crossed = rounded(attend(rounded(matmul(low(first_norm), cross_query)), rounded(matmul(row_mem, cross_key)), rounded(matmul(row_mem, cross_value)), cross_mask))
    second = layer_norm(first_norm + low_back(matmul(crossed, cross_out)), gain_cross, shift_cross)
    hidden = low(jax.nn.gelu(low_back(matmul(low(second), feed_up)), approximate=False))
    third_norm = layer_norm(second + low_back(matmul(hidden, feed_down)), gain_feed, shift_feed)
    logits = low_back(matmul(low(third_norm), table_f.T))
    largest = lax.optimization_barrier(jnp.max(logits, axis=-1, keepdims=True))
    log_total = largest[:, 0] + jnp.log(lax.optimization_barrier(jnp.sum(jnp.exp(logits - largest), axis=-1)))
    picked = jnp.take_along_axis(logits, target[:, None], axis=1)[:, 0]
    return (picked - log_total) * counted

def reference(tokens, memory, segment_ids, answer_ids, loss_mask, doc_scores, slot_place, self_query, self_key, self_value, self_out, cross_query, cross_key, cross_value, cross_out, feed_up, feed_down, gain_self, shift_self, gain_cross, shift_cross, gain_feed, shift_feed, embedding):
    weights = tuple((weight.astype(jnp.float32) for weight in (self_query, self_key, self_value, self_out, cross_query, cross_key, cross_value, cross_out, feed_up, feed_down, gain_self, shift_self, gain_cross, shift_cross, gain_feed, shift_feed)))
    keepers = loss_mask.astype(jnp.float32)

    def forward(weight_set, inputs, memories, table_f, scores):
        rows_in = inputs.reshape(ROWS, L, D)
        rows_mem = memories.reshape(ROWS, SEG_ROW * MEM, D)

        def row_step(state_unused, row_items):
            row_in, row_mem, segment, target, counted = row_items
            return (state_unused, jax.checkpoint(row_forward)(weight_set, table_f, row_in, row_mem, segment, target, counted))
        state_unused, token_logp = lax.scan(row_step, jnp.float32(0.0), (rows_in, rows_mem, segment_ids, answer_ids, keepers))
        global_ids = (segment_ids + (jnp.arange(ROWS, dtype=jnp.int32) * SEG_ROW)[:, None]).reshape(-1)
        seg_sums = jax.ops.segment_sum(token_logp.reshape(-1), global_ids, SEGMENTS)
        counts = jax.ops.segment_sum(keepers.reshape(-1), global_ids, SEGMENTS)
        likely = seg_sums / jnp.maximum(counts, 1.0)
        joint_score = jax.nn.log_softmax(scores, axis=1) + likely[slot_place].reshape(QUESTIONS, K)
        return -jnp.sum(jax.nn.logsumexp(joint_score, axis=1))
    loss, pullback = jax.vjp(forward, weights, tokens.astype(jnp.float32), memory.astype(jnp.float32), embedding.astype(jnp.float32), doc_scores)
    weight_grads, tokens_grad, memory_grad, embedding_grad, scores_grad = pullback(jnp.ones_like(loss))
    g_sq, g_sk, g_sv, g_so, g_cq, g_ck, g_cv, g_co, g_up, g_down, g_gs, g_ss, g_gc, g_sc, g_gf, g_sf = weight_grads
    return (loss, tokens_grad, memory_grad, g_sq, g_sk, g_sv, g_so, g_cq, g_ck, g_cv, g_co, g_up, g_down, g_gs, g_ss, g_gc, g_sc, g_gf, g_sf, embedding_grad, scores_grad)
```

```python
import jax
import jax.numpy as jnp
from jax import lax
from jax.sharding import PartitionSpec as P

HEAD_DIM = 64
SEG_ROW = 8
MEM = 128


masked_score = -1e30
norm_eps = 1e-05
highest = lax.Precision.HIGHEST


def product(left_side, right_side):
    return jnp.dot(left_side, right_side, preferred_element_type=jnp.float32)


def product_tn(left_side, right_side):
    return lax.dot_general(
        left_side, right_side, (((0,), (0,)), ((), ())), preferred_element_type=jnp.float32
    )


def product_nt(left_side, right_side):
    return lax.dot_general(
        left_side, right_side, (((1,), (1,)), ((), ())), preferred_element_type=jnp.float32
    )


def layer_norm(inputs, gain_vec, shift_vec):
    center = inputs - jnp.mean(inputs, axis=-1, keepdims=True)
    spread = jnp.mean(center * center, axis=-1, keepdims=True)
    return center * lax.rsqrt(spread + norm_eps) * gain_vec + shift_vec


def norm_back(residual, gain_vec, shift_vec, grad_out):
    outputs, pullback = jax.vjp(layer_norm, residual, gain_vec, shift_vec)
    return pullback(grad_out)


def gelu_exact(inputs):
    return jax.nn.gelu(inputs, approximate=False)


def split_heads(matrix):
    return matrix.reshape(matrix.shape[0], matrix.shape[1] // HEAD_DIM, HEAD_DIM)


def attention_scores(queries, keys, allowed):
    scores = jnp.einsum(
        "qhd,khd->hqk", split_heads(queries), split_heads(keys), preferred_element_type=jnp.float32
    ) * HEAD_DIM ** (-0.5)
    return jnp.where(allowed[None], scores, masked_score)


def attend_forward(queries, keys, values, allowed):
    scores = attention_scores(queries, keys, allowed)
    largest = jnp.max(scores, axis=-1, keepdims=True)
    weights = jnp.exp(scores - largest)
    total = jnp.sum(weights, axis=-1, keepdims=True)
    probabilities = (weights / total).astype(jnp.bfloat16)
    mixed_out = jnp.einsum(
        "hqk,khd->qhd", probabilities, split_heads(values), preferred_element_type=jnp.float32
    )
    return (mixed_out.reshape(queries.shape[0], queries.shape[1]), largest + jnp.log(total))


def attend_backward(queries, keys, values, allowed, log_total, grad_out):
    scores = attention_scores(queries, keys, allowed)
    probabilities = jnp.exp(scores - log_total)
    heads_grad = split_heads(grad_out)
    grad_prob = jnp.einsum(
        "qhd,khd->hqk", heads_grad, split_heads(values), preferred_element_type=jnp.float32
    )
    grad_values = jnp.einsum(
        "hqk,qhd->khd",
        probabilities.astype(jnp.bfloat16),
        heads_grad,
        preferred_element_type=jnp.float32,
    )
    row_dot = jnp.sum(grad_prob * probabilities, axis=-1, keepdims=True)
    grad_scores = (probabilities * (grad_prob - row_dot)).astype(jnp.bfloat16)
    grad_queries = jnp.einsum(
        "hqk,khd->qhd", grad_scores, split_heads(keys), preferred_element_type=jnp.float32
    ) * HEAD_DIM ** (-0.5)
    grad_keys = jnp.einsum(
        "hqk,qhd->khd", grad_scores, split_heads(queries), preferred_element_type=jnp.float32
    ) * HEAD_DIM ** (-0.5)
    width = queries.shape[1]
    return (
        grad_queries.reshape(-1, width).astype(jnp.bfloat16),
        grad_keys.reshape(-1, width).astype(jnp.bfloat16),
        grad_values.reshape(-1, width).astype(jnp.bfloat16),
    )


def run_rows(queries, keys, values, masks):
    mixed_out, log_total = attend_forward(queries, keys, values, masks[0])
    totals = [log_total]
    return (mixed_out.astype(jnp.bfloat16), totals)


def back_rows(queries, keys, values, masks, totals, grad_mix):
    parts_query, parts_key, parts_value = ([], [], [])
    grad_query, grad_key, grad_value = attend_backward(
        queries, keys, values, masks[0], totals[0], grad_mix
    )
    parts_query.append(grad_query)
    parts_key.append(grad_key)
    parts_value.append(grad_value)
    return (parts_query[0], parts_key[0], parts_value[0])


def join_heads(partial_value):
    return lax.psum(partial_value, "mp")


def join_grads(partial_value):
    return lax.psum(partial_value, "mp")


def shift_pairs(total, step):
    return [(index, (index + step) % total) for index in range(total)]


def spread_rows(table):
    total = lax.axis_size("dp")
    place = lax.axis_index("dp")
    width = table.shape[1]
    part = table.shape[0] // total
    whole = jnp.zeros((part, width * total), table.dtype)
    for step in range(total):
        block = lax.dynamic_slice_in_dim(table, (place + step) % total * part, part, 0)
        if step:
            block = lax.ppermute(block, "dp", shift_pairs(total, step))
        whole = lax.dynamic_update_slice_in_dim(
            whole, block, (place - step) % total * width, 1
        )
    return whole


def return_rows(rows, height):
    total = lax.axis_size("dp")
    place = lax.axis_index("dp")
    part = rows.shape[0]
    width = rows.shape[1] // total
    whole = jnp.zeros((height, width), rows.dtype)
    for step in range(total):
        block = lax.dynamic_slice_in_dim(rows, (place + step) % total * width, width, 1)
        if step:
            block = lax.ppermute(block, "dp", shift_pairs(total, step))
        whole = lax.dynamic_update_slice_in_dim(
            whole, block, (place - step) % total * part, 0
        )
    return whole


def local(
    tokens,
    memory,
    segment_ids,
    answer_ids,
    loss_mask,
    doc_scores,
    slot_place,
    self_query,
    self_key,
    self_value,
    self_out,
    cross_query,
    cross_key,
    cross_value,
    cross_out,
    feed_up,
    feed_down,
    gain_self,
    shift_self,
    gain_cross,
    shift_cross,
    gain_feed,
    shift_feed,
    embedding,
):
    row_count, row_len = segment_ids.shape
    table_rows = spread_rows(embedding)
    segments_all, answers_all, kept_all = (
        lax.all_gather(ids, "dp", axis=0, tiled=True)
        for ids in (segment_ids, answer_ids, loss_mask)
    )
    span = SEG_ROW * MEM
    inputs = tokens.astype(jnp.float32)
    places = jnp.arange(row_len, dtype=jnp.int32)
    owners = jnp.arange(span, dtype=jnp.int32) // MEM
    self_masks = [
        (segment_ids[0][:, None] == segment_ids[0][None, :]) & (places[None, :] <= places[:, None])
    ]
    cross_masks = [segment_ids[0][:, None] == owners[None, :]]
    query_self = product(tokens, self_query).astype(jnp.bfloat16)
    key_self = product(tokens, self_key).astype(jnp.bfloat16)
    value_self = product(tokens, self_value).astype(jnp.bfloat16)
    self_mix, self_totals = run_rows(query_self, key_self, value_self, self_masks)
    branch_self = join_heads(product(self_mix, self_out))
    first_norm = layer_norm(inputs + branch_self, gain_self, shift_self)
    first_low = first_norm.astype(jnp.bfloat16)
    query_cross = product(first_low, cross_query).astype(jnp.bfloat16)
    key_cross = product(memory, cross_key).astype(jnp.bfloat16)
    value_cross = product(memory, cross_value).astype(jnp.bfloat16)
    cross_mix, cross_totals = run_rows(query_cross, key_cross, value_cross, cross_masks)
    branch_cross = join_heads(product(cross_mix, cross_out))
    second_norm = layer_norm(first_norm + branch_cross, gain_cross, shift_cross)
    second_low = second_norm.astype(jnp.bfloat16)
    feed_pre = product(second_low, feed_up)
    feed_act = gelu_exact(feed_pre).astype(jnp.bfloat16)
    branch_feed = join_heads(product(feed_act, feed_down))
    third_norm = layer_norm(second_norm + branch_feed, gain_feed, shift_feed)
    third_low = third_norm.astype(jnp.bfloat16)
    vocab_local = embedding.shape[0]
    part = table_rows.shape[0]
    states = lax.all_gather(third_low, "dp", axis=0, tiled=True)
    logits = product_nt(states, table_rows)
    offset = lax.axis_index("mp") * vocab_local + lax.axis_index("dp") * part
    local_target = answers_all.reshape(-1) - offset
    vocab_ids = jnp.arange(part, dtype=jnp.int32)
    answer_hot = local_target[:, None] == vocab_ids[None, :]
    picked_part = jnp.sum(jnp.where(answer_hot, logits, 0.0), axis=1)
    global_top = lax.pmax(jnp.max(logits, axis=1), ("dp", "mp"))
    global_sum, picked = lax.psum(
        (jnp.sum(jnp.exp(logits - global_top[:, None]), axis=1), picked_part), ("dp", "mp")
    )
    log_total = global_top + jnp.log(global_sum)
    keeper = kept_all.astype(jnp.float32)
    token_logp = (picked - log_total).reshape(keeper.shape) * keeper
    seg_hot = (
        segments_all[:, :, None] == jnp.arange(SEG_ROW, dtype=jnp.int32)[None, None, :]
    ).astype(jnp.float32)
    seg_sums = jnp.sum(seg_hot * token_logp[:, :, None], axis=1)
    counts = jnp.sum(seg_hot * keeper[:, :, None], axis=1)
    likely_all = (seg_sums / jnp.maximum(counts, 1.0)).reshape(-1)
    place_hot = (
        slot_place[:, None] == jnp.arange(likely_all.shape[0], dtype=jnp.int32)[None, :]
    ).astype(jnp.float32)

    def marginal(scores, likely):
        joint_score = jax.nn.log_softmax(scores, axis=1) + jnp.dot(
            place_hot, likely, precision=highest
        ).reshape(scores.shape)
        return -jnp.sum(jax.nn.logsumexp(joint_score, axis=1))

    loss, pullback = jax.vjp(marginal, doc_scores, likely_all)
    grad_scores, grad_likely = pullback(jnp.ones_like(loss))
    per_segment = grad_likely.reshape(counts.shape) / jnp.maximum(counts, 1.0)
    grad_logp = (jnp.sum(seg_hot * per_segment[:, None, :], axis=2) * keeper).reshape(-1)
    grad_logits = (
        grad_logp[:, None]
        * (answer_hot.astype(jnp.float32) - jnp.exp(logits - log_total[:, None]))
    ).astype(jnp.bfloat16)
    grad_third = join_grads(
        lax.psum_scatter(
            product(grad_logits, table_rows).astype(jnp.bfloat16),
            "dp",
            scatter_dimension=0,
            tiled=True,
        ).astype(jnp.float32)
    )
    grad_table = return_rows(
        product_tn(grad_logits, states).astype(jnp.bfloat16), vocab_local
    ).astype(jnp.float32)
    grad_res3, grad_gain_feed, grad_shift_feed = norm_back(
        second_norm + branch_feed, gain_feed, shift_feed, grad_third
    )
    grad_branch = grad_res3.astype(jnp.bfloat16)
    grad_feed_down = product_tn(feed_act, grad_branch)
    grad_act = product_nt(grad_branch, feed_down)
    act_value, act_pull = jax.vjp(gelu_exact, feed_pre)
    grad_pre = act_pull(grad_act)[0].astype(jnp.bfloat16)
    grad_feed_up = product_tn(second_low, grad_pre)
    grad_second = grad_res3 + join_grads(product_nt(grad_pre, feed_up))
    grad_res2, grad_gain_cross, grad_shift_cross = norm_back(
        first_norm + branch_cross, gain_cross, shift_cross, grad_second
    )
    grad_branch = grad_res2.astype(jnp.bfloat16)
    grad_cross_out = product_tn(cross_mix, grad_branch)
    grad_mix = product_nt(grad_branch, cross_out).astype(jnp.bfloat16)
    cross_gq, cross_gk, cross_gv = back_rows(
        query_cross, key_cross, value_cross, cross_masks, cross_totals, grad_mix
    )
    grad_cross_query = product_tn(first_low, cross_gq)
    grad_cross_key = product_tn(memory, cross_gk)
    grad_cross_value = product_tn(memory, cross_gv)
    grad_memory_part = product_nt(cross_gk, cross_key) + product_nt(cross_gv, cross_value)
    grad_first = grad_res2 + join_grads(product_nt(cross_gq, cross_query))
    grad_res1, grad_gain_self, grad_shift_self = norm_back(
        inputs + branch_self, gain_self, shift_self, grad_first
    )
    grad_branch = grad_res1.astype(jnp.bfloat16)
    grad_self_out = product_tn(self_mix, grad_branch)
    grad_mix = product_nt(grad_branch, self_out).astype(jnp.bfloat16)
    self_gq, self_gk, self_gv = back_rows(
        query_self, key_self, value_self, self_masks, self_totals, grad_mix
    )
    grad_self_query = product_tn(tokens, self_gq)
    grad_self_key = product_tn(tokens, self_gk)
    grad_self_value = product_tn(tokens, self_gv)
    grad_input_part = (
        product_nt(self_gq, self_query)
        + product_nt(self_gk, self_key)
        + product_nt(self_gv, self_value)
    )
    input_share, memory_share = (
        lax.psum_scatter(
            grad_input_part.astype(jnp.bfloat16), "mp", scatter_dimension=1, tiled=True
        ).astype(jnp.float32),
        lax.psum_scatter(
            grad_memory_part.astype(jnp.bfloat16), "mp", scatter_dimension=1, tiled=True
        ).astype(jnp.float32),
    )
    column_start = lax.axis_index("mp") * input_share.shape[1]
    grad_tokens = input_share + lax.dynamic_slice_in_dim(
        grad_res1, column_start, input_share.shape[1], 1
    )
    (
        sum_sq,
        sum_sk,
        sum_sv,
        sum_so,
        sum_cq,
        sum_ck,
        sum_cv,
        sum_co,
        sum_up,
        sum_down,
        sum_gs,
        sum_ss,
        sum_gc,
        sum_sc,
        sum_gf,
        sum_sf,
    ) = (
        lax.psum(grad_self_query.astype(jnp.bfloat16), "dp").astype(jnp.float32),
        lax.psum(grad_self_key.astype(jnp.bfloat16), "dp").astype(jnp.float32),
        lax.psum(grad_self_value.astype(jnp.bfloat16), "dp").astype(jnp.float32),
        lax.psum(grad_self_out.astype(jnp.bfloat16), "dp").astype(jnp.float32),
        lax.psum(grad_cross_query.astype(jnp.bfloat16), "dp").astype(jnp.float32),
        lax.psum(grad_cross_key.astype(jnp.bfloat16), "dp").astype(jnp.float32),
        lax.psum(grad_cross_value.astype(jnp.bfloat16), "dp").astype(jnp.float32),
        lax.psum(grad_cross_out.astype(jnp.bfloat16), "dp").astype(jnp.float32),
        lax.psum(grad_feed_up.astype(jnp.bfloat16), "dp").astype(jnp.float32),
        lax.psum(grad_feed_down.astype(jnp.bfloat16), "dp").astype(jnp.float32),
        lax.psum(grad_gain_self.astype(jnp.bfloat16), "dp").astype(jnp.float32),
        lax.psum(grad_shift_self.astype(jnp.bfloat16), "dp").astype(jnp.float32),
        lax.psum(grad_gain_cross.astype(jnp.bfloat16), "dp").astype(jnp.float32),
        lax.psum(grad_shift_cross.astype(jnp.bfloat16), "dp").astype(jnp.float32),
        lax.psum(grad_gain_feed.astype(jnp.bfloat16), "dp").astype(jnp.float32),
        lax.psum(grad_shift_feed.astype(jnp.bfloat16), "dp").astype(jnp.float32),
    )
    return (
        loss,
        grad_tokens,
        memory_share,
        sum_sq,
        sum_sk,
        sum_sv,
        sum_so,
        sum_cq,
        sum_ck,
        sum_cv,
        sum_co,
        sum_up,
        sum_down,
        sum_gs,
        sum_ss,
        sum_gc,
        sum_sc,
        sum_gf,
        sum_sf,
        grad_table,
        grad_scores,
    )


def solution(mesh):
    return jax.shard_map(
        local,
        mesh=mesh,
        in_specs=(
            P("dp", None),
            P("dp", None),
            P("dp", None),
            P("dp", None),
            P("dp", None),
            P(),
            P(),
            P(None, "mp"),
            P(None, "mp"),
            P(None, "mp"),
            P("mp", None),
            P(None, "mp"),
            P(None, "mp"),
            P(None, "mp"),
            P("mp", None),
            P(None, "mp"),
            P("mp", None),
            P(),
            P(),
            P(),
            P(),
            P(),
            P(),
            P("mp", "dp"),
        ),
        out_specs=(
            P(),
            P("dp", "mp"),
            P("dp", "mp"),
            P(None, "mp"),
            P(None, "mp"),
            P(None, "mp"),
            P("mp", None),
            P(None, "mp"),
            P(None, "mp"),
            P(None, "mp"),
            P("mp", None),
            P(None, "mp"),
            P("mp", None),
            P(),
            P(),
            P(),
            P(),
            P(),
            P(),
            P("mp", "dp"),
            P(),
        ),
        check_vma=False,
    )
```

```python
import functools

import jax
import jax.numpy as jnp
from jax import lax
from jax.experimental import pallas as pl
from jax.experimental.pallas import tpu as pltpu
from jax.sharding import PartitionSpec as P

HEAD_DIM = 64
SEG_ROW = 8
MEM = 128


masked_score = -1e30
norm_eps = 1e-05
highest = lax.Precision.HIGHEST


def product(left_side, right_side):
    return jnp.dot(left_side, right_side, preferred_element_type=jnp.float32)


def product_tn(left_side, right_side):
    return lax.dot_general(
        left_side, right_side, (((0,), (0,)), ((), ())), preferred_element_type=jnp.float32
    )


def product_nt(left_side, right_side):
    return lax.dot_general(
        left_side, right_side, (((1,), (1,)), ((), ())), preferred_element_type=jnp.float32
    )


def gelu_exact(inputs):
    return jax.nn.gelu(inputs, approximate=False)


def split_heads(matrix):
    return matrix.reshape(matrix.shape[0], matrix.shape[1] // HEAD_DIM, HEAD_DIM)


def attention_scores(queries, keys, allowed):
    scores = jnp.einsum(
        "qhd,khd->hqk", split_heads(queries), split_heads(keys), preferred_element_type=jnp.float32
    ) * HEAD_DIM ** (-0.5)
    return jnp.where(allowed[None], scores, masked_score)


def attend_forward(queries, keys, values, allowed):
    scores = attention_scores(queries, keys, allowed)
    largest = jnp.max(scores, axis=-1, keepdims=True)
    weights = jnp.exp(scores - largest)
    total = jnp.sum(weights, axis=-1, keepdims=True)
    probabilities = (weights / total).astype(jnp.bfloat16)
    mixed_out = jnp.einsum(
        "hqk,khd->qhd", probabilities, split_heads(values), preferred_element_type=jnp.float32
    )
    return (mixed_out.reshape(queries.shape[0], queries.shape[1]), largest + jnp.log(total))


def attend_backward(queries, keys, values, allowed, log_total, grad_out):
    scores = attention_scores(queries, keys, allowed)
    probabilities = jnp.exp(scores - log_total)
    heads_grad = split_heads(grad_out)
    grad_prob = jnp.einsum(
        "qhd,khd->hqk", heads_grad, split_heads(values), preferred_element_type=jnp.float32
    )
    grad_values = jnp.einsum(
        "hqk,qhd->khd",
        probabilities.astype(jnp.bfloat16),
        heads_grad,
        preferred_element_type=jnp.float32,
    )
    row_dot = jnp.sum(grad_prob * probabilities, axis=-1, keepdims=True)
    grad_scores = (probabilities * (grad_prob - row_dot)).astype(jnp.bfloat16)
    grad_queries = jnp.einsum(
        "hqk,khd->qhd", grad_scores, split_heads(keys), preferred_element_type=jnp.float32
    ) * HEAD_DIM ** (-0.5)
    grad_keys = jnp.einsum(
        "hqk,qhd->khd", grad_scores, split_heads(queries), preferred_element_type=jnp.float32
    ) * HEAD_DIM ** (-0.5)
    width = queries.shape[1]
    return (
        grad_queries.reshape(-1, width).astype(jnp.bfloat16),
        grad_keys.reshape(-1, width).astype(jnp.bfloat16),
        grad_values.reshape(-1, width).astype(jnp.bfloat16),
    )


def run_rows(queries, keys, values, masks):
    mixed_out, log_total = attend_forward(queries, keys, values, masks[0])
    totals = [log_total]
    return (mixed_out.astype(jnp.bfloat16), totals)


def back_rows(queries, keys, values, masks, totals, grad_mix):
    parts_query, parts_key, parts_value = ([], [], [])
    grad_query, grad_key, grad_value = attend_backward(
        queries, keys, values, masks[0], totals[0], grad_mix
    )
    parts_query.append(grad_query)
    parts_key.append(grad_key)
    parts_value.append(grad_value)
    return (parts_query[0], parts_key[0], parts_value[0])


MESH = pl.DeviceIdType.MESH
VMEM = pl.BlockSpec(memory_space=pltpu.VMEM)
ANY = pl.BlockSpec(memory_space=pl.ANY)
DMA = pltpu.SemaphoreType.DMA
QUARTERS = 4


def flip(index, mask):
    for bit in range(mask.bit_length()):
        if mask >> bit & 1:
            step = 1 << bit
            index = index + step * (1 - 2 * lax.rem(lax.div(index, step), 2))
    return index


def greet(peers):
    barrier = pltpu.get_barrier_semaphore()
    for peer in peers:
        pl.semaphore_signal(barrier, inc=1, device_id=peer, device_id_type=MESH)
    pl.semaphore_wait(barrier, len(peers))


def remote(source, target, send_sem, recv_sem, peer):
    copy = pltpu.make_async_remote_copy(
        src_ref=source,
        dst_ref=target,
        send_sem=send_sem,
        recv_sem=recv_sem,
        device_id=peer,
        device_id_type=MESH,
    )
    copy.start()
    return copy


def sum_quarter(place, block_of, near, far, sib_send, sib_recv, far_send, far_recv, sems):
    copies = []
    for slot, mask in enumerate((3, 1)):
        sib_send[slot] = block_of(flip(place, mask)).astype(jnp.bfloat16)
        copies.append(
            remote(
                sib_send.at[slot], sib_recv.at[slot], sems.at[0, slot], sems.at[1, slot], near
            )
        )
    distant = block_of(flip(place, 2))
    own = block_of(place)
    copies[0].wait_recv()
    far_send[...] = (distant + sib_recv[0].astype(jnp.float32)).astype(jnp.bfloat16)
    last = remote(far_send, far_recv, sems.at[0, 2], sems.at[1, 2], far)
    copies[1].wait_recv()
    own = own + sib_recv[1].astype(jnp.float32)
    last.wait_recv()
    own = own + far_recv[...].astype(jnp.float32)
    return own, copies + [last]


def share_quarter(place, quarters, near, far, sems):
    here = quarters.at[place]
    to_far = remote(here, here, sems.at[0, 3], sems.at[1, 3], far)
    to_near = remote(here, here, sems.at[0, 4], sems.at[1, 4], near)
    to_far.wait_recv()
    there = quarters.at[flip(place, 2)]
    passed = remote(there, there, sems.at[0, 5], sems.at[1, 5], near)
    to_near.wait_recv()
    passed.wait_recv()
    return [to_far, to_near, passed]


def norm_rows(rows, gain, shift):
    center = rows - jnp.mean(rows, axis=-1, keepdims=True)
    spread = jnp.mean(center * center, axis=-1, keepdims=True)
    return center * lax.rsqrt(spread + norm_eps) * gain + shift


def norm_rows_back(rows, gain, grad):
    center = rows - jnp.mean(rows, axis=-1, keepdims=True)
    scale = lax.rsqrt(jnp.mean(center * center, axis=-1, keepdims=True) + norm_eps)
    normed = center * scale
    inner = grad * gain
    grad_rows = scale * (
        inner
        - jnp.mean(inner, axis=-1, keepdims=True)
        - normed * jnp.mean(inner * normed, axis=-1, keepdims=True)
    )
    return (
        grad_rows,
        jnp.sum(grad * normed, axis=0, keepdims=True),
        jnp.sum(grad, axis=0, keepdims=True),
    )


def rows_of(ref, height, index):
    return ref[pl.ds(pl.multiple_of(index * height, height), height), :]


def exchange_scratch(height, width):
    return [
        pltpu.VMEM((2, height, width), jnp.bfloat16),
        pltpu.VMEM((2, height, width), jnp.bfloat16),
        pltpu.VMEM((height, width), jnp.bfloat16),
        pltpu.VMEM((height, width), jnp.bfloat16),
        DMA((2, 6)),
    ]


def mix_norm_kernel(
    total, left, weight, kept, gain, shift, ids, quarters, normed, rows, ids_all,
    sib_send, sib_recv, far_send, far_recv, sems, ids_sems, ids_local,
):
    block, place = lax.axis_index("dp"), lax.axis_index("mp")
    near, far = (block, flip(place, 1)), (block, flip(place, 2))
    height = kept.shape[0]
    peers = [near, far]
    if ids is not None:
        peers += [(flip(block, mask), place) for mask in range(1, total)]
    greet(peers)
    copies = []
    if ids is not None:
        own = pltpu.make_async_copy(ids, ids_all.at[block], ids_local)
        own.start()
        for mask in range(1, total):
            copies.append(
                remote(
                    ids, ids_all.at[block], ids_sems.at[0, mask], ids_sems.at[1, mask],
                    (flip(block, mask), place),
                )
            )

    def block_of(index):
        return jnp.dot(
            rows_of(left, height, index), weight[...], preferred_element_type=jnp.float32
        )

    branch, more = sum_quarter(
        place, block_of, near, far, sib_send, sib_recv, far_send, far_recv, sems
    )
    outcome = kept[...].astype(jnp.float32) + branch
    rows[...] = outcome
    outcome = norm_rows(outcome, gain[...], shift[...])
    normed[...] = outcome
    quarters[place] = outcome.astype(jnp.bfloat16)
    more += share_quarter(place, quarters, near, far, sems)
    for copy in copies:
        copy.wait_recv()
    for copy in copies + more:
        copy.wait_send()
    if ids is not None:
        own.wait()


def mix_norm(left, weight, kept, gain, shift, number, ids=None):
    height, width = kept.shape
    total = lax.axis_size("dp")
    quarter = jax.ShapeDtypeStruct((height, width), jnp.float32)
    out_shape = [
        jax.ShapeDtypeStruct((QUARTERS, height, width), jnp.bfloat16), quarter, quarter
    ]
    given = [left, weight, kept, gain.reshape(1, -1), shift.reshape(1, -1)]
    scratch = exchange_scratch(height, width)
    if ids is None:
        def kernel(left, weight, kept, gain, shift, quarters, normed, rows, *scratch):
            mix_norm_kernel(
                total, left, weight, kept, gain, shift, None, quarters, normed, rows, None,
                *scratch, None, None,
            )
    else:
        kernel = functools.partial(mix_norm_kernel, total)
        given.append(ids)
        out_shape.append(jax.ShapeDtypeStruct((total,) + ids.shape, ids.dtype))
        scratch += [DMA((2, total)), DMA]
    outcome = pl.pallas_call(
        kernel,
        out_shape=out_shape,
        in_specs=[VMEM] * len(given),
        out_specs=[VMEM] * len(out_shape),
        scratch_shapes=scratch,
        compiler_params=pltpu.CompilerParams(
            collective_id=number, has_side_effects=True, vmem_limit_bytes=48 * 2**20
        ),
    )(*given)
    return (outcome[0].reshape(-1, width),) + tuple(outcome[1:])


def feed_norm_kernel(
    total, left, weight, kept, gain, shift, states, rows,
    low, sib_send, sib_recv, far_send, far_recv, sems, hops, own_sem,
):
    block, place = lax.axis_index("dp"), lax.axis_index("mp")
    near, far = (block, flip(place, 1)), (block, flip(place, 2))
    beside = (flip(block, 1), place)
    height = kept.shape[0]
    greet([near, far, beside] + [(flip(block, mask), place) for mask in range(2, total, 2)])

    def block_of(index):
        return jnp.dot(
            rows_of(left, height, index), weight[...], preferred_element_type=jnp.float32
        )

    branch, sent = sum_quarter(
        place, block_of, near, far, sib_send, sib_recv, far_send, far_recv, sems
    )
    outcome = kept[...] + branch
    rows[...] = outcome
    low[...] = norm_rows(outcome, gain[...], shift[...]).astype(jnp.bfloat16)
    own = pltpu.make_async_copy(low, states.at[block, place], own_sem)
    own.start()
    across = flip(place, 2)

    def hop(kind, mask, source, peer, row, column):
        copy = remote(
            source, states.at[row, column], hops.at[0, kind, mask], hops.at[1, kind, mask], peer
        )
        sent.append(copy)
        return copy

    first = {}
    for mask in range(2, total, 2):
        first[mask] = hop(0, mask, low, (flip(block, mask), place), block, place)
    over = {}
    ends = []

    def pass_on(mask):
        over[mask].wait_recv()
        row = flip(block, mask)
        ends.append(hop(3, mask, states.at[row, across], near, row, across))

    for mask in range(total):
        row = flip(block, mask)
        if mask:
            first[mask].wait_recv()
        source = states.at[row, place] if mask else low
        if mask % 2 == 0:
            first[mask + 1] = hop(0, mask + 1, source, beside, row, place)
        over[mask] = hop(1, mask, source, far, row, place)
        ends.append(hop(2, mask, source, near, row, place))
        if mask >= 2:
            pass_on(mask - 2)
    for mask in range(max(total - 2, 0), total):
        pass_on(mask)
    for copy in ends:
        copy.wait_recv()
    for copy in sent:
        copy.wait_send()
    own.wait()


def feed_norm(left, weight, kept, gain, shift, number):
    height, width = kept.shape
    total = lax.axis_size("dp")
    states, rows = pl.pallas_call(
        functools.partial(feed_norm_kernel, total),
        out_shape=[
            jax.ShapeDtypeStruct((total, QUARTERS, height, width), jnp.bfloat16),
            jax.ShapeDtypeStruct((height, width), jnp.float32),
        ],
        in_specs=[VMEM] * 5,
        out_specs=[ANY, VMEM],
        scratch_shapes=[pltpu.VMEM((height, width), jnp.bfloat16)]
        + exchange_scratch(height, width)
        + [DMA((2, 4, total)), DMA],
        compiler_params=pltpu.CompilerParams(
            collective_id=number, has_side_effects=True, vmem_limit_bytes=48 * 2**20
        ),
    )(left, weight, kept, gain.reshape(1, -1), shift.reshape(1, -1))
    return states.reshape(-1, width), rows


def back_norm_kernel(
    left, weight, kept, rows, gain, quarters, grad_rows, grad_vecs,
    sib_send, sib_recv, far_send, far_recv, sems,
):
    block, place = lax.axis_index("dp"), lax.axis_index("mp")
    near, far = (block, flip(place, 1)), (block, flip(place, 2))
    height = kept.shape[0]
    greet([near, far])

    def block_of(index):
        return lax.dot_general(
            rows_of(left, height, index),
            weight[...],
            (((1,), (1,)), ((), ())),
            preferred_element_type=jnp.float32,
        )

    branch, sent = sum_quarter(
        place, block_of, near, far, sib_send, sib_recv, far_send, far_recv, sems
    )
    outcome, grad_gain, grad_shift = norm_rows_back(rows[...], gain[...], kept[...] + branch)
    grad_rows[...] = outcome
    grad_vecs[0:1] = grad_gain
    grad_vecs[1:2] = grad_shift
    quarters[place] = outcome.astype(jnp.bfloat16)
    sent += share_quarter(place, quarters, near, far, sems)
    for copy in sent:
        copy.wait_send()


def back_norm(left, weight, kept, rows, gain, number):
    height, width = kept.shape
    quarters, grad_rows, grad_vecs = pl.pallas_call(
        back_norm_kernel,
        out_shape=[
            jax.ShapeDtypeStruct((QUARTERS, height, width), jnp.bfloat16),
            jax.ShapeDtypeStruct((height, width), jnp.float32),
            jax.ShapeDtypeStruct((2, width), jnp.float32),
        ],
        in_specs=[VMEM] * 5,
        out_specs=[VMEM] * 3,
        scratch_shapes=exchange_scratch(height, width),
        compiler_params=pltpu.CompilerParams(
            collective_id=number, has_side_effects=True, vmem_limit_bytes=48 * 2**20
        ),
    )(left, weight, kept, rows, gain.reshape(1, -1))
    return quarters.reshape(-1, width), grad_rows, grad_vecs


def join_totals_kernel(total, given, outcome, sends, recvs, sems):
    block, place = lax.axis_index("dp"), lax.axis_index("mp")
    peers = [((block, flip(place, 1)), lax.rem(place, 2))]
    peers.append(((block, flip(place, 2)), lax.div(place, 2)))
    step = 1
    while step < total:
        peers.append(((flip(block, step), place), lax.rem(lax.div(block, step), 2)))
        step *= 2
    greet([peer for peer, _ in peers])
    values = [given[0], given[1], given[2]]
    copies = []
    for stage, (peer, side) in enumerate(peers):
        for index in range(3):
            sends[stage, index] = values[index]
        copy = remote(
            sends.at[stage], recvs.at[stage], sems.at[0, stage], sems.at[1, stage], peer
        )
        copy.wait_recv()
        copies.append(copy)
        ahead = side == 0
        theirs = [recvs[stage, index] for index in range(3)]
        early = [jnp.where(ahead, mine, other) for mine, other in zip(values, theirs)]
        late = [jnp.where(ahead, other, mine) for mine, other in zip(values, theirs)]
        top = jnp.maximum(early[0], late[0])
        values = [
            top,
            early[1] * jnp.exp(early[0] - top) + late[1] * jnp.exp(late[0] - top),
            early[2] + late[2],
        ]
    for index in range(3):
        outcome[index] = values[index]
    for copy in copies:
        copy.wait_send()


def join_totals(top, amount, picked, number):
    total = lax.axis_size("dp")
    stages = 2 + (total - 1).bit_length()
    given = jnp.stack([top, amount, picked]).reshape(3, -1, 128)
    outcome = pl.pallas_call(
        functools.partial(join_totals_kernel, total),
        out_shape=jax.ShapeDtypeStruct(given.shape, jnp.float32),
        in_specs=[VMEM],
        out_specs=VMEM,
        scratch_shapes=[
            pltpu.VMEM((stages,) + given.shape, jnp.float32),
            pltpu.VMEM((stages,) + given.shape, jnp.float32),
            DMA((2, stages)),
        ],
        compiler_params=pltpu.CompilerParams(collective_id=number, has_side_effects=True),
    )(given)
    return outcome.reshape(3, -1)


def head_back_kernel(
    total, parts, rows, gain, quarters, grad_rows, grad_vecs,
    mine, sib_recv, far_recv, beside_recv, end_recv, sems, sib_sems, far_sems, beside_sems,
    end_sems, load_sems,
):
    block, place = lax.axis_index("dp"), lax.axis_index("mp")
    near, far = (block, flip(place, 1)), (block, flip(place, 2))
    beside = (flip(block, 1), place)
    greet([near, far, beside] + [(flip(block, mask), place) for mask in range(2, total, 2)])
    order = [mask for mask in range(total - 1, -1, -1) if mask % 2]
    order += [mask for mask in range(total - 1, -1, -1) if mask % 2 == 0]
    sent, loads, sib, across, over, ends = [], {}, {}, {}, {}, {}
    for mask in order:
        row = flip(block, mask)
        for slot, turn in enumerate((2, 0)):
            loads[mask, slot] = pltpu.make_async_copy(
                parts.at[row, flip(place, turn)], mine.at[mask, slot], load_sems.at[mask, slot]
            )
            loads[mask, slot].start()
            sib[mask, slot] = remote(
                parts.at[row, flip(place, turn + 1)],
                sib_recv.at[mask, slot],
                sib_sems.at[0, mask, slot],
                sib_sems.at[1, mask, slot],
                near,
            )
            sent.append(sib[mask, slot])

    def join(mask, slot, *others):
        value = mine[mask, slot].astype(jnp.float32)
        for other in others:
            value = value + other.astype(jnp.float32)
        return value

    def to_far(mask):
        for slot in (0, 1):
            loads[mask, slot].wait()
            sib[mask, slot].wait_recv()
        mine[mask, 0] = join(mask, 0, sib_recv[mask, 0]).astype(jnp.bfloat16)
        across[mask] = remote(
            mine.at[mask, 0], far_recv.at[mask], far_sems.at[0, mask], far_sems.at[1, mask], far
        )
        sent.append(across[mask])

    def to_beside(mask):
        across[mask].wait_recv()
        mine[mask, 1] = join(mask, 1, sib_recv[mask, 1], far_recv[mask]).astype(jnp.bfloat16)
        over[mask] = remote(
            mine.at[mask, 1],
            beside_recv.at[mask // 2],
            beside_sems.at[0, mask // 2],
            beside_sems.at[1, mask // 2],
            beside,
        )
        sent.append(over[mask])

    def to_end(mask):
        across[mask].wait_recv()
        over[mask + 1].wait_recv()
        value = join(mask, 1, sib_recv[mask, 1], far_recv[mask], beside_recv[mask // 2])
        if mask == 0:
            return value
        mine[mask, 1] = value.astype(jnp.bfloat16)
        ends[mask] = remote(
            mine.at[mask, 1],
            end_recv.at[mask // 2],
            end_sems.at[0, mask // 2],
            end_sems.at[1, mask // 2],
            (flip(block, mask), place),
        )
        sent.append(ends[mask])
        return None

    outcome = None
    for step in range(len(order) + 2):
        if step < len(order):
            to_far(order[step])
        if step >= 2:
            mask = order[step - 2]
            if mask % 2:
                to_beside(mask)
            else:
                outcome = to_end(mask)
    for mask in range(total - 2, 0, -2):
        ends[mask].wait_recv()
        outcome = outcome + end_recv[mask // 2].astype(jnp.float32)
    outcome, grad_gain, grad_shift = norm_rows_back(rows[...], gain[...], outcome)
    grad_rows[...] = outcome
    grad_vecs[0:1] = grad_gain
    grad_vecs[1:2] = grad_shift
    quarters[place] = outcome.astype(jnp.bfloat16)
    sent += share_quarter(place, quarters, near, far, sems)
    for copy in sent:
        copy.wait_send()


def head_back(parts, rows, gain, number):
    height, width = rows.shape
    total = lax.axis_size("dp")
    half = total // 2
    block = (height, width)
    quarters, grad_rows, grad_vecs = pl.pallas_call(
        functools.partial(head_back_kernel, total),
        out_shape=[
            jax.ShapeDtypeStruct((QUARTERS,) + block, jnp.bfloat16),
            jax.ShapeDtypeStruct(block, jnp.float32),
            jax.ShapeDtypeStruct((2, width), jnp.float32),
        ],
        in_specs=[ANY, VMEM, VMEM],
        out_specs=[VMEM] * 3,
        scratch_shapes=[
            pltpu.VMEM((total, 2) + block, jnp.bfloat16),
            pltpu.VMEM((total, 2) + block, jnp.bfloat16),
            pltpu.VMEM((total,) + block, jnp.bfloat16),
            pltpu.VMEM((half,) + block, jnp.bfloat16),
            pltpu.VMEM((half,) + block, jnp.bfloat16),
            DMA((2, 6)),
            DMA((2, total, 2)),
            DMA((2, total)),
            DMA((2, half)),
            DMA((2, half)),
            DMA((total, 2)),
        ],
        compiler_params=pltpu.CompilerParams(
            collective_id=number, has_side_effects=True, vmem_limit_bytes=60 * 2**20
        ),
    )(parts.reshape((total, QUARTERS) + block), rows, gain.reshape(1, -1))
    return quarters.reshape(-1, width), grad_rows, grad_vecs


def shift_pairs(total, step):
    return [(index, (index + step) % total) for index in range(total)]


def spread_rows(table):
    total = lax.axis_size("dp")
    place = lax.axis_index("dp")
    width = table.shape[1]
    part = table.shape[0] // total
    whole = jnp.zeros((part, width * total), table.dtype)
    for step in range(total):
        block = lax.dynamic_slice_in_dim(table, (place + step) % total * part, part, 0)
        if step:
            block = lax.ppermute(block, "dp", shift_pairs(total, step))
        whole = lax.dynamic_update_slice_in_dim(
            whole, block, (place - step) % total * width, 1
        )
    return whole


def return_rows(rows, height):
    total = lax.axis_size("dp")
    place = lax.axis_index("dp")
    part = rows.shape[0]
    width = rows.shape[1] // total
    whole = jnp.zeros((height, width), rows.dtype)
    for step in range(total):
        block = lax.dynamic_slice_in_dim(rows, (place + step) % total * width, width, 1)
        if step:
            block = lax.ppermute(block, "dp", shift_pairs(total, step))
        whole = lax.dynamic_update_slice_in_dim(
            whole, block, (place - step) % total * part, 0
        )
    return whole


def local(
    tokens,
    memory,
    segment_ids,
    answer_ids,
    loss_mask,
    doc_scores,
    slot_place,
    self_query,
    self_key,
    self_value,
    self_out,
    cross_query,
    cross_key,
    cross_value,
    cross_out,
    feed_up,
    feed_down,
    gain_self,
    shift_self,
    gain_cross,
    shift_cross,
    gain_feed,
    shift_feed,
    embedding,
):
    row_count, row_len = segment_ids.shape
    table_rows = spread_rows(embedding)
    span = SEG_ROW * MEM
    quarter = tokens.shape[0] // QUARTERS
    inputs = lax.dynamic_slice_in_dim(tokens, lax.axis_index("mp") * quarter, quarter, 0)
    places = jnp.arange(row_len, dtype=jnp.int32)
    owners = jnp.arange(span, dtype=jnp.int32) // MEM
    self_masks = [
        (segment_ids[0][:, None] == segment_ids[0][None, :]) & (places[None, :] <= places[:, None])
    ]
    cross_masks = [segment_ids[0][:, None] == owners[None, :]]
    query_self = product(tokens, self_query).astype(jnp.bfloat16)
    key_self = product(tokens, self_key).astype(jnp.bfloat16)
    value_self = product(tokens, self_value).astype(jnp.bfloat16)
    self_mix, self_totals = run_rows(query_self, key_self, value_self, self_masks)
    first_low, first_norm, rows_self, ids_all = mix_norm(
        self_mix, self_out, inputs, gain_self, shift_self, 0,
        jnp.concatenate([segment_ids, answer_ids, loss_mask], axis=0),
    )
    segments_all, answers_all, kept_all = (
        ids_all[:, kind * row_count : (kind + 1) * row_count].reshape(-1, row_len)
        for kind in range(3)
    )
    query_cross = product(first_low, cross_query).astype(jnp.bfloat16)
    key_cross = product(memory, cross_key).astype(jnp.bfloat16)
    value_cross = product(memory, cross_value).astype(jnp.bfloat16)
    cross_mix, cross_totals = run_rows(query_cross, key_cross, value_cross, cross_masks)
    second_low, second_norm, rows_cross = mix_norm(
        cross_mix, cross_out, first_norm, gain_cross, shift_cross, 1
    )
    feed_pre = product(second_low, feed_up)
    feed_act = gelu_exact(feed_pre).astype(jnp.bfloat16)
    states, rows_feed = feed_norm(
        feed_act, feed_down, second_norm, gain_feed, shift_feed, 2
    )
    vocab_local = embedding.shape[0]
    part = table_rows.shape[0]
    logits = product_nt(states, table_rows)
    offset = lax.axis_index("mp") * vocab_local + lax.axis_index("dp") * part
    local_target = answers_all.reshape(-1) - offset
    vocab_ids = jnp.arange(part, dtype=jnp.int32)
    answer_hot = local_target[:, None] == vocab_ids[None, :]
    picked_part = jnp.sum(jnp.where(answer_hot, logits, 0.0), axis=1)
    local_top = jnp.max(logits, axis=1)
    global_top, global_sum, picked = join_totals(
        local_top, jnp.sum(jnp.exp(logits - local_top[:, None]), axis=1), picked_part, 3
    )
    log_total = global_top + jnp.log(global_sum)
    keeper = kept_all.astype(jnp.float32)
    token_logp = (picked - log_total).reshape(keeper.shape) * keeper
    seg_hot = (
        segments_all[:, :, None] == jnp.arange(SEG_ROW, dtype=jnp.int32)[None, None, :]
    ).astype(jnp.float32)
    seg_sums = jnp.sum(seg_hot * token_logp[:, :, None], axis=1)
    counts = jnp.sum(seg_hot * keeper[:, :, None], axis=1)
    likely_all = (seg_sums / jnp.maximum(counts, 1.0)).reshape(-1)
    place_hot = (
        slot_place[:, None] == jnp.arange(likely_all.shape[0], dtype=jnp.int32)[None, :]
    ).astype(jnp.float32)

    def marginal(scores, likely):
        joint_score = jax.nn.log_softmax(scores, axis=1) + jnp.dot(
            place_hot, likely, precision=highest
        ).reshape(scores.shape)
        return -jnp.sum(jax.nn.logsumexp(joint_score, axis=1))

    loss, pullback = jax.vjp(marginal, doc_scores, likely_all)
    grad_scores, grad_likely = pullback(jnp.ones_like(loss))
    per_segment = grad_likely.reshape(counts.shape) / jnp.maximum(counts, 1.0)
    grad_logp = (jnp.sum(seg_hot * per_segment[:, None, :], axis=2) * keeper).reshape(-1)
    grad_logits = (
        grad_logp[:, None]
        * (answer_hot.astype(jnp.float32) - jnp.exp(logits - log_total[:, None]))
    ).astype(jnp.bfloat16)
    grad_branch, grad_res3, grad_vecs_feed = head_back(
        product(grad_logits, table_rows).astype(jnp.bfloat16), rows_feed, gain_feed, 4
    )
    grad_table = return_rows(
        product_tn(grad_logits, states).astype(jnp.bfloat16), vocab_local
    ).astype(jnp.float32)
    grad_feed_down = product_tn(feed_act, grad_branch)
    grad_act = product_nt(grad_branch, feed_down)
    act_value, act_pull = jax.vjp(gelu_exact, feed_pre)
    grad_pre = act_pull(grad_act)[0].astype(jnp.bfloat16)
    grad_feed_up = product_tn(second_low, grad_pre)
    grad_branch, grad_res2, grad_vecs_cross = back_norm(
        grad_pre, feed_up, grad_res3, rows_cross, gain_cross, 5
    )
    grad_cross_out = product_tn(cross_mix, grad_branch)
    grad_mix = product_nt(grad_branch, cross_out).astype(jnp.bfloat16)
    cross_gq, cross_gk, cross_gv = back_rows(
        query_cross, key_cross, value_cross, cross_masks, cross_totals, grad_mix
    )
    grad_cross_query = product_tn(first_low, cross_gq)
    grad_cross_key = product_tn(memory, cross_gk)
    grad_cross_value = product_tn(memory, cross_gv)
    grad_memory_part = product_nt(cross_gk, cross_key) + product_nt(cross_gv, cross_value)
    grad_branch, _, grad_vecs_self = back_norm(
        cross_gq, cross_query, grad_res2, rows_self, gain_self, 6
    )
    grad_self_out = product_tn(self_mix, grad_branch)
    grad_mix = product_nt(grad_branch, self_out).astype(jnp.bfloat16)
    self_gq, self_gk, self_gv = back_rows(
        query_self, key_self, value_self, self_masks, self_totals, grad_mix
    )
    grad_self_query = product_tn(tokens, self_gq)
    grad_self_key = product_tn(tokens, self_gk)
    grad_self_value = product_tn(tokens, self_gv)
    grad_input_part = (
        product_nt(self_gq, self_query)
        + product_nt(self_gk, self_key)
        + product_nt(self_gv, self_value)
    )
    input_share, memory_share = (
        lax.psum_scatter(
            grad_input_part.astype(jnp.bfloat16), "mp", scatter_dimension=1, tiled=True
        ).astype(jnp.float32),
        lax.psum_scatter(
            grad_memory_part.astype(jnp.bfloat16), "mp", scatter_dimension=1, tiled=True
        ).astype(jnp.float32),
    )
    column_start = lax.axis_index("mp") * input_share.shape[1]
    grad_tokens = input_share + lax.dynamic_slice_in_dim(
        grad_branch, column_start, input_share.shape[1], 1
    ).astype(jnp.float32)
    grad_vecs = lax.psum(
        jnp.concatenate([grad_vecs_self, grad_vecs_cross, grad_vecs_feed], axis=0), ("dp", "mp")
    )
    (
        sum_sq,
        sum_sk,
        sum_sv,
        sum_so,
        sum_cq,
        sum_ck,
        sum_cv,
        sum_co,
        sum_up,
        sum_down,
    ) = (
        lax.psum(grad_self_query.astype(jnp.bfloat16), "dp").astype(jnp.float32),
        lax.psum(grad_self_key.astype(jnp.bfloat16), "dp").astype(jnp.float32),
        lax.psum(grad_self_value.astype(jnp.bfloat16), "dp").astype(jnp.float32),
        lax.psum(grad_self_out.astype(jnp.bfloat16), "dp").astype(jnp.float32),
        lax.psum(grad_cross_query.astype(jnp.bfloat16), "dp").astype(jnp.float32),
        lax.psum(grad_cross_key.astype(jnp.bfloat16), "dp").astype(jnp.float32),
        lax.psum(grad_cross_value.astype(jnp.bfloat16), "dp").astype(jnp.float32),
        lax.psum(grad_cross_out.astype(jnp.bfloat16), "dp").astype(jnp.float32),
        lax.psum(grad_feed_up.astype(jnp.bfloat16), "dp").astype(jnp.float32),
        lax.psum(grad_feed_down.astype(jnp.bfloat16), "dp").astype(jnp.float32),
    )
    return (
        loss,
        grad_tokens,
        memory_share,
        sum_sq,
        sum_sk,
        sum_sv,
        sum_so,
        sum_cq,
        sum_ck,
        sum_cv,
        sum_co,
        sum_up,
        sum_down,
        *grad_vecs,
        grad_table,
        grad_scores,
    )


def solution(mesh):
    return jax.shard_map(
        local,
        mesh=mesh,
        in_specs=(
            P("dp", None),
            P("dp", None),
            P("dp", None),
            P("dp", None),
            P("dp", None),
            P(),
            P(),
            P(None, "mp"),
            P(None, "mp"),
            P(None, "mp"),
            P("mp", None),
            P(None, "mp"),
            P(None, "mp"),
            P(None, "mp"),
            P("mp", None),
            P(None, "mp"),
            P("mp", None),
            P(),
            P(),
            P(),
            P(),
            P(),
            P(),
            P("mp", "dp"),
        ),
        out_specs=(
            P(),
            P("dp", "mp"),
            P("dp", "mp"),
            P(None, "mp"),
            P(None, "mp"),
            P(None, "mp"),
            P("mp", None),
            P(None, "mp"),
            P(None, "mp"),
            P(None, "mp"),
            P("mp", None),
            P(None, "mp"),
            P("mp", None),
            P(),
            P(),
            P(),
            P(),
            P(),
            P(),
            P("mp", "dp"),
            P(),
        ),
        check_vma=False,
    )
```

```python
import functools

import jax
import jax.numpy as jnp
from jax import lax
from jax.experimental import pallas as pl
from jax.experimental.pallas import tpu as pltpu
from jax.sharding import PartitionSpec as P

HEAD_DIM = 64
SEG_ROW = 8
MEM = 128


masked_score = -1e30
norm_eps = 1e-05
highest = lax.Precision.HIGHEST


def product(left_side, right_side):
    return jnp.dot(left_side, right_side, preferred_element_type=jnp.float32)


def product_tn(left_side, right_side):
    return lax.dot_general(
        left_side, right_side, (((0,), (0,)), ((), ())), preferred_element_type=jnp.float32
    )


def product_nt(left_side, right_side):
    return lax.dot_general(
        left_side, right_side, (((1,), (1,)), ((), ())), preferred_element_type=jnp.float32
    )


def gelu_exact(inputs):
    return jax.nn.gelu(inputs, approximate=False)


def split_heads(matrix):
    return matrix.reshape(matrix.shape[0], matrix.shape[1] // HEAD_DIM, HEAD_DIM)


def attention_scores(queries, keys, allowed):
    scores = jnp.einsum(
        "qhd,khd->hqk", split_heads(queries), split_heads(keys), preferred_element_type=jnp.float32
    ) * HEAD_DIM ** (-0.5)
    return jnp.where(allowed[None], scores, masked_score)


def attend_forward(queries, keys, values, allowed):
    scores = attention_scores(queries, keys, allowed)
    largest = jnp.max(scores, axis=-1, keepdims=True)
    weights = jnp.exp(scores - largest)
    total = jnp.sum(weights, axis=-1, keepdims=True)
    probabilities = (weights / total).astype(jnp.bfloat16)
    mixed_out = jnp.einsum(
        "hqk,khd->qhd", probabilities, split_heads(values), preferred_element_type=jnp.float32
    )
    return (mixed_out.reshape(queries.shape[0], queries.shape[1]), largest + jnp.log(total))


def attend_backward(queries, keys, values, allowed, log_total, grad_out):
    scores = attention_scores(queries, keys, allowed)
    probabilities = jnp.exp(scores - log_total)
    heads_grad = split_heads(grad_out)
    grad_prob = jnp.einsum(
        "qhd,khd->hqk", heads_grad, split_heads(values), preferred_element_type=jnp.float32
    )
    grad_values = jnp.einsum(
        "hqk,qhd->khd",
        probabilities.astype(jnp.bfloat16),
        heads_grad,
        preferred_element_type=jnp.float32,
    )
    row_dot = jnp.sum(grad_prob * probabilities, axis=-1, keepdims=True)
    grad_scores = (probabilities * (grad_prob - row_dot)).astype(jnp.bfloat16)
    grad_queries = jnp.einsum(
        "hqk,khd->qhd", grad_scores, split_heads(keys), preferred_element_type=jnp.float32
    ) * HEAD_DIM ** (-0.5)
    grad_keys = jnp.einsum(
        "hqk,qhd->khd", grad_scores, split_heads(queries), preferred_element_type=jnp.float32
    ) * HEAD_DIM ** (-0.5)
    width = queries.shape[1]
    return (
        grad_queries.reshape(-1, width).astype(jnp.bfloat16),
        grad_keys.reshape(-1, width).astype(jnp.bfloat16),
        grad_values.reshape(-1, width).astype(jnp.bfloat16),
    )


def run_rows(queries, keys, values, masks):
    mixed_out, log_total = attend_forward(queries, keys, values, masks[0])
    totals = [log_total]
    return (mixed_out.astype(jnp.bfloat16), totals)


def back_rows(queries, keys, values, masks, totals, grad_mix):
    parts_query, parts_key, parts_value = ([], [], [])
    grad_query, grad_key, grad_value = attend_backward(
        queries, keys, values, masks[0], totals[0], grad_mix
    )
    parts_query.append(grad_query)
    parts_key.append(grad_key)
    parts_value.append(grad_value)
    return (parts_query[0], parts_key[0], parts_value[0])


MESH = pl.DeviceIdType.MESH
VMEM = pl.BlockSpec(memory_space=pltpu.VMEM)
ANY = pl.BlockSpec(memory_space=pl.ANY)
DMA = pltpu.SemaphoreType.DMA
QUARTERS = 4


def flip(index, mask):
    for bit in range(mask.bit_length()):
        if mask >> bit & 1:
            step = 1 << bit
            index = index + step * (1 - 2 * lax.rem(lax.div(index, step), 2))
    return index


def greet(peers):
    barrier = pltpu.get_barrier_semaphore()
    for peer in peers:
        pl.semaphore_signal(barrier, inc=1, device_id=peer, device_id_type=MESH)
    pl.semaphore_wait(barrier, len(peers))


def remote(source, target, send_sem, recv_sem, peer):
    copy = pltpu.make_async_remote_copy(
        src_ref=source,
        dst_ref=target,
        send_sem=send_sem,
        recv_sem=recv_sem,
        device_id=peer,
        device_id_type=MESH,
    )
    copy.start()
    return copy


def sum_quarter(place, block_of, near, far, sib_send, sib_recv, far_send, far_recv, sems):
    copies = []
    for slot, mask in enumerate((3, 1)):
        sib_send[slot] = block_of(flip(place, mask)).astype(jnp.bfloat16)
        copies.append(
            remote(
                sib_send.at[slot], sib_recv.at[slot], sems.at[0, slot], sems.at[1, slot], near
            )
        )
    distant = block_of(flip(place, 2))
    own = block_of(place)
    copies[0].wait_recv()
    far_send[...] = (distant + sib_recv[0].astype(jnp.float32)).astype(jnp.bfloat16)
    last = remote(far_send, far_recv, sems.at[0, 2], sems.at[1, 2], far)
    copies[1].wait_recv()
    own = own + sib_recv[1].astype(jnp.float32)
    last.wait_recv()
    own = own + far_recv[...].astype(jnp.float32)
    return own, copies + [last]


def share_quarter(place, quarters, near, far, sems):
    here = quarters.at[place]
    to_far = remote(here, here, sems.at[0, 3], sems.at[1, 3], far)
    to_near = remote(here, here, sems.at[0, 4], sems.at[1, 4], near)
    to_far.wait_recv()
    there = quarters.at[flip(place, 2)]
    passed = remote(there, there, sems.at[0, 5], sems.at[1, 5], near)
    to_near.wait_recv()
    passed.wait_recv()
    return [to_far, to_near, passed]


def table_copies(masks, back, source, target, sems):
    block, place = lax.axis_index("dp"), lax.axis_index("mp")
    total = lax.axis_size("dp")
    part, width = (source if back else target).shape[0], (target if back else source).shape[1]
    copies = []
    for slot, mask in enumerate(masks):
        other = flip(block, mask)
        here = pl.ds(pl.multiple_of((block if back else other) * part, part), part)
        there = pl.ds(pl.multiple_of((other if back else block) * width, width), width)
        if back:
            start, end = source.at[:, there], target.at[here, :]
        else:
            start, end = source.at[here, :], target.at[:, there]
        if mask:
            copies.append(remote(start, end, sems.at[0, slot], sems.at[1, slot], (other, place)))
        else:
            copy = pltpu.make_async_copy(start, end, sems.at[0, slot])
            copy.start()
            copies.append(copy)
    return copies


def finish(copies):
    for copy in copies:
        copy.wait()


def split_refs(refs, *counts):
    groups, start = [], 0
    for count in counts:
        groups.append(list(refs[start : start + count]))
        start += count
    return groups


def norm_rows(rows, gain, shift):
    center = rows - jnp.mean(rows, axis=-1, keepdims=True)
    spread = jnp.mean(center * center, axis=-1, keepdims=True)
    return center * lax.rsqrt(spread + norm_eps) * gain + shift


def norm_rows_back(rows, gain, grad):
    center = rows - jnp.mean(rows, axis=-1, keepdims=True)
    scale = lax.rsqrt(jnp.mean(center * center, axis=-1, keepdims=True) + norm_eps)
    normed = center * scale
    inner = grad * gain
    grad_rows = scale * (
        inner
        - jnp.mean(inner, axis=-1, keepdims=True)
        - normed * jnp.mean(inner * normed, axis=-1, keepdims=True)
    )
    return (
        grad_rows,
        jnp.sum(grad * normed, axis=0, keepdims=True),
        jnp.sum(grad, axis=0, keepdims=True),
    )


def rows_of(ref, height, index):
    return ref[pl.ds(pl.multiple_of(index * height, height), height), :]


def exchange_scratch(height, width):
    return [
        pltpu.VMEM((2, height, width), jnp.bfloat16),
        pltpu.VMEM((2, height, width), jnp.bfloat16),
        pltpu.VMEM((height, width), jnp.bfloat16),
        pltpu.VMEM((height, width), jnp.bfloat16),
        DMA((2, 6)),
    ]


def mix_norm_kernel(total, with_ids, masks, chained, *refs):
    (left, weight, kept, gain, shift), ids, table, (quarters, normed, rows), ids_all, wide, refs = (
        split_refs(
            refs, 5, with_ids, (1 + chained) * bool(masks), 3, with_ids, bool(masks), len(refs)
        )
    )
    sib_send, sib_recv, far_send, far_recv, sems = refs[:5]
    refs = refs[5:]
    block, place = lax.axis_index("dp"), lax.axis_index("mp")
    near, far = (block, flip(place, 1)), (block, flip(place, 2))
    height = kept.shape[0]
    others = range(1, total) if with_ids else [mask for mask in masks if mask]
    greet([near, far] + [(flip(block, mask), place) for mask in others])
    copies = []
    if with_ids:
        ids_sems, ids_local = refs[:2]
        refs = refs[2:]
        own = pltpu.make_async_copy(ids[0], ids_all[0].at[block], ids_local)
        own.start()
        copies.append(own)
        for mask in range(1, total):
            copies.append(
                remote(
                    ids[0], ids_all[0].at[block], ids_sems.at[0, mask], ids_sems.at[1, mask],
                    (flip(block, mask), place),
                )
            )

    def block_of(index):
        return jnp.dot(
            rows_of(left, height, index), weight[...], preferred_element_type=jnp.float32
        )

    branch, sent = sum_quarter(
        place, block_of, near, far, sib_send, sib_recv, far_send, far_recv, sems
    )
    if masks:
        copies += table_copies(masks, False, table[0], wide[0], refs[0])
    outcome = kept[...].astype(jnp.float32) + branch
    rows[...] = outcome
    outcome = norm_rows(outcome, gain[...], shift[...])
    normed[...] = outcome
    quarters[place] = outcome.astype(jnp.bfloat16)
    sent += share_quarter(place, quarters, near, far, sems)
    finish(copies)
    for copy in sent:
        copy.wait_send()


def mix_norm(left, weight, kept, gain, shift, number, ids=None, table=None, wide=None, masks=()):
    height, width = kept.shape
    total = lax.axis_size("dp")
    quarter = jax.ShapeDtypeStruct((height, width), jnp.float32)
    out_shape = [
        jax.ShapeDtypeStruct((QUARTERS, height, width), jnp.bfloat16), quarter, quarter
    ]
    out_specs = [VMEM] * 3
    given = [left, weight, kept, gain.reshape(1, -1), shift.reshape(1, -1)]
    in_specs = [VMEM] * 5
    scratch = exchange_scratch(height, width)
    aliases = {}
    if ids is not None:
        given.append(ids)
        in_specs.append(VMEM)
        out_shape.append(jax.ShapeDtypeStruct((total,) + ids.shape, ids.dtype))
        out_specs.append(VMEM)
        scratch += [DMA((2, total)), DMA]
    if masks:
        given.append(table)
        in_specs.append(ANY)
        if wide is not None:
            aliases = {len(given): len(out_shape)}
            given.append(wide)
            in_specs.append(ANY)
        out_shape.append(
            jax.ShapeDtypeStruct((table.shape[0] // total, table.shape[1] * total), table.dtype)
        )
        out_specs.append(ANY)
        scratch.append(DMA((2, len(masks))))
    outcome = pl.pallas_call(
        functools.partial(
            mix_norm_kernel, total, int(ids is not None), tuple(masks), int(wide is not None)
        ),
        out_shape=out_shape,
        in_specs=in_specs,
        out_specs=out_specs,
        scratch_shapes=scratch,
        input_output_aliases=aliases,
        compiler_params=pltpu.CompilerParams(
            collective_id=number, has_side_effects=True, vmem_limit_bytes=48 * 2**20
        ),
    )(*given)
    return (outcome[0].reshape(-1, width),) + tuple(outcome[1:])


def feed_norm_kernel(total, early, late, *refs):
    (left, weight, kept, gain, shift), table, (states, rows), wide, refs = split_refs(
        refs, 5, 2 * bool(early), 2, bool(early), len(refs)
    )
    low, sib_send, sib_recv, far_send, far_recv, sems, hops, own_sem = refs[:8]
    block, place = lax.axis_index("dp"), lax.axis_index("mp")
    near, far = (block, flip(place, 1)), (block, flip(place, 2))
    beside = (flip(block, 1), place)
    height = kept.shape[0]
    others = range(1, total) if early else [1] + list(range(2, total, 2))
    greet([near, far] + [(flip(block, mask), place) for mask in others])

    def block_of(index):
        return jnp.dot(
            rows_of(left, height, index), weight[...], preferred_element_type=jnp.float32
        )

    moved = []
    if early:
        moved = table_copies(early, False, table[0], wide[0], refs[8])
    branch, sent = sum_quarter(
        place, block_of, near, far, sib_send, sib_recv, far_send, far_recv, sems
    )
    outcome = kept[...] + branch
    rows[...] = outcome
    low[...] = norm_rows(outcome, gain[...], shift[...]).astype(jnp.bfloat16)
    own = pltpu.make_async_copy(low, states.at[block, place], own_sem)
    own.start()
    across = flip(place, 2)

    def hop(kind, mask, source, peer, row, column):
        copy = remote(
            source, states.at[row, column], hops.at[0, kind, mask], hops.at[1, kind, mask], peer
        )
        sent.append(copy)
        return copy

    first = {}
    for mask in range(2, total, 2):
        first[mask] = hop(0, mask, low, (flip(block, mask), place), block, place)
    if late:
        moved += table_copies(late, False, table[0], wide[0], refs[9])
    over = {}
    ends = []

    def pass_on(mask):
        over[mask].wait_recv()
        row = flip(block, mask)
        ends.append(hop(3, mask, states.at[row, across], near, row, across))

    for mask in range(total):
        row = flip(block, mask)
        if mask:
            first[mask].wait_recv()
        source = states.at[row, place] if mask else low
        if mask % 2 == 0:
            first[mask + 1] = hop(0, mask + 1, source, beside, row, place)
        over[mask] = hop(1, mask, source, far, row, place)
        ends.append(hop(2, mask, source, near, row, place))
        if mask >= 2:
            pass_on(mask - 2)
    for mask in range(max(total - 2, 0), total):
        pass_on(mask)
    for copy in ends:
        copy.wait_recv()
    for copy in sent:
        copy.wait_send()
    own.wait()
    finish(moved)


def feed_norm(left, weight, kept, gain, shift, number, table=None, wide=None, early=(), late=()):
    height, width = kept.shape
    total = lax.axis_size("dp")
    given = [left, weight, kept, gain.reshape(1, -1), shift.reshape(1, -1)]
    in_specs = [VMEM] * 5
    out_shape = [
        jax.ShapeDtypeStruct((total, QUARTERS, height, width), jnp.bfloat16),
        jax.ShapeDtypeStruct((height, width), jnp.float32),
    ]
    out_specs = [ANY, VMEM]
    scratch = [pltpu.VMEM((height, width), jnp.bfloat16)] + exchange_scratch(height, width)
    scratch += [DMA((2, 4, total)), DMA]
    aliases = {}
    if early:
        given += [table, wide]
        in_specs += [ANY] * 2
        out_shape.append(jax.ShapeDtypeStruct(wide.shape, wide.dtype))
        out_specs.append(ANY)
        aliases = {6: 2}
        scratch += [DMA((2, len(early))), DMA((2, len(late)))]
    outcome = pl.pallas_call(
        functools.partial(feed_norm_kernel, total, tuple(early), tuple(late)),
        out_shape=out_shape,
        in_specs=in_specs,
        out_specs=out_specs,
        scratch_shapes=scratch,
        input_output_aliases=aliases,
        compiler_params=pltpu.CompilerParams(
            collective_id=number, has_side_effects=True, vmem_limit_bytes=48 * 2**20
        ),
    )(*given)
    return (outcome[0].reshape(-1, width),) + tuple(outcome[1:])


def back_norm_kernel(masks, *refs):
    (left, weight, kept, rows, gain), table, (quarters, grad_rows, grad_vecs), narrow, refs = (
        split_refs(refs, 5, 2 * bool(masks), 3, bool(masks), len(refs))
    )
    sib_send, sib_recv, far_send, far_recv, sems = refs[:5]
    block, place = lax.axis_index("dp"), lax.axis_index("mp")
    near, far = (block, flip(place, 1)), (block, flip(place, 2))
    height = kept.shape[0]
    greet([near, far] + [(flip(block, mask), place) for mask in masks])
    moved = []
    if masks:
        moved = table_copies(masks, True, table[0], narrow[0], refs[5])

    def block_of(index):
        return lax.dot_general(
            rows_of(left, height, index),
            weight[...],
            (((1,), (1,)), ((), ())),
            preferred_element_type=jnp.float32,
        )

    branch, sent = sum_quarter(
        place, block_of, near, far, sib_send, sib_recv, far_send, far_recv, sems
    )
    outcome, grad_gain, grad_shift = norm_rows_back(rows[...], gain[...], kept[...] + branch)
    grad_rows[...] = outcome
    grad_vecs[0:1] = grad_gain
    grad_vecs[1:2] = grad_shift
    quarters[place] = outcome.astype(jnp.bfloat16)
    sent += share_quarter(place, quarters, near, far, sems)
    for copy in sent:
        copy.wait_send()
    finish(moved)


def back_norm(left, weight, kept, rows, gain, number, table=None, narrow=None, masks=()):
    height, width = kept.shape
    given = [left, weight, kept, rows, gain.reshape(1, -1)]
    in_specs = [VMEM] * 5
    out_shape = [
        jax.ShapeDtypeStruct((QUARTERS, height, width), jnp.bfloat16),
        jax.ShapeDtypeStruct((height, width), jnp.float32),
        jax.ShapeDtypeStruct((2, width), jnp.float32),
    ]
    out_specs = [VMEM] * 3
    scratch = exchange_scratch(height, width)
    aliases = {}
    if masks:
        given += [table, narrow]
        in_specs += [ANY] * 2
        out_shape.append(jax.ShapeDtypeStruct(narrow.shape, narrow.dtype))
        out_specs.append(ANY)
        aliases = {6: 3}
        scratch.append(DMA((2, len(masks))))
    outcome = pl.pallas_call(
        functools.partial(back_norm_kernel, tuple(masks)),
        out_shape=out_shape,
        in_specs=in_specs,
        out_specs=out_specs,
        scratch_shapes=scratch,
        input_output_aliases=aliases,
        compiler_params=pltpu.CompilerParams(
            collective_id=number, has_side_effects=True, vmem_limit_bytes=48 * 2**20
        ),
    )(*given)
    return (outcome[0].reshape(-1, width),) + tuple(outcome[1:])


def join_totals_kernel(total, given, outcome, sends, recvs, sems):
    block, place = lax.axis_index("dp"), lax.axis_index("mp")
    peers = [((block, flip(place, 1)), lax.rem(place, 2))]
    peers.append(((block, flip(place, 2)), lax.div(place, 2)))
    step = 1
    while step < total:
        peers.append(((flip(block, step), place), lax.rem(lax.div(block, step), 2)))
        step *= 2
    greet([peer for peer, _ in peers])
    values = [given[0], given[1], given[2]]
    copies = []
    for stage, (peer, side) in enumerate(peers):
        for index in range(3):
            sends[stage, index] = values[index]
        copy = remote(
            sends.at[stage], recvs.at[stage], sems.at[0, stage], sems.at[1, stage], peer
        )
        copy.wait_recv()
        copies.append(copy)
        ahead = side == 0
        theirs = [recvs[stage, index] for index in range(3)]
        early = [jnp.where(ahead, mine, other) for mine, other in zip(values, theirs)]
        late = [jnp.where(ahead, other, mine) for mine, other in zip(values, theirs)]
        top = jnp.maximum(early[0], late[0])
        values = [
            top,
            early[1] * jnp.exp(early[0] - top) + late[1] * jnp.exp(late[0] - top),
            early[2] + late[2],
        ]
    for index in range(3):
        outcome[index] = values[index]
    for copy in copies:
        copy.wait_send()


def join_totals(top, amount, picked, number):
    total = lax.axis_size("dp")
    stages = 2 + (total - 1).bit_length()
    given = jnp.stack([top, amount, picked]).reshape(3, -1, 128)
    outcome = pl.pallas_call(
        functools.partial(join_totals_kernel, total),
        out_shape=jax.ShapeDtypeStruct(given.shape, jnp.float32),
        in_specs=[VMEM],
        out_specs=VMEM,
        scratch_shapes=[
            pltpu.VMEM((stages,) + given.shape, jnp.float32),
            pltpu.VMEM((stages,) + given.shape, jnp.float32),
            DMA((2, stages)),
        ],
        compiler_params=pltpu.CompilerParams(collective_id=number, has_side_effects=True),
    )(given)
    return outcome.reshape(3, -1)


def head_back_kernel(total, masks, *refs):
    (parts, rows, gain), table, (quarters, grad_rows, grad_vecs), narrow, refs = split_refs(
        refs, 3, bool(masks), 3, bool(masks), len(refs)
    )
    mine, sib_recv, far_recv, beside_recv, end_recv, sems = refs[:6]
    sib_sems, far_sems, beside_sems, end_sems, load_sems = refs[6:11]
    block, place = lax.axis_index("dp"), lax.axis_index("mp")
    near, far = (block, flip(place, 1)), (block, flip(place, 2))
    beside = (flip(block, 1), place)
    others = range(1, total) if masks else [1] + list(range(2, total, 2))
    greet([near, far] + [(flip(block, mask), place) for mask in others])
    moved = []
    if masks:
        moved = table_copies(masks, True, table[0], narrow[0], refs[11])
    order = [mask for mask in range(total - 1, -1, -1) if mask % 2]
    order += [mask for mask in range(total - 1, -1, -1) if mask % 2 == 0]
    sent, loads, sib, across, over, ends = [], {}, {}, {}, {}, {}
    for mask in order:
        row = flip(block, mask)
        for slot, turn in enumerate((2, 0)):
            loads[mask, slot] = pltpu.make_async_copy(
                parts.at[row, flip(place, turn)], mine.at[mask, slot], load_sems.at[mask, slot]
            )
            loads[mask, slot].start()
            sib[mask, slot] = remote(
                parts.at[row, flip(place, turn + 1)],
                sib_recv.at[mask, slot],
                sib_sems.at[0, mask, slot],
                sib_sems.at[1, mask, slot],
                near,
            )
            sent.append(sib[mask, slot])

    def join(mask, slot, *others):
        value = mine[mask, slot].astype(jnp.float32)
        for other in others:
            value = value + other.astype(jnp.float32)
        return value

    def to_far(mask):
        for slot in (0, 1):
            loads[mask, slot].wait()
            sib[mask, slot].wait_recv()
        mine[mask, 0] = join(mask, 0, sib_recv[mask, 0]).astype(jnp.bfloat16)
        across[mask] = remote(
            mine.at[mask, 0], far_recv.at[mask], far_sems.at[0, mask], far_sems.at[1, mask], far
        )
        sent.append(across[mask])

    def to_beside(mask):
        across[mask].wait_recv()
        mine[mask, 1] = join(mask, 1, sib_recv[mask, 1], far_recv[mask]).astype(jnp.bfloat16)
        over[mask] = remote(
            mine.at[mask, 1],
            beside_recv.at[mask // 2],
            beside_sems.at[0, mask // 2],
            beside_sems.at[1, mask // 2],
            beside,
        )
        sent.append(over[mask])

    def to_end(mask):
        across[mask].wait_recv()
        over[mask + 1].wait_recv()
        value = join(mask, 1, sib_recv[mask, 1], far_recv[mask], beside_recv[mask // 2])
        if mask == 0:
            return value
        mine[mask, 1] = value.astype(jnp.bfloat16)
        ends[mask] = remote(
            mine.at[mask, 1],
            end_recv.at[mask // 2],
            end_sems.at[0, mask // 2],
            end_sems.at[1, mask // 2],
            (flip(block, mask), place),
        )
        sent.append(ends[mask])
        return None

    outcome = None
    for step in range(len(order) + 2):
        if step < len(order):
            to_far(order[step])
        if step >= 2:
            mask = order[step - 2]
            if mask % 2:
                to_beside(mask)
            else:
                outcome = to_end(mask)
    for mask in range(total - 2, 0, -2):
        ends[mask].wait_recv()
        outcome = outcome + end_recv[mask // 2].astype(jnp.float32)
    outcome, grad_gain, grad_shift = norm_rows_back(rows[...], gain[...], outcome)
    grad_rows[...] = outcome
    grad_vecs[0:1] = grad_gain
    grad_vecs[1:2] = grad_shift
    quarters[place] = outcome.astype(jnp.bfloat16)
    sent += share_quarter(place, quarters, near, far, sems)
    for copy in sent:
        copy.wait_send()
    finish(moved)


def head_back(parts, rows, gain, number, table=None, masks=()):
    height, width = rows.shape
    total = lax.axis_size("dp")
    half = total // 2
    block = (height, width)
    given = [parts.reshape((total, QUARTERS) + block), rows, gain.reshape(1, -1)]
    in_specs = [ANY, VMEM, VMEM]
    out_shape = [
        jax.ShapeDtypeStruct((QUARTERS,) + block, jnp.bfloat16),
        jax.ShapeDtypeStruct(block, jnp.float32),
        jax.ShapeDtypeStruct((2, width), jnp.float32),
    ]
    out_specs = [VMEM] * 3
    scratch = [
        pltpu.VMEM((total, 2) + block, jnp.bfloat16),
        pltpu.VMEM((total, 2) + block, jnp.bfloat16),
        pltpu.VMEM((total,) + block, jnp.bfloat16),
        pltpu.VMEM((half,) + block, jnp.bfloat16),
        pltpu.VMEM((half,) + block, jnp.bfloat16),
        DMA((2, 6)),
        DMA((2, total, 2)),
        DMA((2, total)),
        DMA((2, half)),
        DMA((2, half)),
        DMA((total, 2)),
    ]
    if masks:
        given.append(table)
        in_specs.append(ANY)
        out_shape.append(
            jax.ShapeDtypeStruct((table.shape[0] * total, table.shape[1] // total), table.dtype)
        )
        out_specs.append(ANY)
        scratch.append(DMA((2, len(masks))))
    outcome = pl.pallas_call(
        functools.partial(head_back_kernel, total, tuple(masks)),
        out_shape=out_shape,
        in_specs=in_specs,
        out_specs=out_specs,
        scratch_shapes=scratch,
        compiler_params=pltpu.CompilerParams(
            collective_id=number, has_side_effects=True, vmem_limit_bytes=60 * 2**20
        ),
    )(*given)
    return (outcome[0].reshape(-1, width),) + tuple(outcome[1:])


def join_weights_kernel(total, orders, given, vecs, outcome, vec_sums, work, recv, vec_send,
                        vec_recv, sum_sems, gather_sems, vec_sems):
    block, place = lax.axis_index("dp"), lax.axis_index("mp")
    bits = (total - 1).bit_length()
    height = given.shape[1]
    near, far = (block, flip(place, 1)), (block, flip(place, 2))
    over = [(flip(block, 1 << bit), place) for bit in range(bits)]
    sides = [lax.rem(lax.div(block, 1 << bit), 2) for bit in range(bits)]
    greet([near, far] + over)
    pieces = range(len(orders))
    kept = [[0] for _ in pieces]
    copies, sent = {}, []

    def part(ref, piece, start, rows):
        unit = height >> bits
        return ref.at[piece, pl.ds(pl.multiple_of(start, unit), rows), :]

    def send_sum(piece, stage):
        bit, rows = orders[piece][stage], height >> (stage + 1)
        start = kept[piece][stage]
        away = start + (1 - sides[bit]) * rows
        kept[piece].append(start + sides[bit] * rows)
        offset = height - 2 * rows
        copies[piece, stage] = remote(
            part(work if stage else given, piece, away, rows),
            recv.at[piece, pl.ds(offset, rows), :],
            sum_sems.at[0, piece, stage],
            sum_sems.at[1, piece, stage],
            over[bit],
        )
        sent.append(copies[piece, stage])

    def take_sum(piece, stage):
        rows = height >> (stage + 1)
        copies[piece, stage].wait_recv()
        start = kept[piece][stage + 1]
        offset = height - 2 * rows
        part(work if stage + 1 < bits else outcome, piece, start, rows)[...] = (
            part(work if stage else given, piece, start, rows)[...].astype(jnp.float32)
            + recv[piece, pl.ds(offset, rows), :].astype(jnp.float32)
        ).astype(outcome.dtype)

    def send_whole(piece, stage):
        rows = height >> (stage + 1)
        here = part(outcome, piece, kept[piece][stage + 1], rows)
        copies[piece, stage, "whole"] = remote(
            here, here, gather_sems.at[0, piece, stage], gather_sems.at[1, piece, stage],
            over[orders[piece][stage]],
        )
        sent.append(copies[piece, stage, "whole"])

    vec_peers = [(near, lax.rem(place, 2)), (far, lax.div(place, 2))]
    vec_peers += list(zip(over, sides))
    vec_copies = {}

    def vec_start(stage, value):
        vec_send[stage] = value
        vec_copies[stage] = remote(
            vec_send.at[stage], vec_recv.at[stage], vec_sems.at[0, stage], vec_sems.at[1, stage],
            vec_peers[stage][0],
        )
        sent.append(vec_copies[stage])

    def vec_end(stage):
        vec_copies[stage].wait_recv()
        return vec_send[stage] + vec_recv[stage]

    for piece in pieces:
        send_sum(piece, 0)
    vec_start(0, vecs[...])
    stages = len(vec_peers)
    done = 0

    def vec_next(done):
        if done < stages:
            value = vec_end(done)
            if done + 1 < stages:
                vec_start(done + 1, value)
            else:
                vec_sums[...] = value
        return done + 1

    for stage in range(bits):
        for piece in pieces:
            take_sum(piece, stage)
            if stage + 1 < bits:
                send_sum(piece, stage + 1)
            else:
                send_whole(piece, stage)
        done = vec_next(done)
    for stage in range(bits - 1, -1, -1):
        for piece in pieces:
            copies[piece, stage, "whole"].wait_recv()
            if stage:
                send_whole(piece, stage - 1)
        done = vec_next(done)
    while done < stages:
        done = vec_next(done)
    for copy in sent:
        copy.wait_send()


def join_weights(given, vecs, number):
    total = lax.axis_size("dp")
    bits = (total - 1).bit_length()
    rest = list(range(2, bits))
    orders = [[0, 1] + rest if piece % 4 else [1, 0] + rest for piece in range(given.shape[0])]
    stages = bits + 2
    return pl.pallas_call(
        functools.partial(join_weights_kernel, total, orders),
        out_shape=[
            jax.ShapeDtypeStruct(given.shape, given.dtype),
            jax.ShapeDtypeStruct(vecs.shape, vecs.dtype),
        ],
        in_specs=[VMEM] * 2,
        out_specs=[VMEM] * 2,
        scratch_shapes=[
            pltpu.VMEM(given.shape, given.dtype),
            pltpu.VMEM(given.shape, given.dtype),
            pltpu.VMEM((stages,) + vecs.shape, vecs.dtype),
            pltpu.VMEM((stages,) + vecs.shape, vecs.dtype),
            DMA((2, given.shape[0], bits)),
            DMA((2, given.shape[0], bits)),
            DMA((2, stages)),
        ],
        compiler_params=pltpu.CompilerParams(
            collective_id=number, has_side_effects=True, vmem_limit_bytes=48 * 2**20
        ),
    )(given, vecs)


def fold(matrix, width):
    return jnp.concatenate(
        [matrix[:, start : start + width] for start in range(0, matrix.shape[1], width)], axis=0
    )


def unfold(matrix, height):
    return jnp.concatenate(
        [matrix[start : start + height] for start in range(0, matrix.shape[0], height)], axis=1
    )


def shift_pairs(total, step):
    return [(index, (index + step) % total) for index in range(total)]


def spread_rows(table):
    total = lax.axis_size("dp")
    place = lax.axis_index("dp")
    width = table.shape[1]
    part = table.shape[0] // total
    whole = jnp.zeros((part, width * total), table.dtype)
    for step in range(total):
        block = lax.dynamic_slice_in_dim(table, (place + step) % total * part, part, 0)
        if step:
            block = lax.ppermute(block, "dp", shift_pairs(total, step))
        whole = lax.dynamic_update_slice_in_dim(
            whole, block, (place - step) % total * width, 1
        )
    return whole


def return_rows(rows, height):
    total = lax.axis_size("dp")
    place = lax.axis_index("dp")
    part = rows.shape[0]
    width = rows.shape[1] // total
    whole = jnp.zeros((height, width), rows.dtype)
    for step in range(total):
        block = lax.dynamic_slice_in_dim(rows, (place + step) % total * width, width, 1)
        if step:
            block = lax.ppermute(block, "dp", shift_pairs(total, step))
        whole = lax.dynamic_update_slice_in_dim(
            whole, block, (place - step) % total * part, 0
        )
    return whole


def local(
    tokens,
    memory,
    segment_ids,
    answer_ids,
    loss_mask,
    doc_scores,
    slot_place,
    self_query,
    self_key,
    self_value,
    self_out,
    cross_query,
    cross_key,
    cross_value,
    cross_out,
    feed_up,
    feed_down,
    gain_self,
    shift_self,
    gain_cross,
    shift_cross,
    gain_feed,
    shift_feed,
    embedding,
):
    row_count, row_len = segment_ids.shape
    total = lax.axis_size("dp")
    direct = total == 8 and embedding.shape[1] % 128 == 0
    span = SEG_ROW * MEM
    quarter = tokens.shape[0] // QUARTERS
    inputs = lax.dynamic_slice_in_dim(tokens, lax.axis_index("mp") * quarter, quarter, 0)
    places = jnp.arange(row_len, dtype=jnp.int32)
    owners = jnp.arange(span, dtype=jnp.int32) // MEM
    self_masks = [
        (segment_ids[0][:, None] == segment_ids[0][None, :]) & (places[None, :] <= places[:, None])
    ]
    cross_masks = [segment_ids[0][:, None] == owners[None, :]]
    query_self = product(tokens, self_query).astype(jnp.bfloat16)
    key_self = product(tokens, self_key).astype(jnp.bfloat16)
    value_self = product(tokens, self_value).astype(jnp.bfloat16)
    self_mix, self_totals = run_rows(query_self, key_self, value_self, self_masks)
    first_low, first_norm, rows_self, ids_all, *wide = mix_norm(
        self_mix, self_out, inputs, gain_self, shift_self, 0,
        jnp.concatenate([segment_ids, answer_ids, loss_mask], axis=0),
        embedding, None, (4, 1, 0) if direct else (),
    )
    segments_all, answers_all, kept_all = (
        ids_all[:, kind * row_count : (kind + 1) * row_count].reshape(-1, row_len)
        for kind in range(3)
    )
    query_cross = product(first_low, cross_query).astype(jnp.bfloat16)
    key_cross = product(memory, cross_key).astype(jnp.bfloat16)
    value_cross = product(memory, cross_value).astype(jnp.bfloat16)
    cross_mix, cross_totals = run_rows(query_cross, key_cross, value_cross, cross_masks)
    second_low, second_norm, rows_cross, *wide = mix_norm(
        cross_mix, cross_out, first_norm, gain_cross, shift_cross, 1, None,
        embedding, *wide, masks=(5, 2) if direct else (),
    )
    feed_pre = product(second_low, feed_up)
    feed_act = gelu_exact(feed_pre).astype(jnp.bfloat16)
    states, rows_feed, *wide = feed_norm(
        feed_act, feed_down, second_norm, gain_feed, shift_feed, 2,
        embedding, *wide, early=(6, 3) if direct else (), late=(7,) if direct else (),
    )
    table_rows = wide[0] if direct else spread_rows(embedding)
    vocab_local = embedding.shape[0]
    part = table_rows.shape[0]
    logits = product_nt(states, table_rows)
    offset = lax.axis_index("mp") * vocab_local + lax.axis_index("dp") * part
    local_target = answers_all.reshape(-1) - offset
    vocab_ids = jnp.arange(part, dtype=jnp.int32)
    answer_hot = local_target[:, None] == vocab_ids[None, :]
    picked_part = jnp.sum(jnp.where(answer_hot, logits, 0.0), axis=1)
    local_top = jnp.max(logits, axis=1)
    global_top, global_sum, picked = join_totals(
        local_top, jnp.sum(jnp.exp(logits - local_top[:, None]), axis=1), picked_part, 3
    )
    log_total = global_top + jnp.log(global_sum)
    keeper = kept_all.astype(jnp.float32)
    token_logp = (picked - log_total).reshape(keeper.shape) * keeper
    seg_hot = (
        segments_all[:, :, None] == jnp.arange(SEG_ROW, dtype=jnp.int32)[None, None, :]
    ).astype(jnp.float32)
    seg_sums = jnp.sum(seg_hot * token_logp[:, :, None], axis=1)
    counts = jnp.sum(seg_hot * keeper[:, :, None], axis=1)
    likely_all = (seg_sums / jnp.maximum(counts, 1.0)).reshape(-1)
    place_hot = (
        slot_place[:, None] == jnp.arange(likely_all.shape[0], dtype=jnp.int32)[None, :]
    ).astype(jnp.float32)

    def marginal(scores, likely):
        joint_score = jax.nn.log_softmax(scores, axis=1) + jnp.dot(
            place_hot, likely, precision=highest
        ).reshape(scores.shape)
        return -jnp.sum(jax.nn.logsumexp(joint_score, axis=1))

    loss, pullback = jax.vjp(marginal, doc_scores, likely_all)
    grad_scores, grad_likely = pullback(jnp.ones_like(loss))
    per_segment = grad_likely.reshape(counts.shape) / jnp.maximum(counts, 1.0)
    grad_logp = (jnp.sum(seg_hot * per_segment[:, None, :], axis=2) * keeper).reshape(-1)
    grad_logits = (
        grad_logp[:, None]
        * (answer_hot.astype(jnp.float32) - jnp.exp(logits - log_total[:, None]))
    ).astype(jnp.bfloat16)
    grad_rows = product_tn(grad_logits, states).astype(jnp.bfloat16)
    grad_states = product(grad_logits, table_rows).astype(jnp.bfloat16)
    grad_states, grad_rows = lax.optimization_barrier((grad_states, grad_rows))
    grad_branch, grad_res3, grad_vecs_feed, *narrow = head_back(
        grad_states, rows_feed, gain_feed, 4, grad_rows, (4, 5, 1, 2, 3, 0) if direct else ()
    )
    grad_feed_down = product_tn(feed_act, grad_branch)
    grad_act = product_nt(grad_branch, feed_down)
    act_value, act_pull = jax.vjp(gelu_exact, feed_pre)
    grad_pre = act_pull(grad_act)[0].astype(jnp.bfloat16)
    grad_feed_up = product_tn(second_low, grad_pre)
    grad_pre, grad_feed_up, grad_feed_down = lax.optimization_barrier(
        (grad_pre, grad_feed_up.astype(jnp.bfloat16), grad_feed_down.astype(jnp.bfloat16))
    )
    sum_up, sum_down = (
        part.astype(jnp.float32) for part in lax.psum((grad_feed_up, grad_feed_down), "dp")
    )
    grad_branch, grad_res2, grad_vecs_cross, *narrow = back_norm(
        grad_pre, feed_up, grad_res3, rows_cross, gain_cross, 5,
        grad_rows, *narrow, masks=(6,) if direct else (),
    )
    grad_cross_out = product_tn(cross_mix, grad_branch)
    grad_mix = product_nt(grad_branch, cross_out).astype(jnp.bfloat16)
    cross_gq, cross_gk, cross_gv = back_rows(
        query_cross, key_cross, value_cross, cross_masks, cross_totals, grad_mix
    )
    grad_cross_query = product_tn(first_low, cross_gq)
    grad_cross_key = product_tn(memory, cross_gk)
    grad_cross_value = product_tn(memory, cross_gv)
    grad_memory_part = product_nt(cross_gk, cross_key) + product_nt(cross_gv, cross_value)
    grad_branch, _, grad_vecs_self, *narrow = back_norm(
        cross_gq, cross_query, grad_res2, rows_self, gain_self, 6,
        grad_rows, *narrow, masks=(7,) if direct else (),
    )
    grad_table = (
        narrow[0] if direct else return_rows(grad_rows, vocab_local)
    ).astype(jnp.float32)
    grad_self_out = product_tn(self_mix, grad_branch)
    grad_mix = product_nt(grad_branch, self_out).astype(jnp.bfloat16)
    self_gq, self_gk, self_gv = back_rows(
        query_self, key_self, value_self, self_masks, self_totals, grad_mix
    )
    grad_self_query = product_tn(tokens, self_gq)
    grad_self_key = product_tn(tokens, self_gk)
    grad_self_value = product_tn(tokens, self_gv)
    grad_input_part = (
        product_nt(self_gq, self_query)
        + product_nt(self_gk, self_key)
        + product_nt(self_gv, self_value)
    )
    input_share, memory_share = (
        lax.psum_scatter(
            grad_input_part.astype(jnp.bfloat16), "mp", scatter_dimension=1, tiled=True
        ).astype(jnp.float32),
        lax.psum_scatter(
            grad_memory_part.astype(jnp.bfloat16), "mp", scatter_dimension=1, tiled=True
        ).astype(jnp.float32),
    )
    column_start = lax.axis_index("mp") * input_share.shape[1]
    grad_tokens = input_share + lax.dynamic_slice_in_dim(
        grad_branch, column_start, input_share.shape[1], 1
    ).astype(jnp.float32)
    width = grad_self_query.shape[1]
    sums, grad_vecs = join_weights(
        jnp.stack(
            [
                grad_cross_query,
                grad_cross_key,
                grad_cross_value,
                fold(grad_cross_out, width),
                grad_self_query,
                grad_self_key,
                grad_self_value,
                fold(grad_self_out, width),
            ]
        ).astype(jnp.bfloat16),
        jnp.concatenate([grad_vecs_self, grad_vecs_cross, grad_vecs_feed], axis=0),
        7,
    )
    sum_cq, sum_ck, sum_cv, sum_co, sum_sq, sum_sk, sum_sv, sum_so = (
        part.astype(jnp.float32) for part in sums
    )
    sum_co, sum_so = (unfold(part, grad_self_out.shape[0]) for part in (sum_co, sum_so))
    return (
        loss,
        grad_tokens,
        memory_share,
        sum_sq,
        sum_sk,
        sum_sv,
        sum_so,
        sum_cq,
        sum_ck,
        sum_cv,
        sum_co,
        sum_up,
        sum_down,
        *grad_vecs,
        grad_table,
        grad_scores,
    )


def solution(mesh):
    return jax.shard_map(
        local,
        mesh=mesh,
        in_specs=(
            P("dp", None),
            P("dp", None),
            P("dp", None),
            P("dp", None),
            P("dp", None),
            P(),
            P(),
            P(None, "mp"),
            P(None, "mp"),
            P(None, "mp"),
            P("mp", None),
            P(None, "mp"),
            P(None, "mp"),
            P(None, "mp"),
            P("mp", None),
            P(None, "mp"),
            P("mp", None),
            P(),
            P(),
            P(),
            P(),
            P(),
            P(),
            P("mp", "dp"),
        ),
        out_specs=(
            P(),
            P("dp", "mp"),
            P("dp", "mp"),
            P(None, "mp"),
            P(None, "mp"),
            P(None, "mp"),
            P("mp", None),
            P(None, "mp"),
            P(None, "mp"),
            P(None, "mp"),
            P("mp", None),
            P(None, "mp"),
            P("mp", None),
            P(),
            P(),
            P(),
            P(),
            P(),
            P(),
            P("mp", "dp"),
            P(),
        ),
        check_vma=False,
    )
```

```python
import functools
import typing

import jax
import jax.numpy as jnp
from jax import lax
from jax.experimental import pallas as pl
from jax.experimental.pallas import tpu as pltpu
from jax.sharding import PartitionSpec as P

HEAD_DIM = 64
SEG_ROW = 8
MEM = 128


masked_score = -1e30
norm_eps = 1e-05
highest = lax.Precision.HIGHEST


def product(left_side, right_side):
    return jnp.dot(left_side, right_side, preferred_element_type=jnp.float32)


def product_tn(left_side, right_side):
    return lax.dot_general(
        left_side, right_side, (((0,), (0,)), ((), ())), preferred_element_type=jnp.float32
    )


def product_nt(left_side, right_side):
    return lax.dot_general(
        left_side, right_side, (((1,), (1,)), ((), ())), preferred_element_type=jnp.float32
    )


def gelu_exact(inputs):
    return jax.nn.gelu(inputs, approximate=False)


def split_heads(matrix):
    return matrix.reshape(matrix.shape[0], matrix.shape[1] // HEAD_DIM, HEAD_DIM)


def attention_scores(queries, keys, allowed):
    scores = jnp.einsum(
        "qhd,khd->hqk", split_heads(queries), split_heads(keys), preferred_element_type=jnp.float32
    ) * HEAD_DIM ** (-0.5)
    return jnp.where(allowed[None], scores, masked_score)


def attend_forward(queries, keys, values, allowed):
    scores = attention_scores(queries, keys, allowed)
    largest = jnp.max(scores, axis=-1, keepdims=True)
    weights = jnp.exp(scores - largest)
    total = jnp.sum(weights, axis=-1, keepdims=True)
    probabilities = (weights / total).astype(jnp.bfloat16)
    mixed_out = jnp.einsum(
        "hqk,khd->qhd", probabilities, split_heads(values), preferred_element_type=jnp.float32
    )
    return (mixed_out.reshape(queries.shape[0], queries.shape[1]), largest + jnp.log(total))


def run_rows(queries, keys, values, masks):
    mixed_out, log_total = attend_forward(queries, keys, values, masks[0])
    totals = [log_total]
    return (mixed_out.astype(jnp.bfloat16), totals)


MESH = pl.DeviceIdType.MESH
VMEM = pl.BlockSpec(memory_space=pltpu.VMEM)
ANY = pl.BlockSpec(memory_space=pl.ANY)
DMA = pltpu.SemaphoreType.DMA
QUARTERS = 4


def flip(index, mask):
    for bit in range(mask.bit_length()):
        if mask >> bit & 1:
            step = 1 << bit
            index = index + step * (1 - 2 * lax.rem(lax.div(index, step), 2))
    return index


def greet(peers):
    barrier = pltpu.get_barrier_semaphore()
    for peer in peers:
        pl.semaphore_signal(barrier, inc=1, device_id=peer, device_id_type=MESH)
    pl.semaphore_wait(barrier, len(peers))


def remote(source, target, send_sem, recv_sem, peer):
    copy = pltpu.make_async_remote_copy(
        src_ref=source,
        dst_ref=target,
        send_sem=send_sem,
        recv_sem=recv_sem,
        device_id=peer,
        device_id_type=MESH,
    )
    copy.start()
    return copy


def sum_quarter_steps(
    place, block_of, near, far, sib_send, sib_recv, far_send, far_recv, sems, outcome, sent
):
    copies = []
    for slot, mask in enumerate((3, 1)):
        sib_send[slot] = block_of(flip(place, mask)).astype(jnp.bfloat16)
        copies.append(
            remote(
                sib_send.at[slot], sib_recv.at[slot], sems.at[0, slot], sems.at[1, slot], near
            )
        )
    distant = block_of(flip(place, 2))
    copies[0].wait_recv()
    far_send[...] = (distant + sib_recv[0].astype(jnp.float32)).astype(jnp.bfloat16)
    copies.append(remote(far_send, far_recv, sems.at[0, 2], sems.at[1, 2], far))
    sent += copies
    own = block_of(place)
    copies[1].wait_recv()
    yield
    copies[2].wait_recv()
    outcome.append(own + sib_recv[1].astype(jnp.float32) + far_recv[...].astype(jnp.float32))


def share_quarter_steps(place, quarters, near, far, sems, sent):
    here = quarters.at[place]
    to_far = remote(here, here, sems.at[0, 3], sems.at[1, 3], far)
    to_near = remote(here, here, sems.at[0, 4], sems.at[1, 4], near)
    yield
    to_far.wait_recv()
    there = quarters.at[flip(place, 2)]
    passed = remote(there, there, sems.at[0, 5], sems.at[1, 5], near)
    to_near.wait_recv()
    passed.wait_recv()
    sent += [to_far, to_near, passed]


def run(steps, between=None):
    for _ in steps:
        if between is not None:
            between()


def sum_quarter(place, block_of, near, far, *buffers):
    outcome, sent = [], []
    run(sum_quarter_steps(place, block_of, near, far, *buffers, outcome, sent))
    return outcome[0], sent


def share_quarter(place, quarters, near, far, sems):
    sent = []
    run(share_quarter_steps(place, quarters, near, far, sems, sent))
    return sent


def table_copies(masks, back, source, target, sems):
    block, place = lax.axis_index("dp"), lax.axis_index("mp")
    total = lax.axis_size("dp")
    part, width = (source if back else target).shape[0], (target if back else source).shape[1]
    copies = []
    for slot, mask in enumerate(masks):
        other = flip(block, mask)
        here = pl.ds(pl.multiple_of((block if back else other) * part, part), part)
        there = pl.ds(pl.multiple_of((other if back else block) * width, width), width)
        if back:
            start, end = source.at[:, there], target.at[here, :]
        else:
            start, end = source.at[here, :], target.at[:, there]
        if mask:
            copies.append(remote(start, end, sems.at[0, slot], sems.at[1, slot], (other, place)))
        else:
            copy = pltpu.make_async_copy(start, end, sems.at[0, slot])
            copy.start()
            copies.append(copy)
    return copies


def finish(copies):
    for copy in copies:
        copy.wait()


def split_refs(refs, *counts):
    groups, start = [], 0
    for count in counts:
        groups.append(list(refs[start : start + count]))
        start += count
    return groups


def norm_rows(rows, gain, shift):
    center = rows - jnp.mean(rows, axis=-1, keepdims=True)
    spread = jnp.mean(center * center, axis=-1, keepdims=True)
    return center * lax.rsqrt(spread + norm_eps) * gain + shift


def norm_rows_back(rows, gain, grad):
    center = rows - jnp.mean(rows, axis=-1, keepdims=True)
    scale = lax.rsqrt(jnp.mean(center * center, axis=-1, keepdims=True) + norm_eps)
    normed = center * scale
    inner = grad * gain
    grad_rows = scale * (
        inner
        - jnp.mean(inner, axis=-1, keepdims=True)
        - normed * jnp.mean(inner * normed, axis=-1, keepdims=True)
    )
    return (
        grad_rows,
        jnp.sum(grad * normed, axis=0, keepdims=True),
        jnp.sum(grad, axis=0, keepdims=True),
    )


def rows_of(ref, height, index):
    return ref[pl.ds(pl.multiple_of(index * height, height), height), :]


def exchange_scratch(height, width):
    return [
        pltpu.VMEM((2, height, width), jnp.bfloat16),
        pltpu.VMEM((2, height, width), jnp.bfloat16),
        pltpu.VMEM((height, width), jnp.bfloat16),
        pltpu.VMEM((height, width), jnp.bfloat16),
        DMA((2, 6)),
    ]


def mix_norm_kernel(total, with_ids, masks, chained, *refs):
    (left, weight, kept, gain, shift), ids, table, (quarters, normed, rows), ids_all, wide, refs = (
        split_refs(
            refs, 5, with_ids, (1 + chained) * bool(masks), 3, with_ids, bool(masks), len(refs)
        )
    )
    sib_send, sib_recv, far_send, far_recv, sems = refs[:5]
    refs = refs[5:]
    block, place = lax.axis_index("dp"), lax.axis_index("mp")
    near, far = (block, flip(place, 1)), (block, flip(place, 2))
    height = kept.shape[0]
    others = range(1, total) if with_ids else [mask for mask in masks if mask]
    greet([near, far] + [(flip(block, mask), place) for mask in others])
    copies = []
    if with_ids:
        ids_sems, ids_local = refs[:2]
        refs = refs[2:]
        own = pltpu.make_async_copy(ids[0], ids_all[0].at[block], ids_local)
        own.start()
        copies.append(own)
        for mask in range(1, total):
            copies.append(
                remote(
                    ids[0], ids_all[0].at[block], ids_sems.at[0, mask], ids_sems.at[1, mask],
                    (flip(block, mask), place),
                )
            )

    def block_of(index):
        return jnp.dot(
            rows_of(left, height, index), weight[...], preferred_element_type=jnp.float32
        )

    if masks:
        copies += table_copies(masks, False, table[0], wide[0], refs[0])
    branch, sent = sum_quarter(
        place, block_of, near, far, sib_send, sib_recv, far_send, far_recv, sems
    )
    outcome = kept[...].astype(jnp.float32) + branch
    rows[...] = outcome
    outcome = norm_rows(outcome, gain[...], shift[...])
    normed[...] = outcome
    quarters[place] = outcome.astype(jnp.bfloat16)
    sent += share_quarter(place, quarters, near, far, sems)
    finish(copies)
    for copy in sent:
        copy.wait_send()


def mix_norm(left, weight, kept, gain, shift, number, ids=None, table=None, wide=None, masks=()):
    height, width = kept.shape
    total = lax.axis_size("dp")
    quarter = jax.ShapeDtypeStruct((height, width), jnp.float32)
    out_shape = [
        jax.ShapeDtypeStruct((QUARTERS, height, width), jnp.bfloat16), quarter, quarter
    ]
    out_specs = [VMEM] * 3
    given = [left, weight, kept, gain.reshape(1, -1), shift.reshape(1, -1)]
    in_specs = [VMEM] * 5
    scratch = exchange_scratch(height, width)
    aliases = {}
    if ids is not None:
        given.append(ids)
        in_specs.append(VMEM)
        out_shape.append(jax.ShapeDtypeStruct((total,) + ids.shape, ids.dtype))
        out_specs.append(VMEM)
        scratch += [DMA((2, total)), DMA]
    if masks:
        given.append(table)
        in_specs.append(ANY)
        if wide is not None:
            aliases = {len(given): len(out_shape)}
            given.append(wide)
            in_specs.append(ANY)
        out_shape.append(
            jax.ShapeDtypeStruct((table.shape[0] // total, table.shape[1] * total), table.dtype)
        )
        out_specs.append(ANY)
        scratch.append(DMA((2, len(masks))))
    outcome = pl.pallas_call(
        functools.partial(
            mix_norm_kernel, total, int(ids is not None), tuple(masks), int(wide is not None)
        ),
        out_shape=out_shape,
        in_specs=in_specs,
        out_specs=out_specs,
        scratch_shapes=scratch,
        input_output_aliases=aliases,
        compiler_params=pltpu.CompilerParams(
            collective_id=number, has_side_effects=True, vmem_limit_bytes=48 * 2**20
        ),
    )(*given)
    return (outcome[0].reshape(-1, width),) + tuple(outcome[1:])


def chunk_of(rows):
    return max(size for size in range(16, min(rows, 400) + 1, 16) if rows % size == 0)


def feed_norm_kernel(total, early, *refs):
    (left, weight, kept, gain, shift, targets), words, (states, rows, logits, totals), wide, refs = (
        split_refs(refs, 6, 1 + 2 * bool(early), 4, bool(early), len(refs))
    )
    last = words[-1]
    low, sib_send, sib_recv, far_send, far_recv, sems, hops, own_sem = refs[:8]
    (held, staged, sends, recvs, held_sem, staged_sems, stage_sems), refs = refs[8:15], refs[15:]
    block, place = lax.axis_index("dp"), lax.axis_index("mp")
    near, far = (block, flip(place, 1)), (block, flip(place, 2))
    beside = (flip(block, 1), place)
    height = kept.shape[0]
    bits = (total - 1).bit_length()
    others = set(range(1, total) if early else range(2, total, 2))
    others |= {1 << bit for bit in range(bits)}
    greet([near, far] + [(flip(block, mask), place) for mask in sorted(others)])

    def block_of(index):
        return jnp.dot(
            rows_of(left, height, index), weight[...], preferred_element_type=jnp.float32
        )

    moved = []
    if early:
        moved = table_copies(early, False, words[0], wide[0], refs[0])
    branch, sent = sum_quarter(
        place, block_of, near, far, sib_send, sib_recv, far_send, far_recv, sems
    )
    outcome = kept[...] + branch
    rows[...] = outcome
    low[...] = norm_rows(outcome, gain[...], shift[...]).astype(jnp.bfloat16)
    own = pltpu.make_async_copy(low, states.at[block, place], own_sem)
    own.start()
    across = flip(place, 2)

    def hop(kind, mask, source, peer, row, column):
        copy = remote(
            source, states.at[row, column], hops.at[0, kind, mask], hops.at[1, kind, mask], peer
        )
        sent.append(copy)
        return copy

    first = {}
    for mask in range(2, total, 2):
        first[mask] = hop(0, mask, low, (flip(block, mask), place), block, place)
    over, ends = {}, {}

    def pass_on(mask):
        over[mask].wait_recv()
        row = flip(block, mask)
        ends[mask, 1] = hop(3, mask, states.at[row, across], near, row, across)

    def arrive(mask):
        row = flip(block, mask)
        if mask:
            first[mask].wait_recv()
        source = states.at[row, place] if mask else low
        if mask % 2 == 0:
            first[mask + 1] = hop(0, mask + 1, source, beside, row, place)
        over[mask] = hop(1, mask, source, far, row, place)
        ends[mask, 0] = hop(2, mask, source, near, row, place)

    part, width = held.shape
    chunk = chunk_of(part)
    span = QUARTERS * height
    writes = {}

    def make(mask):
        row, slot = flip(block, mask), mask % 2
        for side in (0, 1):
            ends[mask, side].wait_recv()
        if mask >= 2:
            writes[mask - 2].wait()
        block_states = states[row].reshape(span, width)
        target = targets[row]

        def body(turn, carry):
            top, amount, picked = carry
            start = pl.multiple_of(turn * chunk, chunk)
            scores = product_nt(held[pl.ds(start, chunk), :], block_states)
            staged[slot, pl.ds(start, chunk), :] = scores
            ahead = jnp.maximum(top, jnp.max(scores, axis=0, keepdims=True))
            ids = start + lax.broadcasted_iota(jnp.int32, (chunk, 1), 0)
            return (
                ahead,
                amount * jnp.exp(top - ahead)
                + jnp.sum(jnp.exp(scores - ahead), axis=0, keepdims=True),
                picked
                + jnp.sum(jnp.where(ids == target, scores, 0.0), axis=0, keepdims=True),
            )

        scores = product_nt(held[0:chunk, :], block_states)
        staged[slot, 0:chunk, :] = scores
        top = jnp.max(scores, axis=0, keepdims=True)
        ids = lax.broadcasted_iota(jnp.int32, (chunk, 1), 0)
        carry = (
            top,
            jnp.sum(jnp.exp(scores - top), axis=0, keepdims=True),
            jnp.sum(jnp.where(ids == target, scores, 0.0), axis=0, keepdims=True),
        )
        if part > chunk:
            carry = lax.fori_loop(1, part // chunk, body, carry)
        for index in range(3):
            sends[0, index, pl.ds(row, 1), :] = carry[index]
        writes[mask] = pltpu.make_async_copy(
            staged.at[slot], logits.at[row], staged_sems.at[slot]
        )
        writes[mask].start()

    lag = 3
    for step in range(total + lag):
        if step < total:
            arrive(step)
        if 2 <= step < total + 2:
            pass_on(step - 2)
        if step == lag:
            finish(moved)
            load = pltpu.make_async_copy(wide[0] if early else words[0], held, held_sem)
            load.start()
            own.wait()
            load.wait()
            if early:
                spot = pl.ds(pl.multiple_of(flip(block, total - 1) * last.shape[1], 128), 128)
                load = pltpu.make_async_copy(last, held.at[:, spot], held_sem)
                load.start()
                load.wait()
        if step >= lag:
            make(step - lag)
    lead = max(total - 2, 0)
    for mask in range(lead, total):
        writes[mask].wait()

    peers = [(near, lax.rem(place, 2)), (far, lax.div(place, 2))]
    for bit in range(bits):
        step = 1 << bit
        peers.append(((flip(block, step), place), lax.rem(lax.div(block, step), 2)))
    for stage, (peer, side) in enumerate(peers):
        copy = remote(
            sends.at[stage], recvs.at[stage], stage_sems.at[0, stage], stage_sems.at[1, stage],
            peer,
        )
        copy.wait_recv()
        sent.append(copy)
        mine = [sends[stage, index] for index in range(3)]
        theirs = [recvs[stage, index] for index in range(3)]
        leading = side == 0
        soon = [jnp.where(leading, one, other) for one, other in zip(mine, theirs)]
        late_ones = [jnp.where(leading, other, one) for one, other in zip(mine, theirs)]
        top = jnp.maximum(soon[0], late_ones[0])
        values = [
            top,
            soon[1] * jnp.exp(soon[0] - top) + late_ones[1] * jnp.exp(late_ones[0] - top),
            soon[2] + late_ones[2],
        ]
        for index in range(3):
            if stage + 1 < len(peers):
                sends[stage + 1, index] = values[index]
            else:
                totals[index] = values[index]
    for copy in sent:
        copy.wait_send()


def feed_norm(
    left, weight, kept, gain, shift, targets, number, table, wide=None, last=None, early=()
):
    height, width = kept.shape
    total = lax.axis_size("dp")
    stages = 2 + (total - 1).bit_length()
    span = QUARTERS * height
    words = wide if early else table
    part = words.shape[0]
    given = [left, weight, kept, gain.reshape(1, -1), shift.reshape(1, -1), targets, table]
    in_specs = [VMEM] * 6 + [ANY]
    out_shape = [
        jax.ShapeDtypeStruct((total, QUARTERS, height, width), jnp.bfloat16),
        jax.ShapeDtypeStruct((height, width), jnp.float32),
        jax.ShapeDtypeStruct((total, part, span), jnp.float32),
        jax.ShapeDtypeStruct((3, total, span), jnp.float32),
    ]
    out_specs = [VMEM, VMEM, ANY, VMEM]
    scratch = [pltpu.VMEM((height, width), jnp.bfloat16)] + exchange_scratch(height, width)
    scratch += [
        DMA((2, 4, total)),
        DMA,
        pltpu.VMEM((part, width), jnp.bfloat16),
        pltpu.VMEM((2, part, span), jnp.float32),
        pltpu.VMEM((stages, 3, total, span), jnp.float32),
        pltpu.VMEM((stages, 3, total, span), jnp.float32),
        DMA,
        DMA((2,)),
        DMA((2, stages)),
    ]
    aliases = {}
    if early:
        given += [wide, last]
        in_specs += [ANY] * 2
        out_shape.append(jax.ShapeDtypeStruct(wide.shape, wide.dtype))
        out_specs.append(ANY)
        aliases = {7: 4}
        scratch.append(DMA((2, len(early))))
    outcome = pl.pallas_call(
        functools.partial(feed_norm_kernel, total, tuple(early)),
        out_shape=out_shape,
        in_specs=in_specs,
        out_specs=out_specs,
        scratch_shapes=scratch,
        input_output_aliases=aliases,
        compiler_params=pltpu.CompilerParams(
            collective_id=number, has_side_effects=True, vmem_limit_bytes=62 * 2**20
        ),
    )(*given)
    return tuple(outcome)


def head_back_kernel(total, masks, fused, *refs):
    (parts, rows, gain), more, (quarters, grad_rows, grad_vecs), table, narrow, refs = split_refs(
        refs, 3, 5 * fused, 3, fused, bool(masks), len(refs)
    )
    mine, sib_recv, far_recv, beside_recv, across_recv, end_recv, sems = refs[:7]
    sib_sems, far_sems, beside_sems, end_sems, load_sems = refs[7:12]
    refs = refs[12:]
    block, place = lax.axis_index("dp"), lax.axis_index("mp")
    near, far = (block, flip(place, 1)), (block, flip(place, 2))
    beside = (flip(block, 1), place)
    height = rows.shape[0]
    others = range(1, total) if masks else [1] + list(range(2, total, 2))
    greet([near, far] + [(flip(block, mask), place) for mask in others])
    moved = []
    aside = [mask + 1 for mask in range(0, total // 2, 2)]
    order = []
    for late, soon in zip(range(total - 1, total // 2, -2), aside[::-1]):
        order += [late, soon]
    order += [mask for mask in range(total - 1, -1, -1) if mask % 2 == 0]
    sent, loads, sib, across, over, ends = [], {}, {}, {}, {}, {}

    def to_near(mask, slot, source):
        sib[mask, slot] = remote(
            source,
            sib_recv.at[mask, slot],
            sib_sems.at[0, mask, slot],
            sib_sems.at[1, mask, slot],
            near,
        )
        sent.append(sib[mask, slot])

    if fused:
        words, states, log_totals, grad_logp, targets = more
        if masks:
            move_sems, refs = refs[0], refs[1:]
        logits, held, grads, acc, held_sems = refs
        part = words.shape[0]
        chunk = chunk_of(part)
        span = grads.shape[2]

        def load(step):
            slot = step % 2
            loads[step] = pltpu.make_async_copy(
                parts.at[flip(block, order[step])], logits.at[slot], load_sems.at[slot, 0]
            )
            loads[step].start()

        def load_states(step):
            slot = step % 2
            loads[step, None] = pltpu.make_async_copy(
                states.at[flip(block, order[step])], held.at[slot], held_sems.at[slot]
            )
            loads[step, None].start()

        load(0)
    else:
        for mask in order:
            row = flip(block, mask)
            for turn in range(QUARTERS):
                if turn % 2 == 0:
                    loads[mask, turn] = pltpu.make_async_copy(
                        parts.at[row, flip(place, turn)],
                        mine.at[mask, 1 - turn // 2],
                        load_sems.at[mask, turn // 2],
                    )
                    loads[mask, turn].start()
                else:
                    to_near(mask, (3 - turn) // 2, parts.at[row, flip(place, turn)])

    def make(step):
        mask = order[step]
        if not fused:
            for turn in (0, 2):
                loads[mask, turn].wait()
            return
        if step + 1 < len(order):
            load(step + 1)
        elif masks or fused:
            load_states(0)
        loads[step].wait()
        row, slot = flip(block, mask), step % 2
        target, log_total, scale = targets[row], log_totals[row], grad_logp[row]

        def body(turn, carry):
            start = pl.multiple_of(turn * chunk, chunk)
            ids = start + lax.broadcasted_iota(jnp.int32, (chunk, 1), 0)
            hot = (ids == target).astype(jnp.float32)
            chances = jnp.exp(logits[slot, pl.ds(start, chunk), :] - log_total)
            grads[step, pl.ds(start, chunk), :] = (scale * (hot - chances)).astype(jnp.bfloat16)
            return carry

        lax.fori_loop(0, part // chunk, body, 0)
        mine[mask] = (
            product_tn(grads[step], words[...]).astype(jnp.bfloat16).reshape(mine.shape[1:])
        )
        for slot, turn in enumerate((3, 1)):
            to_near(mask, slot, mine.at[mask, flip(place, turn)])

    def make_rows(step):
        if step + 1 < len(order):
            load_states(step + 1)
        loads[step, None].wait()
        block_states = held[step % 2].reshape(span, rows.shape[1])

        def body(turn, carry):
            here = pl.ds(pl.multiple_of(turn * chunk, chunk), chunk)
            value = dot_nn(grads[step, here, :], block_states)
            if step:
                value = value + acc[here, :]
            if step + 1 < len(order):
                acc[here, :] = value
            else:
                table[0][here, :] = value.astype(jnp.bfloat16)
            return carry

        lax.fori_loop(0, part // chunk, body, 0)

    own = (flip(place, 2), place) if fused else (0, 1)

    def join(mask, slot, *others):
        value = mine[mask, own[slot]].astype(jnp.float32)
        for other in others:
            value = value + other.astype(jnp.float32)
        return value

    def send_beside(mask, slot, target, sem_row):
        index = mask // 2
        copy = remote(
            mine.at[mask, own[slot]],
            target.at[index],
            beside_sems.at[0, sem_row, index],
            beside_sems.at[1, sem_row, index],
            beside,
        )
        sent.append(copy)
        return copy

    def to_far(mask):
        for slot in (0, 1):
            sib[mask, slot].wait_recv()
        terms = [sib_recv[mask, 0]]
        if mask + 1 in aside:
            across[mask + 1].wait_recv()
            terms.append(across_recv[mask // 2])
        mine[mask, own[0]] = join(mask, 0, *terms).astype(jnp.bfloat16)
        if mask in aside:
            mine[mask, own[1]] = join(mask, 1, sib_recv[mask, 1]).astype(jnp.bfloat16)
            across[mask] = send_beside(mask, 0, across_recv, 0)
            over[mask] = send_beside(mask, 1, beside_recv, 1)
            return
        across[mask] = remote(
            mine.at[mask, own[0]], far_recv.at[mask], far_sems.at[0, mask], far_sems.at[1, mask], far
        )
        sent.append(across[mask])

    def to_beside(mask):
        if mask in aside:
            return
        across[mask].wait_recv()
        mine[mask, own[1]] = join(mask, 1, sib_recv[mask, 1], far_recv[mask]).astype(jnp.bfloat16)
        over[mask] = send_beside(mask, 1, beside_recv, 1)

    def to_end(mask):
        across[mask].wait_recv()
        over[mask + 1].wait_recv()
        value = join(mask, 1, sib_recv[mask, 1], far_recv[mask], beside_recv[mask // 2])
        if mask == 0:
            return value
        mine[mask, own[1]] = value.astype(jnp.bfloat16)
        ends[mask] = remote(
            mine.at[mask, own[1]],
            end_recv.at[mask // 2],
            end_sems.at[0, mask // 2],
            end_sems.at[1, mask // 2],
            (flip(block, mask), place),
        )
        sent.append(ends[mask])
        return None

    outcome = None
    count = len(order)
    make(0)
    rows_made = 0
    for step in range(count + 2):
        if step + 1 < count:
            make(step + 1)
        if step < count:
            to_far(order[step])
        if step >= 2:
            mask = order[step - 2]
            if mask % 2:
                to_beside(mask)
            else:
                outcome = to_end(mask)
        if fused and step + 2 >= count:
            for _ in range(2):
                make_rows(rows_made)
                rows_made += 1
    if fused:
        while rows_made < count:
            make_rows(rows_made)
            rows_made += 1
        if masks:
            moved = table_copies(masks, True, table[0], narrow[0], move_sems)
    for mask in range(total - 2, 0, -2):
        ends[mask].wait_recv()
        outcome = outcome + end_recv[mask // 2].astype(jnp.float32)
    outcome, grad_gain, grad_shift = norm_rows_back(rows[...], gain[...], outcome)
    grad_rows[...] = outcome
    grad_vecs[0:1] = grad_gain
    grad_vecs[1:2] = grad_shift
    quarters[place] = outcome.astype(jnp.bfloat16)
    sent += share_quarter(place, quarters, near, far, sems)
    for copy in sent:
        copy.wait_send()
    finish(moved)


def head_back(values, rows, gain, number, masks=()):
    height, width = rows.shape
    total = lax.axis_size("dp")
    half = total // 2
    block = (height, width)
    fused = len(values) > 1
    out_shape = [
        jax.ShapeDtypeStruct((QUARTERS,) + block, jnp.bfloat16),
        jax.ShapeDtypeStruct(block, jnp.float32),
        jax.ShapeDtypeStruct((2, width), jnp.float32),
    ]
    out_specs = [VMEM] * 3
    scratch = [
        pltpu.VMEM((total, QUARTERS if fused else 2) + block, jnp.bfloat16),
        pltpu.VMEM((total, 2) + block, jnp.bfloat16),
        pltpu.VMEM((total,) + block, jnp.bfloat16),
        pltpu.VMEM((half,) + block, jnp.bfloat16),
        pltpu.VMEM((half,) + block, jnp.bfloat16),
        pltpu.VMEM((half,) + block, jnp.bfloat16),
        DMA((2, 6)),
        DMA((2, total, 2)),
        DMA((2, total)),
        DMA((2, 2, half)),
        DMA((2, half)),
        DMA((total, 2)),
    ]
    given = [values[0], rows, gain.reshape(1, -1)]
    in_specs = [ANY, VMEM, VMEM]
    if fused:
        words, states = values[1:3]
        part, span = values[0].shape[1:]
        given += list(values[1:])
        in_specs += [VMEM, ANY, VMEM, VMEM, VMEM]
        out_shape.append(jax.ShapeDtypeStruct(words.shape, jnp.bfloat16))
        out_specs.append(VMEM)
        if masks:
            narrow = (part * total, width // total)
            out_shape.append(jax.ShapeDtypeStruct(narrow, jnp.bfloat16))
            out_specs.append(ANY)
            scratch.append(DMA((2, len(masks))))
        scratch += [
            pltpu.VMEM((2, part, span), jnp.float32),
            pltpu.VMEM((2, QUARTERS) + block, jnp.bfloat16),
            pltpu.VMEM((total, part, span), jnp.bfloat16),
            pltpu.VMEM((part, width), jnp.float32),
            DMA((2,)),
        ]
    outcome = pl.pallas_call(
        functools.partial(head_back_kernel, total, tuple(masks), int(fused)),
        out_shape=out_shape,
        in_specs=in_specs,
        out_specs=out_specs,
        scratch_shapes=scratch,
        compiler_params=pltpu.CompilerParams(
            collective_id=number, has_side_effects=True, vmem_limit_bytes=63 * 2**20
        ),
    )(*given)
    return (outcome[0].reshape(-1, width),) + tuple(outcome[1:])


def dot_nn(left, right):
    return jnp.dot(left, right, preferred_element_type=jnp.float32)


def attend_back(queries, keys, values, grads, totals, allowed_at, acc_keys, acc_values, grad_queries,
                grad_keys, grad_values):
    span, width = keys.shape
    rows = queries.shape[0]
    step = min(256, rows)
    pair = 2 * HEAD_DIM
    lanes = lax.broadcasted_iota(jnp.int32, (1, pair), 1)
    sides = [(lanes // HEAD_DIM == side).astype(jnp.bfloat16) for side in range(2)]
    acc_keys[0:span] = jnp.zeros((span, width), jnp.float32)
    acc_values[0:span] = jnp.zeros((span, width), jnp.float32)

    def body(turn, carry):
        here = pl.ds(pl.multiple_of(turn * step, step), step)
        allowed = allowed_at(here)
        for start in range(0, width, pair):
            group = slice(start, start + pair)
            key, value = keys[:, group], values[:, group]
            query, grad = queries[here, group], grads[here, group]
            grad_query = jnp.zeros((step, pair), jnp.float32)
            for side in range(2):
                head = start // HEAD_DIM + side
                query_head, grad_head = query * sides[side], grad * sides[side]
                scores = product_nt(key, query_head) * HEAD_DIM ** (-0.5)
                scores = jnp.where(allowed, scores, masked_score)
                weights = jnp.exp(scores - totals[head : head + 1, here])
                grad_weights = product_nt(value, grad_head)
                row_dot = jnp.sum(grad_weights * weights, axis=0, keepdims=True)
                grad_scores = (weights * (grad_weights - row_dot)).astype(jnp.bfloat16)
                acc_values[0:span, group] += dot_nn(weights.astype(jnp.bfloat16), grad_head)
                acc_keys[0:span, group] += dot_nn(grad_scores, query_head)
                grad_query += product_tn(grad_scores, key * sides[side])
            grad_queries[here, group] = (grad_query * HEAD_DIM ** (-0.5)).astype(jnp.bfloat16)
        return carry

    lax.fori_loop(0, rows // step, body, 0)
    grad_keys[...] = (acc_keys[0:span] * HEAD_DIM ** (-0.5)).astype(jnp.bfloat16)
    grad_values[...] = acc_values[0:span].astype(jnp.bfloat16)


class Loaded(typing.NamedTuple):
    grad_out: typing.Any
    feed_down: typing.Any
    gelu_slope: typing.Any
    feed_up: typing.Any
    feed_act: typing.Any
    second_low: typing.Any
    cross_out: typing.Any
    cross_query: typing.Any
    query_cross: typing.Any
    key_cross: typing.Any
    value_cross: typing.Any
    cross_totals: typing.Any
    cross_mix: typing.Any
    first_low: typing.Any
    memory: typing.Any
    cross_key: typing.Any
    cross_value: typing.Any
    self_out: typing.Any
    query_self: typing.Any
    key_self: typing.Any
    value_self: typing.Any
    self_totals: typing.Any
    self_mix: typing.Any
    tokens: typing.Any
    self_query: typing.Any
    self_key: typing.Any
    self_value: typing.Any


class Plain(typing.NamedTuple):
    grad_rows: typing.Any
    rows_cross: typing.Any
    gain_cross: typing.Any
    rows_self: typing.Any
    gain_self: typing.Any
    grad_vecs: typing.Any
    segment_row: typing.Any
    segment_column: typing.Any


LOADS = len(Loaded._fields)
PIECES = 16


def layer_back_kernel(total, orders, moves, *refs):
    given_hbm, plain, table, outs, narrow, held, refs = split_refs(
        refs, LOADS, len(Plain._fields), 2 * bool(moves), 4, bool(moves), LOADS, len(refs)
    )
    outcome, vec_sums, token_share, memory_share = outs
    load_sems, refs = refs[0], refs[1:]
    (pieces, recv, vec_send, vec_recv, sum_sems, gather_sems, vec_sems), refs = refs[:7], refs[7:]
    norm_buffers = [refs[0:5], refs[5:10]]
    quarters, refs = refs[10:12], refs[12:]
    rows_all = quarters[0].shape[0] * quarters[0].shape[1]
    column_buffers = [
        [pieces.at[0:2], pieces.at[2:4]] + refs[0:3],
        [pieces.at[4:6, 0:rows_all], pieces.at[6:8, 0:rows_all]] + refs[3:6],
    ]
    refs = refs[6:]
    grad_pre, grad_mix, grad_queries, grad_cross, grad_self = refs[:5]
    move_sems = refs[5:]
    loads = [
        pltpu.make_async_copy(source, target, load_sems.at[index])
        for index, (source, target) in enumerate(zip(given_hbm, held))
    ]
    for copy in loads:
        copy.start()
    loaded = set()

    def get(index):
        if index not in loaded:
            loaded.add(index)
            loads[index].wait()
        return held[index]

    at = Loaded(*range(LOADS))
    simple = Plain(*plain)
    block, place = lax.axis_index("dp"), lax.axis_index("mp")
    near, far = (block, flip(place, 1)), (block, flip(place, 2))
    bits = (total - 1).bit_length()
    over = [(flip(block, 1 << bit), place) for bit in range(bits)]
    sides = [lax.rem(lax.div(block, 1 << bit), 2) for bit in range(bits)]
    others = range(1, total) if moves else [1 << bit for bit in range(bits)]
    greet([near, far] + [(flip(block, mask), place) for mask in others])
    sent, moved = [], []
    if moves:
        moved = table_copies(moves, True, table[0], narrow[0], move_sems[0])

    height = pieces.shape[1]
    unit = height >> bits
    kept = [[0] for _ in range(PIECES)]
    copies = {}

    def offset(stage):
        return height - 2 * (height >> (stage + 1))

    def send_sum(piece, stage):
        side, rows = sides[orders[piece][stage]], height >> (stage + 1)
        kept[piece].append(kept[piece][stage] + side * rows)
        if stage:
            source, start = recv, offset(stage - 1) + (1 - side) * rows
        else:
            source, start = pieces, (1 - side) * rows
        copies[piece, stage] = remote(
            source.at[piece, pl.ds(pl.multiple_of(start, unit), rows), :],
            recv.at[piece, pl.ds(offset(stage), rows), :],
            sum_sems.at[0, piece, stage],
            sum_sems.at[1, piece, stage],
            over[orders[piece][stage]],
        )
        if stage or piece >= 8:
            sent.append(copies[piece, stage])

    def take_sum(piece, stage):
        side, rows = sides[orders[piece][stage]], height >> (stage + 1)
        copies[piece, stage].wait_recv()
        if stage:
            source, start = recv, offset(stage - 1) + side * rows
        else:
            source, start = pieces, side * rows
        mine = source[piece, pl.ds(pl.multiple_of(start, unit), rows), :]
        there = pl.ds(offset(stage), rows)
        value = (
            mine.astype(jnp.float32) + recv[piece, there, :].astype(jnp.float32)
        ).astype(jnp.bfloat16)
        if stage + 1 < bits:
            recv[piece, there, :] = value
            send_sum(piece, stage + 1)
        else:
            start = kept[piece][bits]
            outcome[piece, pl.ds(pl.multiple_of(start, unit), rows), :] = value
            send_whole(piece, stage)

    def send_whole(piece, stage):
        rows = height >> (stage + 1)
        start = pl.multiple_of(kept[piece][stage + 1], unit)
        here = outcome.at[piece, pl.ds(start, rows), :]
        copies[piece, stage, True] = remote(
            here, here, gather_sems.at[0, piece, stage], gather_sems.at[1, piece, stage],
            over[orders[piece][stage]],
        )
        sent.append(copies[piece, stage, True])

    def pump(group, turn):
        for piece in group:
            if turn < bits:
                take_sum(piece, turn)
            else:
                stage = 2 * bits - 1 - turn
                copies[piece, stage, True].wait_recv()
                if stage:
                    send_whole(piece, stage - 1)

    def weight_piece(piece, left, right):
        pieces[piece] = product_tn(left, right).astype(jnp.bfloat16)
        send_sum(piece, 0)

    def folded_piece(piece, left, right):
        part = left.shape[1]
        for turn in range(height // part):
            columns = slice(turn * part, (turn + 1) * part)
            pieces[piece, columns, :] = product_tn(left[...], right[:, columns]).astype(
                jnp.bfloat16
            )
        send_sum(piece, 0)

    tasks = []

    def work(amount):
        for task in tasks[:amount]:
            task()
        del tasks[:amount]

    def norm_back(turn, block_of, kept_rows, rows, gain, first_amount):
        outcome_list = []
        run(
            sum_quarter_steps(
                place, block_of, near, far, *norm_buffers[turn], outcome_list, sent
            ),
            lambda: work(first_amount),
        )
        grad, grad_gain, grad_shift = norm_rows_back(
            rows[...], gain[...], kept_rows + outcome_list[0]
        )
        quarters[turn][place] = grad.astype(jnp.bfloat16)
        run(
            share_quarter_steps(place, quarters[turn], near, far, norm_buffers[turn][4], sent),
            lambda: work(len(tasks)),
        )
        return grad, grad_gain, grad_shift

    grad_out = get(at.grad_out)
    grad_act = product_nt(grad_out[...], get(at.feed_down)[...])
    slope = get(at.gelu_slope)
    acc_keys, acc_values = slope.at[0], slope.at[1]
    wide = pieces.shape[2]
    for turn in range(grad_pre.shape[1] // wide):
        columns = slice(turn * wide, (turn + 1) * wide)
        start = turn * rows_all
        grad_pre[:, columns] = (
            slope[start // height, start % height : start % height + rows_all]
            * grad_act[:, columns]
        ).astype(jnp.bfloat16)
    for index in (at.feed_up, at.feed_act, at.second_low):
        get(index)
    for turn in range(4):
        columns = slice(turn * wide, (turn + 1) * wide)
        tasks.append(
            functools.partial(
                lambda turn, columns: weight_piece(
                    turn, get(at.feed_act)[...], grad_out[:, columns]
                ),
                turn, columns,
            )
        )
    for turn in range(4):
        columns = slice(turn * wide, (turn + 1) * wide)
        tasks.append(
            functools.partial(
                lambda turn, columns: weight_piece(
                    4 + turn, get(at.second_low)[...], grad_pre[:, columns]
                ),
                turn, columns,
            )
        )
    quarter = rows_all // QUARTERS
    grad_second, *vecs_cross = norm_back(
        0,
        lambda index: product_nt(rows_of(grad_pre, quarter, index), get(at.feed_up)[...]),
        simple.grad_rows[...], simple.rows_cross, simple.gain_cross, 4,
    )

    grad_out = quarters[0]
    for index in range(QUARTERS):
        grad_mix[index * quarter : (index + 1) * quarter] = product_nt(
            grad_out[index], get(at.cross_out)[...]
        ).astype(jnp.bfloat16)
    for index in (at.query_cross, at.key_cross, at.value_cross, at.cross_totals):
        get(index)
    span = get(at.key_cross).shape[0]
    owners = lax.broadcasted_iota(jnp.int32, (span, 1), 0) // MEM
    attend_back(
        get(at.query_cross), get(at.key_cross), get(at.value_cross), grad_mix, get(at.cross_totals),
        lambda here: owners == simple.segment_row[:, here],
        acc_keys, acc_values, grad_queries, grad_cross.at[0], grad_cross.at[1],
    )
    pump(range(0, 8), 0)
    for piece in range(8):
        copies[piece, 0].wait_send()
    for index in (at.cross_query, at.cross_mix, at.first_low, at.memory, at.cross_key, at.cross_value):
        get(index)
    for kind in range(2):
        tasks.append(
            functools.partial(
                lambda kind: weight_piece(8 + kind, get(at.memory)[...], grad_cross[kind]), kind
            )
        )
    tasks.append(lambda: weight_piece(10, get(at.first_low)[...], grad_queries[...]))
    tasks.append(
        lambda: folded_piece(
            11, get(at.cross_mix), grad_out[...].reshape(rows_all, grad_out.shape[2])
        )
    )

    def memory_block(index):
        return product_nt(
            grad_cross[0], rows_of(get(at.cross_key), wide, index)
        ) + product_nt(grad_cross[1], rows_of(get(at.cross_value), wide, index))

    memory_total = []
    memory_steps = sum_quarter_steps(
        place, memory_block, near, far, *column_buffers[0], memory_total, sent
    )
    grad_first, *vecs_self = norm_back(
        1,
        lambda index: product_nt(rows_of(grad_queries, quarter, index), get(at.cross_query)[...]),
        grad_second, simple.rows_self, simple.gain_self, 3,
    )
    vec_peers = [near, far] + over

    def vec_start(stage, value):
        vec_send[stage] = value
        copies[None, stage] = remote(
            vec_send.at[stage], vec_recv.at[stage], vec_sems.at[0, stage], vec_sems.at[1, stage],
            vec_peers[stage],
        )
        sent.append(copies[None, stage])

    def vec_next(stage):
        if stage >= len(vec_peers):
            return
        copies[None, stage].wait_recv()
        value = vec_send[stage] + vec_recv[stage]
        if stage + 1 < len(vec_peers):
            vec_start(stage + 1, value)
        else:
            vec_sums[...] = value

    vec_start(
        0, jnp.concatenate(vecs_self + vecs_cross + [simple.grad_vecs[...]], axis=0)
    )

    grad_out = quarters[1]
    pump(range(0, 8), 1)
    for index in range(QUARTERS):
        grad_mix[index * quarter : (index + 1) * quarter] = product_nt(
            grad_out[index], get(at.self_out)[...]
        ).astype(jnp.bfloat16)
    for index in (at.query_self, at.key_self, at.value_self, at.self_totals):
        get(index)
    key_place = lax.broadcasted_iota(jnp.int32, (rows_all, 1), 0)

    def allowed_self(here):
        query_place = here.start + lax.broadcasted_iota(jnp.int32, (1, here.size), 1)
        return (simple.segment_column[...] == simple.segment_row[:, here]) & (
            key_place <= query_place
        )

    attend_back(
        get(at.query_self), get(at.key_self), get(at.value_self), grad_mix, get(at.self_totals),
        allowed_self, acc_keys, acc_values, grad_queries, grad_self.at[0], grad_self.at[1],
    )
    for index in (at.tokens, at.self_mix, at.self_query, at.self_key, at.self_value):
        get(index)
    weight_piece(12, get(at.tokens)[...], grad_queries[...])
    weight_piece(13, get(at.tokens)[...], grad_self[0])
    weight_piece(14, get(at.tokens)[...], grad_self[1])
    folded_piece(15, get(at.self_mix), grad_out[...].reshape(rows_all, grad_out.shape[2]))
    pump(range(8, 12), 0)
    vec_next(0)
    pump(range(0, 8), 2)

    def token_block(index):
        return (
            product_nt(grad_queries[...], rows_of(get(at.self_query), wide, index))
            + product_nt(grad_self[0], rows_of(get(at.self_key), wide, index))
            + product_nt(grad_self[1], rows_of(get(at.self_value), wide, index))
        )

    token_total = []
    token_steps = sum_quarter_steps(
        place, token_block, near, far, *column_buffers[1], token_total, sent
    )
    next(token_steps)
    next(memory_steps)
    pump(range(12, 16), 0)
    vec_next(1)
    pump(range(8, 12), 1)
    run(token_steps)
    own_columns = pl.ds(pl.multiple_of(place * wide, wide), wide)
    token_share[...] = token_total[0] + quarters[1][:, :, own_columns].reshape(
        rows_all, wide
    ).astype(jnp.float32)
    pump(range(0, 8), 3)
    vec_next(2)
    run(memory_steps)
    memory_share[...] = memory_total[0]
    groups = [(range(0, 8), 4), (range(8, 12), 2), (range(12, 16), 1)]
    stage = 3
    while groups:
        for group, turn in groups:
            pump(group, turn)
        vec_next(stage)
        stage += 1
        groups = [(group, turn + 1) for group, turn in groups if turn + 1 < 2 * bits]
    while stage < len(vec_peers):
        vec_next(stage)
        stage += 1
    for copy in sent:
        copy.wait_send()
    finish(moved)


def layer_back(values, plain, number, table=None, narrow=None, moves=()):
    total = lax.axis_size("dp")
    bits = (total - 1).bit_length()
    rest = list(range(2, bits))
    orders = [[0, 1] + rest if piece % 4 else [1, 0] + rest for piece in range(PIECES)]
    given = list(values) + list(plain)
    in_specs = [ANY] * len(values) + [VMEM] * len(plain)
    rows, width = values.tokens.shape
    span = values.memory.shape[0]
    part = values.self_query.shape[1]
    quarter = rows // QUARTERS
    stages = bits + 2
    vecs = (6, width)
    out_shape = [
        jax.ShapeDtypeStruct((PIECES, width, part), jnp.bfloat16),
        jax.ShapeDtypeStruct(vecs, jnp.float32),
        jax.ShapeDtypeStruct((rows, part), jnp.float32),
        jax.ShapeDtypeStruct((span, part), jnp.float32),
    ]
    out_specs = [VMEM] * 4
    scratch = [pltpu.VMEM(value.shape, value.dtype) for value in values]
    scratch += [
        DMA((LOADS,)),
        pltpu.VMEM((PIECES, width, part), jnp.bfloat16),
        pltpu.VMEM((PIECES, width - (width >> bits), part), jnp.bfloat16),
        pltpu.VMEM((stages,) + vecs, jnp.float32),
        pltpu.VMEM((stages,) + vecs, jnp.float32),
        DMA((2, PIECES, bits)),
        DMA((2, PIECES, bits)),
        DMA((2, stages)),
    ]
    scratch += exchange_scratch(quarter, width) * 2
    scratch += [pltpu.VMEM((QUARTERS, quarter, width), jnp.bfloat16)] * 2
    scratch += exchange_scratch(span, part)[2:] + exchange_scratch(rows, part)[2:]
    scratch += [
        pltpu.VMEM((rows, values.feed_up.shape[1]), jnp.bfloat16),
        pltpu.VMEM((rows, part), jnp.bfloat16),
        pltpu.VMEM((rows, part), jnp.bfloat16),
        pltpu.VMEM((2, span, part), jnp.bfloat16),
        pltpu.VMEM((2, rows, part), jnp.bfloat16),
    ]
    aliases = {}
    if moves:
        aliases = {len(given) + 1: len(out_shape)}
        given += [table, narrow]
        in_specs += [ANY] * 2
        out_shape.append(jax.ShapeDtypeStruct(narrow.shape, narrow.dtype))
        out_specs.append(ANY)
        scratch.append(DMA((2, len(moves))))
    return pl.pallas_call(
        functools.partial(layer_back_kernel, total, orders, tuple(moves)),
        out_shape=out_shape,
        in_specs=in_specs,
        out_specs=out_specs,
        scratch_shapes=scratch,
        input_output_aliases=aliases,
        compiler_params=pltpu.CompilerParams(
            collective_id=number, has_side_effects=True, vmem_limit_bytes=62 * 2**20
        ),
    )(*given)


def unfold(matrix, height):
    return jnp.concatenate(
        [matrix[start : start + height] for start in range(0, matrix.shape[0], height)], axis=1
    )


def shift_pairs(total, step):
    return [(index, (index + step) % total) for index in range(total)]


def spread_rows(table):
    total = lax.axis_size("dp")
    place = lax.axis_index("dp")
    width = table.shape[1]
    part = table.shape[0] // total
    whole = jnp.zeros((part, width * total), table.dtype)
    for step in range(total):
        block = lax.dynamic_slice_in_dim(table, (place + step) % total * part, part, 0)
        if step:
            block = lax.ppermute(block, "dp", shift_pairs(total, step))
        whole = lax.dynamic_update_slice_in_dim(
            whole, block, (place - step) % total * width, 1
        )
    return whole


def return_rows(rows, height):
    total = lax.axis_size("dp")
    place = lax.axis_index("dp")
    part = rows.shape[0]
    width = rows.shape[1] // total
    whole = jnp.zeros((height, width), rows.dtype)
    for step in range(total):
        block = lax.dynamic_slice_in_dim(rows, (place + step) % total * width, width, 1)
        if step:
            block = lax.ppermute(block, "dp", shift_pairs(total, step))
        whole = lax.dynamic_update_slice_in_dim(
            whole, block, (place - step) % total * part, 0
        )
    return whole


def local(
    tokens,
    memory,
    segment_ids,
    answer_ids,
    loss_mask,
    doc_scores,
    slot_place,
    self_query,
    self_key,
    self_value,
    self_out,
    cross_query,
    cross_key,
    cross_value,
    cross_out,
    feed_up,
    feed_down,
    gain_self,
    shift_self,
    gain_cross,
    shift_cross,
    gain_feed,
    shift_feed,
    embedding,
):
    row_count, row_len = segment_ids.shape
    total = lax.axis_size("dp")
    direct = total == 8 and embedding.shape[1] % 128 == 0
    last = None
    if direct:
        part = embedding.shape[0] // total
        last = lax.ppermute(
            lax.dynamic_slice_in_dim(
                embedding, (total - 1 - lax.axis_index("dp")) * part, part, 0
            ),
            "dp",
            [(index, total - 1 - index) for index in range(total)],
        )
    span = SEG_ROW * MEM
    quarter = tokens.shape[0] // QUARTERS
    inputs = lax.dynamic_slice_in_dim(tokens, lax.axis_index("mp") * quarter, quarter, 0)
    places = jnp.arange(row_len, dtype=jnp.int32)
    owners = jnp.arange(span, dtype=jnp.int32) // MEM
    self_masks = [
        (segment_ids[0][:, None] == segment_ids[0][None, :]) & (places[None, :] <= places[:, None])
    ]
    cross_masks = [segment_ids[0][:, None] == owners[None, :]]
    query_self = product(tokens, self_query).astype(jnp.bfloat16)
    key_self = product(tokens, self_key).astype(jnp.bfloat16)
    value_self = product(tokens, self_value).astype(jnp.bfloat16)
    self_mix, self_totals = run_rows(query_self, key_self, value_self, self_masks)
    first_low, first_norm, rows_self, ids_all, *wide = mix_norm(
        self_mix, self_out, inputs, gain_self, shift_self, 0,
        jnp.concatenate([segment_ids, answer_ids, loss_mask], axis=0),
        embedding, None, (4, 1, 0) if direct else (),
    )
    segments_all, answers_all, kept_all = (
        ids_all[:, kind * row_count : (kind + 1) * row_count].reshape(-1, row_len)
        for kind in range(3)
    )
    query_cross = product(first_low, cross_query).astype(jnp.bfloat16)
    key_cross = product(memory, cross_key).astype(jnp.bfloat16)
    value_cross = product(memory, cross_value).astype(jnp.bfloat16)
    cross_mix, cross_totals = run_rows(query_cross, key_cross, value_cross, cross_masks)
    second_low, second_norm, rows_cross, *wide = mix_norm(
        cross_mix, cross_out, first_norm, gain_cross, shift_cross, 1, None,
        embedding, *wide, masks=(5, 2) if direct else (),
    )
    feed_pre = product(second_low, feed_up)
    feed_act, gelu_pull = jax.vjp(gelu_exact, feed_pre)
    gelu_slope = gelu_pull(jnp.ones_like(feed_pre))[0]
    feed_act = feed_act.astype(jnp.bfloat16)
    vocab_local = embedding.shape[0]
    part = vocab_local // total
    offset = lax.axis_index("mp") * vocab_local + lax.axis_index("dp") * part
    targets = (answers_all - offset)[:, None, :]
    table = embedding if direct else spread_rows(embedding)
    states, rows_feed, logits, totals, *wide = feed_norm(
        feed_act, feed_down, second_norm, gain_feed, shift_feed, targets, 2,
        table, *wide, last=last, early=(6, 3) if direct else (),
    )
    if direct:
        spot = (total - 1 - lax.axis_index("dp")) * last.shape[1]
        table_rows = lax.dynamic_update_slice_in_dim(wide[0], last, spot, 1)
    else:
        table_rows = table
    log_total = totals[0] + jnp.log(totals[1])
    picked = totals[2]
    keeper = kept_all.astype(jnp.float32)
    token_logp = (picked - log_total) * keeper
    seg_hot = (
        segments_all[:, :, None] == jnp.arange(SEG_ROW, dtype=jnp.int32)[None, None, :]
    ).astype(jnp.float32)
    seg_sums = jnp.sum(seg_hot * token_logp[:, :, None], axis=1)
    counts = jnp.sum(seg_hot * keeper[:, :, None], axis=1)
    likely_all = (seg_sums / jnp.maximum(counts, 1.0)).reshape(-1)
    place_hot = (
        slot_place[:, None] == jnp.arange(likely_all.shape[0], dtype=jnp.int32)[None, :]
    ).astype(jnp.float32)

    def marginal(scores, likely):
        joint_score = jax.nn.log_softmax(scores, axis=1) + jnp.dot(
            place_hot, likely, precision=highest
        ).reshape(scores.shape)
        return -jnp.sum(jax.nn.logsumexp(joint_score, axis=1))

    loss, pullback = jax.vjp(marginal, doc_scores, likely_all)
    grad_scores, grad_likely = pullback(jnp.ones_like(loss))
    per_segment = grad_likely.reshape(counts.shape) / jnp.maximum(counts, 1.0)
    grad_logp = (jnp.sum(seg_hot * per_segment[:, None, :], axis=2) * keeper)[:, None, :]
    log_total = log_total[:, None, :]
    if direct:
        head_values = (logits, table_rows, states, log_total, grad_logp, targets)
    else:
        hot = (targets == jnp.arange(part, dtype=jnp.int32)[None, :, None]).astype(jnp.float32)
        grad_logits = (grad_logp * (hot - jnp.exp(logits - log_total))).astype(jnp.bfloat16)
        parts = jnp.einsum(
            "rvt,vd->rtd", grad_logits, table_rows, preferred_element_type=jnp.float32
        ).astype(jnp.bfloat16)
        head_values = (parts.reshape(states.shape),)
        grad_words = jnp.einsum(
            "rvt,rtd->vd",
            grad_logits,
            states.reshape(total, -1, states.shape[3]),
            preferred_element_type=jnp.float32,
        ).astype(jnp.bfloat16)
    grad_branch, grad_res3, grad_vecs_feed, *words = head_back(
        head_values, rows_feed, gain_feed, 3, (4, 1, 0) if direct else ()
    )
    grad_words, *narrow = words if direct else (grad_words,)
    values = Loaded(
        grad_out=grad_branch,
        feed_down=feed_down,
        gelu_slope=jnp.concatenate(
            jnp.split(gelu_slope, gelu_slope.shape[1] // self_query.shape[1], axis=1), axis=0
        ).reshape((2,) + self_query.shape),
        feed_up=feed_up,
        feed_act=feed_act,
        second_low=second_low,
        cross_out=cross_out,
        cross_query=cross_query,
        query_cross=query_cross,
        key_cross=key_cross,
        value_cross=value_cross,
        cross_totals=cross_totals[0][..., 0],
        cross_mix=cross_mix,
        first_low=first_low,
        memory=memory,
        cross_key=cross_key,
        cross_value=cross_value,
        self_out=self_out,
        query_self=query_self,
        key_self=key_self,
        value_self=value_self,
        self_totals=self_totals[0][..., 0],
        self_mix=self_mix,
        tokens=tokens,
        self_query=self_query,
        self_key=self_key,
        self_value=self_value,
    )
    plain = Plain(
        grad_rows=grad_res3,
        rows_cross=rows_cross,
        gain_cross=gain_cross.reshape(1, -1),
        rows_self=rows_self,
        gain_self=gain_self.reshape(1, -1),
        grad_vecs=grad_vecs_feed,
        segment_row=segment_ids.reshape(1, -1),
        segment_column=segment_ids.reshape(-1, 1),
    )
    sums, grad_vecs, grad_tokens, memory_share, *narrow = layer_back(
        values, plain, 4, grad_words, *narrow, moves=(5, 6, 7, 2, 3) if direct else ()
    )
    grad_table = (
        narrow[0] if direct else return_rows(grad_words, vocab_local)
    ).astype(jnp.float32)
    sums = [part.astype(jnp.float32) for part in sums]
    sum_down = jnp.concatenate(sums[0:4], axis=1)
    sum_up = jnp.concatenate(sums[4:8], axis=1)
    sum_ck, sum_cv, sum_cq, sum_co, sum_sq, sum_sk, sum_sv, sum_so = sums[8:]
    sum_co, sum_so = (unfold(part, self_out.shape[0]) for part in (sum_co, sum_so))
    return (
        loss,
        grad_tokens,
        memory_share,
        sum_sq,
        sum_sk,
        sum_sv,
        sum_so,
        sum_cq,
        sum_ck,
        sum_cv,
        sum_co,
        sum_up,
        sum_down,
        *grad_vecs,
        grad_table,
        grad_scores,
    )


def solution(mesh):
    return jax.shard_map(
        local,
        mesh=mesh,
        in_specs=(
            P("dp", None),
            P("dp", None),
            P("dp", None),
            P("dp", None),
            P("dp", None),
            P(),
            P(),
            P(None, "mp"),
            P(None, "mp"),
            P(None, "mp"),
            P("mp", None),
            P(None, "mp"),
            P(None, "mp"),
            P(None, "mp"),
            P("mp", None),
            P(None, "mp"),
            P("mp", None),
            P(),
            P(),
            P(),
            P(),
            P(),
            P(),
            P("mp", "dp"),
        ),
        out_specs=(
            P(),
            P("dp", "mp"),
            P("dp", "mp"),
            P(None, "mp"),
            P(None, "mp"),
            P(None, "mp"),
            P("mp", None),
            P(None, "mp"),
            P(None, "mp"),
            P(None, "mp"),
            P("mp", None),
            P(None, "mp"),
            P("mp", None),
            P(),
            P(),
            P(),
            P(),
            P(),
            P(),
            P("mp", "dp"),
            P(),
        ),
        check_vma=False,
    )
```

```python
import functools
import typing

import jax
import jax.numpy as jnp
from jax import lax
from jax.experimental import pallas as pl
from jax.experimental.pallas import tpu as pltpu
from jax.sharding import PartitionSpec as P

HEAD_DIM = 64
SEG_ROW = 8
MEM = 128


masked_score = -1e30
norm_eps = 1e-05
highest = lax.Precision.HIGHEST


def product(left_side, right_side):
    return jnp.dot(left_side, right_side, preferred_element_type=jnp.float32)


def product_tn(left_side, right_side):
    return lax.dot_general(
        left_side, right_side, (((0,), (0,)), ((), ())), preferred_element_type=jnp.float32
    )


def product_nt(left_side, right_side):
    return lax.dot_general(
        left_side, right_side, (((1,), (1,)), ((), ())), preferred_element_type=jnp.float32
    )


def gelu_exact(inputs):
    return jax.nn.gelu(inputs, approximate=False)


def split_heads(matrix):
    return matrix.reshape(matrix.shape[0], matrix.shape[1] // HEAD_DIM, HEAD_DIM)


def attention_scores(queries, keys, allowed):
    scores = jnp.einsum(
        "qhd,khd->hqk", split_heads(queries), split_heads(keys), preferred_element_type=jnp.float32
    ) * HEAD_DIM ** (-0.5)
    return jnp.where(allowed[None], scores, masked_score)


def attend_forward(queries, keys, values, allowed):
    scores = attention_scores(queries, keys, allowed)
    largest = jnp.max(scores, axis=-1, keepdims=True)
    weights = jnp.exp(scores - largest)
    total = jnp.sum(weights, axis=-1, keepdims=True)
    probabilities = (weights / total).astype(jnp.bfloat16)
    mixed_out = jnp.einsum(
        "hqk,khd->qhd", probabilities, split_heads(values), preferred_element_type=jnp.float32
    )
    mixed_out = mixed_out.reshape(queries.shape).astype(jnp.bfloat16)
    return mixed_out, (largest + jnp.log(total))[..., 0]


MESH = pl.DeviceIdType.MESH
VMEM = pl.BlockSpec(memory_space=pltpu.VMEM)
ANY = pl.BlockSpec(memory_space=pl.ANY)
DMA = pltpu.SemaphoreType.DMA
QUARTERS = 4


def flip(index, mask):
    for bit in range(mask.bit_length()):
        if mask >> bit & 1:
            step = 1 << bit
            index = index + step * (1 - 2 * lax.rem(lax.div(index, step), 2))
    return index


def greet(peers):
    barrier = pltpu.get_barrier_semaphore()
    for peer in peers:
        pl.semaphore_signal(barrier, inc=1, device_id=peer, device_id_type=MESH)
    pl.semaphore_wait(barrier, len(peers))


def remote(source, target, send_sem, recv_sem, peer):
    copy = pltpu.make_async_remote_copy(
        src_ref=source,
        dst_ref=target,
        send_sem=send_sem,
        recv_sem=recv_sem,
        device_id=peer,
        device_id_type=MESH,
    )
    copy.start()
    return copy


def sum_quarter_steps(
    place, block_of, near, far, sib_send, sib_recv, far_send, far_recv, sems, outcome, sent
):
    copies = []
    for slot, mask in enumerate((3, 1)):
        sib_send[slot] = block_of(flip(place, mask)).astype(jnp.bfloat16)
        copies.append(
            remote(
                sib_send.at[slot], sib_recv.at[slot], sems.at[0, slot], sems.at[1, slot], near
            )
        )
    distant = block_of(flip(place, 2))
    copies[0].wait_recv()
    far_send[...] = (distant + sib_recv[0].astype(jnp.float32)).astype(jnp.bfloat16)
    copies.append(remote(far_send, far_recv, sems.at[0, 2], sems.at[1, 2], far))
    sent += copies
    own = block_of(place)
    copies[1].wait_recv()
    yield
    copies[2].wait_recv()
    outcome.append(own + sib_recv[1].astype(jnp.float32) + far_recv[...].astype(jnp.float32))


def share_quarter_steps(place, quarters, near, far, sems, sent):
    here = quarters.at[place]
    to_far = remote(here, here, sems.at[0, 3], sems.at[1, 3], far)
    to_near = remote(here, here, sems.at[0, 4], sems.at[1, 4], near)
    yield
    to_far.wait_recv()
    there = quarters.at[flip(place, 2)]
    passed = remote(there, there, sems.at[0, 5], sems.at[1, 5], near)
    to_near.wait_recv()
    passed.wait_recv()
    sent += [to_far, to_near, passed]


def run(steps, between=None):
    for _ in steps:
        if between is not None:
            between()


def sum_quarter(place, block_of, near, far, *buffers):
    outcome, sent = [], []
    run(sum_quarter_steps(place, block_of, near, far, *buffers, outcome, sent))
    return outcome[0], sent


def share_quarter(place, quarters, near, far, sems):
    sent = []
    run(share_quarter_steps(place, quarters, near, far, sems, sent))
    return sent


def table_copies(masks, back, source, target, sems):
    block, place = lax.axis_index("dp"), lax.axis_index("mp")
    total = lax.axis_size("dp")
    part, width = (source if back else target).shape[0], (target if back else source).shape[1]
    copies = []
    for slot, mask in enumerate(masks):
        other = flip(block, mask)
        here = pl.ds(pl.multiple_of((block if back else other) * part, part), part)
        there = pl.ds(pl.multiple_of((other if back else block) * width, width), width)
        if back:
            start, end = source.at[:, there], target.at[here, :]
        else:
            start, end = source.at[here, :], target.at[:, there]
        if mask:
            copies.append(remote(start, end, sems.at[0, slot], sems.at[1, slot], (other, place)))
        else:
            copy = pltpu.make_async_copy(start, end, sems.at[0, slot])
            copy.start()
            copies.append(copy)
    return copies


def finish(copies):
    for copy in copies:
        copy.wait()


def split_refs(refs, *counts):
    groups, start = [], 0
    for count in counts:
        groups.append(list(refs[start : start + count]))
        start += count
    return groups


def norm_rows(rows, gain, shift):
    center = rows - jnp.mean(rows, axis=-1, keepdims=True)
    spread = jnp.mean(center * center, axis=-1, keepdims=True)
    return center * lax.rsqrt(spread + norm_eps) * gain + shift


def norm_rows_back(rows, gain, grad):
    center = rows - jnp.mean(rows, axis=-1, keepdims=True)
    scale = lax.rsqrt(jnp.mean(center * center, axis=-1, keepdims=True) + norm_eps)
    normed = center * scale
    inner = grad * gain
    grad_rows = scale * (
        inner
        - jnp.mean(inner, axis=-1, keepdims=True)
        - normed * jnp.mean(inner * normed, axis=-1, keepdims=True)
    )
    return (
        grad_rows,
        jnp.sum(grad * normed, axis=0, keepdims=True),
        jnp.sum(grad, axis=0, keepdims=True),
    )


def rows_of(ref, height, index):
    return ref[pl.ds(pl.multiple_of(index * height, height), height), :]


def exchange_scratch(height, width):
    return [
        pltpu.VMEM((2, height, width), jnp.bfloat16),
        pltpu.VMEM((2, height, width), jnp.bfloat16),
        pltpu.VMEM((height, width), jnp.bfloat16),
        pltpu.VMEM((height, width), jnp.bfloat16),
        DMA((2, 6)),
    ]


def mix_norm_kernel(total, with_ids, masks, chained, *refs):
    (left, weight, kept, gain, shift), ids, table, (quarters, normed, rows), ids_all, wide, refs = (
        split_refs(
            refs, 5, with_ids, (1 + chained) * bool(masks), 3, with_ids, bool(masks), len(refs)
        )
    )
    sib_send, sib_recv, far_send, far_recv, sems = refs[:5]
    refs = refs[5:]
    block, place = lax.axis_index("dp"), lax.axis_index("mp")
    near, far = (block, flip(place, 1)), (block, flip(place, 2))
    height = kept.shape[0]
    others = range(1, total) if with_ids else [mask for mask in masks if mask]
    greet([near, far] + [(flip(block, mask), place) for mask in others])
    copies = []
    if with_ids:
        ids_sems, ids_local = refs[:2]
        refs = refs[2:]
        own = pltpu.make_async_copy(ids[0], ids_all[0].at[block], ids_local)
        own.start()
        copies.append(own)
        for mask in range(1, total):
            copies.append(
                remote(
                    ids[0], ids_all[0].at[block], ids_sems.at[0, mask], ids_sems.at[1, mask],
                    (flip(block, mask), place),
                )
            )

    def block_of(index):
        return jnp.dot(
            rows_of(left, height, index), weight[...], preferred_element_type=jnp.float32
        )

    if masks:
        copies += table_copies(masks, False, table[0], wide[0], refs[0])
    branch, sent = sum_quarter(
        place, block_of, near, far, sib_send, sib_recv, far_send, far_recv, sems
    )
    outcome = kept[...].astype(jnp.float32) + branch
    rows[...] = outcome
    outcome = norm_rows(outcome, gain[...], shift[...])
    normed[...] = outcome
    quarters[place] = outcome.astype(jnp.bfloat16)
    sent += share_quarter(place, quarters, near, far, sems)
    finish(copies)
    for copy in sent:
        copy.wait_send()


def mix_norm(left, weight, kept, gain, shift, number, ids=None, table=None, wide=None, masks=()):
    height, width = kept.shape
    total = lax.axis_size("dp")
    quarter = jax.ShapeDtypeStruct((height, width), jnp.float32)
    out_shape = [
        jax.ShapeDtypeStruct((QUARTERS, height, width), jnp.bfloat16), quarter, quarter
    ]
    out_specs = [VMEM] * 3
    given = [left, weight, kept, gain.reshape(1, -1), shift.reshape(1, -1)]
    in_specs = [VMEM] * 5
    scratch = exchange_scratch(height, width)
    aliases = {}
    if ids is not None:
        given.append(ids)
        in_specs.append(VMEM)
        out_shape.append(jax.ShapeDtypeStruct((total,) + ids.shape, ids.dtype))
        out_specs.append(VMEM)
        scratch += [DMA((2, total)), DMA]
    if masks:
        given.append(table)
        in_specs.append(ANY)
        if wide is not None:
            aliases = {len(given): len(out_shape)}
            given.append(wide)
            in_specs.append(ANY)
        out_shape.append(
            jax.ShapeDtypeStruct((table.shape[0] // total, table.shape[1] * total), table.dtype)
        )
        out_specs.append(ANY)
        scratch.append(DMA((2, len(masks))))
    outcome = pl.pallas_call(
        functools.partial(
            mix_norm_kernel, total, int(ids is not None), tuple(masks), int(wide is not None)
        ),
        out_shape=out_shape,
        in_specs=in_specs,
        out_specs=out_specs,
        scratch_shapes=scratch,
        input_output_aliases=aliases,
        compiler_params=pltpu.CompilerParams(
            collective_id=number, has_side_effects=True, vmem_limit_bytes=48 * 2**20
        ),
    )(*given)
    return (outcome[0].reshape(-1, width),) + tuple(outcome[1:])


def chunk_of(rows):
    return max(size for size in range(16, min(rows, 400) + 1, 16) if rows % size == 0)


def feed_norm_kernel(total, early, *refs):
    (left, weight, kept, gain, shift, targets), words, (states, rows, logits, totals), wide, refs = (
        split_refs(refs, 6, 1 + 2 * bool(early), 4, bool(early), len(refs))
    )
    last = words[-1]
    low, sib_send, sib_recv, far_send, far_recv, sems, hops, own_sem = refs[:8]
    (held, staged, sends, recvs, held_sem, staged_sems, stage_sems), refs = refs[8:15], refs[15:]
    block, place = lax.axis_index("dp"), lax.axis_index("mp")
    near, far = (block, flip(place, 1)), (block, flip(place, 2))
    beside = (flip(block, 1), place)
    height = kept.shape[0]
    bits = (total - 1).bit_length()
    others = set(range(1, total) if early else range(2, total, 2))
    others |= {1 << bit for bit in range(bits)}
    greet([near, far] + [(flip(block, mask), place) for mask in sorted(others)])

    def block_of(index):
        return jnp.dot(
            rows_of(left, height, index), weight[...], preferred_element_type=jnp.float32
        )

    moved = []
    if early:
        moved = table_copies(early, False, words[0], wide[0], refs[0])
    branch, sent = sum_quarter(
        place, block_of, near, far, sib_send, sib_recv, far_send, far_recv, sems
    )
    outcome = kept[...] + branch
    rows[...] = outcome
    low[...] = norm_rows(outcome, gain[...], shift[...]).astype(jnp.bfloat16)
    own = pltpu.make_async_copy(low, states.at[block, place], own_sem)
    own.start()
    across = flip(place, 2)

    def hop(kind, mask, source, peer, row, column):
        copy = remote(
            source, states.at[row, column], hops.at[0, kind, mask], hops.at[1, kind, mask], peer
        )
        sent.append(copy)
        return copy

    first = {}

    def spread(masks):
        for mask in masks:
            first[mask] = hop(0, mask, low, (flip(block, mask), place), block, place)

    spread([2])
    nearest = len(sent) - 1
    over, ends = {}, {}

    def pass_on(mask):
        over[mask].wait_recv()
        row = flip(block, mask)
        ends[mask, 1] = hop(3, mask, states.at[row, across], near, row, across)

    def arrive(mask):
        row = flip(block, mask)
        if mask:
            first[mask].wait_recv()
        source = states.at[row, place] if mask else low
        if mask % 2 == 0:
            first[mask + 1] = hop(0, mask + 1, source, beside, row, place)
        over[mask] = hop(1, mask, source, far, row, place)
        ends[mask, 0] = hop(2, mask, source, near, row, place)

    part, width = held.shape
    chunk = chunk_of(part)
    span = QUARTERS * height
    writes = {}

    def make(mask):
        row, slot = flip(block, mask), mask % 2
        for side in (0, 1):
            ends[mask, side].wait_recv()
        if mask >= 2:
            writes[mask - 2].wait()
        block_states = states[row].reshape(span, width)
        target = targets[row]

        def body(turn, carry):
            top, amount, picked = carry
            start = pl.multiple_of(turn * chunk, chunk)
            scores = product_nt(held[pl.ds(start, chunk), :], block_states)
            staged[slot, pl.ds(start, chunk), :] = scores
            ahead = jnp.maximum(top, jnp.max(scores, axis=0, keepdims=True))
            ids = start + lax.broadcasted_iota(jnp.int32, (chunk, 1), 0)
            return (
                ahead,
                amount * jnp.exp(top - ahead)
                + jnp.sum(jnp.exp(scores - ahead), axis=0, keepdims=True),
                picked
                + jnp.sum(jnp.where(ids == target, scores, 0.0), axis=0, keepdims=True),
            )

        scores = product_nt(held[0:chunk, :], block_states)
        staged[slot, 0:chunk, :] = scores
        top = jnp.max(scores, axis=0, keepdims=True)
        ids = lax.broadcasted_iota(jnp.int32, (chunk, 1), 0)
        carry = (
            top,
            jnp.sum(jnp.exp(scores - top), axis=0, keepdims=True),
            jnp.sum(jnp.where(ids == target, scores, 0.0), axis=0, keepdims=True),
        )
        if part > chunk:
            carry = lax.fori_loop(1, part // chunk, body, carry)
        for index in range(3):
            sends[0, index, pl.ds(row, 1), :] = carry[index]
        writes[mask] = pltpu.make_async_copy(
            staged.at[slot], logits.at[row], staged_sems.at[slot]
        )
        writes[mask].start()

    lag = 3
    for step in range(total + lag):
        if step < total:
            arrive(step)
        if step == 0:
            del sent[nearest]
            first[2].wait_send()
            spread(range(4, total, 2))
        if 2 <= step < total + 2:
            pass_on(step - 2)
        if step == lag:
            finish(moved)
            load = pltpu.make_async_copy(wide[0] if early else words[0], held, held_sem)
            load.start()
            own.wait()
            load.wait()
            if early:
                spot = pl.ds(pl.multiple_of(flip(block, total - 1) * last.shape[1], 128), 128)
                load = pltpu.make_async_copy(last, held.at[:, spot], held_sem)
                load.start()
                load.wait()
        if step >= lag:
            make(step - lag)
    lead = max(total - 2, 0)
    for mask in range(lead, total):
        writes[mask].wait()

    peers = [(near, lax.rem(place, 2)), (far, lax.div(place, 2))]
    for bit in range(bits):
        step = 1 << bit
        peers.append(((flip(block, step), place), lax.rem(lax.div(block, step), 2)))
    for stage, (peer, side) in enumerate(peers):
        copy = remote(
            sends.at[stage], recvs.at[stage], stage_sems.at[0, stage], stage_sems.at[1, stage],
            peer,
        )
        copy.wait_recv()
        sent.append(copy)
        mine = [sends[stage, index] for index in range(3)]
        theirs = [recvs[stage, index] for index in range(3)]
        leading = side == 0
        soon = [jnp.where(leading, one, other) for one, other in zip(mine, theirs)]
        late_ones = [jnp.where(leading, other, one) for one, other in zip(mine, theirs)]
        top = jnp.maximum(soon[0], late_ones[0])
        values = [
            top,
            soon[1] * jnp.exp(soon[0] - top) + late_ones[1] * jnp.exp(late_ones[0] - top),
            soon[2] + late_ones[2],
        ]
        for index in range(3):
            if stage + 1 < len(peers):
                sends[stage + 1, index] = values[index]
            else:
                totals[index] = values[index]
    for copy in sent:
        copy.wait_send()


def feed_norm(
    left, weight, kept, gain, shift, targets, number, table, wide=None, last=None, early=()
):
    height, width = kept.shape
    total = lax.axis_size("dp")
    stages = 2 + (total - 1).bit_length()
    span = QUARTERS * height
    words = wide if early else table
    part = words.shape[0]
    given = [left, weight, kept, gain.reshape(1, -1), shift.reshape(1, -1), targets, table]
    in_specs = [VMEM] * 6 + [ANY]
    out_shape = [
        jax.ShapeDtypeStruct((total, QUARTERS, height, width), jnp.bfloat16),
        jax.ShapeDtypeStruct((height, width), jnp.float32),
        jax.ShapeDtypeStruct((total, part, span), jnp.float32),
        jax.ShapeDtypeStruct((3, total, span), jnp.float32),
    ]
    out_specs = [VMEM, VMEM, ANY, VMEM]
    scratch = [pltpu.VMEM((height, width), jnp.bfloat16)] + exchange_scratch(height, width)
    scratch += [
        DMA((2, 4, total)),
        DMA,
        pltpu.VMEM((part, width), jnp.bfloat16),
        pltpu.VMEM((2, part, span), jnp.float32),
        pltpu.VMEM((stages, 3, total, span), jnp.float32),
        pltpu.VMEM((stages, 3, total, span), jnp.float32),
        DMA,
        DMA((2,)),
        DMA((2, stages)),
    ]
    aliases = {}
    if early:
        given += [wide, last]
        in_specs += [ANY] * 2
        out_shape.append(jax.ShapeDtypeStruct(wide.shape, wide.dtype))
        out_specs.append(ANY)
        aliases = {7: 4}
        scratch.append(DMA((2, len(early))))
    outcome = pl.pallas_call(
        functools.partial(feed_norm_kernel, total, tuple(early)),
        out_shape=out_shape,
        in_specs=in_specs,
        out_specs=out_specs,
        scratch_shapes=scratch,
        input_output_aliases=aliases,
        compiler_params=pltpu.CompilerParams(
            collective_id=number, has_side_effects=True, vmem_limit_bytes=62 * 2**20
        ),
    )(*given)
    return tuple(outcome)


def head_back_kernel(total, masks, fused, *refs):
    (parts, rows, gain), more, (quarters, grad_rows, grad_vecs), table, narrow, refs = split_refs(
        refs, 3, 5 * fused, 3, fused, bool(masks), len(refs)
    )
    mine, sib_recv, far_recv, beside_recv, across_recv, end_recv, sems = refs[:7]
    sib_sems, far_sems, beside_sems, end_sems, load_sems = refs[7:12]
    refs = refs[12:]
    block, place = lax.axis_index("dp"), lax.axis_index("mp")
    near, far = (block, flip(place, 1)), (block, flip(place, 2))
    beside = (flip(block, 1), place)
    height = rows.shape[0]
    others = range(1, total) if masks else [1] + list(range(2, total, 2))
    greet([near, far] + [(flip(block, mask), place) for mask in others])
    moved = []
    aside = [1]
    order = [mask for mask in range(total - 1, -1, -1) if mask != 1]
    order.insert(1, 1)
    sent, loads, sib, across, over, ends = [], {}, {}, {}, {}, {}

    def to_near(mask, slot, source):
        sib[mask, slot] = remote(
            source,
            sib_recv.at[mask, slot],
            sib_sems.at[0, mask, slot],
            sib_sems.at[1, mask, slot],
            near,
        )
        sent.append(sib[mask, slot])

    if fused:
        words, states, log_totals, grad_logp, targets = more
        if masks:
            move_sems, refs = refs[0], refs[1:]
        logits, held, grads, acc, held_sems = refs
        part = words.shape[0]
        chunk = chunk_of(part)
        span = grads.shape[2]

        def load(step):
            slot = step % 2
            loads[step] = pltpu.make_async_copy(
                parts.at[flip(block, order[step])], logits.at[slot], load_sems.at[slot, 0]
            )
            loads[step].start()

        def load_states(step):
            slot = step % 2
            loads[step, None] = pltpu.make_async_copy(
                states.at[flip(block, order[step])], held.at[slot], held_sems.at[slot]
            )
            loads[step, None].start()

        load(0)
    else:
        for mask in order:
            row = flip(block, mask)
            for turn in range(QUARTERS):
                if turn % 2 == 0:
                    loads[mask, turn] = pltpu.make_async_copy(
                        parts.at[row, flip(place, turn)],
                        mine.at[mask, 1 - turn // 2],
                        load_sems.at[mask, turn // 2],
                    )
                    loads[mask, turn].start()
                else:
                    to_near(mask, (3 - turn) // 2, parts.at[row, flip(place, turn)])

    def make(step):
        mask = order[step]
        if not fused:
            for turn in (0, 2):
                loads[mask, turn].wait()
            return
        if step + 1 < len(order):
            load(step + 1)
        elif masks or fused:
            load_states(0)
        loads[step].wait()
        row, slot = flip(block, mask), step % 2
        target, log_total, scale = targets[row], log_totals[row], grad_logp[row]

        def body(turn, carry):
            start = pl.multiple_of(turn * chunk, chunk)
            ids = start + lax.broadcasted_iota(jnp.int32, (chunk, 1), 0)
            hot = (ids == target).astype(jnp.float32)
            chances = jnp.exp(logits[slot, pl.ds(start, chunk), :] - log_total)
            grads[step, pl.ds(start, chunk), :] = (scale * (hot - chances)).astype(jnp.bfloat16)
            return carry

        lax.fori_loop(0, part // chunk, body, 0)
        mine[mask] = (
            product_tn(grads[step], words[...]).astype(jnp.bfloat16).reshape(mine.shape[1:])
        )
        for slot, turn in enumerate((3, 1)):
            to_near(mask, slot, mine.at[mask, flip(place, turn)])

    def make_rows(step):
        if step + 1 < len(order):
            load_states(step + 1)
        loads[step, None].wait()
        block_states = held[step % 2].reshape(span, rows.shape[1])

        def body(turn, carry):
            here = pl.ds(pl.multiple_of(turn * chunk, chunk), chunk)
            value = dot_nn(grads[step, here, :], block_states)
            if step:
                value = value + acc[here, :]
            if step + 1 < len(order):
                acc[here, :] = value
            else:
                table[0][here, :] = value.astype(jnp.bfloat16)
            return carry

        lax.fori_loop(0, part // chunk, body, 0)

    own = (flip(place, 2), place) if fused else (0, 1)

    def join(mask, slot, *others):
        value = mine[mask, own[slot]].astype(jnp.float32)
        for other in others:
            value = value + other.astype(jnp.float32)
        return value

    def send_beside(mask, slot, target, sem_row):
        index = mask // 2
        copy = remote(
            mine.at[mask, own[slot]],
            target.at[index],
            beside_sems.at[0, sem_row, index],
            beside_sems.at[1, sem_row, index],
            beside,
        )
        sent.append(copy)
        return copy

    def to_far(mask):
        for slot in (0, 1):
            sib[mask, slot].wait_recv()
        terms = [sib_recv[mask, 0]]
        if mask + 1 in aside:
            across[mask + 1].wait_recv()
            terms.append(across_recv[mask // 2])
        mine[mask, own[0]] = join(mask, 0, *terms).astype(jnp.bfloat16)
        if mask in aside:
            mine[mask, own[1]] = join(mask, 1, sib_recv[mask, 1]).astype(jnp.bfloat16)
            across[mask] = send_beside(mask, 0, across_recv, 0)
            over[mask] = send_beside(mask, 1, beside_recv, 1)
            return
        across[mask] = remote(
            mine.at[mask, own[0]], far_recv.at[mask], far_sems.at[0, mask], far_sems.at[1, mask], far
        )
        sent.append(across[mask])

    def to_beside(mask):
        if mask in aside:
            return
        across[mask].wait_recv()
        mine[mask, own[1]] = join(mask, 1, sib_recv[mask, 1], far_recv[mask]).astype(jnp.bfloat16)
        over[mask] = send_beside(mask, 1, beside_recv, 1)

    def to_end(mask):
        across[mask].wait_recv()
        over[mask + 1].wait_recv()
        value = join(mask, 1, sib_recv[mask, 1], far_recv[mask], beside_recv[mask // 2])
        if mask == 0:
            return value
        mine[mask, own[1]] = value.astype(jnp.bfloat16)
        ends[mask] = remote(
            mine.at[mask, own[1]],
            end_recv.at[mask // 2],
            end_sems.at[0, mask // 2],
            end_sems.at[1, mask // 2],
            (flip(block, mask), place),
        )
        sent.append(ends[mask])
        return None

    outcome = None
    count = len(order)
    make(0)
    rows_made = 0
    for step in range(count + 2):
        if step + 1 < count:
            make(step + 1)
        if step < count:
            to_far(order[step])
        if step >= 2:
            mask = order[step - 2]
            if mask % 2:
                to_beside(mask)
            else:
                outcome = to_end(mask)
        if fused and step + 2 >= count:
            for _ in range(2):
                make_rows(rows_made)
                rows_made += 1
    if fused:
        while rows_made < count:
            make_rows(rows_made)
            rows_made += 1
        if masks:
            moved = table_copies(masks, True, table[0], narrow[0], move_sems)
    for mask in range(total - 2, 0, -2):
        ends[mask].wait_recv()
        outcome = outcome + end_recv[mask // 2].astype(jnp.float32)
    outcome, grad_gain, grad_shift = norm_rows_back(rows[...], gain[...], outcome)
    grad_rows[...] = outcome
    grad_vecs[0:1] = grad_gain
    grad_vecs[1:2] = grad_shift
    quarters[place] = outcome.astype(jnp.bfloat16)
    sent += share_quarter(place, quarters, near, far, sems)
    for copy in sent:
        copy.wait_send()
    finish(moved)


def head_back(values, rows, gain, number, masks=()):
    height, width = rows.shape
    total = lax.axis_size("dp")
    half = total // 2
    block = (height, width)
    fused = len(values) > 1
    out_shape = [
        jax.ShapeDtypeStruct((QUARTERS,) + block, jnp.bfloat16),
        jax.ShapeDtypeStruct(block, jnp.float32),
        jax.ShapeDtypeStruct((2, width), jnp.float32),
    ]
    out_specs = [VMEM] * 3
    scratch = [
        pltpu.VMEM((total, QUARTERS if fused else 2) + block, jnp.bfloat16),
        pltpu.VMEM((total, 2) + block, jnp.bfloat16),
        pltpu.VMEM((total,) + block, jnp.bfloat16),
        pltpu.VMEM((half,) + block, jnp.bfloat16),
        pltpu.VMEM((half,) + block, jnp.bfloat16),
        pltpu.VMEM((half,) + block, jnp.bfloat16),
        DMA((2, 6)),
        DMA((2, total, 2)),
        DMA((2, total)),
        DMA((2, 2, half)),
        DMA((2, half)),
        DMA((total, 2)),
    ]
    given = [values[0], rows, gain.reshape(1, -1)]
    in_specs = [ANY, VMEM, VMEM]
    if fused:
        words, states = values[1:3]
        part, span = values[0].shape[1:]
        given += list(values[1:])
        in_specs += [VMEM, ANY, VMEM, VMEM, VMEM]
        out_shape.append(jax.ShapeDtypeStruct(words.shape, jnp.bfloat16))
        out_specs.append(VMEM)
        if masks:
            narrow = (part * total, width // total)
            out_shape.append(jax.ShapeDtypeStruct(narrow, jnp.bfloat16))
            out_specs.append(ANY)
            scratch.append(DMA((2, len(masks))))
        scratch += [
            pltpu.VMEM((2, part, span), jnp.float32),
            pltpu.VMEM((2, QUARTERS) + block, jnp.bfloat16),
            pltpu.VMEM((total, part, span), jnp.bfloat16),
            pltpu.VMEM((part, width), jnp.float32),
            DMA((2,)),
        ]
    outcome = pl.pallas_call(
        functools.partial(head_back_kernel, total, tuple(masks), int(fused)),
        out_shape=out_shape,
        in_specs=in_specs,
        out_specs=out_specs,
        scratch_shapes=scratch,
        compiler_params=pltpu.CompilerParams(
            collective_id=number, has_side_effects=True, vmem_limit_bytes=63 * 2**20
        ),
    )(*given)
    return (outcome[0].reshape(-1, width),) + tuple(outcome[1:])


def dot_nn(left, right):
    return jnp.dot(left, right, preferred_element_type=jnp.float32)


def attend_back(queries, keys, values, grads, totals, allowed_at, acc_keys, acc_values, grad_queries,
                grad_keys, grad_values):
    span, width = keys.shape
    rows = queries.shape[0]
    step = min(256, rows)
    pair = 2 * HEAD_DIM
    lanes = lax.broadcasted_iota(jnp.int32, (1, pair), 1)
    sides = [(lanes // HEAD_DIM == side).astype(jnp.bfloat16) for side in range(2)]
    acc_keys[0:span] = jnp.zeros((span, width), jnp.float32)
    acc_values[0:span] = jnp.zeros((span, width), jnp.float32)

    def body(turn, carry):
        here = pl.ds(pl.multiple_of(turn * step, step), step)
        allowed = allowed_at(here)
        for start in range(0, width, pair):
            group = slice(start, start + pair)
            key, value = keys[:, group], values[:, group]
            query, grad = queries[here, group], grads[here, group]
            grad_query = jnp.zeros((step, pair), jnp.float32)
            for side in range(2):
                head = start // HEAD_DIM + side
                query_head, grad_head = query * sides[side], grad * sides[side]
                scores = product_nt(key, query_head) * HEAD_DIM ** (-0.5)
                scores = jnp.where(allowed, scores, masked_score)
                weights = jnp.exp(scores - totals[head : head + 1, here])
                grad_weights = product_nt(value, grad_head)
                row_dot = jnp.sum(grad_weights * weights, axis=0, keepdims=True)
                grad_scores = (weights * (grad_weights - row_dot)).astype(jnp.bfloat16)
                acc_values[0:span, group] += dot_nn(weights.astype(jnp.bfloat16), grad_head)
                acc_keys[0:span, group] += dot_nn(grad_scores, query_head)
                grad_query += product_tn(grad_scores, key * sides[side])
            grad_queries[here, group] = (grad_query * HEAD_DIM ** (-0.5)).astype(jnp.bfloat16)
        return carry

    lax.fori_loop(0, rows // step, body, 0)
    grad_keys[...] = (acc_keys[0:span] * HEAD_DIM ** (-0.5)).astype(jnp.bfloat16)
    grad_values[...] = acc_values[0:span].astype(jnp.bfloat16)


def attend(queries, keys, values, allowed_at, mixed, totals):
    rows, width = queries.shape
    step = min(256, rows)
    pair = 2 * HEAD_DIM
    lanes = lax.broadcasted_iota(jnp.int32, (1, pair), 1)
    sides = [(lanes // HEAD_DIM == side).astype(jnp.bfloat16) for side in range(2)]

    def body(turn, carry):
        here = pl.ds(pl.multiple_of(turn * step, step), step)
        allowed = allowed_at(here)
        for start in range(0, width, pair):
            group = slice(start, start + pair)
            key, value, query = keys[:, group], values[:, group], queries[here, group]
            mix = jnp.zeros((step, pair), jnp.float32)
            for side in range(2):
                head = start // HEAD_DIM + side
                scores = product_nt(key, query * sides[side]) * HEAD_DIM ** (-0.5)
                scores = jnp.where(allowed, scores, masked_score)
                largest = jnp.max(scores, axis=0, keepdims=True)
                weights = jnp.exp(scores - largest)
                amount = jnp.sum(weights, axis=0, keepdims=True)
                chances = (weights * (1.0 / amount)).astype(jnp.bfloat16)
                mix += product_tn(chances, value * sides[side])
                totals[head : head + 1, here] = largest + jnp.log(amount)
            mixed[here, group] = mix.astype(jnp.bfloat16)
        return carry

    lax.fori_loop(0, rows // step, body, 0)


class Given(typing.NamedTuple):
    tokens: typing.Any
    self_query: typing.Any
    self_key: typing.Any
    self_value: typing.Any
    self_out: typing.Any
    memory: typing.Any
    cross_key: typing.Any
    cross_value: typing.Any
    cross_query: typing.Any
    cross_out: typing.Any
    feed_up: typing.Any
    feed_down: typing.Any


class Small(typing.NamedTuple):
    ids: typing.Any
    segment_row: typing.Any
    segment_column: typing.Any
    gain_self: typing.Any
    shift_self: typing.Any
    gain_cross: typing.Any
    shift_cross: typing.Any
    gain_feed: typing.Any
    shift_feed: typing.Any


class Kept(typing.NamedTuple):
    query_self: typing.Any
    key_self: typing.Any
    value_self: typing.Any
    self_totals: typing.Any
    self_mix: typing.Any
    first_low: typing.Any
    rows_self: typing.Any
    key_cross: typing.Any
    value_cross: typing.Any
    query_cross: typing.Any
    cross_totals: typing.Any
    cross_mix: typing.Any
    second_low: typing.Any
    rows_cross: typing.Any
    feed_act: typing.Any
    gelu_slope: typing.Any
    rows_feed: typing.Any
    words: typing.Any
    states: typing.Any


def layer_kernel(total, *refs):
    count, made = len(Given._fields), len(Kept._fields)
    sources, small, table, targets, (logits, totals, ids_all), held, kept, refs = split_refs(
        refs, count, len(Small._fields), 1, made, 3, count, made, len(refs)
    )
    load_sems, keep_sems, ids_sems, ids_local, move_sems = refs[:5]
    buffers, refs = [refs[5:10], refs[10:15], refs[15:20]], refs[20:]
    normed, hops, staged, sends, recvs, staged_sems, stage_sems = refs
    small, kept = Small(*small), Kept(*kept)
    block, place = lax.axis_index("dp"), lax.axis_index("mp")
    near, far = (block, flip(place, 1)), (block, flip(place, 2))
    beside = (flip(block, 1), place)
    bits = (total - 1).bit_length()
    loads = [
        pltpu.make_async_copy(source, target, load_sems.at[index])
        for index, (source, target) in enumerate(zip(sources, held))
    ]
    for copy in loads:
        copy.start()
    loaded = set()

    def get(index):
        if index not in loaded:
            loaded.add(index)
            loads[index].wait()
        return held[index]

    at = Given(*range(count))
    places = Kept(*range(made))
    saves = [
        pltpu.make_async_copy(source, target, keep_sems.at[index])
        for index, (source, target) in enumerate(zip(kept, targets))
    ]

    def save(*indices):
        for index in indices:
            saves[index].start()

    greet([near, far] + [(flip(block, mask), place) for mask in range(1, total)])
    moved = table_copies((4, 5, 6, 7, 1, 2, 3, 0), False, table[0], kept.words, move_sems)
    ids_copies = [pltpu.make_async_copy(small.ids, ids_all.at[block], ids_local)]
    ids_copies[0].start()
    for mask in range(1, total):
        ids_copies.append(
            remote(
                small.ids, ids_all.at[block], ids_sems.at[0, mask], ids_sems.at[1, mask],
                (flip(block, mask), place),
            )
        )
    sent = []
    tokens = get(at.tokens)
    span, width = tokens.shape
    height = span // QUARTERS
    for weight, outcome, index in (
        (at.self_query, kept.query_self, places.query_self),
        (at.self_key, kept.key_self, places.key_self),
        (at.self_value, kept.value_self, places.value_self),
    ):
        outcome[...] = dot_nn(tokens[...], get(weight)[...]).astype(jnp.bfloat16)
        save(index)
    key_place = lax.broadcasted_iota(jnp.int32, (span, 1), 0)

    def allowed_self(here):
        query_place = here.start + lax.broadcasted_iota(jnp.int32, (1, here.size), 1)
        return (small.segment_column[...] == small.segment_row[:, here]) & (
            key_place <= query_place
        )

    attend(
        kept.query_self, kept.key_self, kept.value_self, allowed_self, kept.self_mix,
        kept.self_totals,
    )
    save(places.self_totals, places.self_mix)

    def join(turn, left, weight, residual, rows, fill):
        outcome = []
        run(
            sum_quarter_steps(
                place,
                lambda index: dot_nn(rows_of(left, height, index), weight[...]),
                near, far, *buffers[turn], outcome, sent,
            ),
            fill,
        )
        rows[...] = residual + outcome[0]

    def share(turn, quarters, fill):
        run(share_quarter_steps(place, quarters, near, far, buffers[turn][4], sent), fill)

    def make_keys():
        kept.key_cross[...] = dot_nn(get(at.memory)[...], get(at.cross_key)[...]).astype(
            jnp.bfloat16
        )

    def make_values():
        kept.value_cross[...] = dot_nn(get(at.memory)[...], get(at.cross_value)[...]).astype(
            jnp.bfloat16
        )

    join(
        0, kept.self_mix, get(at.self_out),
        rows_of(tokens, height, place).astype(jnp.float32), kept.rows_self, make_keys,
    )
    normed[...] = norm_rows(kept.rows_self[...], small.gain_self[...], small.shift_self[...])
    kept.first_low[place] = normed[...].astype(jnp.bfloat16)
    share(0, kept.first_low, make_values)
    save(places.key_cross, places.value_cross, places.rows_self, places.first_low)

    kept.query_cross[...] = dot_nn(
        kept.first_low[...].reshape(span, width), get(at.cross_query)[...]
    ).astype(jnp.bfloat16)
    owners = lax.broadcasted_iota(jnp.int32, (kept.key_cross.shape[0], 1), 0) // MEM
    attend(
        kept.query_cross, kept.key_cross, kept.value_cross,
        lambda here: owners == small.segment_row[:, here], kept.cross_mix, kept.cross_totals,
    )
    save(places.query_cross, places.cross_totals, places.cross_mix)
    join(1, kept.cross_mix, get(at.cross_out), normed[...], kept.rows_cross, None)
    normed[...] = norm_rows(kept.rows_cross[...], small.gain_cross[...], small.shift_cross[...])
    kept.second_low[place] = normed[...].astype(jnp.bfloat16)
    share(1, kept.second_low, None)
    save(places.rows_cross, places.second_low)

    get(at.feed_up)
    wide = kept.gelu_slope.shape[2]
    depth = kept.gelu_slope.shape[1]
    second = kept.second_low[...].reshape(span, width)
    for turn in range(kept.feed_act.shape[1] // wide):
        columns = slice(turn * wide, (turn + 1) * wide)
        pre = dot_nn(second, get(at.feed_up)[:, columns])
        chance = 0.5 + 0.5 * lax.erf(pre * 0.5**0.5)
        kept.feed_act[:, columns] = (pre * chance).astype(jnp.bfloat16)
        start = turn * span
        kept.gelu_slope[start // depth, start % depth : start % depth + span] = (
            chance + pre * jnp.exp(-0.5 * pre * pre) * (0.5 / jnp.pi) ** 0.5
        )
    save(places.feed_act, places.gelu_slope)
    join(2, kept.feed_act, get(at.feed_down), normed[...], kept.rows_feed, None)
    save(places.rows_feed)
    states = kept.states
    low = states.at[block, place]
    low[...] = norm_rows(
        kept.rows_feed[...], small.gain_feed[...], small.shift_feed[...]
    ).astype(jnp.bfloat16)
    across = flip(place, 2)

    def hop(kind, mask, peer, row, column):
        here = states.at[row, column]
        copy = remote(here, here, hops.at[0, kind, mask], hops.at[1, kind, mask], peer)
        sent.append(copy)
        return copy

    first, over, ends = {}, {}, {}

    def spread(masks):
        for mask in masks:
            first[mask] = hop(0, mask, (flip(block, mask), place), block, place)

    def pass_on(mask):
        over[mask].wait_recv()
        ends[mask, 1] = hop(3, mask, near, flip(block, mask), across)

    def arrive(mask):
        row = flip(block, mask)
        if mask:
            first[mask].wait_recv()
        if mask % 2 == 0:
            first[mask + 1] = hop(0, mask + 1, beside, row, place)
        over[mask] = hop(1, mask, far, row, place)
        ends[mask, 0] = hop(2, mask, near, row, place)

    words = kept.words
    part = words.shape[0]
    chunk = chunk_of(part)
    offset = (place * total + block) * part
    writes = {}

    def make(mask):
        row, slot = flip(block, mask), mask % 2
        for side in (0, 1):
            ends[mask, side].wait_recv()
        if mask >= 2:
            writes[mask - 2].wait()
        block_states = states[row].reshape(span, width)
        target = ids_all[row, 1:2] - offset

        def chunk_at(start):
            scores = product_nt(words[pl.ds(start, chunk), :], block_states)
            staged[slot, pl.ds(start, chunk), :] = scores
            ids = start + lax.broadcasted_iota(jnp.int32, (chunk, 1), 0)
            return (
                scores,
                jnp.max(scores, axis=0, keepdims=True),
                jnp.sum(jnp.where(ids == target, scores, 0.0), axis=0, keepdims=True),
            )

        def body(turn, carry):
            top, amount, picked = carry
            scores, ahead, more = chunk_at(pl.multiple_of(turn * chunk, chunk))
            ahead = jnp.maximum(top, ahead)
            return (
                ahead,
                amount * jnp.exp(top - ahead)
                + jnp.sum(jnp.exp(scores - ahead), axis=0, keepdims=True),
                picked + more,
            )

        scores, top, picked = chunk_at(0)
        carry = (top, jnp.sum(jnp.exp(scores - top), axis=0, keepdims=True), picked)
        carry = lax.fori_loop(1, part // chunk, body, carry)
        for index in range(3):
            sends[0, index, pl.ds(row, 1), :] = carry[index]
        writes[mask] = pltpu.make_async_copy(
            staged.at[slot], logits.at[row], staged_sems.at[slot]
        )
        writes[mask].start()

    spread([2])
    nearest = len(sent) - 1
    lag = 3
    for step in range(total + lag):
        if step < total:
            arrive(step)
        if step == 0:
            del sent[nearest]
            first[2].wait_send()
            spread(range(4, total, 2))
        if 2 <= step < total + 2:
            pass_on(step - 2)
        if step == lag:
            finish(ids_copies)
            finish(moved)
            save(places.words)
        if step >= lag:
            make(step - lag)
    save(places.states)

    peers = [(near, lax.rem(place, 2)), (far, lax.div(place, 2))]
    for bit in range(bits):
        step = 1 << bit
        peers.append(((flip(block, step), place), lax.rem(lax.div(block, step), 2)))
    for stage, (peer, side) in enumerate(peers):
        copy = remote(
            sends.at[stage], recvs.at[stage], stage_sems.at[0, stage], stage_sems.at[1, stage],
            peer,
        )
        copy.wait_recv()
        sent.append(copy)
        mine = [sends[stage, index] for index in range(3)]
        theirs = [recvs[stage, index] for index in range(3)]
        leading = side == 0
        soon = [jnp.where(leading, one, other) for one, other in zip(mine, theirs)]
        later = [jnp.where(leading, other, one) for one, other in zip(mine, theirs)]
        top = jnp.maximum(soon[0], later[0])
        values = [
            top,
            soon[1] * jnp.exp(soon[0] - top) + later[1] * jnp.exp(later[0] - top),
            soon[2] + later[2],
        ]
        for index in range(3):
            if stage + 1 < len(peers):
                sends[stage + 1, index] = values[index]
            else:
                totals[index] = values[index]
    for mask in range(total - 2, total):
        writes[mask].wait()
    for copy in sent:
        copy.wait_send()
    for copy in saves:
        copy.wait()


def layer_forward(given, small, table, number):
    total = lax.axis_size("dp")
    rows, width = given.tokens.shape
    span = given.memory.shape[0]
    part = given.self_query.shape[1]
    hidden = given.feed_up.shape[1]
    height = rows // QUARTERS
    words = table.shape[0] // total
    stages = 2 + (total - 1).bit_length()
    heads = part // HEAD_DIM

    def low(*shape):
        return jax.ShapeDtypeStruct(shape, jnp.bfloat16)

    def full(*shape):
        return jax.ShapeDtypeStruct(shape, jnp.float32)

    kept = Kept(
        query_self=low(rows, part),
        key_self=low(rows, part),
        value_self=low(rows, part),
        self_totals=full(heads, rows),
        self_mix=low(rows, part),
        first_low=low(QUARTERS, height, width),
        rows_self=full(height, width),
        key_cross=low(span, part),
        value_cross=low(span, part),
        query_cross=low(rows, part),
        cross_totals=full(heads, rows),
        cross_mix=low(rows, part),
        second_low=low(QUARTERS, height, width),
        rows_cross=full(height, width),
        feed_act=low(rows, hidden),
        gelu_slope=full(rows * hidden // (width * part), width, part),
        rows_feed=full(height, width),
        words=low(words, width),
        states=low(total, QUARTERS, height, width),
    )
    out_shape = list(kept) + [
        full(total, words, rows),
        full(3, total, rows),
        jax.ShapeDtypeStruct((total,) + small.ids.shape, small.ids.dtype),
    ]
    outcome = pl.pallas_call(
        functools.partial(layer_kernel, total),
        out_shape=out_shape,
        in_specs=[ANY] * len(given) + [VMEM] * len(small) + [ANY],
        out_specs=[ANY] * len(kept) + [ANY, VMEM, VMEM],
        scratch_shapes=[pltpu.VMEM(value.shape, value.dtype) for value in given]
        + [pltpu.VMEM(value.shape, value.dtype) for value in kept]
        + [DMA((len(given),)), DMA((len(kept),)), DMA((2, total)), DMA, DMA((2, total))]
        + exchange_scratch(height, width) * 3
        + [
            pltpu.VMEM((height, width), jnp.float32),
            DMA((2, 4, total)),
            pltpu.VMEM((2, words, rows), jnp.float32),
            pltpu.VMEM((stages, 3, total, rows), jnp.float32),
            pltpu.VMEM((stages, 3, total, rows), jnp.float32),
            DMA((2,)),
            DMA((2, stages)),
        ],
        compiler_params=pltpu.CompilerParams(
            collective_id=number, has_side_effects=True, vmem_limit_bytes=62 * 2**20
        ),
    )(*given, *small, table)
    return (Kept(*outcome[: len(kept)]),) + tuple(outcome[len(kept) :])


class Loaded(typing.NamedTuple):
    grad_out: typing.Any
    feed_down: typing.Any
    gelu_slope: typing.Any
    feed_up: typing.Any
    feed_act: typing.Any
    second_low: typing.Any
    cross_out: typing.Any
    cross_query: typing.Any
    query_cross: typing.Any
    key_cross: typing.Any
    value_cross: typing.Any
    cross_totals: typing.Any
    cross_mix: typing.Any
    first_low: typing.Any
    memory: typing.Any
    cross_key: typing.Any
    cross_value: typing.Any
    self_out: typing.Any
    query_self: typing.Any
    key_self: typing.Any
    value_self: typing.Any
    self_totals: typing.Any
    self_mix: typing.Any
    tokens: typing.Any
    self_query: typing.Any
    self_key: typing.Any
    self_value: typing.Any


class Plain(typing.NamedTuple):
    grad_rows: typing.Any
    rows_cross: typing.Any
    gain_cross: typing.Any
    rows_self: typing.Any
    gain_self: typing.Any
    grad_vecs: typing.Any
    segment_row: typing.Any
    segment_column: typing.Any


LOADS = len(Loaded._fields)
PIECES = 16


def layer_back_kernel(total, orders, moves, *refs):
    given_hbm, plain, table, outs, narrow, held, refs = split_refs(
        refs, LOADS, len(Plain._fields), 2 * bool(moves), 4, bool(moves), LOADS, len(refs)
    )
    outcome, vec_sums, token_share, memory_share = outs
    load_sems, refs = refs[0], refs[1:]
    (pieces, recv, vec_send, vec_recv, sum_sems, gather_sems, vec_sems), refs = refs[:7], refs[7:]
    norm_buffers = [refs[0:5], refs[5:10]]
    quarters, refs = refs[10:12], refs[12:]
    rows_all = quarters[0].shape[0] * quarters[0].shape[1]
    column_buffers = [
        [pieces.at[0:2], pieces.at[2:4]] + refs[0:3],
        [pieces.at[4:6, 0:rows_all], pieces.at[6:8, 0:rows_all]] + refs[3:6],
    ]
    refs = refs[6:]
    grad_pre, grad_mix, grad_queries, grad_cross, grad_self = refs[:5]
    move_sems = refs[5:]
    loads = [
        pltpu.make_async_copy(source, target, load_sems.at[index])
        for index, (source, target) in enumerate(zip(given_hbm, held))
    ]
    for copy in loads:
        copy.start()
    loaded = set()

    def get(index):
        if index not in loaded:
            loaded.add(index)
            loads[index].wait()
        return held[index]

    at = Loaded(*range(LOADS))
    simple = Plain(*plain)
    block, place = lax.axis_index("dp"), lax.axis_index("mp")
    near, far = (block, flip(place, 1)), (block, flip(place, 2))
    bits = (total - 1).bit_length()
    over = [(flip(block, 1 << bit), place) for bit in range(bits)]
    sides = [lax.rem(lax.div(block, 1 << bit), 2) for bit in range(bits)]
    others = range(1, total) if moves else [1 << bit for bit in range(bits)]
    greet([near, far] + [(flip(block, mask), place) for mask in others])
    sent, moved = [], []
    if moves:
        moved = table_copies(moves, True, table[0], narrow[0], move_sems[0])

    height = pieces.shape[1]
    unit = height >> bits
    kept = [[0] for _ in range(PIECES)]
    copies = {}

    def offset(stage):
        return height - 2 * (height >> (stage + 1))

    def send_sum(piece, stage):
        side, rows = sides[orders[piece][stage]], height >> (stage + 1)
        kept[piece].append(kept[piece][stage] + side * rows)
        if stage:
            source, start = recv, offset(stage - 1) + (1 - side) * rows
        else:
            source, start = pieces, (1 - side) * rows
        copies[piece, stage] = remote(
            source.at[piece, pl.ds(pl.multiple_of(start, unit), rows), :],
            recv.at[piece, pl.ds(offset(stage), rows), :],
            sum_sems.at[0, piece, stage],
            sum_sems.at[1, piece, stage],
            over[orders[piece][stage]],
        )
        if stage or piece >= 8:
            sent.append(copies[piece, stage])

    def take_sum(piece, stage):
        side, rows = sides[orders[piece][stage]], height >> (stage + 1)
        copies[piece, stage].wait_recv()
        if stage:
            source, start = recv, offset(stage - 1) + side * rows
        else:
            source, start = pieces, side * rows
        mine = source[piece, pl.ds(pl.multiple_of(start, unit), rows), :]
        there = pl.ds(offset(stage), rows)
        value = (
            mine.astype(jnp.float32) + recv[piece, there, :].astype(jnp.float32)
        ).astype(jnp.bfloat16)
        if stage + 1 < bits:
            recv[piece, there, :] = value
            send_sum(piece, stage + 1)
        else:
            start = kept[piece][bits]
            outcome[piece, pl.ds(pl.multiple_of(start, unit), rows), :] = value
            send_whole(piece, stage)

    def send_whole(piece, stage):
        rows = height >> (stage + 1)
        start = pl.multiple_of(kept[piece][stage + 1], unit)
        here = outcome.at[piece, pl.ds(start, rows), :]
        copies[piece, stage, True] = remote(
            here, here, gather_sems.at[0, piece, stage], gather_sems.at[1, piece, stage],
            over[orders[piece][stage]],
        )
        sent.append(copies[piece, stage, True])

    def pump(group, turn):
        for piece in group:
            if turn < bits:
                take_sum(piece, turn)
            else:
                stage = 2 * bits - 1 - turn
                copies[piece, stage, True].wait_recv()
                if stage:
                    send_whole(piece, stage - 1)

    def weight_piece(piece, left, right):
        pieces[piece] = product_tn(left, right).astype(jnp.bfloat16)
        send_sum(piece, 0)

    def folded_piece(piece, left, right):
        part = left.shape[1]
        for turn in range(height // part):
            columns = slice(turn * part, (turn + 1) * part)
            pieces[piece, columns, :] = product_tn(left[...], right[:, columns]).astype(
                jnp.bfloat16
            )
        send_sum(piece, 0)

    tasks = []

    def work(amount):
        for task in tasks[:amount]:
            task()
        del tasks[:amount]

    def norm_back(turn, block_of, kept_rows, rows, gain, first_amount):
        outcome_list = []
        run(
            sum_quarter_steps(
                place, block_of, near, far, *norm_buffers[turn], outcome_list, sent
            ),
            lambda: work(first_amount),
        )
        grad, grad_gain, grad_shift = norm_rows_back(
            rows[...], gain[...], kept_rows + outcome_list[0]
        )
        quarters[turn][place] = grad.astype(jnp.bfloat16)
        run(
            share_quarter_steps(place, quarters[turn], near, far, norm_buffers[turn][4], sent),
            lambda: work(len(tasks)),
        )
        return grad, grad_gain, grad_shift

    grad_out = get(at.grad_out)
    grad_act = product_nt(grad_out[...], get(at.feed_down)[...])
    slope = get(at.gelu_slope)
    acc_keys, acc_values = slope.at[0], slope.at[1]
    wide = pieces.shape[2]
    for turn in range(grad_pre.shape[1] // wide):
        columns = slice(turn * wide, (turn + 1) * wide)
        start = turn * rows_all
        grad_pre[:, columns] = (
            slope[start // height, start % height : start % height + rows_all]
            * grad_act[:, columns]
        ).astype(jnp.bfloat16)
    for index in (at.feed_up, at.feed_act, at.second_low):
        get(index)
    for turn in range(4):
        columns = slice(turn * wide, (turn + 1) * wide)
        tasks.append(
            functools.partial(
                lambda turn, columns: weight_piece(
                    turn, get(at.feed_act)[...], grad_out[:, columns]
                ),
                turn, columns,
            )
        )
    for turn in range(4):
        columns = slice(turn * wide, (turn + 1) * wide)
        tasks.append(
            functools.partial(
                lambda turn, columns: weight_piece(
                    4 + turn, get(at.second_low)[...], grad_pre[:, columns]
                ),
                turn, columns,
            )
        )
    quarter = rows_all // QUARTERS
    grad_second, *vecs_cross = norm_back(
        0,
        lambda index: product_nt(rows_of(grad_pre, quarter, index), get(at.feed_up)[...]),
        simple.grad_rows[...], simple.rows_cross, simple.gain_cross, 4,
    )

    grad_out = quarters[0]
    for index in range(QUARTERS):
        grad_mix[index * quarter : (index + 1) * quarter] = product_nt(
            grad_out[index], get(at.cross_out)[...]
        ).astype(jnp.bfloat16)
    for index in (at.query_cross, at.key_cross, at.value_cross, at.cross_totals):
        get(index)
    span = get(at.key_cross).shape[0]
    owners = lax.broadcasted_iota(jnp.int32, (span, 1), 0) // MEM
    attend_back(
        get(at.query_cross), get(at.key_cross), get(at.value_cross), grad_mix, get(at.cross_totals),
        lambda here: owners == simple.segment_row[:, here],
        acc_keys, acc_values, grad_queries, grad_cross.at[0], grad_cross.at[1],
    )
    pump(range(0, 8), 0)
    for piece in range(8):
        copies[piece, 0].wait_send()
    for index in (at.cross_query, at.cross_mix, at.first_low, at.memory, at.cross_key, at.cross_value):
        get(index)
    for kind in range(2):
        tasks.append(
            functools.partial(
                lambda kind: weight_piece(8 + kind, get(at.memory)[...], grad_cross[kind]), kind
            )
        )
    tasks.append(lambda: weight_piece(10, get(at.first_low)[...], grad_queries[...]))
    tasks.append(
        lambda: folded_piece(
            11, get(at.cross_mix), grad_out[...].reshape(rows_all, grad_out.shape[2])
        )
    )

    def memory_block(index):
        return product_nt(
            grad_cross[0], rows_of(get(at.cross_key), wide, index)
        ) + product_nt(grad_cross[1], rows_of(get(at.cross_value), wide, index))

    memory_total = []
    memory_steps = sum_quarter_steps(
        place, memory_block, near, far, *column_buffers[0], memory_total, sent
    )
    grad_first, *vecs_self = norm_back(
        1,
        lambda index: product_nt(rows_of(grad_queries, quarter, index), get(at.cross_query)[...]),
        grad_second, simple.rows_self, simple.gain_self, 3,
    )
    vec_peers = [near, far] + over

    def vec_start(stage, value):
        vec_send[stage] = value
        copies[None, stage] = remote(
            vec_send.at[stage], vec_recv.at[stage], vec_sems.at[0, stage], vec_sems.at[1, stage],
            vec_peers[stage],
        )
        sent.append(copies[None, stage])

    def vec_next(stage):
        if stage >= len(vec_peers):
            return
        copies[None, stage].wait_recv()
        value = vec_send[stage] + vec_recv[stage]
        if stage + 1 < len(vec_peers):
            vec_start(stage + 1, value)
        else:
            vec_sums[...] = value

    vec_start(
        0, jnp.concatenate(vecs_self + vecs_cross + [simple.grad_vecs[...]], axis=0)
    )

    grad_out = quarters[1]
    pump(range(0, 8), 1)
    for index in range(QUARTERS):
        grad_mix[index * quarter : (index + 1) * quarter] = product_nt(
            grad_out[index], get(at.self_out)[...]
        ).astype(jnp.bfloat16)
    for index in (at.query_self, at.key_self, at.value_self, at.self_totals):
        get(index)
    key_place = lax.broadcasted_iota(jnp.int32, (rows_all, 1), 0)

    def allowed_self(here):
        query_place = here.start + lax.broadcasted_iota(jnp.int32, (1, here.size), 1)
        return (simple.segment_column[...] == simple.segment_row[:, here]) & (
            key_place <= query_place
        )

    attend_back(
        get(at.query_self), get(at.key_self), get(at.value_self), grad_mix, get(at.self_totals),
        allowed_self, acc_keys, acc_values, grad_queries, grad_self.at[0], grad_self.at[1],
    )
    for index in (at.tokens, at.self_mix, at.self_query, at.self_key, at.self_value):
        get(index)
    weight_piece(12, get(at.tokens)[...], grad_queries[...])
    weight_piece(13, get(at.tokens)[...], grad_self[0])
    weight_piece(14, get(at.tokens)[...], grad_self[1])
    folded_piece(15, get(at.self_mix), grad_out[...].reshape(rows_all, grad_out.shape[2]))
    pump(range(8, 12), 0)
    vec_next(0)
    pump(range(0, 8), 2)

    def token_block(index):
        return (
            product_nt(grad_queries[...], rows_of(get(at.self_query), wide, index))
            + product_nt(grad_self[0], rows_of(get(at.self_key), wide, index))
            + product_nt(grad_self[1], rows_of(get(at.self_value), wide, index))
        )

    token_total = []
    token_steps = sum_quarter_steps(
        place, token_block, near, far, *column_buffers[1], token_total, sent
    )
    next(token_steps)
    next(memory_steps)
    pump(range(12, 16), 0)
    vec_next(1)
    pump(range(8, 12), 1)
    run(token_steps)
    own_columns = pl.ds(pl.multiple_of(place * wide, wide), wide)
    token_share[...] = token_total[0] + quarters[1][:, :, own_columns].reshape(
        rows_all, wide
    ).astype(jnp.float32)
    pump(range(0, 8), 3)
    vec_next(2)
    run(memory_steps)
    memory_share[...] = memory_total[0]
    groups = [(range(0, 8), 4), (range(8, 12), 2), (range(12, 16), 1)]
    stage = 3
    while groups:
        for group, turn in groups:
            pump(group, turn)
        vec_next(stage)
        stage += 1
        groups = [(group, turn + 1) for group, turn in groups if turn + 1 < 2 * bits]
    while stage < len(vec_peers):
        vec_next(stage)
        stage += 1
    for copy in sent:
        copy.wait_send()
    finish(moved)


def layer_back(values, plain, number, table=None, narrow=None, moves=()):
    total = lax.axis_size("dp")
    bits = (total - 1).bit_length()
    rest = list(range(2, bits))
    orders = [[0, 1] + rest if piece % 4 else [1, 0] + rest for piece in range(PIECES)]
    given = list(values) + list(plain)
    in_specs = [ANY] * len(values) + [VMEM] * len(plain)
    rows, width = values.tokens.shape
    span = values.memory.shape[0]
    part = values.self_query.shape[1]
    quarter = rows // QUARTERS
    stages = bits + 2
    vecs = (6, width)
    out_shape = [
        jax.ShapeDtypeStruct((PIECES, width, part), jnp.bfloat16),
        jax.ShapeDtypeStruct(vecs, jnp.float32),
        jax.ShapeDtypeStruct((rows, part), jnp.float32),
        jax.ShapeDtypeStruct((span, part), jnp.float32),
    ]
    out_specs = [VMEM] * 4
    scratch = [pltpu.VMEM(value.shape, value.dtype) for value in values]
    scratch += [
        DMA((LOADS,)),
        pltpu.VMEM((PIECES, width, part), jnp.bfloat16),
        pltpu.VMEM((PIECES, width - (width >> bits), part), jnp.bfloat16),
        pltpu.VMEM((stages,) + vecs, jnp.float32),
        pltpu.VMEM((stages,) + vecs, jnp.float32),
        DMA((2, PIECES, bits)),
        DMA((2, PIECES, bits)),
        DMA((2, stages)),
    ]
    scratch += exchange_scratch(quarter, width) * 2
    scratch += [pltpu.VMEM((QUARTERS, quarter, width), jnp.bfloat16)] * 2
    scratch += exchange_scratch(span, part)[2:] + exchange_scratch(rows, part)[2:]
    scratch += [
        pltpu.VMEM((rows, values.feed_up.shape[1]), jnp.bfloat16),
        pltpu.VMEM((rows, part), jnp.bfloat16),
        pltpu.VMEM((rows, part), jnp.bfloat16),
        pltpu.VMEM((2, span, part), jnp.bfloat16),
        pltpu.VMEM((2, rows, part), jnp.bfloat16),
    ]
    aliases = {}
    if moves:
        aliases = {len(given) + 1: len(out_shape)}
        given += [table, narrow]
        in_specs += [ANY] * 2
        out_shape.append(jax.ShapeDtypeStruct(narrow.shape, narrow.dtype))
        out_specs.append(ANY)
        scratch.append(DMA((2, len(moves))))
    return pl.pallas_call(
        functools.partial(layer_back_kernel, total, orders, tuple(moves)),
        out_shape=out_shape,
        in_specs=in_specs,
        out_specs=out_specs,
        scratch_shapes=scratch,
        input_output_aliases=aliases,
        compiler_params=pltpu.CompilerParams(
            collective_id=number, has_side_effects=True, vmem_limit_bytes=62 * 2**20
        ),
    )(*given)


def unfold(matrix, height):
    return jnp.concatenate(
        [matrix[start : start + height] for start in range(0, matrix.shape[0], height)], axis=1
    )


def shift_pairs(total, step):
    return [(index, (index + step) % total) for index in range(total)]


def spread_rows(table):
    total = lax.axis_size("dp")
    place = lax.axis_index("dp")
    width = table.shape[1]
    part = table.shape[0] // total
    whole = jnp.zeros((part, width * total), table.dtype)
    for step in range(total):
        block = lax.dynamic_slice_in_dim(table, (place + step) % total * part, part, 0)
        if step:
            block = lax.ppermute(block, "dp", shift_pairs(total, step))
        whole = lax.dynamic_update_slice_in_dim(
            whole, block, (place - step) % total * width, 1
        )
    return whole


def return_rows(rows, height):
    total = lax.axis_size("dp")
    place = lax.axis_index("dp")
    part = rows.shape[0]
    width = rows.shape[1] // total
    whole = jnp.zeros((height, width), rows.dtype)
    for step in range(total):
        block = lax.dynamic_slice_in_dim(rows, (place + step) % total * width, width, 1)
        if step:
            block = lax.ppermute(block, "dp", shift_pairs(total, step))
        whole = lax.dynamic_update_slice_in_dim(
            whole, block, (place - step) % total * part, 0
        )
    return whole


def layer_apart(
    tokens, memory, segment_ids, ids, offset, words, self_query, self_key, self_value, self_out,
    cross_query, cross_key, cross_value, cross_out, feed_up, feed_down, gain_self, shift_self,
    gain_cross, shift_cross, gain_feed, shift_feed,
):
    row_len = segment_ids.shape[1]
    places = jnp.arange(row_len, dtype=jnp.int32)
    owners = jnp.arange(memory.shape[0], dtype=jnp.int32) // MEM
    self_mask = (segment_ids[0][:, None] == segment_ids[0][None, :]) & (
        places[None, :] <= places[:, None]
    )
    cross_mask = segment_ids[0][:, None] == owners[None, :]
    quarter = tokens.shape[0] // QUARTERS
    inputs = lax.dynamic_slice_in_dim(tokens, lax.axis_index("mp") * quarter, quarter, 0)
    query_self = product(tokens, self_query).astype(jnp.bfloat16)
    key_self = product(tokens, self_key).astype(jnp.bfloat16)
    value_self = product(tokens, self_value).astype(jnp.bfloat16)
    self_mix, self_totals = attend_forward(query_self, key_self, value_self, self_mask)
    first_low, first_norm, rows_self, ids_all = mix_norm(
        self_mix, self_out, inputs, gain_self, shift_self, 0, ids
    )
    query_cross = product(first_low, cross_query).astype(jnp.bfloat16)
    key_cross = product(memory, cross_key).astype(jnp.bfloat16)
    value_cross = product(memory, cross_value).astype(jnp.bfloat16)
    cross_mix, cross_totals = attend_forward(query_cross, key_cross, value_cross, cross_mask)
    second_low, second_norm, rows_cross = mix_norm(
        cross_mix, cross_out, first_norm, gain_cross, shift_cross, 1
    )
    feed_pre = product(second_low, feed_up)
    feed_act, gelu_pull = jax.vjp(gelu_exact, feed_pre)
    gelu_slope = gelu_pull(jnp.ones_like(feed_pre))[0]
    feed_act = feed_act.astype(jnp.bfloat16)
    answers = ids_all[:, ids.shape[0] // 3 : 2 * (ids.shape[0] // 3)].reshape(-1, 1, row_len)
    states, rows_feed, logits, totals = feed_norm(
        feed_act, feed_down, second_norm, gain_feed, shift_feed, answers - offset, 2, words
    )
    gelu_slope = jnp.concatenate(
        jnp.split(gelu_slope, gelu_slope.shape[1] // self_query.shape[1], axis=1), axis=0
    ).reshape((2,) + self_query.shape)
    kept = Kept(
        query_self, key_self, value_self, self_totals, self_mix, first_low, rows_self, key_cross,
        value_cross, query_cross, cross_totals, cross_mix, second_low, rows_cross, feed_act,
        gelu_slope, rows_feed, words, states,
    )
    return kept, logits, totals, ids_all


def local(
    tokens,
    memory,
    segment_ids,
    answer_ids,
    loss_mask,
    doc_scores,
    slot_place,
    self_query,
    self_key,
    self_value,
    self_out,
    cross_query,
    cross_key,
    cross_value,
    cross_out,
    feed_up,
    feed_down,
    gain_self,
    shift_self,
    gain_cross,
    shift_cross,
    gain_feed,
    shift_feed,
    embedding,
):
    row_count, row_len = segment_ids.shape
    total = lax.axis_size("dp")
    direct = total == 8 and embedding.shape[1] % 128 == 0
    vocab_local = embedding.shape[0]
    part = vocab_local // total
    offset = lax.axis_index("mp") * vocab_local + lax.axis_index("dp") * part
    ids = jnp.concatenate([segment_ids, answer_ids, loss_mask], axis=0)
    norms = (gain_self, shift_self, gain_cross, shift_cross, gain_feed, shift_feed)
    if direct:
        kept, logits, totals, ids_all = layer_forward(
            Given(
                tokens, self_query, self_key, self_value, self_out, memory, cross_key,
                cross_value, cross_query, cross_out, feed_up, feed_down,
            ),
            Small(
                ids, segment_ids.reshape(1, -1), segment_ids.reshape(-1, 1),
                *(vector.reshape(1, -1) for vector in norms),
            ),
            embedding,
            0,
        )
        words = kept.words
    else:
        words = spread_rows(embedding)
        kept, logits, totals, ids_all = layer_apart(
            tokens, memory, segment_ids, ids, offset, words, self_query, self_key, self_value,
            self_out, cross_query, cross_key, cross_value, cross_out, feed_up, feed_down, *norms,
        )
    segments_all, answers_all, kept_all = (
        ids_all[:, kind * row_count : (kind + 1) * row_count].reshape(-1, row_len)
        for kind in range(3)
    )
    targets = (answers_all - offset)[:, None, :]
    log_total = totals[0] + jnp.log(totals[1])
    picked = totals[2]
    keeper = kept_all.astype(jnp.float32)
    token_logp = (picked - log_total) * keeper
    seg_hot = (
        segments_all[:, :, None] == jnp.arange(SEG_ROW, dtype=jnp.int32)[None, None, :]
    ).astype(jnp.float32)
    seg_sums = jnp.sum(seg_hot * token_logp[:, :, None], axis=1)
    counts = jnp.sum(seg_hot * keeper[:, :, None], axis=1)
    likely_all = (seg_sums / jnp.maximum(counts, 1.0)).reshape(-1)
    place_hot = (
        slot_place[:, None] == jnp.arange(likely_all.shape[0], dtype=jnp.int32)[None, :]
    ).astype(jnp.float32)

    def marginal(scores, likely):
        joint_score = jax.nn.log_softmax(scores, axis=1) + jnp.dot(
            place_hot, likely, precision=highest
        ).reshape(scores.shape)
        return -jnp.sum(jax.nn.logsumexp(joint_score, axis=1))

    loss, pullback = jax.vjp(marginal, doc_scores, likely_all)
    grad_scores, grad_likely = pullback(jnp.ones_like(loss))
    per_segment = grad_likely.reshape(counts.shape) / jnp.maximum(counts, 1.0)
    grad_logp = (jnp.sum(seg_hot * per_segment[:, None, :], axis=2) * keeper)[:, None, :]
    log_total = log_total[:, None, :]
    if direct:
        head_values = (logits, words, kept.states, log_total, grad_logp, targets)
    else:
        hot = (targets == jnp.arange(part, dtype=jnp.int32)[None, :, None]).astype(jnp.float32)
        grad_logits = (grad_logp * (hot - jnp.exp(logits - log_total))).astype(jnp.bfloat16)
        parts = jnp.einsum(
            "rvt,vd->rtd", grad_logits, words, preferred_element_type=jnp.float32
        ).astype(jnp.bfloat16)
        head_values = (parts.reshape(kept.states.shape),)
        grad_words = jnp.einsum(
            "rvt,rtd->vd",
            grad_logits,
            kept.states.reshape(total, -1, kept.states.shape[3]),
            preferred_element_type=jnp.float32,
        ).astype(jnp.bfloat16)
    grad_branch, grad_res3, grad_vecs_feed, *made = head_back(
        head_values, kept.rows_feed, gain_feed, 3, (4, 1, 0) if direct else ()
    )
    grad_words, *narrow = made if direct else (grad_words,)
    values = Loaded(
        grad_out=grad_branch,
        feed_down=feed_down,
        gelu_slope=kept.gelu_slope,
        feed_up=feed_up,
        feed_act=kept.feed_act,
        second_low=kept.second_low.reshape(tokens.shape),
        cross_out=cross_out,
        cross_query=cross_query,
        query_cross=kept.query_cross,
        key_cross=kept.key_cross,
        value_cross=kept.value_cross,
        cross_totals=kept.cross_totals,
        cross_mix=kept.cross_mix,
        first_low=kept.first_low.reshape(tokens.shape),
        memory=memory,
        cross_key=cross_key,
        cross_value=cross_value,
        self_out=self_out,
        query_self=kept.query_self,
        key_self=kept.key_self,
        value_self=kept.value_self,
        self_totals=kept.self_totals,
        self_mix=kept.self_mix,
        tokens=tokens,
        self_query=self_query,
        self_key=self_key,
        self_value=self_value,
    )
    plain = Plain(
        grad_rows=grad_res3,
        rows_cross=kept.rows_cross,
        gain_cross=gain_cross.reshape(1, -1),
        rows_self=kept.rows_self,
        gain_self=gain_self.reshape(1, -1),
        grad_vecs=grad_vecs_feed,
        segment_row=segment_ids.reshape(1, -1),
        segment_column=segment_ids.reshape(-1, 1),
    )
    sums, grad_vecs, grad_tokens, memory_share, *narrow = layer_back(
        values, plain, 4, grad_words, *narrow, moves=(5, 6, 7, 2, 3) if direct else ()
    )
    grad_table = (
        narrow[0] if direct else return_rows(grad_words, vocab_local)
    ).astype(jnp.float32)
    sums = [part.astype(jnp.float32) for part in sums]
    sum_down = jnp.concatenate(sums[0:4], axis=1)
    sum_up = jnp.concatenate(sums[4:8], axis=1)
    sum_ck, sum_cv, sum_cq, sum_co, sum_sq, sum_sk, sum_sv, sum_so = sums[8:]
    sum_co, sum_so = (unfold(part, self_out.shape[0]) for part in (sum_co, sum_so))
    return (
        loss,
        grad_tokens,
        memory_share,
        sum_sq,
        sum_sk,
        sum_sv,
        sum_so,
        sum_cq,
        sum_ck,
        sum_cv,
        sum_co,
        sum_up,
        sum_down,
        *grad_vecs,
        grad_table,
        grad_scores,
    )


def solution(mesh):
    return jax.shard_map(
        local,
        mesh=mesh,
        in_specs=(
            P("dp", None),
            P("dp", None),
            P("dp", None),
            P("dp", None),
            P("dp", None),
            P(),
            P(),
            P(None, "mp"),
            P(None, "mp"),
            P(None, "mp"),
            P("mp", None),
            P(None, "mp"),
            P(None, "mp"),
            P(None, "mp"),
            P("mp", None),
            P(None, "mp"),
            P("mp", None),
            P(),
            P(),
            P(),
            P(),
            P(),
            P(),
            P("mp", "dp"),
        ),
        out_specs=(
            P(),
            P("dp", "mp"),
            P("dp", "mp"),
            P(None, "mp"),
            P(None, "mp"),
            P(None, "mp"),
            P("mp", None),
            P(None, "mp"),
            P(None, "mp"),
            P(None, "mp"),
            P("mp", None),
            P(None, "mp"),
            P("mp", None),
            P(),
            P(),
            P(),
            P(),
            P(),
            P(),
            P("mp", "dp"),
            P(),
        ),
        check_vma=False,
    )
```

```python
import functools
import typing

import jax
import jax.numpy as jnp
from jax import lax
from jax.experimental import pallas as pl
from jax.experimental.pallas import tpu as pltpu
from jax.sharding import PartitionSpec as P

HEAD_DIM = 64
SEG_ROW = 8
MEM = 128


masked_score = -1e30
norm_eps = 1e-05
highest = lax.Precision.HIGHEST


def product(left_side, right_side):
    return jnp.dot(left_side, right_side, preferred_element_type=jnp.float32)


def product_tn(left_side, right_side):
    return lax.dot_general(
        left_side, right_side, (((0,), (0,)), ((), ())), preferred_element_type=jnp.float32
    )


def product_nt(left_side, right_side):
    return lax.dot_general(
        left_side, right_side, (((1,), (1,)), ((), ())), preferred_element_type=jnp.float32
    )


def gelu_exact(inputs):
    return jax.nn.gelu(inputs, approximate=False)


def split_heads(matrix):
    return matrix.reshape(matrix.shape[0], matrix.shape[1] // HEAD_DIM, HEAD_DIM)


def attention_scores(queries, keys, allowed):
    scores = jnp.einsum(
        "qhd,khd->hqk", split_heads(queries), split_heads(keys), preferred_element_type=jnp.float32
    ) * HEAD_DIM ** (-0.5)
    return jnp.where(allowed[None], scores, masked_score)


def attend_forward(queries, keys, values, allowed):
    scores = attention_scores(queries, keys, allowed)
    largest = jnp.max(scores, axis=-1, keepdims=True)
    weights = jnp.exp(scores - largest)
    total = jnp.sum(weights, axis=-1, keepdims=True)
    probabilities = (weights / total).astype(jnp.bfloat16)
    mixed_out = jnp.einsum(
        "hqk,khd->qhd", probabilities, split_heads(values), preferred_element_type=jnp.float32
    )
    mixed_out = mixed_out.reshape(queries.shape).astype(jnp.bfloat16)
    return mixed_out, (largest + jnp.log(total))[..., 0]


MESH = pl.DeviceIdType.MESH
VMEM = pl.BlockSpec(memory_space=pltpu.VMEM)
ANY = pl.BlockSpec(memory_space=pl.ANY)
DMA = pltpu.SemaphoreType.DMA
QUARTERS = 4


def flip(index, mask):
    for bit in range(mask.bit_length()):
        if mask >> bit & 1:
            step = 1 << bit
            index = index + step * (1 - 2 * lax.rem(lax.div(index, step), 2))
    return index


def greet(peers):
    barrier = pltpu.get_barrier_semaphore()
    for peer in peers:
        pl.semaphore_signal(barrier, inc=1, device_id=peer, device_id_type=MESH)
    pl.semaphore_wait(barrier, len(peers))


def remote(source, target, send_sem, recv_sem, peer):
    copy = pltpu.make_async_remote_copy(
        src_ref=source,
        dst_ref=target,
        send_sem=send_sem,
        recv_sem=recv_sem,
        device_id=peer,
        device_id_type=MESH,
    )
    copy.start()
    return copy


def sum_quarter_steps(
    place, block_of, near, far, sib_send, sib_recv, far_send, far_recv, sems, outcome, sent
):
    copies = []
    sends, recvs = (
        slots if isinstance(slots, list) else [slots.at[0], slots.at[1]]
        for slots in (sib_send, sib_recv)
    )
    for slot, mask in enumerate((3, 1)):
        sends[slot][...] = block_of(flip(place, mask)).astype(jnp.bfloat16)
        copies.append(
            remote(sends[slot], recvs[slot], sems.at[0, slot], sems.at[1, slot], near)
        )
    distant = block_of(flip(place, 2))
    copies[0].wait_recv()
    far_send[...] = (distant + recvs[0][...].astype(jnp.float32)).astype(jnp.bfloat16)
    copies.append(remote(far_send, far_recv, sems.at[0, 2], sems.at[1, 2], far))
    sent += copies
    own = block_of(place)
    copies[1].wait_recv()
    yield
    copies[2].wait_recv()
    outcome.append(own + recvs[1][...].astype(jnp.float32) + far_recv[...].astype(jnp.float32))


def share_quarter_steps(place, quarters, near, far, sems, sent):
    here = quarters.at[place]
    to_far = remote(here, here, sems.at[0, 3], sems.at[1, 3], far)
    to_near = remote(here, here, sems.at[0, 4], sems.at[1, 4], near)
    yield
    to_far.wait_recv()
    there = quarters.at[flip(place, 2)]
    passed = remote(there, there, sems.at[0, 5], sems.at[1, 5], near)
    to_near.wait_recv()
    passed.wait_recv()
    sent += [to_far, to_near, passed]


def run(steps, between=None):
    for _ in steps:
        if between is not None:
            between()


def sum_quarter(place, block_of, near, far, *buffers):
    outcome, sent = [], []
    run(sum_quarter_steps(place, block_of, near, far, *buffers, outcome, sent))
    return outcome[0], sent


def share_quarter(place, quarters, near, far, sems):
    sent = []
    run(share_quarter_steps(place, quarters, near, far, sems, sent))
    return sent


def table_copies(masks, back, source, target, sems):
    block, place = lax.axis_index("dp"), lax.axis_index("mp")
    total = lax.axis_size("dp")
    part, width = (source if back else target).shape[0], (target if back else source).shape[1]
    copies = []
    for slot, mask in enumerate(masks):
        other = flip(block, mask)
        here = pl.ds(pl.multiple_of((block if back else other) * part, part), part)
        there = pl.ds(pl.multiple_of((other if back else block) * width, width), width)
        if back:
            start, end = source.at[:, there], target.at[here, :]
        else:
            start, end = source.at[here, :], target.at[:, there]
        if mask:
            copies.append(remote(start, end, sems.at[0, slot], sems.at[1, slot], (other, place)))
        else:
            copy = pltpu.make_async_copy(start, end, sems.at[0, slot])
            copy.start()
            copies.append(copy)
    return copies


def finish(copies):
    for copy in copies:
        copy.wait()


def split_refs(refs, *counts):
    groups, start = [], 0
    for count in counts:
        groups.append(list(refs[start : start + count]))
        start += count
    return groups


def norm_rows(rows, gain, shift):
    center = rows - jnp.mean(rows, axis=-1, keepdims=True)
    spread = jnp.mean(center * center, axis=-1, keepdims=True)
    return center * lax.rsqrt(spread + norm_eps) * gain + shift


def norm_rows_back(rows, gain, grad):
    center = rows - jnp.mean(rows, axis=-1, keepdims=True)
    scale = lax.rsqrt(jnp.mean(center * center, axis=-1, keepdims=True) + norm_eps)
    normed = center * scale
    inner = grad * gain
    grad_rows = scale * (
        inner
        - jnp.mean(inner, axis=-1, keepdims=True)
        - normed * jnp.mean(inner * normed, axis=-1, keepdims=True)
    )
    return (
        grad_rows,
        jnp.sum(grad * normed, axis=0, keepdims=True),
        jnp.sum(grad, axis=0, keepdims=True),
    )


def rows_of(ref, height, index):
    return ref[pl.ds(pl.multiple_of(index * height, height), height), :]


def exchange_scratch(height, width):
    return [
        pltpu.VMEM((2, height, width), jnp.bfloat16),
        pltpu.VMEM((2, height, width), jnp.bfloat16),
        pltpu.VMEM((height, width), jnp.bfloat16),
        pltpu.VMEM((height, width), jnp.bfloat16),
        DMA((2, 6)),
    ]


def mix_norm_kernel(total, with_ids, masks, chained, *refs):
    (left, weight, kept, gain, shift), ids, table, (quarters, normed, rows), ids_all, wide, refs = (
        split_refs(
            refs, 5, with_ids, (1 + chained) * bool(masks), 3, with_ids, bool(masks), len(refs)
        )
    )
    sib_send, sib_recv, far_send, far_recv, sems = refs[:5]
    refs = refs[5:]
    block, place = lax.axis_index("dp"), lax.axis_index("mp")
    near, far = (block, flip(place, 1)), (block, flip(place, 2))
    height = kept.shape[0]
    others = range(1, total) if with_ids else [mask for mask in masks if mask]
    greet([near, far] + [(flip(block, mask), place) for mask in others])
    copies = []
    if with_ids:
        ids_sems, ids_local = refs[:2]
        refs = refs[2:]
        own = pltpu.make_async_copy(ids[0], ids_all[0].at[block], ids_local)
        own.start()
        copies.append(own)
        for mask in range(1, total):
            copies.append(
                remote(
                    ids[0], ids_all[0].at[block], ids_sems.at[0, mask], ids_sems.at[1, mask],
                    (flip(block, mask), place),
                )
            )

    def block_of(index):
        return jnp.dot(
            rows_of(left, height, index), weight[...], preferred_element_type=jnp.float32
        )

    if masks:
        copies += table_copies(masks, False, table[0], wide[0], refs[0])
    branch, sent = sum_quarter(
        place, block_of, near, far, sib_send, sib_recv, far_send, far_recv, sems
    )
    outcome = kept[...].astype(jnp.float32) + branch
    rows[...] = outcome
    outcome = norm_rows(outcome, gain[...], shift[...])
    normed[...] = outcome
    quarters[place] = outcome.astype(jnp.bfloat16)
    sent += share_quarter(place, quarters, near, far, sems)
    finish(copies)
    for copy in sent:
        copy.wait_send()


def mix_norm(left, weight, kept, gain, shift, number, ids=None, table=None, wide=None, masks=()):
    height, width = kept.shape
    total = lax.axis_size("dp")
    quarter = jax.ShapeDtypeStruct((height, width), jnp.float32)
    out_shape = [
        jax.ShapeDtypeStruct((QUARTERS, height, width), jnp.bfloat16), quarter, quarter
    ]
    out_specs = [VMEM] * 3
    given = [left, weight, kept, gain.reshape(1, -1), shift.reshape(1, -1)]
    in_specs = [VMEM] * 5
    scratch = exchange_scratch(height, width)
    aliases = {}
    if ids is not None:
        given.append(ids)
        in_specs.append(VMEM)
        out_shape.append(jax.ShapeDtypeStruct((total,) + ids.shape, ids.dtype))
        out_specs.append(VMEM)
        scratch += [DMA((2, total)), DMA]
    if masks:
        given.append(table)
        in_specs.append(ANY)
        if wide is not None:
            aliases = {len(given): len(out_shape)}
            given.append(wide)
            in_specs.append(ANY)
        out_shape.append(
            jax.ShapeDtypeStruct((table.shape[0] // total, table.shape[1] * total), table.dtype)
        )
        out_specs.append(ANY)
        scratch.append(DMA((2, len(masks))))
    outcome = pl.pallas_call(
        functools.partial(
            mix_norm_kernel, total, int(ids is not None), tuple(masks), int(wide is not None)
        ),
        out_shape=out_shape,
        in_specs=in_specs,
        out_specs=out_specs,
        scratch_shapes=scratch,
        input_output_aliases=aliases,
        compiler_params=pltpu.CompilerParams(
            collective_id=number, has_side_effects=True, vmem_limit_bytes=48 * 2**20
        ),
    )(*given)
    return (outcome[0].reshape(-1, width),) + tuple(outcome[1:])


def chunk_of(rows):
    return max(size for size in range(16, min(rows, 400) + 1, 16) if rows % size == 0)


def feed_norm_kernel(total, early, *refs):
    (left, weight, kept, gain, shift, targets), words, (states, rows, logits, totals), wide, refs = (
        split_refs(refs, 6, 1 + 2 * bool(early), 4, bool(early), len(refs))
    )
    last = words[-1]
    low, sib_send, sib_recv, far_send, far_recv, sems, hops, own_sem = refs[:8]
    (held, staged, sends, recvs, held_sem, staged_sems, stage_sems), refs = refs[8:15], refs[15:]
    block, place = lax.axis_index("dp"), lax.axis_index("mp")
    near, far = (block, flip(place, 1)), (block, flip(place, 2))
    beside = (flip(block, 1), place)
    height = kept.shape[0]
    bits = (total - 1).bit_length()
    others = set(range(1, total) if early else range(2, total, 2))
    others |= {1 << bit for bit in range(bits)}
    greet([near, far] + [(flip(block, mask), place) for mask in sorted(others)])

    def block_of(index):
        return jnp.dot(
            rows_of(left, height, index), weight[...], preferred_element_type=jnp.float32
        )

    moved = []
    if early:
        moved = table_copies(early, False, words[0], wide[0], refs[0])
    branch, sent = sum_quarter(
        place, block_of, near, far, sib_send, sib_recv, far_send, far_recv, sems
    )
    outcome = kept[...] + branch
    rows[...] = outcome
    low[...] = norm_rows(outcome, gain[...], shift[...]).astype(jnp.bfloat16)
    own = pltpu.make_async_copy(low, states.at[block, place], own_sem)
    own.start()
    across = flip(place, 2)

    def hop(kind, mask, source, peer, row, column):
        copy = remote(
            source, states.at[row, column], hops.at[0, kind, mask], hops.at[1, kind, mask], peer
        )
        sent.append(copy)
        return copy

    first = {}

    def spread(masks):
        for mask in masks:
            first[mask] = hop(0, mask, low, (flip(block, mask), place), block, place)

    spread([2])
    nearest = len(sent) - 1
    over, ends = {}, {}

    def pass_on(mask):
        over[mask].wait_recv()
        row = flip(block, mask)
        ends[mask, 1] = hop(3, mask, states.at[row, across], near, row, across)

    def arrive(mask):
        row = flip(block, mask)
        if mask:
            first[mask].wait_recv()
        source = states.at[row, place] if mask else low
        if mask % 2 == 0:
            first[mask + 1] = hop(0, mask + 1, source, beside, row, place)
        over[mask] = hop(1, mask, source, far, row, place)
        ends[mask, 0] = hop(2, mask, source, near, row, place)

    part, width = held.shape
    chunk = chunk_of(part)
    span = QUARTERS * height
    writes = {}

    def make(mask):
        row, slot = flip(block, mask), mask % 2
        for side in (0, 1):
            ends[mask, side].wait_recv()
        if mask >= 2:
            writes[mask - 2].wait()
        block_states = states[row].reshape(span, width)
        target = targets[row]

        def body(turn, carry):
            top, amount, picked = carry
            start = pl.multiple_of(turn * chunk, chunk)
            scores = product_nt(held[pl.ds(start, chunk), :], block_states)
            staged[slot, pl.ds(start, chunk), :] = scores
            ahead = jnp.maximum(top, jnp.max(scores, axis=0, keepdims=True))
            ids = start + lax.broadcasted_iota(jnp.int32, (chunk, 1), 0)
            return (
                ahead,
                amount * jnp.exp(top - ahead)
                + jnp.sum(jnp.exp(scores - ahead), axis=0, keepdims=True),
                picked
                + jnp.sum(jnp.where(ids == target, scores, 0.0), axis=0, keepdims=True),
            )

        scores = product_nt(held[0:chunk, :], block_states)
        staged[slot, 0:chunk, :] = scores
        top = jnp.max(scores, axis=0, keepdims=True)
        ids = lax.broadcasted_iota(jnp.int32, (chunk, 1), 0)
        carry = (
            top,
            jnp.sum(jnp.exp(scores - top), axis=0, keepdims=True),
            jnp.sum(jnp.where(ids == target, scores, 0.0), axis=0, keepdims=True),
        )
        if part > chunk:
            carry = lax.fori_loop(1, part // chunk, body, carry)
        for index in range(3):
            sends[0, index, pl.ds(row, 1), :] = carry[index]
        writes[mask] = pltpu.make_async_copy(
            staged.at[slot], logits.at[row], staged_sems.at[slot]
        )
        writes[mask].start()

    lag = 3
    for step in range(total + lag):
        if step < total:
            arrive(step)
        if step == 0:
            del sent[nearest]
            first[2].wait_send()
            spread(range(4, total, 2))
        if 2 <= step < total + 2:
            pass_on(step - 2)
        if step == lag:
            finish(moved)
            load = pltpu.make_async_copy(wide[0] if early else words[0], held, held_sem)
            load.start()
            own.wait()
            load.wait()
            if early:
                spot = pl.ds(pl.multiple_of(flip(block, total - 1) * last.shape[1], 128), 128)
                load = pltpu.make_async_copy(last, held.at[:, spot], held_sem)
                load.start()
                load.wait()
        if step >= lag:
            make(step - lag)
    lead = max(total - 2, 0)
    for mask in range(lead, total):
        writes[mask].wait()

    peers = [(near, lax.rem(place, 2)), (far, lax.div(place, 2))]
    for bit in range(bits):
        step = 1 << bit
        peers.append(((flip(block, step), place), lax.rem(lax.div(block, step), 2)))
    for stage, (peer, side) in enumerate(peers):
        copy = remote(
            sends.at[stage], recvs.at[stage], stage_sems.at[0, stage], stage_sems.at[1, stage],
            peer,
        )
        copy.wait_recv()
        sent.append(copy)
        mine = [sends[stage, index] for index in range(3)]
        theirs = [recvs[stage, index] for index in range(3)]
        leading = side == 0
        soon = [jnp.where(leading, one, other) for one, other in zip(mine, theirs)]
        late_ones = [jnp.where(leading, other, one) for one, other in zip(mine, theirs)]
        top = jnp.maximum(soon[0], late_ones[0])
        values = [
            top,
            soon[1] * jnp.exp(soon[0] - top) + late_ones[1] * jnp.exp(late_ones[0] - top),
            soon[2] + late_ones[2],
        ]
        for index in range(3):
            if stage + 1 < len(peers):
                sends[stage + 1, index] = values[index]
            else:
                totals[index] = values[index]
    for copy in sent:
        copy.wait_send()


def feed_norm(
    left, weight, kept, gain, shift, targets, number, table, wide=None, last=None, early=()
):
    height, width = kept.shape
    total = lax.axis_size("dp")
    stages = 2 + (total - 1).bit_length()
    span = QUARTERS * height
    words = wide if early else table
    part = words.shape[0]
    given = [left, weight, kept, gain.reshape(1, -1), shift.reshape(1, -1), targets, table]
    in_specs = [VMEM] * 6 + [ANY]
    out_shape = [
        jax.ShapeDtypeStruct((total, QUARTERS, height, width), jnp.bfloat16),
        jax.ShapeDtypeStruct((height, width), jnp.float32),
        jax.ShapeDtypeStruct((total, part, span), jnp.float32),
        jax.ShapeDtypeStruct((3, total, span), jnp.float32),
    ]
    out_specs = [VMEM, VMEM, ANY, VMEM]
    scratch = [pltpu.VMEM((height, width), jnp.bfloat16)] + exchange_scratch(height, width)
    scratch += [
        DMA((2, 4, total)),
        DMA,
        pltpu.VMEM((part, width), jnp.bfloat16),
        pltpu.VMEM((2, part, span), jnp.float32),
        pltpu.VMEM((stages, 3, total, span), jnp.float32),
        pltpu.VMEM((stages, 3, total, span), jnp.float32),
        DMA,
        DMA((2,)),
        DMA((2, stages)),
    ]
    aliases = {}
    if early:
        given += [wide, last]
        in_specs += [ANY] * 2
        out_shape.append(jax.ShapeDtypeStruct(wide.shape, wide.dtype))
        out_specs.append(ANY)
        aliases = {7: 4}
        scratch.append(DMA((2, len(early))))
    outcome = pl.pallas_call(
        functools.partial(feed_norm_kernel, total, tuple(early)),
        out_shape=out_shape,
        in_specs=in_specs,
        out_specs=out_specs,
        scratch_shapes=scratch,
        input_output_aliases=aliases,
        compiler_params=pltpu.CompilerParams(
            collective_id=number, has_side_effects=True, vmem_limit_bytes=62 * 2**20
        ),
    )(*given)
    return tuple(outcome)


def head_back_kernel(total, masks, fused, *refs):
    (parts, rows, gain), more, (quarters, grad_rows, grad_vecs), table, narrow, refs = split_refs(
        refs, 3, 5 * fused, 3, fused, bool(masks), len(refs)
    )
    mine, sib_recv, far_recv, beside_recv, across_recv, end_recv, sems = refs[:7]
    sib_sems, far_sems, beside_sems, end_sems, load_sems = refs[7:12]
    refs = refs[12:]
    block, place = lax.axis_index("dp"), lax.axis_index("mp")
    near, far = (block, flip(place, 1)), (block, flip(place, 2))
    beside = (flip(block, 1), place)
    height = rows.shape[0]
    others = range(1, total) if masks else [1] + list(range(2, total, 2))
    greet([near, far] + [(flip(block, mask), place) for mask in others])
    moved = []
    aside = [1]
    order = [mask for mask in range(total - 1, -1, -1) if mask != 1]
    order.insert(1, 1)
    sent, loads, sib, across, over, ends = [], {}, {}, {}, {}, {}

    def to_near(mask, slot, source):
        sib[mask, slot] = remote(
            source,
            sib_recv.at[mask, slot],
            sib_sems.at[0, mask, slot],
            sib_sems.at[1, mask, slot],
            near,
        )
        sent.append(sib[mask, slot])

    if fused:
        words, states, log_totals, grad_logp, targets = more
        if masks:
            move_sems, refs = refs[0], refs[1:]
        logits, held, grads, acc, held_sems = refs
        part = words.shape[0]
        chunk = chunk_of(part)
        span = grads.shape[2]

        def load(step):
            slot = step % 2
            loads[step] = pltpu.make_async_copy(
                parts.at[flip(block, order[step])], logits.at[slot], load_sems.at[slot, 0]
            )
            loads[step].start()

        def load_states(step):
            slot = step % 2
            loads[step, None] = pltpu.make_async_copy(
                states.at[flip(block, order[step])], held.at[slot], held_sems.at[slot]
            )
            loads[step, None].start()

        load(0)
        load_states(0)
    else:
        for mask in order:
            row = flip(block, mask)
            for turn in range(QUARTERS):
                if turn % 2 == 0:
                    loads[mask, turn] = pltpu.make_async_copy(
                        parts.at[row, flip(place, turn)],
                        mine.at[mask, 1 - turn // 2],
                        load_sems.at[mask, turn // 2],
                    )
                    loads[mask, turn].start()
                else:
                    to_near(mask, (3 - turn) // 2, parts.at[row, flip(place, turn)])

    def make(step):
        mask = order[step]
        if not fused:
            for turn in (0, 2):
                loads[mask, turn].wait()
            return
        if step + 1 < len(order):
            load(step + 1)
        loads[step].wait()
        row, slot = flip(block, mask), step % 2
        target, log_total, scale = targets[row], log_totals[row], grad_logp[row]

        def body(turn, carry):
            start = pl.multiple_of(turn * chunk, chunk)
            ids = start + lax.broadcasted_iota(jnp.int32, (chunk, 1), 0)
            hot = (ids == target).astype(jnp.float32)
            chances = jnp.exp(logits[slot, pl.ds(start, chunk), :] - log_total)
            grads[step, pl.ds(start, chunk), :] = (scale * (hot - chances)).astype(jnp.bfloat16)
            return carry

        lax.fori_loop(0, part // chunk, body, 0)
        mine[mask] = (
            product_tn(grads[step], words[...]).astype(jnp.bfloat16).reshape(mine.shape[1:])
        )
        for slot, turn in enumerate((3, 1)):
            to_near(mask, slot, mine.at[mask, flip(place, turn)])

    def make_rows(step):
        if step + 1 < len(order):
            load_states(step + 1)
        loads[step, None].wait()
        block_states = held[step % 2].reshape(span, rows.shape[1])

        def body(turn, carry):
            here = pl.ds(pl.multiple_of(turn * chunk, chunk), chunk)
            value = dot_nn(grads[step, here, :], block_states)
            if step:
                value = value + acc[here, :]
            if step + 1 < len(order):
                acc[here, :] = value
            else:
                table[0][here, :] = value.astype(jnp.bfloat16)
            return carry

        lax.fori_loop(0, part // chunk, body, 0)

    own = (flip(place, 2), place) if fused else (0, 1)

    def join(mask, slot, *others):
        value = mine[mask, own[slot]].astype(jnp.float32)
        for other in others:
            value = value + other.astype(jnp.float32)
        return value

    def send_beside(mask, slot, target, sem_row):
        index = mask // 2
        copy = remote(
            mine.at[mask, own[slot]],
            target.at[index],
            beside_sems.at[0, sem_row, index],
            beside_sems.at[1, sem_row, index],
            beside,
        )
        sent.append(copy)
        return copy

    def to_far(mask):
        for slot in (0, 1):
            sib[mask, slot].wait_recv()
        terms = [sib_recv[mask, 0]]
        if mask + 1 in aside:
            across[mask + 1].wait_recv()
            terms.append(across_recv[mask // 2])
        mine[mask, own[0]] = join(mask, 0, *terms).astype(jnp.bfloat16)
        if mask in aside:
            mine[mask, own[1]] = join(mask, 1, sib_recv[mask, 1]).astype(jnp.bfloat16)
            across[mask] = send_beside(mask, 0, across_recv, 0)
            over[mask] = send_beside(mask, 1, beside_recv, 1)
            return
        across[mask] = remote(
            mine.at[mask, own[0]], far_recv.at[mask], far_sems.at[0, mask], far_sems.at[1, mask], far
        )
        sent.append(across[mask])

    def to_beside(mask):
        if mask in aside:
            return
        across[mask].wait_recv()
        mine[mask, own[1]] = join(mask, 1, sib_recv[mask, 1], far_recv[mask]).astype(jnp.bfloat16)
        over[mask] = send_beside(mask, 1, beside_recv, 1)

    def to_end(mask):
        across[mask].wait_recv()
        over[mask + 1].wait_recv()
        value = join(mask, 1, sib_recv[mask, 1], far_recv[mask], beside_recv[mask // 2])
        if mask == 0:
            return value
        mine[mask, own[1]] = value.astype(jnp.bfloat16)
        ends[mask] = remote(
            mine.at[mask, own[1]],
            end_recv.at[mask // 2],
            end_sems.at[0, mask // 2],
            end_sems.at[1, mask // 2],
            (flip(block, mask), place),
        )
        sent.append(ends[mask])
        return None

    outcome = None
    count = len(order)
    make(0)
    for step in range(count + 2):
        if step + 1 < count:
            make(step + 1)
        if step < count:
            to_far(order[step])
        if step >= 2:
            mask = order[step - 2]
            if mask % 2:
                to_beside(mask)
            else:
                outcome = to_end(mask)
        if fused and 1 <= step <= count:
            make_rows(step - 1)
            if masks and step == count:
                moved = table_copies(masks, True, table[0], narrow[0], move_sems)
    for mask in range(total - 2, 0, -2):
        ends[mask].wait_recv()
        outcome = outcome + end_recv[mask // 2].astype(jnp.float32)
    outcome, grad_gain, grad_shift = norm_rows_back(rows[...], gain[...], outcome)
    grad_rows[...] = outcome
    grad_vecs[0:1] = grad_gain
    grad_vecs[1:2] = grad_shift
    quarters[place] = outcome.astype(jnp.bfloat16)
    sent += share_quarter(place, quarters, near, far, sems)
    for copy in sent:
        copy.wait_send()
    finish(moved)


def head_back(values, rows, gain, number, masks=()):
    height, width = rows.shape
    total = lax.axis_size("dp")
    half = total // 2
    block = (height, width)
    fused = len(values) > 1
    out_shape = [
        jax.ShapeDtypeStruct((QUARTERS,) + block, jnp.bfloat16),
        jax.ShapeDtypeStruct(block, jnp.float32),
        jax.ShapeDtypeStruct((2, width), jnp.float32),
    ]
    out_specs = [VMEM] * 3
    scratch = [
        pltpu.VMEM((total, QUARTERS if fused else 2) + block, jnp.bfloat16),
        pltpu.VMEM((total, 2) + block, jnp.bfloat16),
        pltpu.VMEM((total,) + block, jnp.bfloat16),
        pltpu.VMEM((half,) + block, jnp.bfloat16),
        pltpu.VMEM((half,) + block, jnp.bfloat16),
        pltpu.VMEM((half,) + block, jnp.bfloat16),
        DMA((2, 6)),
        DMA((2, total, 2)),
        DMA((2, total)),
        DMA((2, 2, half)),
        DMA((2, half)),
        DMA((total, 2)),
    ]
    given = [values[0], rows, gain.reshape(1, -1)]
    in_specs = [ANY, VMEM, VMEM]
    if fused:
        words, states = values[1:3]
        part, span = values[0].shape[1:]
        given += list(values[1:])
        in_specs += [VMEM, ANY, VMEM, VMEM, VMEM]
        out_shape.append(jax.ShapeDtypeStruct(words.shape, jnp.bfloat16))
        out_specs.append(VMEM)
        if masks:
            narrow = (part * total, width // total)
            out_shape.append(jax.ShapeDtypeStruct(narrow, jnp.bfloat16))
            out_specs.append(ANY)
            scratch.append(DMA((2, len(masks))))
        scratch += [
            pltpu.VMEM((2, part, span), jnp.float32),
            pltpu.VMEM((2, QUARTERS) + block, jnp.bfloat16),
            pltpu.VMEM((total, part, span), jnp.bfloat16),
            pltpu.VMEM((part, width), jnp.float32),
            DMA((2,)),
        ]
    outcome = pl.pallas_call(
        functools.partial(head_back_kernel, total, tuple(masks), int(fused)),
        out_shape=out_shape,
        in_specs=in_specs,
        out_specs=out_specs,
        scratch_shapes=scratch,
        compiler_params=pltpu.CompilerParams(
            collective_id=number, has_side_effects=True, vmem_limit_bytes=63 * 2**20
        ),
    )(*given)
    return (outcome[0].reshape(-1, width),) + tuple(outcome[1:])


def dot_nn(left, right):
    return jnp.dot(left, right, preferred_element_type=jnp.float32)


def attend_back(queries, keys, values, grads, totals, allowed_at, acc_keys, acc_values, grad_queries,
                grad_keys, grad_values):
    span, width = keys.shape
    rows = queries.shape[0]
    step = min(256, rows)
    pair = 2 * HEAD_DIM
    lanes = lax.broadcasted_iota(jnp.int32, (1, pair), 1)
    sides = [(lanes // HEAD_DIM == side).astype(jnp.bfloat16) for side in range(2)]
    acc_keys[0:span] = jnp.zeros((span, width), jnp.float32)
    acc_values[0:span] = jnp.zeros((span, width), jnp.float32)

    def body(turn, carry):
        here = pl.ds(pl.multiple_of(turn * step, step), step)
        allowed = allowed_at(here)
        for start in range(0, width, pair):
            group = slice(start, start + pair)
            key, value = keys[:, group], values[:, group]
            query, grad = queries[here, group], grads[here, group]
            grad_query = jnp.zeros((step, pair), jnp.float32)
            for side in range(2):
                head = start // HEAD_DIM + side
                query_head, grad_head = query * sides[side], grad * sides[side]
                scores = product_nt(key, query_head) * HEAD_DIM ** (-0.5)
                scores = jnp.where(allowed, scores, masked_score)
                weights = jnp.exp(scores - totals[head : head + 1, here])
                grad_weights = product_nt(value, grad_head)
                row_dot = jnp.sum(grad_weights * weights, axis=0, keepdims=True)
                grad_scores = (weights * (grad_weights - row_dot)).astype(jnp.bfloat16)
                acc_values[0:span, group] += dot_nn(weights.astype(jnp.bfloat16), grad_head)
                acc_keys[0:span, group] += dot_nn(grad_scores, query_head)
                grad_query += product_tn(grad_scores, key * sides[side])
            grad_queries[here, group] = (grad_query * HEAD_DIM ** (-0.5)).astype(jnp.bfloat16)
        return carry

    lax.fori_loop(0, rows // step, body, 0)
    grad_keys[...] = (acc_keys[0:span] * HEAD_DIM ** (-0.5)).astype(jnp.bfloat16)
    grad_values[...] = acc_values[0:span].astype(jnp.bfloat16)


def attend(queries, keys, values, allowed_at, mixed, totals):
    rows, width = queries.shape
    step = min(256, rows)
    pair = 2 * HEAD_DIM
    lanes = lax.broadcasted_iota(jnp.int32, (1, pair), 1)
    sides = [(lanes // HEAD_DIM == side).astype(jnp.bfloat16) for side in range(2)]

    def body(turn, carry):
        here = pl.ds(pl.multiple_of(turn * step, step), step)
        allowed = allowed_at(here)
        for start in range(0, width, pair):
            group = slice(start, start + pair)
            key, value, query = keys[:, group], values[:, group], queries[here, group]
            mix = jnp.zeros((step, pair), jnp.float32)
            for side in range(2):
                head = start // HEAD_DIM + side
                scores = product_nt(key, query * sides[side]) * HEAD_DIM ** (-0.5)
                scores = jnp.where(allowed, scores, masked_score)
                largest = jnp.max(scores, axis=0, keepdims=True)
                weights = jnp.exp(scores - largest)
                amount = jnp.sum(weights, axis=0, keepdims=True)
                chances = (weights * (1.0 / amount)).astype(jnp.bfloat16)
                mix += product_tn(chances, value * sides[side])
                totals[head : head + 1, here] = largest + jnp.log(amount)
            mixed[here, group] = mix.astype(jnp.bfloat16)
        return carry

    lax.fori_loop(0, rows // step, body, 0)


class Given(typing.NamedTuple):
    tokens: typing.Any
    self_query: typing.Any
    self_key: typing.Any
    self_value: typing.Any
    self_out: typing.Any
    memory: typing.Any
    cross_key: typing.Any
    cross_value: typing.Any
    cross_query: typing.Any
    cross_out: typing.Any
    feed_up: typing.Any
    feed_down: typing.Any


class Small(typing.NamedTuple):
    ids: typing.Any
    segment_row: typing.Any
    segment_column: typing.Any
    gain_self: typing.Any
    shift_self: typing.Any
    gain_cross: typing.Any
    shift_cross: typing.Any
    gain_feed: typing.Any
    shift_feed: typing.Any


class Kept(typing.NamedTuple):
    query_self: typing.Any
    key_self: typing.Any
    value_self: typing.Any
    self_totals: typing.Any
    self_mix: typing.Any
    first_low: typing.Any
    rows_self: typing.Any
    key_cross: typing.Any
    value_cross: typing.Any
    query_cross: typing.Any
    cross_totals: typing.Any
    cross_mix: typing.Any
    second_low: typing.Any
    rows_cross: typing.Any
    feed_act: typing.Any
    gelu_slope: typing.Any
    rows_feed: typing.Any
    words: typing.Any
    states: typing.Any


def layer_kernel(total, *refs):
    count, made = len(Given._fields), len(Kept._fields)
    sources, small, table, targets, (logits, totals, ids_all), held, kept, refs = split_refs(
        refs, count, len(Small._fields), 1, made, 3, count, made, len(refs)
    )
    load_sems, keep_sems, ids_sems, ids_local, move_sems = refs[:5]
    buffers, refs = [refs[5:10], refs[10:15], refs[15:20]], refs[20:]
    normed, hops, staged, sends, recvs, staged_sems, stage_sems = refs
    small, kept = Small(*small), Kept(*kept)
    block, place = lax.axis_index("dp"), lax.axis_index("mp")
    near, far = (block, flip(place, 1)), (block, flip(place, 2))
    beside = (flip(block, 1), place)
    bits = (total - 1).bit_length()
    loads = [
        pltpu.make_async_copy(source, target, load_sems.at[index])
        for index, (source, target) in enumerate(zip(sources, held))
    ]
    for copy in loads:
        copy.start()
    loaded = set()

    def get(index):
        if index not in loaded:
            loaded.add(index)
            loads[index].wait()
        return held[index]

    at = Given(*range(count))
    places = Kept(*range(made))
    saves = [
        pltpu.make_async_copy(source, target, keep_sems.at[index])
        for index, (source, target) in enumerate(zip(kept, targets))
    ]

    def save(*indices):
        for index in indices:
            saves[index].start()

    greet([near, far] + [(flip(block, mask), place) for mask in range(1, total)])
    moved = table_copies((4, 5, 6, 7, 1, 2, 3, 0), False, table[0], kept.words, move_sems)
    ids_copies = [pltpu.make_async_copy(small.ids, ids_all.at[block], ids_local)]
    ids_copies[0].start()
    for mask in range(1, total):
        ids_copies.append(
            remote(
                small.ids, ids_all.at[block], ids_sems.at[0, mask], ids_sems.at[1, mask],
                (flip(block, mask), place),
            )
        )
    sent = []
    tokens = get(at.tokens)
    span, width = tokens.shape
    height = span // QUARTERS
    for weight, outcome, index in (
        (at.self_query, kept.query_self, places.query_self),
        (at.self_key, kept.key_self, places.key_self),
        (at.self_value, kept.value_self, places.value_self),
    ):
        outcome[...] = dot_nn(tokens[...], get(weight)[...]).astype(jnp.bfloat16)
        save(index)
    key_place = lax.broadcasted_iota(jnp.int32, (span, 1), 0)

    def allowed_self(here):
        query_place = here.start + lax.broadcasted_iota(jnp.int32, (1, here.size), 1)
        return (small.segment_column[...] == small.segment_row[:, here]) & (
            key_place <= query_place
        )

    attend(
        kept.query_self, kept.key_self, kept.value_self, allowed_self, kept.self_mix,
        kept.self_totals,
    )
    save(places.self_totals, places.self_mix)

    def join(turn, left, weight, residual, rows, fill):
        outcome = []
        run(
            sum_quarter_steps(
                place,
                lambda index: dot_nn(rows_of(left, height, index), weight[...]),
                near, far, *buffers[turn], outcome, sent,
            ),
            fill,
        )
        rows[...] = residual + outcome[0]

    def share(turn, quarters, fill):
        run(share_quarter_steps(place, quarters, near, far, buffers[turn][4], sent), fill)

    def make_keys():
        kept.key_cross[...] = dot_nn(get(at.memory)[...], get(at.cross_key)[...]).astype(
            jnp.bfloat16
        )

    def make_values():
        kept.value_cross[...] = dot_nn(get(at.memory)[...], get(at.cross_value)[...]).astype(
            jnp.bfloat16
        )

    join(
        0, kept.self_mix, get(at.self_out),
        rows_of(tokens, height, place).astype(jnp.float32), kept.rows_self, make_keys,
    )
    normed[...] = norm_rows(kept.rows_self[...], small.gain_self[...], small.shift_self[...])
    kept.first_low[place] = normed[...].astype(jnp.bfloat16)
    share(0, kept.first_low, make_values)
    save(places.key_cross, places.value_cross, places.rows_self, places.first_low)

    kept.query_cross[...] = dot_nn(
        kept.first_low[...].reshape(span, width), get(at.cross_query)[...]
    ).astype(jnp.bfloat16)
    owners = lax.broadcasted_iota(jnp.int32, (kept.key_cross.shape[0], 1), 0) // MEM
    attend(
        kept.query_cross, kept.key_cross, kept.value_cross,
        lambda here: owners == small.segment_row[:, here], kept.cross_mix, kept.cross_totals,
    )
    save(places.query_cross, places.cross_totals, places.cross_mix)
    join(1, kept.cross_mix, get(at.cross_out), normed[...], kept.rows_cross, None)
    normed[...] = norm_rows(kept.rows_cross[...], small.gain_cross[...], small.shift_cross[...])
    kept.second_low[place] = normed[...].astype(jnp.bfloat16)
    share(1, kept.second_low, None)
    save(places.rows_cross, places.second_low)

    get(at.feed_up)
    wide = kept.gelu_slope.shape[2]
    depth = kept.gelu_slope.shape[1]
    second = kept.second_low[...].reshape(span, width)
    for turn in range(kept.feed_act.shape[1] // wide):
        columns = slice(turn * wide, (turn + 1) * wide)
        pre = dot_nn(second, get(at.feed_up)[:, columns])
        chance = 0.5 + 0.5 * lax.erf(pre * 0.5**0.5)
        kept.feed_act[:, columns] = (pre * chance).astype(jnp.bfloat16)
        start = turn * span
        kept.gelu_slope[start // depth, start % depth : start % depth + span] = (
            chance + pre * jnp.exp(-0.5 * pre * pre) * (0.5 / jnp.pi) ** 0.5
        )
    save(places.feed_act, places.gelu_slope)
    join(2, kept.feed_act, get(at.feed_down), normed[...], kept.rows_feed, None)
    save(places.rows_feed)
    states = kept.states
    low = states.at[block, place]
    low[...] = norm_rows(
        kept.rows_feed[...], small.gain_feed[...], small.shift_feed[...]
    ).astype(jnp.bfloat16)
    across = flip(place, 2)

    def hop(kind, mask, peer, row, column):
        here = states.at[row, column]
        copy = remote(here, here, hops.at[0, kind, mask], hops.at[1, kind, mask], peer)
        sent.append(copy)
        return copy

    first, over, ends = {}, {}, {}

    def spread(masks):
        for mask in masks:
            first[mask] = hop(0, mask, (flip(block, mask), place), block, place)

    def pass_on(mask):
        over[mask].wait_recv()
        ends[mask, 1] = hop(3, mask, near, flip(block, mask), across)

    def arrive(mask):
        row = flip(block, mask)
        if mask:
            first[mask].wait_recv()
        if mask % 2 == 0:
            first[mask + 1] = hop(0, mask + 1, beside, row, place)
        over[mask] = hop(1, mask, far, row, place)
        ends[mask, 0] = hop(2, mask, near, row, place)

    words = kept.words
    part = words.shape[0]
    chunk = chunk_of(part)
    offset = (place * total + block) * part
    writes = {}

    def make(mask):
        row, slot = flip(block, mask), mask % 2
        for side in (0, 1):
            ends[mask, side].wait_recv()
        if mask >= 2:
            writes[mask - 2].wait()
        block_states = states[row].reshape(span, width)
        target = ids_all[row, 1:2] - offset

        def chunk_at(start):
            scores = product_nt(words[pl.ds(start, chunk), :], block_states)
            staged[slot, pl.ds(start, chunk), :] = scores
            ids = start + lax.broadcasted_iota(jnp.int32, (chunk, 1), 0)
            return (
                scores,
                jnp.max(scores, axis=0, keepdims=True),
                jnp.sum(jnp.where(ids == target, scores, 0.0), axis=0, keepdims=True),
            )

        def body(turn, carry):
            top, amount, picked = carry
            scores, ahead, more = chunk_at(pl.multiple_of(turn * chunk, chunk))
            ahead = jnp.maximum(top, ahead)
            return (
                ahead,
                amount * jnp.exp(top - ahead)
                + jnp.sum(jnp.exp(scores - ahead), axis=0, keepdims=True),
                picked + more,
            )

        scores, top, picked = chunk_at(0)
        carry = (top, jnp.sum(jnp.exp(scores - top), axis=0, keepdims=True), picked)
        carry = lax.fori_loop(1, part // chunk, body, carry)
        for index in range(3):
            sends[0, index, pl.ds(row, 1), :] = carry[index]
        writes[mask] = pltpu.make_async_copy(
            staged.at[slot], logits.at[row], staged_sems.at[slot]
        )
        writes[mask].start()

    spread([2])
    nearest = len(sent) - 1
    lag = 3
    for step in range(total + lag):
        if step < total:
            arrive(step)
        if step == 0:
            del sent[nearest]
            first[2].wait_send()
            spread(range(4, total, 2))
        if 2 <= step < total + 2:
            pass_on(step - 2)
        if step == lag:
            finish(ids_copies)
            finish(moved)
            save(places.words)
        if step >= lag:
            make(step - lag)
    save(places.states)

    peers = [(near, lax.rem(place, 2)), (far, lax.div(place, 2))]
    for bit in range(bits):
        step = 1 << bit
        peers.append(((flip(block, step), place), lax.rem(lax.div(block, step), 2)))
    for stage, (peer, side) in enumerate(peers):
        copy = remote(
            sends.at[stage], recvs.at[stage], stage_sems.at[0, stage], stage_sems.at[1, stage],
            peer,
        )
        copy.wait_recv()
        sent.append(copy)
        mine = [sends[stage, index] for index in range(3)]
        theirs = [recvs[stage, index] for index in range(3)]
        leading = side == 0
        soon = [jnp.where(leading, one, other) for one, other in zip(mine, theirs)]
        later = [jnp.where(leading, other, one) for one, other in zip(mine, theirs)]
        top = jnp.maximum(soon[0], later[0])
        values = [
            top,
            soon[1] * jnp.exp(soon[0] - top) + later[1] * jnp.exp(later[0] - top),
            soon[2] + later[2],
        ]
        for index in range(3):
            if stage + 1 < len(peers):
                sends[stage + 1, index] = values[index]
            else:
                totals[index] = values[index]
    for mask in range(total - 2, total):
        writes[mask].wait()
    for copy in sent:
        copy.wait_send()
    for copy in saves:
        copy.wait()


def layer_forward(given, small, table, number):
    total = lax.axis_size("dp")
    rows, width = given.tokens.shape
    span = given.memory.shape[0]
    part = given.self_query.shape[1]
    hidden = given.feed_up.shape[1]
    height = rows // QUARTERS
    words = table.shape[0] // total
    stages = 2 + (total - 1).bit_length()
    heads = part // HEAD_DIM

    def low(*shape):
        return jax.ShapeDtypeStruct(shape, jnp.bfloat16)

    def full(*shape):
        return jax.ShapeDtypeStruct(shape, jnp.float32)

    kept = Kept(
        query_self=low(rows, part),
        key_self=low(rows, part),
        value_self=low(rows, part),
        self_totals=full(heads, rows),
        self_mix=low(rows, part),
        first_low=low(QUARTERS, height, width),
        rows_self=full(height, width),
        key_cross=low(span, part),
        value_cross=low(span, part),
        query_cross=low(rows, part),
        cross_totals=full(heads, rows),
        cross_mix=low(rows, part),
        second_low=low(QUARTERS, height, width),
        rows_cross=full(height, width),
        feed_act=low(rows, hidden),
        gelu_slope=full(rows * hidden // (width * part), width, part),
        rows_feed=full(height, width),
        words=low(words, width),
        states=low(total, QUARTERS, height, width),
    )
    out_shape = list(kept) + [
        full(total, words, rows),
        full(3, total, rows),
        jax.ShapeDtypeStruct((total,) + small.ids.shape, small.ids.dtype),
    ]
    outcome = pl.pallas_call(
        functools.partial(layer_kernel, total),
        out_shape=out_shape,
        in_specs=[ANY] * len(given) + [VMEM] * len(small) + [ANY],
        out_specs=[ANY] * len(kept) + [ANY, VMEM, VMEM],
        scratch_shapes=[pltpu.VMEM(value.shape, value.dtype) for value in given]
        + [pltpu.VMEM(value.shape, value.dtype) for value in kept]
        + [DMA((len(given),)), DMA((len(kept),)), DMA((2, total)), DMA, DMA((2, total))]
        + exchange_scratch(height, width) * 3
        + [
            pltpu.VMEM((height, width), jnp.float32),
            DMA((2, 4, total)),
            pltpu.VMEM((2, words, rows), jnp.float32),
            pltpu.VMEM((stages, 3, total, rows), jnp.float32),
            pltpu.VMEM((stages, 3, total, rows), jnp.float32),
            DMA((2,)),
            DMA((2, stages)),
        ],
        compiler_params=pltpu.CompilerParams(
            collective_id=number, has_side_effects=True, vmem_limit_bytes=62 * 2**20
        ),
    )(*given, *small, table)
    return (Kept(*outcome[: len(kept)]),) + tuple(outcome[len(kept) :])


class Loaded(typing.NamedTuple):
    grad_out: typing.Any
    feed_down: typing.Any
    gelu_slope: typing.Any
    feed_up: typing.Any
    feed_act: typing.Any
    second_low: typing.Any
    cross_out: typing.Any
    cross_query: typing.Any
    query_cross: typing.Any
    key_cross: typing.Any
    value_cross: typing.Any
    cross_totals: typing.Any
    cross_mix: typing.Any
    first_low: typing.Any
    memory: typing.Any
    cross_key: typing.Any
    cross_value: typing.Any
    self_out: typing.Any
    query_self: typing.Any
    key_self: typing.Any
    value_self: typing.Any
    self_totals: typing.Any
    self_mix: typing.Any
    tokens: typing.Any
    self_query: typing.Any
    self_key: typing.Any
    self_value: typing.Any


class Plain(typing.NamedTuple):
    grad_rows: typing.Any
    rows_cross: typing.Any
    gain_cross: typing.Any
    rows_self: typing.Any
    gain_self: typing.Any
    grad_vecs: typing.Any
    segment_row: typing.Any
    segment_column: typing.Any


LOADS = len(Loaded._fields)
PIECES = 16
CROSSWISE = (8, 11)
PLANS = (
    (
        0, 6,
    ),
    (
        1, 7, 12, 18, 48,
    ),
    (
        2, 24, 8, 13, 30, 66,
    ),
    (
        3, 19, 25, 36,
    ),
    (
        9, 42, 14, 31, 54, 4, 20, 60, 26, 37, 49, 10, 67, 43, 15, 72, 32, 55, 21, 61, 78, 27,
        16, 38, 84, 50, 68, 73, 90, 44, 22, 33, 5, 56, 62, 79, 11, 28, 39, 17, 85, 51, 23, 69,
        91, 74, 29, 34, 45, 52, 57, 70, 40, 63, 80, 35, 46, 86, 92, 41, 75, 53, 47, 58, 71, 59,
        64, 81, 76, 87, 65, 93, 82, 88, 77, 94, 83, 89, 95,
    ),
)


def plans_of(bits):
    turns = 2 * bits
    if turns == 6:
        return [[divmod(code, turns) for code in plan] for plan in PLANS]
    feed, rest = range(0, 8), range(8, PIECES)
    plans = [
        [(piece, 0) for piece in feed],
        [(piece, 1) for piece in feed],
        [],
        [(piece, 0) for piece in range(8, 12)],
    ]
    plans.append([(piece, 0) for piece in range(12, PIECES)])
    plans[4] += [(piece, 1) for piece in rest]
    plans[4] += [(piece, turn) for turn in range(2, turns) for piece in range(PIECES)]
    return plans


def layer_back_kernel(total, orders, plans, moves, *refs):
    given_hbm, plain, table, outs, narrow, held, refs = split_refs(
        refs, LOADS, len(Plain._fields), 2 * bool(moves), 4, bool(moves), LOADS, len(refs)
    )
    outcome, vec_sums, token_share, memory_share = outs
    load_sems, refs = refs[0], refs[1:]
    (pieces, recv, vec_send, vec_recv, sum_sems, gather_sems, vec_sems), refs = refs[:7], refs[7:]
    norm_buffers = [refs[0:5], refs[5:10]]
    quarters, refs = refs[10:12], refs[12:]
    rows_all = quarters[0].shape[0] * quarters[0].shape[1]
    down, up = held[1], held[3]
    part = pieces.shape[2]
    column_buffers = [
        [
            [weight.at[0:size, turn * part : (turn + 1) * part] for turn in pair]
            for pair in ((0, 1), (2, 3))
        ]
        + refs[start : start + 3]
        for weight, size, start in ((down, pieces.shape[1], 0), (up, rows_all, 3))
    ]
    refs = refs[6:]
    grad_pre, grad_mix, grad_queries, grad_cross, grad_self = refs[:5]
    move_sems = refs[5:]
    loads = [
        pltpu.make_async_copy(source, target, load_sems.at[index])
        for index, (source, target) in enumerate(zip(given_hbm, held))
    ]
    for copy in loads:
        copy.start()
    loaded = set()

    def get(index):
        if index not in loaded:
            loaded.add(index)
            loads[index].wait()
        return held[index]

    at = Loaded(*range(LOADS))
    simple = Plain(*plain)
    block, place = lax.axis_index("dp"), lax.axis_index("mp")
    near, far = (block, flip(place, 1)), (block, flip(place, 2))
    bits = (total - 1).bit_length()
    over = [(flip(block, 1 << bit), place) for bit in range(bits)]
    sides = [lax.rem(lax.div(block, 1 << bit), 2) for bit in range(bits)]
    others = range(1, total) if moves else [1 << bit for bit in range(bits)]
    greet([near, far] + [(flip(block, mask), place) for mask in others])
    sent, moved = [], []
    if moves:
        moved = table_copies(moves, True, table[0], narrow[0], move_sems[0])

    height = pieces.shape[1]
    unit = height >> bits
    kept = [[0] for _ in range(PIECES)]
    copies = {}

    def offset(stage):
        return height - 2 * (height >> (stage + 1))

    def send_sum(piece, stage):
        side, rows = sides[orders[piece][stage]], height >> (stage + 1)
        kept[piece].append(kept[piece][stage] + side * rows)
        if stage:
            source, start = recv, offset(stage - 1) + (1 - side) * rows
        else:
            source, start = pieces, (1 - side) * rows
        copies[piece, stage] = remote(
            source.at[piece, pl.ds(pl.multiple_of(start, unit), rows), :],
            recv.at[piece, pl.ds(offset(stage), rows), :],
            sum_sems.at[0, piece, stage],
            sum_sems.at[1, piece, stage],
            over[orders[piece][stage]],
        )
        sent.append(copies[piece, stage])

    def take_sum(piece, stage):
        side, rows = sides[orders[piece][stage]], height >> (stage + 1)
        copies[piece, stage].wait_recv()
        if stage:
            source, start = recv, offset(stage - 1) + side * rows
        else:
            source, start = pieces, side * rows
        mine = source[piece, pl.ds(pl.multiple_of(start, unit), rows), :]
        there = pl.ds(offset(stage), rows)
        value = (
            mine.astype(jnp.float32) + recv[piece, there, :].astype(jnp.float32)
        ).astype(jnp.bfloat16)
        if stage + 1 < bits:
            recv[piece, there, :] = value
            send_sum(piece, stage + 1)
        else:
            start = kept[piece][bits]
            outcome[piece, pl.ds(pl.multiple_of(start, unit), rows), :] = value
            send_whole(piece, stage)

    def send_whole(piece, stage):
        rows = height >> (stage + 1)
        start = pl.multiple_of(kept[piece][stage + 1], unit)
        here = outcome.at[piece, pl.ds(start, rows), :]
        copies[piece, stage, True] = remote(
            here, here, gather_sems.at[0, piece, stage], gather_sems.at[1, piece, stage],
            over[orders[piece][stage]],
        )
        sent.append(copies[piece, stage, True])

    def move_on(plan):
        for piece, turn in plan:
            if turn < bits:
                take_sum(piece, turn)
                continue
            stage = 2 * bits - 1 - turn
            copies[piece, stage, True].wait_recv()
            if stage:
                send_whole(piece, stage - 1)

    def weight_piece(piece, left, right):
        pieces[piece] = product_tn(left, right).astype(jnp.bfloat16)
        send_sum(piece, 0)

    def folded_piece(piece, left, right):
        part = left.shape[1]
        for turn in range(height // part):
            columns = slice(turn * part, (turn + 1) * part)
            pieces[piece, columns, :] = product_tn(left[...], right[:, columns]).astype(
                jnp.bfloat16
            )
        send_sum(piece, 0)

    tasks = []

    def work(amount):
        for task in tasks[:amount]:
            task()
        del tasks[:amount]

    def norm_back(turn, block_of, kept_rows, rows, gain, first_amount):
        outcome_list = []
        run(
            sum_quarter_steps(
                place, block_of, near, far, *norm_buffers[turn], outcome_list, sent
            ),
            lambda: work(first_amount),
        )
        grad, grad_gain, grad_shift = norm_rows_back(
            rows[...], gain[...], kept_rows + outcome_list[0]
        )
        quarters[turn][place] = grad.astype(jnp.bfloat16)
        run(
            share_quarter_steps(place, quarters[turn], near, far, norm_buffers[turn][4], sent),
            lambda: work(len(tasks)),
        )
        return grad, grad_gain, grad_shift

    grad_out = get(at.grad_out)
    grad_act = product_nt(grad_out[...], get(at.feed_down)[...])
    slope = get(at.gelu_slope)
    acc_keys, acc_values = slope.at[0], slope.at[1]
    wide = pieces.shape[2]
    for turn in range(grad_pre.shape[1] // wide):
        columns = slice(turn * wide, (turn + 1) * wide)
        start = turn * rows_all
        grad_pre[:, columns] = (
            slope[start // height, start % height : start % height + rows_all]
            * grad_act[:, columns]
        ).astype(jnp.bfloat16)
    for index in (at.feed_up, at.feed_act, at.second_low):
        get(index)
    for turn in range(4):
        columns = slice(turn * wide, (turn + 1) * wide)
        tasks.append(
            functools.partial(
                lambda turn, columns: weight_piece(
                    turn, get(at.feed_act)[...], grad_out[:, columns]
                ),
                turn, columns,
            )
        )
    for turn in range(4):
        columns = slice(turn * wide, (turn + 1) * wide)
        tasks.append(
            functools.partial(
                lambda turn, columns: weight_piece(
                    4 + turn, get(at.second_low)[...], grad_pre[:, columns]
                ),
                turn, columns,
            )
        )
    quarter = rows_all // QUARTERS
    grad_second, *vecs_cross = norm_back(
        0,
        lambda index: product_nt(rows_of(grad_pre, quarter, index), get(at.feed_up)[...]),
        simple.grad_rows[...], simple.rows_cross, simple.gain_cross, 4,
    )

    grad_out = quarters[0]
    for index in range(QUARTERS):
        grad_mix[index * quarter : (index + 1) * quarter] = product_nt(
            grad_out[index], get(at.cross_out)[...]
        ).astype(jnp.bfloat16)
    for index in (at.query_cross, at.key_cross, at.value_cross, at.cross_totals):
        get(index)
    span = get(at.key_cross).shape[0]
    owners = lax.broadcasted_iota(jnp.int32, (span, 1), 0) // MEM
    attend_back(
        get(at.query_cross), get(at.key_cross), get(at.value_cross), grad_mix, get(at.cross_totals),
        lambda here: owners == simple.segment_row[:, here],
        acc_keys, acc_values, grad_queries, grad_cross.at[0], grad_cross.at[1],
    )
    move_on(plans[0])
    for index in (at.cross_query, at.cross_mix, at.first_low, at.memory, at.cross_key, at.cross_value):
        get(index)
    for kind in range(2):
        tasks.append(
            functools.partial(
                lambda kind: weight_piece(8 + kind, get(at.memory)[...], grad_cross[kind]), kind
            )
        )
    tasks.append(lambda: weight_piece(10, get(at.first_low)[...], grad_queries[...]))
    tasks.append(
        lambda: folded_piece(
            11, get(at.cross_mix), grad_out[...].reshape(rows_all, grad_out.shape[2])
        )
    )

    def memory_block(index):
        return product_nt(
            grad_cross[0], rows_of(get(at.cross_key), wide, index)
        ) + product_nt(grad_cross[1], rows_of(get(at.cross_value), wide, index))

    memory_total = []
    memory_steps = sum_quarter_steps(
        place, memory_block, near, far, *column_buffers[0], memory_total, sent
    )
    grad_first, *vecs_self = norm_back(
        1,
        lambda index: product_nt(rows_of(grad_queries, quarter, index), get(at.cross_query)[...]),
        grad_second, simple.rows_self, simple.gain_self, 3,
    )
    vec_peers = [near, far] + over

    def vec_start(stage, value):
        vec_send[stage] = value
        copies[None, stage] = remote(
            vec_send.at[stage], vec_recv.at[stage], vec_sems.at[0, stage], vec_sems.at[1, stage],
            vec_peers[stage],
        )
        sent.append(copies[None, stage])

    def vec_next(stage):
        if stage >= len(vec_peers):
            return
        copies[None, stage].wait_recv()
        value = vec_send[stage] + vec_recv[stage]
        if stage + 1 < len(vec_peers):
            vec_start(stage + 1, value)
        else:
            vec_sums[...] = value

    vec_start(
        0, jnp.concatenate(vecs_self + vecs_cross + [simple.grad_vecs[...]], axis=0)
    )

    grad_out = quarters[1]
    move_on(plans[1])
    for index in range(QUARTERS):
        grad_mix[index * quarter : (index + 1) * quarter] = product_nt(
            grad_out[index], get(at.self_out)[...]
        ).astype(jnp.bfloat16)
    for index in (at.query_self, at.key_self, at.value_self, at.self_totals):
        get(index)
    key_place = lax.broadcasted_iota(jnp.int32, (rows_all, 1), 0)

    def allowed_self(here):
        query_place = here.start + lax.broadcasted_iota(jnp.int32, (1, here.size), 1)
        return (simple.segment_column[...] == simple.segment_row[:, here]) & (
            key_place <= query_place
        )

    attend_back(
        get(at.query_self), get(at.key_self), get(at.value_self), grad_mix, get(at.self_totals),
        allowed_self, acc_keys, acc_values, grad_queries, grad_self.at[0], grad_self.at[1],
    )
    for index in (at.tokens, at.self_mix, at.self_query, at.self_key, at.self_value):
        get(index)
    move_on(plans[2])
    weight_piece(12, get(at.tokens)[...], grad_queries[...])
    weight_piece(13, get(at.tokens)[...], grad_self[0])
    weight_piece(14, get(at.tokens)[...], grad_self[1])
    folded_piece(15, get(at.self_mix), grad_out[...].reshape(rows_all, grad_out.shape[2]))
    move_on(plans[3])
    vec_next(0)

    def token_block(index):
        return (
            product_nt(grad_queries[...], rows_of(get(at.self_query), wide, index))
            + product_nt(grad_self[0], rows_of(get(at.self_key), wide, index))
            + product_nt(grad_self[1], rows_of(get(at.self_value), wide, index))
        )

    token_total = []
    token_steps = sum_quarter_steps(
        place, token_block, near, far, *column_buffers[1], token_total, sent
    )
    next(token_steps)
    next(memory_steps)
    own_columns = pl.ds(pl.multiple_of(place * wide, wide), wide)
    step = 12
    for turn, start in enumerate(range(0, len(plans[4]), step)):
        move_on(plans[4][start : start + step])
        if turn == 0:
            run(token_steps)
            token_share[...] = token_total[0] + quarters[1][:, :, own_columns].reshape(
                rows_all, wide
            ).astype(jnp.float32)
        if turn == 1:
            run(memory_steps)
            memory_share[...] = memory_total[0]
        vec_next(turn + 1)
    for turn in range(-(-len(plans[4]) // step) + 1, len(vec_peers)):
        vec_next(turn)
    for copy in sent:
        copy.wait_send()
    finish(moved)


def layer_back(values, plain, number, table=None, narrow=None, moves=()):
    total = lax.axis_size("dp")
    bits = (total - 1).bit_length()
    rest = list(range(2, bits))
    orders = [[1, 0] + rest if piece in CROSSWISE else [0, 1] + rest for piece in range(PIECES)]
    given = list(values) + list(plain)
    in_specs = [ANY] * len(values) + [VMEM] * len(plain)
    rows, width = values.tokens.shape
    span = values.memory.shape[0]
    part = values.self_query.shape[1]
    quarter = rows // QUARTERS
    stages = bits + 2
    vecs = (6, width)
    out_shape = [
        jax.ShapeDtypeStruct((PIECES, width, part), jnp.bfloat16),
        jax.ShapeDtypeStruct(vecs, jnp.float32),
        jax.ShapeDtypeStruct((rows, part), jnp.float32),
        jax.ShapeDtypeStruct((span, part), jnp.float32),
    ]
    out_specs = [VMEM] * 4
    scratch = [pltpu.VMEM(value.shape, value.dtype) for value in values]
    scratch += [
        DMA((LOADS,)),
        pltpu.VMEM((PIECES, width, part), jnp.bfloat16),
        pltpu.VMEM((PIECES, width - (width >> bits), part), jnp.bfloat16),
        pltpu.VMEM((stages,) + vecs, jnp.float32),
        pltpu.VMEM((stages,) + vecs, jnp.float32),
        DMA((2, PIECES, bits)),
        DMA((2, PIECES, bits)),
        DMA((2, stages)),
    ]
    scratch += exchange_scratch(quarter, width) * 2
    scratch += [pltpu.VMEM((QUARTERS, quarter, width), jnp.bfloat16)] * 2
    scratch += exchange_scratch(span, part)[2:] + exchange_scratch(rows, part)[2:]
    scratch += [
        pltpu.VMEM((rows, values.feed_up.shape[1]), jnp.bfloat16),
        pltpu.VMEM((rows, part), jnp.bfloat16),
        pltpu.VMEM((rows, part), jnp.bfloat16),
        pltpu.VMEM((2, span, part), jnp.bfloat16),
        pltpu.VMEM((2, rows, part), jnp.bfloat16),
    ]
    aliases = {}
    if moves:
        aliases = {len(given) + 1: len(out_shape)}
        given += [table, narrow]
        in_specs += [ANY] * 2
        out_shape.append(jax.ShapeDtypeStruct(narrow.shape, narrow.dtype))
        out_specs.append(ANY)
        scratch.append(DMA((2, len(moves))))
    return pl.pallas_call(
        functools.partial(layer_back_kernel, total, orders, plans_of(bits), tuple(moves)),
        out_shape=out_shape,
        in_specs=in_specs,
        out_specs=out_specs,
        scratch_shapes=scratch,
        input_output_aliases=aliases,
        compiler_params=pltpu.CompilerParams(
            collective_id=number, has_side_effects=True, vmem_limit_bytes=62 * 2**20
        ),
    )(*given)


def unfold(matrix, height):
    return jnp.concatenate(
        [matrix[start : start + height] for start in range(0, matrix.shape[0], height)], axis=1
    )


def shift_pairs(total, step):
    return [(index, (index + step) % total) for index in range(total)]


def spread_rows(table):
    total = lax.axis_size("dp")
    place = lax.axis_index("dp")
    width = table.shape[1]
    part = table.shape[0] // total
    whole = jnp.zeros((part, width * total), table.dtype)
    for step in range(total):
        block = lax.dynamic_slice_in_dim(table, (place + step) % total * part, part, 0)
        if step:
            block = lax.ppermute(block, "dp", shift_pairs(total, step))
        whole = lax.dynamic_update_slice_in_dim(
            whole, block, (place - step) % total * width, 1
        )
    return whole


def return_rows(rows, height):
    total = lax.axis_size("dp")
    place = lax.axis_index("dp")
    part = rows.shape[0]
    width = rows.shape[1] // total
    whole = jnp.zeros((height, width), rows.dtype)
    for step in range(total):
        block = lax.dynamic_slice_in_dim(rows, (place + step) % total * width, width, 1)
        if step:
            block = lax.ppermute(block, "dp", shift_pairs(total, step))
        whole = lax.dynamic_update_slice_in_dim(
            whole, block, (place - step) % total * part, 0
        )
    return whole


def layer_apart(
    tokens, memory, segment_ids, ids, offset, words, self_query, self_key, self_value, self_out,
    cross_query, cross_key, cross_value, cross_out, feed_up, feed_down, gain_self, shift_self,
    gain_cross, shift_cross, gain_feed, shift_feed,
):
    row_len = segment_ids.shape[1]
    places = jnp.arange(row_len, dtype=jnp.int32)
    owners = jnp.arange(memory.shape[0], dtype=jnp.int32) // MEM
    self_mask = (segment_ids[0][:, None] == segment_ids[0][None, :]) & (
        places[None, :] <= places[:, None]
    )
    cross_mask = segment_ids[0][:, None] == owners[None, :]
    quarter = tokens.shape[0] // QUARTERS
    inputs = lax.dynamic_slice_in_dim(tokens, lax.axis_index("mp") * quarter, quarter, 0)
    query_self = product(tokens, self_query).astype(jnp.bfloat16)
    key_self = product(tokens, self_key).astype(jnp.bfloat16)
    value_self = product(tokens, self_value).astype(jnp.bfloat16)
    self_mix, self_totals = attend_forward(query_self, key_self, value_self, self_mask)
    first_low, first_norm, rows_self, ids_all = mix_norm(
        self_mix, self_out, inputs, gain_self, shift_self, 0, ids
    )
    query_cross = product(first_low, cross_query).astype(jnp.bfloat16)
    key_cross = product(memory, cross_key).astype(jnp.bfloat16)
    value_cross = product(memory, cross_value).astype(jnp.bfloat16)
    cross_mix, cross_totals = attend_forward(query_cross, key_cross, value_cross, cross_mask)
    second_low, second_norm, rows_cross = mix_norm(
        cross_mix, cross_out, first_norm, gain_cross, shift_cross, 1
    )
    feed_pre = product(second_low, feed_up)
    feed_act, gelu_pull = jax.vjp(gelu_exact, feed_pre)
    gelu_slope = gelu_pull(jnp.ones_like(feed_pre))[0]
    feed_act = feed_act.astype(jnp.bfloat16)
    answers = ids_all[:, ids.shape[0] // 3 : 2 * (ids.shape[0] // 3)].reshape(-1, 1, row_len)
    states, rows_feed, logits, totals = feed_norm(
        feed_act, feed_down, second_norm, gain_feed, shift_feed, answers - offset, 2, words
    )
    gelu_slope = jnp.concatenate(
        jnp.split(gelu_slope, gelu_slope.shape[1] // self_query.shape[1], axis=1), axis=0
    ).reshape((2,) + self_query.shape)
    kept = Kept(
        query_self, key_self, value_self, self_totals, self_mix, first_low, rows_self, key_cross,
        value_cross, query_cross, cross_totals, cross_mix, second_low, rows_cross, feed_act,
        gelu_slope, rows_feed, words, states,
    )
    return kept, logits, totals, ids_all


def local(
    tokens,
    memory,
    segment_ids,
    answer_ids,
    loss_mask,
    doc_scores,
    slot_place,
    self_query,
    self_key,
    self_value,
    self_out,
    cross_query,
    cross_key,
    cross_value,
    cross_out,
    feed_up,
    feed_down,
    gain_self,
    shift_self,
    gain_cross,
    shift_cross,
    gain_feed,
    shift_feed,
    embedding,
):
    row_count, row_len = segment_ids.shape
    total = lax.axis_size("dp")
    direct = total == 8 and embedding.shape[1] % 128 == 0
    vocab_local = embedding.shape[0]
    part = vocab_local // total
    offset = lax.axis_index("mp") * vocab_local + lax.axis_index("dp") * part
    ids = jnp.concatenate([segment_ids, answer_ids, loss_mask], axis=0)
    norms = (gain_self, shift_self, gain_cross, shift_cross, gain_feed, shift_feed)
    if direct:
        kept, logits, totals, ids_all = layer_forward(
            Given(
                tokens, self_query, self_key, self_value, self_out, memory, cross_key,
                cross_value, cross_query, cross_out, feed_up, feed_down,
            ),
            Small(
                ids, segment_ids.reshape(1, -1), segment_ids.reshape(-1, 1),
                *(vector.reshape(1, -1) for vector in norms),
            ),
            embedding,
            0,
        )
        words = kept.words
    else:
        words = spread_rows(embedding)
        kept, logits, totals, ids_all = layer_apart(
            tokens, memory, segment_ids, ids, offset, words, self_query, self_key, self_value,
            self_out, cross_query, cross_key, cross_value, cross_out, feed_up, feed_down, *norms,
        )
    segments_all, answers_all, kept_all = (
        ids_all[:, kind * row_count : (kind + 1) * row_count].reshape(-1, row_len)
        for kind in range(3)
    )
    targets = (answers_all - offset)[:, None, :]
    log_total = totals[0] + jnp.log(totals[1])
    picked = totals[2]
    keeper = kept_all.astype(jnp.float32)
    token_logp = (picked - log_total) * keeper
    seg_hot = (
        segments_all[:, :, None] == jnp.arange(SEG_ROW, dtype=jnp.int32)[None, None, :]
    ).astype(jnp.float32)
    seg_sums = jnp.sum(seg_hot * token_logp[:, :, None], axis=1)
    counts = jnp.sum(seg_hot * keeper[:, :, None], axis=1)
    likely_all = (seg_sums / jnp.maximum(counts, 1.0)).reshape(-1)
    place_hot = (
        slot_place[:, None] == jnp.arange(likely_all.shape[0], dtype=jnp.int32)[None, :]
    ).astype(jnp.float32)

    def marginal(scores, likely):
        joint_score = jax.nn.log_softmax(scores, axis=1) + jnp.dot(
            place_hot, likely, precision=highest
        ).reshape(scores.shape)
        return -jnp.sum(jax.nn.logsumexp(joint_score, axis=1))

    loss, pullback = jax.vjp(marginal, doc_scores, likely_all)
    grad_scores, grad_likely = pullback(jnp.ones_like(loss))
    per_segment = grad_likely.reshape(counts.shape) / jnp.maximum(counts, 1.0)
    grad_logp = (jnp.sum(seg_hot * per_segment[:, None, :], axis=2) * keeper)[:, None, :]
    log_total = log_total[:, None, :]
    if direct:
        head_values = (logits, words, kept.states, log_total, grad_logp, targets)
    else:
        hot = (targets == jnp.arange(part, dtype=jnp.int32)[None, :, None]).astype(jnp.float32)
        grad_logits = (grad_logp * (hot - jnp.exp(logits - log_total))).astype(jnp.bfloat16)
        parts = jnp.einsum(
            "rvt,vd->rtd", grad_logits, words, preferred_element_type=jnp.float32
        ).astype(jnp.bfloat16)
        head_values = (parts.reshape(kept.states.shape),)
        grad_words = jnp.einsum(
            "rvt,rtd->vd",
            grad_logits,
            kept.states.reshape(total, -1, kept.states.shape[3]),
            preferred_element_type=jnp.float32,
        ).astype(jnp.bfloat16)
    grad_branch, grad_res3, grad_vecs_feed, *made = head_back(
        head_values, kept.rows_feed, gain_feed, 3, (4, 1, 0) if direct else ()
    )
    grad_words, *narrow = made if direct else (grad_words,)
    values = Loaded(
        grad_out=grad_branch,
        feed_down=feed_down,
        gelu_slope=kept.gelu_slope,
        feed_up=feed_up,
        feed_act=kept.feed_act,
        second_low=kept.second_low.reshape(tokens.shape),
        cross_out=cross_out,
        cross_query=cross_query,
        query_cross=kept.query_cross,
        key_cross=kept.key_cross,
        value_cross=kept.value_cross,
        cross_totals=kept.cross_totals,
        cross_mix=kept.cross_mix,
        first_low=kept.first_low.reshape(tokens.shape),
        memory=memory,
        cross_key=cross_key,
        cross_value=cross_value,
        self_out=self_out,
        query_self=kept.query_self,
        key_self=kept.key_self,
        value_self=kept.value_self,
        self_totals=kept.self_totals,
        self_mix=kept.self_mix,
        tokens=tokens,
        self_query=self_query,
        self_key=self_key,
        self_value=self_value,
    )
    plain = Plain(
        grad_rows=grad_res3,
        rows_cross=kept.rows_cross,
        gain_cross=gain_cross.reshape(1, -1),
        rows_self=kept.rows_self,
        gain_self=gain_self.reshape(1, -1),
        grad_vecs=grad_vecs_feed,
        segment_row=segment_ids.reshape(1, -1),
        segment_column=segment_ids.reshape(-1, 1),
    )
    sums, grad_vecs, grad_tokens, memory_share, *narrow = layer_back(
        values, plain, 4, grad_words, *narrow, moves=(5, 6, 7, 2, 3) if direct else ()
    )
    grad_table = (
        narrow[0] if direct else return_rows(grad_words, vocab_local)
    ).astype(jnp.float32)
    sums = [part.astype(jnp.float32) for part in sums]
    sum_down = jnp.concatenate(sums[0:4], axis=1)
    sum_up = jnp.concatenate(sums[4:8], axis=1)
    sum_ck, sum_cv, sum_cq, sum_co, sum_sq, sum_sk, sum_sv, sum_so = sums[8:]
    sum_co, sum_so = (unfold(part, self_out.shape[0]) for part in (sum_co, sum_so))
    return (
        loss,
        grad_tokens,
        memory_share,
        sum_sq,
        sum_sk,
        sum_sv,
        sum_so,
        sum_cq,
        sum_ck,
        sum_cv,
        sum_co,
        sum_up,
        sum_down,
        *grad_vecs,
        grad_table,
        grad_scores,
    )


def solution(mesh):
    return jax.shard_map(
        local,
        mesh=mesh,
        in_specs=(
            P("dp", None),
            P("dp", None),
            P("dp", None),
            P("dp", None),
            P("dp", None),
            P(),
            P(),
            P(None, "mp"),
            P(None, "mp"),
            P(None, "mp"),
            P("mp", None),
            P(None, "mp"),
            P(None, "mp"),
            P(None, "mp"),
            P("mp", None),
            P(None, "mp"),
            P("mp", None),
            P(),
            P(),
            P(),
            P(),
            P(),
            P(),
            P("mp", "dp"),
        ),
        out_specs=(
            P(),
            P("dp", "mp"),
            P("dp", "mp"),
            P(None, "mp"),
            P(None, "mp"),
            P(None, "mp"),
            P("mp", None),
            P(None, "mp"),
            P(None, "mp"),
            P(None, "mp"),
            P("mp", None),
            P(None, "mp"),
            P("mp", None),
            P(),
            P(),
            P(),
            P(),
            P(),
            P(),
            P("mp", "dp"),
            P(),
        ),
        check_vma=False,
    )
```

```python
import functools
import typing

import jax
import jax.numpy as jnp
from jax import lax
from jax.experimental import pallas as pl
from jax.experimental.pallas import tpu as pltpu
from jax.sharding import PartitionSpec as P

HEAD_DIM = 64
SEG_ROW = 8
MEM = 128


masked_score = -1e30
norm_eps = 1e-05
highest = lax.Precision.HIGHEST


def product(left_side, right_side):
    return jnp.dot(left_side, right_side, preferred_element_type=jnp.float32)


def product_tn(left_side, right_side):
    return lax.dot_general(
        left_side, right_side, (((0,), (0,)), ((), ())), preferred_element_type=jnp.float32
    )


def product_nt(left_side, right_side):
    return lax.dot_general(
        left_side, right_side, (((1,), (1,)), ((), ())), preferred_element_type=jnp.float32
    )


def gelu_exact(inputs):
    return jax.nn.gelu(inputs, approximate=False)


def split_heads(matrix):
    return matrix.reshape(matrix.shape[0], matrix.shape[1] // HEAD_DIM, HEAD_DIM)


def attention_scores(queries, keys, allowed):
    scores = jnp.einsum(
        "qhd,khd->hqk", split_heads(queries), split_heads(keys), preferred_element_type=jnp.float32
    ) * HEAD_DIM ** (-0.5)
    return jnp.where(allowed[None], scores, masked_score)


def attend_forward(queries, keys, values, allowed):
    scores = attention_scores(queries, keys, allowed)
    largest = jnp.max(scores, axis=-1, keepdims=True)
    weights = jnp.exp(scores - largest)
    total = jnp.sum(weights, axis=-1, keepdims=True)
    probabilities = (weights / total).astype(jnp.bfloat16)
    mixed_out = jnp.einsum(
        "hqk,khd->qhd", probabilities, split_heads(values), preferred_element_type=jnp.float32
    )
    mixed_out = mixed_out.reshape(queries.shape).astype(jnp.bfloat16)
    return mixed_out, (largest + jnp.log(total))[..., 0]


MESH = pl.DeviceIdType.MESH
VMEM = pl.BlockSpec(memory_space=pltpu.VMEM)
ANY = pl.BlockSpec(memory_space=pl.ANY)
DMA = pltpu.SemaphoreType.DMA
QUARTERS = 4


def flip(index, mask):
    for bit in range(mask.bit_length()):
        if mask >> bit & 1:
            step = 1 << bit
            index = index + step * (1 - 2 * lax.rem(lax.div(index, step), 2))
    return index


def greet(peers):
    barrier = pltpu.get_barrier_semaphore()
    for peer in peers:
        pl.semaphore_signal(barrier, inc=1, device_id=peer, device_id_type=MESH)
    pl.semaphore_wait(barrier, len(peers))


def remote(source, target, send_sem, recv_sem, peer):
    copy = pltpu.make_async_remote_copy(
        src_ref=source,
        dst_ref=target,
        send_sem=send_sem,
        recv_sem=recv_sem,
        device_id=peer,
        device_id_type=MESH,
    )
    copy.start()
    return copy


def sum_quarter_steps(
    place, block_of, near, far, sib_send, sib_recv, far_send, far_recv, sems, outcome, sent
):
    copies = []
    sends, recvs = (
        slots if isinstance(slots, list) else [slots.at[0], slots.at[1]]
        for slots in (sib_send, sib_recv)
    )
    for slot, mask in enumerate((3, 1)):
        sends[slot][...] = block_of(flip(place, mask)).astype(jnp.bfloat16)
        copies.append(
            remote(sends[slot], recvs[slot], sems.at[0, slot], sems.at[1, slot], near)
        )
    distant = block_of(flip(place, 2))
    copies[0].wait_recv()
    far_send[...] = (distant + recvs[0][...].astype(jnp.float32)).astype(jnp.bfloat16)
    copies.append(remote(far_send, far_recv, sems.at[0, 2], sems.at[1, 2], far))
    sent += copies
    own = block_of(place)
    copies[1].wait_recv()
    yield
    copies[2].wait_recv()
    outcome.append(own + recvs[1][...].astype(jnp.float32) + far_recv[...].astype(jnp.float32))


def share_quarter_steps(place, quarters, near, far, sems, sent):
    here = quarters.at[place]
    to_far = remote(here, here, sems.at[0, 3], sems.at[1, 3], far)
    to_near = remote(here, here, sems.at[0, 4], sems.at[1, 4], near)
    yield
    to_far.wait_recv()
    there = quarters.at[flip(place, 2)]
    passed = remote(there, there, sems.at[0, 5], sems.at[1, 5], near)
    to_near.wait_recv()
    passed.wait_recv()
    sent += [to_far, to_near, passed]


def run(steps, between=None):
    for _ in steps:
        if between is not None:
            between()


def sum_quarter(place, block_of, near, far, *buffers):
    outcome, sent = [], []
    run(sum_quarter_steps(place, block_of, near, far, *buffers, outcome, sent))
    return outcome[0], sent


def share_quarter(place, quarters, near, far, sems):
    sent = []
    run(share_quarter_steps(place, quarters, near, far, sems, sent))
    return sent


def table_copies(masks, back, source, target, sems):
    block, place = lax.axis_index("dp"), lax.axis_index("mp")
    total = lax.axis_size("dp")
    part, width = (source if back else target).shape[0], (target if back else source).shape[1]
    copies = []
    for slot, mask in enumerate(masks):
        other = flip(block, mask)
        here = pl.ds(pl.multiple_of((block if back else other) * part, part), part)
        there = pl.ds(pl.multiple_of((other if back else block) * width, width), width)
        if back:
            start, end = source.at[:, there], target.at[here, :]
        else:
            start, end = source.at[here, :], target.at[:, there]
        if mask:
            copies.append(remote(start, end, sems.at[0, slot], sems.at[1, slot], (other, place)))
        else:
            copy = pltpu.make_async_copy(start, end, sems.at[0, slot])
            copy.start()
            copies.append(copy)
    return copies


def finish(copies):
    for copy in copies:
        copy.wait()


def split_refs(refs, *counts):
    groups, start = [], 0
    for count in counts:
        groups.append(list(refs[start : start + count]))
        start += count
    return groups


def norm_rows(rows, gain, shift):
    center = rows - jnp.mean(rows, axis=-1, keepdims=True)
    spread = jnp.mean(center * center, axis=-1, keepdims=True)
    return center * lax.rsqrt(spread + norm_eps) * gain + shift


def norm_rows_back(rows, gain, grad):
    center = rows - jnp.mean(rows, axis=-1, keepdims=True)
    scale = lax.rsqrt(jnp.mean(center * center, axis=-1, keepdims=True) + norm_eps)
    normed = center * scale
    inner = grad * gain
    grad_rows = scale * (
        inner
        - jnp.mean(inner, axis=-1, keepdims=True)
        - normed * jnp.mean(inner * normed, axis=-1, keepdims=True)
    )
    return (
        grad_rows,
        jnp.sum(grad * normed, axis=0, keepdims=True),
        jnp.sum(grad, axis=0, keepdims=True),
    )


def rows_of(ref, height, index):
    return ref[pl.ds(pl.multiple_of(index * height, height), height), :]


def exchange_scratch(height, width):
    return [
        pltpu.VMEM((2, height, width), jnp.bfloat16),
        pltpu.VMEM((2, height, width), jnp.bfloat16),
        pltpu.VMEM((height, width), jnp.bfloat16),
        pltpu.VMEM((height, width), jnp.bfloat16),
        DMA((2, 6)),
    ]


def mix_norm_kernel(total, with_ids, masks, chained, *refs):
    (left, weight, kept, gain, shift), ids, table, (quarters, normed, rows), ids_all, wide, refs = (
        split_refs(
            refs, 5, with_ids, (1 + chained) * bool(masks), 3, with_ids, bool(masks), len(refs)
        )
    )
    sib_send, sib_recv, far_send, far_recv, sems = refs[:5]
    refs = refs[5:]
    block, place = lax.axis_index("dp"), lax.axis_index("mp")
    near, far = (block, flip(place, 1)), (block, flip(place, 2))
    height = kept.shape[0]
    others = range(1, total) if with_ids else [mask for mask in masks if mask]
    greet([near, far] + [(flip(block, mask), place) for mask in others])
    copies = []
    if with_ids:
        ids_sems, ids_local = refs[:2]
        refs = refs[2:]
        own = pltpu.make_async_copy(ids[0], ids_all[0].at[block], ids_local)
        own.start()
        copies.append(own)
        for mask in range(1, total):
            copies.append(
                remote(
                    ids[0], ids_all[0].at[block], ids_sems.at[0, mask], ids_sems.at[1, mask],
                    (flip(block, mask), place),
                )
            )

    def block_of(index):
        return jnp.dot(
            rows_of(left, height, index), weight[...], preferred_element_type=jnp.float32
        )

    if masks:
        copies += table_copies(masks, False, table[0], wide[0], refs[0])
    branch, sent = sum_quarter(
        place, block_of, near, far, sib_send, sib_recv, far_send, far_recv, sems
    )
    outcome = kept[...].astype(jnp.float32) + branch
    rows[...] = outcome
    outcome = norm_rows(outcome, gain[...], shift[...])
    normed[...] = outcome
    quarters[place] = outcome.astype(jnp.bfloat16)
    sent += share_quarter(place, quarters, near, far, sems)
    finish(copies)
    for copy in sent:
        copy.wait_send()


def mix_norm(left, weight, kept, gain, shift, number, ids=None, table=None, wide=None, masks=()):
    height, width = kept.shape
    total = lax.axis_size("dp")
    quarter = jax.ShapeDtypeStruct((height, width), jnp.float32)
    out_shape = [
        jax.ShapeDtypeStruct((QUARTERS, height, width), jnp.bfloat16), quarter, quarter
    ]
    out_specs = [VMEM] * 3
    given = [left, weight, kept, gain.reshape(1, -1), shift.reshape(1, -1)]
    in_specs = [VMEM] * 5
    scratch = exchange_scratch(height, width)
    aliases = {}
    if ids is not None:
        given.append(ids)
        in_specs.append(VMEM)
        out_shape.append(jax.ShapeDtypeStruct((total,) + ids.shape, ids.dtype))
        out_specs.append(VMEM)
        scratch += [DMA((2, total)), DMA]
    if masks:
        given.append(table)
        in_specs.append(ANY)
        if wide is not None:
            aliases = {len(given): len(out_shape)}
            given.append(wide)
            in_specs.append(ANY)
        out_shape.append(
            jax.ShapeDtypeStruct((table.shape[0] // total, table.shape[1] * total), table.dtype)
        )
        out_specs.append(ANY)
        scratch.append(DMA((2, len(masks))))
    outcome = pl.pallas_call(
        functools.partial(
            mix_norm_kernel, total, int(ids is not None), tuple(masks), int(wide is not None)
        ),
        out_shape=out_shape,
        in_specs=in_specs,
        out_specs=out_specs,
        scratch_shapes=scratch,
        input_output_aliases=aliases,
        compiler_params=pltpu.CompilerParams(
            collective_id=number, has_side_effects=True, vmem_limit_bytes=48 * 2**20
        ),
    )(*given)
    return (outcome[0].reshape(-1, width),) + tuple(outcome[1:])


def chunk_of(rows):
    return max(size for size in range(16, min(rows, 400) + 1, 16) if rows % size == 0)


def feed_norm_kernel(total, early, *refs):
    (left, weight, kept, gain, shift, targets), words, (states, rows, logits, totals), wide, refs = (
        split_refs(refs, 6, 1 + 2 * bool(early), 4, bool(early), len(refs))
    )
    last = words[-1]
    low, sib_send, sib_recv, far_send, far_recv, sems, hops, own_sem = refs[:8]
    (held, staged, sends, recvs, held_sem, staged_sems, stage_sems), refs = refs[8:15], refs[15:]
    block, place = lax.axis_index("dp"), lax.axis_index("mp")
    near, far = (block, flip(place, 1)), (block, flip(place, 2))
    beside = (flip(block, 1), place)
    height = kept.shape[0]
    bits = (total - 1).bit_length()
    others = set(range(1, total) if early else range(2, total, 2))
    others |= {1 << bit for bit in range(bits)}
    greet([near, far] + [(flip(block, mask), place) for mask in sorted(others)])

    def block_of(index):
        return jnp.dot(
            rows_of(left, height, index), weight[...], preferred_element_type=jnp.float32
        )

    moved = []
    if early:
        moved = table_copies(early, False, words[0], wide[0], refs[0])
    branch, sent = sum_quarter(
        place, block_of, near, far, sib_send, sib_recv, far_send, far_recv, sems
    )
    outcome = kept[...] + branch
    rows[...] = outcome
    low[...] = norm_rows(outcome, gain[...], shift[...]).astype(jnp.bfloat16)
    own = pltpu.make_async_copy(low, states.at[block, place], own_sem)
    own.start()
    across = flip(place, 2)

    def hop(kind, mask, source, peer, row, column):
        copy = remote(
            source, states.at[row, column], hops.at[0, kind, mask], hops.at[1, kind, mask], peer
        )
        sent.append(copy)
        return copy

    first = {}

    def spread(masks):
        for mask in masks:
            first[mask] = hop(0, mask, low, (flip(block, mask), place), block, place)

    spread([2])
    nearest = len(sent) - 1
    over, ends = {}, {}

    def pass_on(mask):
        over[mask].wait_recv()
        row = flip(block, mask)
        ends[mask, 1] = hop(3, mask, states.at[row, across], near, row, across)

    def arrive(mask):
        row = flip(block, mask)
        if mask:
            first[mask].wait_recv()
        source = states.at[row, place] if mask else low
        if mask % 2 == 0:
            first[mask + 1] = hop(0, mask + 1, source, beside, row, place)
        over[mask] = hop(1, mask, source, far, row, place)
        ends[mask, 0] = hop(2, mask, source, near, row, place)

    part, width = held.shape
    chunk = chunk_of(part)
    span = QUARTERS * height
    writes = {}

    def make(mask):
        row, slot = flip(block, mask), mask % 2
        for side in (0, 1):
            ends[mask, side].wait_recv()
        if mask >= 2:
            writes[mask - 2].wait()
        block_states = states[row].reshape(span, width)
        target = targets[row]

        def body(turn, carry):
            top, amount, picked = carry
            start = pl.multiple_of(turn * chunk, chunk)
            scores = product_nt(held[pl.ds(start, chunk), :], block_states)
            staged[slot, pl.ds(start, chunk), :] = scores
            ahead = jnp.maximum(top, jnp.max(scores, axis=0, keepdims=True))
            ids = start + lax.broadcasted_iota(jnp.int32, (chunk, 1), 0)
            return (
                ahead,
                amount * jnp.exp(top - ahead)
                + jnp.sum(jnp.exp(scores - ahead), axis=0, keepdims=True),
                picked
                + jnp.sum(jnp.where(ids == target, scores, 0.0), axis=0, keepdims=True),
            )

        scores = product_nt(held[0:chunk, :], block_states)
        staged[slot, 0:chunk, :] = scores
        top = jnp.max(scores, axis=0, keepdims=True)
        ids = lax.broadcasted_iota(jnp.int32, (chunk, 1), 0)
        carry = (
            top,
            jnp.sum(jnp.exp(scores - top), axis=0, keepdims=True),
            jnp.sum(jnp.where(ids == target, scores, 0.0), axis=0, keepdims=True),
        )
        if part > chunk:
            carry = lax.fori_loop(1, part // chunk, body, carry)
        for index in range(3):
            sends[0, index, pl.ds(row, 1), :] = carry[index]
        writes[mask] = pltpu.make_async_copy(
            staged.at[slot], logits.at[row], staged_sems.at[slot]
        )
        writes[mask].start()

    lag = 3
    for step in range(total + lag):
        if step < total:
            arrive(step)
        if step == 0:
            del sent[nearest]
            first[2].wait_send()
            spread(range(4, total, 2))
        if 2 <= step < total + 2:
            pass_on(step - 2)
        if step == lag:
            finish(moved)
            load = pltpu.make_async_copy(wide[0] if early else words[0], held, held_sem)
            load.start()
            own.wait()
            load.wait()
            if early:
                spot = pl.ds(pl.multiple_of(flip(block, total - 1) * last.shape[1], 128), 128)
                load = pltpu.make_async_copy(last, held.at[:, spot], held_sem)
                load.start()
                load.wait()
        if step >= lag:
            make(step - lag)
    lead = max(total - 2, 0)
    for mask in range(lead, total):
        writes[mask].wait()

    peers = [(near, lax.rem(place, 2)), (far, lax.div(place, 2))]
    for bit in range(bits):
        step = 1 << bit
        peers.append(((flip(block, step), place), lax.rem(lax.div(block, step), 2)))
    for stage, (peer, side) in enumerate(peers):
        copy = remote(
            sends.at[stage], recvs.at[stage], stage_sems.at[0, stage], stage_sems.at[1, stage],
            peer,
        )
        copy.wait_recv()
        sent.append(copy)
        mine = [sends[stage, index] for index in range(3)]
        theirs = [recvs[stage, index] for index in range(3)]
        leading = side == 0
        soon = [jnp.where(leading, one, other) for one, other in zip(mine, theirs)]
        late_ones = [jnp.where(leading, other, one) for one, other in zip(mine, theirs)]
        top = jnp.maximum(soon[0], late_ones[0])
        values = [
            top,
            soon[1] * jnp.exp(soon[0] - top) + late_ones[1] * jnp.exp(late_ones[0] - top),
            soon[2] + late_ones[2],
        ]
        for index in range(3):
            if stage + 1 < len(peers):
                sends[stage + 1, index] = values[index]
            else:
                totals[index] = values[index]
    for copy in sent:
        copy.wait_send()


def feed_norm(
    left, weight, kept, gain, shift, targets, number, table, wide=None, last=None, early=()
):
    height, width = kept.shape
    total = lax.axis_size("dp")
    stages = 2 + (total - 1).bit_length()
    span = QUARTERS * height
    words = wide if early else table
    part = words.shape[0]
    given = [left, weight, kept, gain.reshape(1, -1), shift.reshape(1, -1), targets, table]
    in_specs = [VMEM] * 6 + [ANY]
    out_shape = [
        jax.ShapeDtypeStruct((total, QUARTERS, height, width), jnp.bfloat16),
        jax.ShapeDtypeStruct((height, width), jnp.float32),
        jax.ShapeDtypeStruct((total, part, span), jnp.float32),
        jax.ShapeDtypeStruct((3, total, span), jnp.float32),
    ]
    out_specs = [VMEM, VMEM, ANY, VMEM]
    scratch = [pltpu.VMEM((height, width), jnp.bfloat16)] + exchange_scratch(height, width)
    scratch += [
        DMA((2, 4, total)),
        DMA,
        pltpu.VMEM((part, width), jnp.bfloat16),
        pltpu.VMEM((2, part, span), jnp.float32),
        pltpu.VMEM((stages, 3, total, span), jnp.float32),
        pltpu.VMEM((stages, 3, total, span), jnp.float32),
        DMA,
        DMA((2,)),
        DMA((2, stages)),
    ]
    aliases = {}
    if early:
        given += [wide, last]
        in_specs += [ANY] * 2
        out_shape.append(jax.ShapeDtypeStruct(wide.shape, wide.dtype))
        out_specs.append(ANY)
        aliases = {7: 4}
        scratch.append(DMA((2, len(early))))
    outcome = pl.pallas_call(
        functools.partial(feed_norm_kernel, total, tuple(early)),
        out_shape=out_shape,
        in_specs=in_specs,
        out_specs=out_specs,
        scratch_shapes=scratch,
        input_output_aliases=aliases,
        compiler_params=pltpu.CompilerParams(
            collective_id=number, has_side_effects=True, vmem_limit_bytes=62 * 2**20
        ),
    )(*given)
    return tuple(outcome)


def head_back_kernel(total, masks, fused, *refs):
    (parts, rows, gain), more, (quarters, grad_rows, grad_vecs), table, narrow, refs = split_refs(
        refs, 3, 5 * fused, 3, fused, bool(masks), len(refs)
    )
    mine, sib_recv, far_recv, beside_recv, across_recv, end_recv, sems = refs[:7]
    sib_sems, far_sems, beside_sems, end_sems, load_sems = refs[7:12]
    refs = refs[12:]
    block, place = lax.axis_index("dp"), lax.axis_index("mp")
    near, far = (block, flip(place, 1)), (block, flip(place, 2))
    beside = (flip(block, 1), place)
    height = rows.shape[0]
    others = range(1, total) if masks else [1] + list(range(2, total, 2))
    greet([near, far] + [(flip(block, mask), place) for mask in others])
    moved = []
    aside = [1]
    order = [mask for mask in range(total - 1, -1, -1) if mask != 1]
    order.insert(1, 1)
    sent, loads, sib, across, over, ends = [], {}, {}, {}, {}, {}

    def to_near(mask, slot, source):
        sib[mask, slot] = remote(
            source,
            sib_recv.at[mask, slot],
            sib_sems.at[0, mask, slot],
            sib_sems.at[1, mask, slot],
            near,
        )
        sent.append(sib[mask, slot])

    if fused:
        words, states, log_totals, grad_logp, ids_all = more
        if masks:
            move_sems, refs = refs[0], refs[1:]
        logits, held, grads, acc, held_sems = refs
        part = words.shape[0]
        chunk = chunk_of(part)
        span = grads.shape[2]

        def load(step):
            slot = step % 2
            loads[step] = pltpu.make_async_copy(
                parts.at[flip(block, order[step])], logits.at[slot], load_sems.at[slot, 0]
            )
            loads[step].start()

        def load_states(step):
            slot = step % 2
            loads[step, None] = pltpu.make_async_copy(
                states.at[flip(block, order[step])], held.at[slot], held_sems.at[slot]
            )
            loads[step, None].start()

        load(0)
        load_states(0)
    else:
        for mask in order:
            row = flip(block, mask)
            for turn in range(QUARTERS):
                if turn % 2 == 0:
                    loads[mask, turn] = pltpu.make_async_copy(
                        parts.at[row, flip(place, turn)],
                        mine.at[mask, 1 - turn // 2],
                        load_sems.at[mask, turn // 2],
                    )
                    loads[mask, turn].start()
                else:
                    to_near(mask, (3 - turn) // 2, parts.at[row, flip(place, turn)])

    def make(step):
        mask = order[step]
        if not fused:
            for turn in (0, 2):
                loads[mask, turn].wait()
            return
        if step + 1 < len(order):
            load(step + 1)
        loads[step].wait()
        row, slot = flip(block, mask), step % 2
        target = ids_all[row, 1:2] - (place * total + block) * part
        log_total, scale = log_totals[pl.ds(row, 1), :], grad_logp[pl.ds(row, 1), :]

        def body(turn, carry):
            start = pl.multiple_of(turn * chunk, chunk)
            ids = start + lax.broadcasted_iota(jnp.int32, (chunk, 1), 0)
            hot = (ids == target).astype(jnp.float32)
            chances = jnp.exp(logits[slot, pl.ds(start, chunk), :] - log_total)
            grads[step, pl.ds(start, chunk), :] = (scale * (hot - chances)).astype(jnp.bfloat16)
            return carry

        lax.fori_loop(0, part // chunk, body, 0)
        mine[mask] = (
            product_tn(grads[step], words[...]).astype(jnp.bfloat16).reshape(mine.shape[1:])
        )
        for slot, turn in enumerate((3, 1)):
            to_near(mask, slot, mine.at[mask, flip(place, turn)])

    def make_rows(step):
        if step + 1 < len(order):
            load_states(step + 1)
        loads[step, None].wait()
        block_states = held[step % 2].reshape(span, rows.shape[1])

        def body(turn, carry):
            here = pl.ds(pl.multiple_of(turn * chunk, chunk), chunk)
            value = dot_nn(grads[step, here, :], block_states)
            if step:
                value = value + acc[here, :]
            if step + 1 < len(order):
                acc[here, :] = value
            else:
                table[0][here, :] = value.astype(jnp.bfloat16)
            return carry

        lax.fori_loop(0, part // chunk, body, 0)

    own = (flip(place, 2), place) if fused else (0, 1)

    def join(mask, slot, *others):
        value = mine[mask, own[slot]].astype(jnp.float32)
        for other in others:
            value = value + other.astype(jnp.float32)
        return value

    def send_beside(mask, slot, target, sem_row):
        index = mask // 2
        copy = remote(
            mine.at[mask, own[slot]],
            target.at[index],
            beside_sems.at[0, sem_row, index],
            beside_sems.at[1, sem_row, index],
            beside,
        )
        sent.append(copy)
        return copy

    def to_far(mask):
        for slot in (0, 1):
            sib[mask, slot].wait_recv()
        terms = [sib_recv[mask, 0]]
        if mask + 1 in aside:
            across[mask + 1].wait_recv()
            terms.append(across_recv[mask // 2])
        mine[mask, own[0]] = join(mask, 0, *terms).astype(jnp.bfloat16)
        if mask in aside:
            mine[mask, own[1]] = join(mask, 1, sib_recv[mask, 1]).astype(jnp.bfloat16)
            across[mask] = send_beside(mask, 0, across_recv, 0)
            over[mask] = send_beside(mask, 1, beside_recv, 1)
            return
        across[mask] = remote(
            mine.at[mask, own[0]], far_recv.at[mask], far_sems.at[0, mask], far_sems.at[1, mask], far
        )
        sent.append(across[mask])

    def to_beside(mask):
        if mask in aside:
            return
        across[mask].wait_recv()
        mine[mask, own[1]] = join(mask, 1, sib_recv[mask, 1], far_recv[mask]).astype(jnp.bfloat16)
        over[mask] = send_beside(mask, 1, beside_recv, 1)

    def to_end(mask):
        across[mask].wait_recv()
        over[mask + 1].wait_recv()
        value = join(mask, 1, sib_recv[mask, 1], far_recv[mask], beside_recv[mask // 2])
        if mask == 0:
            return value
        mine[mask, own[1]] = value.astype(jnp.bfloat16)
        ends[mask] = remote(
            mine.at[mask, own[1]],
            end_recv.at[mask // 2],
            end_sems.at[0, mask // 2],
            end_sems.at[1, mask // 2],
            (flip(block, mask), place),
        )
        sent.append(ends[mask])
        return None

    outcome = None
    count = len(order)
    make(0)
    for step in range(count + 2):
        if step + 1 < count:
            make(step + 1)
        if step < count:
            to_far(order[step])
        if step >= 2:
            mask = order[step - 2]
            if mask % 2:
                to_beside(mask)
            else:
                outcome = to_end(mask)
        if fused and 1 <= step <= count:
            make_rows(step - 1)
            if masks and step == count:
                moved = table_copies(masks, True, table[0], narrow[0], move_sems)
    for mask in range(total - 2, 0, -2):
        ends[mask].wait_recv()
        outcome = outcome + end_recv[mask // 2].astype(jnp.float32)
    outcome, grad_gain, grad_shift = norm_rows_back(rows[...], gain[...], outcome)
    grad_rows[...] = outcome
    grad_vecs[0:1] = grad_gain
    grad_vecs[1:2] = grad_shift
    quarters[place] = outcome.astype(jnp.bfloat16)
    sent += share_quarter(place, quarters, near, far, sems)
    for copy in sent:
        copy.wait_send()
    finish(moved)


def head_back(values, rows, gain, number, masks=()):
    height, width = rows.shape
    total = lax.axis_size("dp")
    half = total // 2
    block = (height, width)
    fused = len(values) > 1
    out_shape = [
        jax.ShapeDtypeStruct((QUARTERS,) + block, jnp.bfloat16),
        jax.ShapeDtypeStruct(block, jnp.float32),
        jax.ShapeDtypeStruct((2, width), jnp.float32),
    ]
    out_specs = [VMEM] * 3
    scratch = [
        pltpu.VMEM((total, QUARTERS if fused else 2) + block, jnp.bfloat16),
        pltpu.VMEM((total, 2) + block, jnp.bfloat16),
        pltpu.VMEM((total,) + block, jnp.bfloat16),
        pltpu.VMEM((half,) + block, jnp.bfloat16),
        pltpu.VMEM((half,) + block, jnp.bfloat16),
        pltpu.VMEM((half,) + block, jnp.bfloat16),
        DMA((2, 6)),
        DMA((2, total, 2)),
        DMA((2, total)),
        DMA((2, 2, half)),
        DMA((2, half)),
        DMA((total, 2)),
    ]
    given = [values[0], rows, gain.reshape(1, -1)]
    in_specs = [ANY, VMEM, VMEM]
    if fused:
        words, states = values[1:3]
        part, span = values[0].shape[1:]
        given += list(values[1:])
        in_specs += [VMEM, ANY, VMEM, VMEM, VMEM]
        out_shape.append(jax.ShapeDtypeStruct(words.shape, jnp.bfloat16))
        out_specs.append(VMEM)
        if masks:
            narrow = (part * total, width // total)
            out_shape.append(jax.ShapeDtypeStruct(narrow, jnp.bfloat16))
            out_specs.append(ANY)
            scratch.append(DMA((2, len(masks))))
        scratch += [
            pltpu.VMEM((2, part, span), jnp.float32),
            pltpu.VMEM((2, QUARTERS) + block, jnp.bfloat16),
            pltpu.VMEM((total, part, span), jnp.bfloat16),
            pltpu.VMEM((part, width), jnp.float32),
            DMA((2,)),
        ]
    outcome = pl.pallas_call(
        functools.partial(head_back_kernel, total, tuple(masks), int(fused)),
        out_shape=out_shape,
        in_specs=in_specs,
        out_specs=out_specs,
        scratch_shapes=scratch,
        compiler_params=pltpu.CompilerParams(
            collective_id=number, has_side_effects=True, vmem_limit_bytes=63 * 2**20
        ),
    )(*given)
    return (outcome[0].reshape(-1, width),) + tuple(outcome[1:])


def dot_nn(left, right):
    return jnp.dot(left, right, preferred_element_type=jnp.float32)


def attend_back(queries, keys, values, grads, totals, allowed_at, acc_keys, acc_values, grad_queries,
                grad_keys, grad_values):
    span, width = keys.shape
    rows = queries.shape[0]
    step = min(256, rows)
    pair = 2 * HEAD_DIM
    lanes = lax.broadcasted_iota(jnp.int32, (1, pair), 1)
    sides = [(lanes // HEAD_DIM == side).astype(jnp.bfloat16) for side in range(2)]
    acc_keys[0:span] = jnp.zeros((span, width), jnp.float32)
    acc_values[0:span] = jnp.zeros((span, width), jnp.float32)

    def body(turn, carry):
        here = pl.ds(pl.multiple_of(turn * step, step), step)
        allowed = allowed_at(here)
        for start in range(0, width, pair):
            group = slice(start, start + pair)
            key, value = keys[:, group], values[:, group]
            query, grad = queries[here, group], grads[here, group]
            grad_query = jnp.zeros((step, pair), jnp.float32)
            for side in range(2):
                head = start // HEAD_DIM + side
                query_head, grad_head = query * sides[side], grad * sides[side]
                scores = product_nt(key, query_head) * HEAD_DIM ** (-0.5)
                scores = jnp.where(allowed, scores, masked_score)
                weights = jnp.exp(scores - totals[head : head + 1, here])
                grad_weights = product_nt(value, grad_head)
                row_dot = jnp.sum(grad_weights * weights, axis=0, keepdims=True)
                grad_scores = (weights * (grad_weights - row_dot)).astype(jnp.bfloat16)
                acc_values[0:span, group] += dot_nn(weights.astype(jnp.bfloat16), grad_head)
                acc_keys[0:span, group] += dot_nn(grad_scores, query_head)
                grad_query += product_tn(grad_scores, key * sides[side])
            grad_queries[here, group] = (grad_query * HEAD_DIM ** (-0.5)).astype(jnp.bfloat16)
        return carry

    lax.fori_loop(0, rows // step, body, 0)
    grad_keys[...] = (acc_keys[0:span] * HEAD_DIM ** (-0.5)).astype(jnp.bfloat16)
    grad_values[...] = acc_values[0:span].astype(jnp.bfloat16)


def attend(queries, keys, values, allowed_at, mixed, totals):
    rows, width = queries.shape
    step = min(256, rows)
    pair = 2 * HEAD_DIM
    lanes = lax.broadcasted_iota(jnp.int32, (1, pair), 1)
    sides = [(lanes // HEAD_DIM == side).astype(jnp.bfloat16) for side in range(2)]

    def body(turn, carry):
        here = pl.ds(pl.multiple_of(turn * step, step), step)
        allowed = allowed_at(here)
        for start in range(0, width, pair):
            group = slice(start, start + pair)
            key, value, query = keys[:, group], values[:, group], queries[here, group]
            mix = jnp.zeros((step, pair), jnp.float32)
            for side in range(2):
                head = start // HEAD_DIM + side
                scores = product_nt(key, query * sides[side]) * HEAD_DIM ** (-0.5)
                scores = jnp.where(allowed, scores, masked_score)
                largest = jnp.max(scores, axis=0, keepdims=True)
                weights = jnp.exp(scores - largest)
                amount = jnp.sum(weights, axis=0, keepdims=True)
                chances = (weights * (1.0 / amount)).astype(jnp.bfloat16)
                mix += product_tn(chances, value * sides[side])
                totals[head : head + 1, here] = largest + jnp.log(amount)
            mixed[here, group] = mix.astype(jnp.bfloat16)
        return carry

    lax.fori_loop(0, rows // step, body, 0)


class Given(typing.NamedTuple):
    tokens: typing.Any
    self_query: typing.Any
    self_key: typing.Any
    self_value: typing.Any
    self_out: typing.Any
    memory: typing.Any
    cross_key: typing.Any
    cross_value: typing.Any
    cross_query: typing.Any
    cross_out: typing.Any
    feed_up: typing.Any
    feed_down: typing.Any


class Small(typing.NamedTuple):
    answers: typing.Any
    counted: typing.Any
    segment_row: typing.Any
    segment_column: typing.Any
    gain_self: typing.Any
    shift_self: typing.Any
    gain_cross: typing.Any
    shift_cross: typing.Any
    gain_feed: typing.Any
    shift_feed: typing.Any


class Kept(typing.NamedTuple):
    query_self: typing.Any
    key_self: typing.Any
    value_self: typing.Any
    self_totals: typing.Any
    self_mix: typing.Any
    first_low: typing.Any
    rows_self: typing.Any
    key_cross: typing.Any
    value_cross: typing.Any
    query_cross: typing.Any
    cross_totals: typing.Any
    cross_mix: typing.Any
    second_low: typing.Any
    rows_cross: typing.Any
    feed_act: typing.Any
    gelu_slope: typing.Any
    rows_feed: typing.Any
    words: typing.Any
    states: typing.Any


def layer_kernel(total, *refs):
    count, made = len(Given._fields), len(Kept._fields)
    sources, small, table, targets, (logits, totals, ids_all), held, kept, refs = split_refs(
        refs, count, len(Small._fields), 1, made, 3, count, made, len(refs)
    )
    load_sems, keep_sems, ids_sems, ids_local, move_sems = refs[:5]
    buffers, refs = [refs[5:10], refs[10:15], refs[15:20]], refs[20:]
    normed, hops, staged, sends, recvs, staged_sems, stage_sems, ids = refs
    small, kept = Small(*small), Kept(*kept)
    block, place = lax.axis_index("dp"), lax.axis_index("mp")
    near, far = (block, flip(place, 1)), (block, flip(place, 2))
    beside = (flip(block, 1), place)
    bits = (total - 1).bit_length()
    loads = [
        pltpu.make_async_copy(source, target, load_sems.at[index])
        for index, (source, target) in enumerate(zip(sources, held))
    ]
    for copy in loads:
        copy.start()
    loaded = set()

    def get(index):
        if index not in loaded:
            loaded.add(index)
            loads[index].wait()
        return held[index]

    at = Given(*range(count))
    places = Kept(*range(made))
    saves = [
        pltpu.make_async_copy(source, target, keep_sems.at[index])
        for index, (source, target) in enumerate(zip(kept, targets))
    ]

    def save(*indices):
        for index in indices:
            saves[index].start()

    for index, source in enumerate((small.segment_row, small.answers, small.counted)):
        ids[index : index + 1] = source[...]
    greet([near, far] + [(flip(block, mask), place) for mask in range(1, total)])
    moved = table_copies((4, 5, 6, 7, 1, 2, 3, 0), False, table[0], kept.words, move_sems)
    ids_copies = [pltpu.make_async_copy(ids, ids_all.at[block], ids_local)]
    ids_copies[0].start()
    for mask in range(1, total):
        ids_copies.append(
            remote(
                ids, ids_all.at[block], ids_sems.at[0, mask], ids_sems.at[1, mask],
                (flip(block, mask), place),
            )
        )
    sent = []
    tokens = get(at.tokens)
    span, width = tokens.shape
    height = span // QUARTERS
    for weight, outcome, index in (
        (at.self_query, kept.query_self, places.query_self),
        (at.self_key, kept.key_self, places.key_self),
        (at.self_value, kept.value_self, places.value_self),
    ):
        outcome[...] = dot_nn(tokens[...], get(weight)[...]).astype(jnp.bfloat16)
        save(index)
    key_place = lax.broadcasted_iota(jnp.int32, (span, 1), 0)

    def allowed_self(here):
        query_place = here.start + lax.broadcasted_iota(jnp.int32, (1, here.size), 1)
        return (small.segment_column[...] == small.segment_row[:, here]) & (
            key_place <= query_place
        )

    attend(
        kept.query_self, kept.key_self, kept.value_self, allowed_self, kept.self_mix,
        kept.self_totals,
    )
    save(places.self_totals, places.self_mix)

    def join(turn, left, weight, residual, rows, fill):
        outcome = []
        run(
            sum_quarter_steps(
                place,
                lambda index: dot_nn(rows_of(left, height, index), weight[...]),
                near, far, *buffers[turn], outcome, sent,
            ),
            fill,
        )
        rows[...] = residual + outcome[0]

    def share(turn, quarters, fill):
        run(share_quarter_steps(place, quarters, near, far, buffers[turn][4], sent), fill)

    def make_keys():
        kept.key_cross[...] = dot_nn(get(at.memory)[...], get(at.cross_key)[...]).astype(
            jnp.bfloat16
        )

    def make_values():
        kept.value_cross[...] = dot_nn(get(at.memory)[...], get(at.cross_value)[...]).astype(
            jnp.bfloat16
        )

    join(
        0, kept.self_mix, get(at.self_out),
        rows_of(tokens, height, place).astype(jnp.float32), kept.rows_self, make_keys,
    )
    normed[...] = norm_rows(kept.rows_self[...], small.gain_self[...], small.shift_self[...])
    kept.first_low[place] = normed[...].astype(jnp.bfloat16)
    share(0, kept.first_low, make_values)
    save(places.key_cross, places.value_cross, places.rows_self, places.first_low)

    kept.query_cross[...] = dot_nn(
        kept.first_low[...].reshape(span, width), get(at.cross_query)[...]
    ).astype(jnp.bfloat16)
    owners = lax.broadcasted_iota(jnp.int32, (kept.key_cross.shape[0], 1), 0) // MEM
    attend(
        kept.query_cross, kept.key_cross, kept.value_cross,
        lambda here: owners == small.segment_row[:, here], kept.cross_mix, kept.cross_totals,
    )
    save(places.query_cross, places.cross_totals, places.cross_mix)
    join(1, kept.cross_mix, get(at.cross_out), normed[...], kept.rows_cross, None)
    normed[...] = norm_rows(kept.rows_cross[...], small.gain_cross[...], small.shift_cross[...])
    kept.second_low[place] = normed[...].astype(jnp.bfloat16)
    share(1, kept.second_low, None)
    save(places.rows_cross, places.second_low)

    get(at.feed_up)
    wide = kept.gelu_slope.shape[2]
    depth = kept.gelu_slope.shape[1]
    second = kept.second_low[...].reshape(span, width)
    for turn in range(kept.feed_act.shape[1] // wide):
        columns = slice(turn * wide, (turn + 1) * wide)
        pre = dot_nn(second, get(at.feed_up)[:, columns])
        chance = 0.5 + 0.5 * lax.erf(pre * 0.5**0.5)
        kept.feed_act[:, columns] = (pre * chance).astype(jnp.bfloat16)
        start = turn * span
        kept.gelu_slope[start // depth, start % depth : start % depth + span] = (
            chance + pre * jnp.exp(-0.5 * pre * pre) * (0.5 / jnp.pi) ** 0.5
        )
    save(places.feed_act, places.gelu_slope)
    join(2, kept.feed_act, get(at.feed_down), normed[...], kept.rows_feed, None)
    save(places.rows_feed)
    states = kept.states
    low = states.at[block, place]
    low[...] = norm_rows(
        kept.rows_feed[...], small.gain_feed[...], small.shift_feed[...]
    ).astype(jnp.bfloat16)
    across = flip(place, 2)

    def hop(kind, mask, peer, row, column):
        here = states.at[row, column]
        copy = remote(here, here, hops.at[0, kind, mask], hops.at[1, kind, mask], peer)
        sent.append(copy)
        return copy

    first, over, ends = {}, {}, {}

    def spread(masks):
        for mask in masks:
            first[mask] = hop(0, mask, (flip(block, mask), place), block, place)

    def pass_on(mask):
        over[mask].wait_recv()
        ends[mask, 1] = hop(3, mask, near, flip(block, mask), across)

    def arrive(mask):
        row = flip(block, mask)
        if mask:
            first[mask].wait_recv()
        if mask % 2 == 0:
            first[mask + 1] = hop(0, mask + 1, beside, row, place)
        over[mask] = hop(1, mask, far, row, place)
        ends[mask, 0] = hop(2, mask, near, row, place)

    words = kept.words
    part = words.shape[0]
    chunk = chunk_of(part)
    offset = (place * total + block) * part
    writes = {}

    def make(mask):
        row, slot = flip(block, mask), mask % 2
        for side in (0, 1):
            ends[mask, side].wait_recv()
        if mask >= 2:
            writes[mask - 2].wait()
        block_states = states[row].reshape(span, width)
        target = ids_all[row, 1:2] - offset

        def chunk_at(start):
            scores = product_nt(words[pl.ds(start, chunk), :], block_states)
            staged[slot, pl.ds(start, chunk), :] = scores
            ids = start + lax.broadcasted_iota(jnp.int32, (chunk, 1), 0)
            return (
                scores,
                jnp.max(scores, axis=0, keepdims=True),
                jnp.sum(jnp.where(ids == target, scores, 0.0), axis=0, keepdims=True),
            )

        def body(turn, carry):
            top, amount, picked = carry
            scores, ahead, more = chunk_at(pl.multiple_of(turn * chunk, chunk))
            ahead = jnp.maximum(top, ahead)
            return (
                ahead,
                amount * jnp.exp(top - ahead)
                + jnp.sum(jnp.exp(scores - ahead), axis=0, keepdims=True),
                picked + more,
            )

        scores, top, picked = chunk_at(0)
        carry = (top, jnp.sum(jnp.exp(scores - top), axis=0, keepdims=True), picked)
        carry = lax.fori_loop(1, part // chunk, body, carry)
        for index in range(3):
            sends[0, index, pl.ds(row, 1), :] = carry[index]
        writes[mask] = pltpu.make_async_copy(
            staged.at[slot], logits.at[row], staged_sems.at[slot]
        )
        writes[mask].start()

    spread([2])
    nearest = len(sent) - 1
    lag = 3
    for step in range(total + lag):
        if step < total:
            arrive(step)
        if step == 0:
            del sent[nearest]
            first[2].wait_send()
            spread(range(4, total, 2))
        if 2 <= step < total + 2:
            pass_on(step - 2)
        if step == lag:
            finish(ids_copies)
            finish(moved)
            save(places.words)
        if step >= lag:
            make(step - lag)
    save(places.states)

    peers = [(near, lax.rem(place, 2)), (far, lax.div(place, 2))]
    for bit in range(bits):
        step = 1 << bit
        peers.append(((flip(block, step), place), lax.rem(lax.div(block, step), 2)))
    for stage, (peer, side) in enumerate(peers):
        copy = remote(
            sends.at[stage], recvs.at[stage], stage_sems.at[0, stage], stage_sems.at[1, stage],
            peer,
        )
        copy.wait_recv()
        sent.append(copy)
        mine = [sends[stage, index] for index in range(3)]
        theirs = [recvs[stage, index] for index in range(3)]
        leading = side == 0
        soon = [jnp.where(leading, one, other) for one, other in zip(mine, theirs)]
        later = [jnp.where(leading, other, one) for one, other in zip(mine, theirs)]
        top = jnp.maximum(soon[0], later[0])
        values = [
            top,
            soon[1] * jnp.exp(soon[0] - top) + later[1] * jnp.exp(later[0] - top),
            soon[2] + later[2],
        ]
        for index in range(3):
            if stage + 1 < len(peers):
                sends[stage + 1, index] = values[index]
            else:
                totals[index] = values[index]
    for mask in range(total - 2, total):
        writes[mask].wait()
    for copy in sent:
        copy.wait_send()
    for copy in saves:
        copy.wait()


def layer_forward(given, small, table, number):
    total = lax.axis_size("dp")
    rows, width = given.tokens.shape
    span = given.memory.shape[0]
    part = given.self_query.shape[1]
    hidden = given.feed_up.shape[1]
    height = rows // QUARTERS
    words = table.shape[0] // total
    stages = 2 + (total - 1).bit_length()
    heads = part // HEAD_DIM

    def low(*shape):
        return jax.ShapeDtypeStruct(shape, jnp.bfloat16)

    def full(*shape):
        return jax.ShapeDtypeStruct(shape, jnp.float32)

    kept = Kept(
        query_self=low(rows, part),
        key_self=low(rows, part),
        value_self=low(rows, part),
        self_totals=full(heads, rows),
        self_mix=low(rows, part),
        first_low=low(QUARTERS, height, width),
        rows_self=full(height, width),
        key_cross=low(span, part),
        value_cross=low(span, part),
        query_cross=low(rows, part),
        cross_totals=full(heads, rows),
        cross_mix=low(rows, part),
        second_low=low(QUARTERS, height, width),
        rows_cross=full(height, width),
        feed_act=low(rows, hidden),
        gelu_slope=full(rows * hidden // (width * part), width, part),
        rows_feed=full(height, width),
        words=low(words, width),
        states=low(total, QUARTERS, height, width),
    )
    out_shape = list(kept) + [
        full(total, words, rows),
        full(3, total, rows),
        jax.ShapeDtypeStruct((total, 3, rows), jnp.int32),
    ]
    outcome = pl.pallas_call(
        functools.partial(layer_kernel, total),
        out_shape=out_shape,
        in_specs=[ANY] * len(given) + [VMEM] * len(small) + [ANY],
        out_specs=[ANY] * len(kept) + [ANY, VMEM, VMEM],
        scratch_shapes=[pltpu.VMEM(value.shape, value.dtype) for value in given]
        + [pltpu.VMEM(value.shape, value.dtype) for value in kept]
        + [DMA((len(given),)), DMA((len(kept),)), DMA((2, total)), DMA, DMA((2, total))]
        + exchange_scratch(height, width) * 3
        + [
            pltpu.VMEM((height, width), jnp.float32),
            DMA((2, 4, total)),
            pltpu.VMEM((2, words, rows), jnp.float32),
            pltpu.VMEM((stages, 3, total, rows), jnp.float32),
            pltpu.VMEM((stages, 3, total, rows), jnp.float32),
            DMA((2,)),
            DMA((2, stages)),
            pltpu.VMEM((3, rows), jnp.int32),
        ],
        compiler_params=pltpu.CompilerParams(
            collective_id=number, has_side_effects=True, vmem_limit_bytes=62 * 2**20
        ),
    )(*given, *small, table)
    return (Kept(*outcome[: len(kept)]),) + tuple(outcome[len(kept) :])


class Loaded(typing.NamedTuple):
    grad_out: typing.Any
    feed_down: typing.Any
    gelu_slope: typing.Any
    feed_up: typing.Any
    feed_act: typing.Any
    second_low: typing.Any
    cross_out: typing.Any
    cross_query: typing.Any
    query_cross: typing.Any
    key_cross: typing.Any
    value_cross: typing.Any
    cross_totals: typing.Any
    cross_mix: typing.Any
    first_low: typing.Any
    memory: typing.Any
    cross_key: typing.Any
    cross_value: typing.Any
    self_out: typing.Any
    query_self: typing.Any
    key_self: typing.Any
    value_self: typing.Any
    self_totals: typing.Any
    self_mix: typing.Any
    tokens: typing.Any
    self_query: typing.Any
    self_key: typing.Any
    self_value: typing.Any


class Plain(typing.NamedTuple):
    grad_rows: typing.Any
    rows_cross: typing.Any
    gain_cross: typing.Any
    rows_self: typing.Any
    gain_self: typing.Any
    grad_vecs: typing.Any
    segment_row: typing.Any
    segment_column: typing.Any


LOADS = len(Loaded._fields)
PIECES = 16
CROSSWISE = (8, 11)
PLANS = (
    (
        0, 6,
    ),
    (
        1, 7, 12, 18, 48,
    ),
    (
        2, 24, 8, 13, 30, 66,
    ),
    (
        3, 19, 25, 36,
    ),
    (
        9, 42, 14, 31, 54, 4, 20, 60, 26, 37, 49, 10, 67, 43, 15, 72, 32, 55, 21, 61, 78, 27,
        16, 38, 84, 50, 68, 73, 90, 44, 22, 33, 5, 56, 62, 79, 11, 28, 39, 17, 85, 51, 23, 69,
        91, 74, 29, 34, 45, 52, 57, 70, 40, 63, 80, 35, 46, 86, 92, 41, 75, 53, 47, 58, 71, 59,
        64, 81, 76, 87, 65, 93, 82, 88, 77, 94, 83, 89, 95,
    ),
)


def plans_of(bits):
    turns = 2 * bits
    if turns == 6:
        return [[divmod(code, turns) for code in plan] for plan in PLANS]
    feed, rest = range(0, 8), range(8, PIECES)
    plans = [
        [(piece, 0) for piece in feed],
        [(piece, 1) for piece in feed],
        [],
        [(piece, 0) for piece in range(8, 12)],
    ]
    plans.append([(piece, 0) for piece in range(12, PIECES)])
    plans[4] += [(piece, 1) for piece in rest]
    plans[4] += [(piece, turn) for turn in range(2, turns) for piece in range(PIECES)]
    return plans


def layer_back_kernel(total, orders, plans, moves, *refs):
    given_hbm, plain, table, outs, narrow, held, refs = split_refs(
        refs, LOADS, len(Plain._fields), 2 * bool(moves), 4, bool(moves), LOADS, len(refs)
    )
    outcome, vec_sums, token_share, memory_share = outs
    load_sems, refs = refs[0], refs[1:]
    (pieces, recv, vec_send, vec_recv, sum_sems, gather_sems, vec_sems), refs = refs[:7], refs[7:]
    norm_buffers = [refs[0:5], refs[5:10]]
    quarters, refs = refs[10:12], refs[12:]
    rows_all = quarters[0].shape[0] * quarters[0].shape[1]
    down, up = held[1], held[3]
    part = pieces.shape[2]
    column_buffers = [
        [
            [weight.at[0:size, turn * part : (turn + 1) * part] for turn in pair]
            for pair in ((0, 1), (2, 3))
        ]
        + refs[start : start + 3]
        for weight, size, start in ((down, pieces.shape[1], 0), (up, rows_all, 3))
    ]
    refs = refs[6:]
    grad_pre, grad_mix, grad_queries, grad_cross, grad_self = refs[:5]
    move_sems = refs[5:]
    loads = [
        pltpu.make_async_copy(source, target, load_sems.at[index])
        for index, (source, target) in enumerate(zip(given_hbm, held))
    ]
    for copy in loads:
        copy.start()
    loaded = set()

    def get(index):
        if index not in loaded:
            loaded.add(index)
            loads[index].wait()
        return held[index]

    at = Loaded(*range(LOADS))
    simple = Plain(*plain)
    block, place = lax.axis_index("dp"), lax.axis_index("mp")
    near, far = (block, flip(place, 1)), (block, flip(place, 2))
    bits = (total - 1).bit_length()
    over = [(flip(block, 1 << bit), place) for bit in range(bits)]
    sides = [lax.rem(lax.div(block, 1 << bit), 2) for bit in range(bits)]
    others = range(1, total) if moves else [1 << bit for bit in range(bits)]
    greet([near, far] + [(flip(block, mask), place) for mask in others])
    sent, moved = [], []
    if moves:
        moved = table_copies(moves, True, table[0], narrow[0], move_sems[0])

    height = pieces.shape[1]
    unit = height >> bits
    kept = [[0] for _ in range(PIECES)]
    copies = {}

    def offset(stage):
        return height - 2 * (height >> (stage + 1))

    def send_sum(piece, stage):
        side, rows = sides[orders[piece][stage]], height >> (stage + 1)
        kept[piece].append(kept[piece][stage] + side * rows)
        if stage:
            source, start = recv, offset(stage - 1) + (1 - side) * rows
        else:
            source, start = pieces, (1 - side) * rows
        copies[piece, stage] = remote(
            source.at[piece, pl.ds(pl.multiple_of(start, unit), rows), :],
            recv.at[piece, pl.ds(offset(stage), rows), :],
            sum_sems.at[0, piece, stage],
            sum_sems.at[1, piece, stage],
            over[orders[piece][stage]],
        )
        sent.append(copies[piece, stage])

    def take_sum(piece, stage):
        side, rows = sides[orders[piece][stage]], height >> (stage + 1)
        copies[piece, stage].wait_recv()
        if stage:
            source, start = recv, offset(stage - 1) + side * rows
        else:
            source, start = pieces, side * rows
        mine = source[piece, pl.ds(pl.multiple_of(start, unit), rows), :]
        there = pl.ds(offset(stage), rows)
        value = (
            mine.astype(jnp.float32) + recv[piece, there, :].astype(jnp.float32)
        ).astype(jnp.bfloat16)
        if stage + 1 < bits:
            recv[piece, there, :] = value
            send_sum(piece, stage + 1)
        else:
            start = kept[piece][bits]
            outcome[piece, pl.ds(pl.multiple_of(start, unit), rows), :] = value
            send_whole(piece, stage)

    def send_whole(piece, stage):
        rows = height >> (stage + 1)
        start = pl.multiple_of(kept[piece][stage + 1], unit)
        here = outcome.at[piece, pl.ds(start, rows), :]
        copies[piece, stage, True] = remote(
            here, here, gather_sems.at[0, piece, stage], gather_sems.at[1, piece, stage],
            over[orders[piece][stage]],
        )
        sent.append(copies[piece, stage, True])

    def move_on(plan):
        for piece, turn in plan:
            if turn < bits:
                take_sum(piece, turn)
                continue
            stage = 2 * bits - 1 - turn
            copies[piece, stage, True].wait_recv()
            if stage:
                send_whole(piece, stage - 1)

    def weight_piece(piece, left, right):
        pieces[piece] = product_tn(left, right).astype(jnp.bfloat16)
        send_sum(piece, 0)

    def folded_piece(piece, left, right):
        part = left.shape[1]
        for turn in range(height // part):
            columns = slice(turn * part, (turn + 1) * part)
            pieces[piece, columns, :] = product_tn(left[...], right[:, columns]).astype(
                jnp.bfloat16
            )
        send_sum(piece, 0)

    tasks = []

    def work(amount):
        for task in tasks[:amount]:
            task()
        del tasks[:amount]

    def norm_back(turn, block_of, kept_rows, rows, gain, first_amount):
        outcome_list = []
        run(
            sum_quarter_steps(
                place, block_of, near, far, *norm_buffers[turn], outcome_list, sent
            ),
            lambda: work(first_amount),
        )
        grad, grad_gain, grad_shift = norm_rows_back(
            rows[...], gain[...], kept_rows + outcome_list[0]
        )
        quarters[turn][place] = grad.astype(jnp.bfloat16)
        run(
            share_quarter_steps(place, quarters[turn], near, far, norm_buffers[turn][4], sent),
            lambda: work(len(tasks)),
        )
        return grad, grad_gain, grad_shift

    grad_out = get(at.grad_out)
    grad_act = product_nt(grad_out[...], get(at.feed_down)[...])
    slope = get(at.gelu_slope)
    acc_keys, acc_values = slope.at[0], slope.at[1]
    wide = pieces.shape[2]
    for turn in range(grad_pre.shape[1] // wide):
        columns = slice(turn * wide, (turn + 1) * wide)
        start = turn * rows_all
        grad_pre[:, columns] = (
            slope[start // height, start % height : start % height + rows_all]
            * grad_act[:, columns]
        ).astype(jnp.bfloat16)
    for index in (at.feed_up, at.feed_act, at.second_low):
        get(index)
    for turn in range(4):
        columns = slice(turn * wide, (turn + 1) * wide)
        tasks.append(
            functools.partial(
                lambda turn, columns: weight_piece(
                    turn, get(at.feed_act)[...], grad_out[:, columns]
                ),
                turn, columns,
            )
        )
    for turn in range(4):
        columns = slice(turn * wide, (turn + 1) * wide)
        tasks.append(
            functools.partial(
                lambda turn, columns: weight_piece(
                    4 + turn, get(at.second_low)[...], grad_pre[:, columns]
                ),
                turn, columns,
            )
        )
    quarter = rows_all // QUARTERS
    grad_second, *vecs_cross = norm_back(
        0,
        lambda index: product_nt(rows_of(grad_pre, quarter, index), get(at.feed_up)[...]),
        simple.grad_rows[...], simple.rows_cross, simple.gain_cross, 4,
    )

    grad_out = quarters[0]
    for index in range(QUARTERS):
        grad_mix[index * quarter : (index + 1) * quarter] = product_nt(
            grad_out[index], get(at.cross_out)[...]
        ).astype(jnp.bfloat16)
    for index in (at.query_cross, at.key_cross, at.value_cross, at.cross_totals):
        get(index)
    span = get(at.key_cross).shape[0]
    owners = lax.broadcasted_iota(jnp.int32, (span, 1), 0) // MEM
    attend_back(
        get(at.query_cross), get(at.key_cross), get(at.value_cross), grad_mix, get(at.cross_totals),
        lambda here: owners == simple.segment_row[:, here],
        acc_keys, acc_values, grad_queries, grad_cross.at[0], grad_cross.at[1],
    )
    move_on(plans[0])
    for index in (at.cross_query, at.cross_mix, at.first_low, at.memory, at.cross_key, at.cross_value):
        get(index)
    for kind in range(2):
        tasks.append(
            functools.partial(
                lambda kind: weight_piece(8 + kind, get(at.memory)[...], grad_cross[kind]), kind
            )
        )
    tasks.append(lambda: weight_piece(10, get(at.first_low)[...], grad_queries[...]))
    tasks.append(
        lambda: folded_piece(
            11, get(at.cross_mix), grad_out[...].reshape(rows_all, grad_out.shape[2])
        )
    )

    def memory_block(index):
        return product_nt(
            grad_cross[0], rows_of(get(at.cross_key), wide, index)
        ) + product_nt(grad_cross[1], rows_of(get(at.cross_value), wide, index))

    memory_total = []
    memory_steps = sum_quarter_steps(
        place, memory_block, near, far, *column_buffers[0], memory_total, sent
    )
    grad_first, *vecs_self = norm_back(
        1,
        lambda index: product_nt(rows_of(grad_queries, quarter, index), get(at.cross_query)[...]),
        grad_second, simple.rows_self, simple.gain_self, 3,
    )
    vec_peers = [near, far] + over

    def vec_start(stage, value):
        vec_send[stage] = value
        copies[None, stage] = remote(
            vec_send.at[stage], vec_recv.at[stage], vec_sems.at[0, stage], vec_sems.at[1, stage],
            vec_peers[stage],
        )
        sent.append(copies[None, stage])

    def vec_next(stage):
        if stage >= len(vec_peers):
            return
        copies[None, stage].wait_recv()
        value = vec_send[stage] + vec_recv[stage]
        if stage + 1 < len(vec_peers):
            vec_start(stage + 1, value)
        else:
            vec_sums[...] = value

    vec_start(
        0, jnp.concatenate(vecs_self + vecs_cross + [simple.grad_vecs[...]], axis=0)
    )

    grad_out = quarters[1]
    move_on(plans[1])
    for index in range(QUARTERS):
        grad_mix[index * quarter : (index + 1) * quarter] = product_nt(
            grad_out[index], get(at.self_out)[...]
        ).astype(jnp.bfloat16)
    for index in (at.query_self, at.key_self, at.value_self, at.self_totals):
        get(index)
    key_place = lax.broadcasted_iota(jnp.int32, (rows_all, 1), 0)

    def allowed_self(here):
        query_place = here.start + lax.broadcasted_iota(jnp.int32, (1, here.size), 1)
        return (simple.segment_column[...] == simple.segment_row[:, here]) & (
            key_place <= query_place
        )

    attend_back(
        get(at.query_self), get(at.key_self), get(at.value_self), grad_mix, get(at.self_totals),
        allowed_self, acc_keys, acc_values, grad_queries, grad_self.at[0], grad_self.at[1],
    )
    for index in (at.tokens, at.self_mix, at.self_query, at.self_key, at.self_value):
        get(index)
    move_on(plans[2])
    weight_piece(12, get(at.tokens)[...], grad_queries[...])
    weight_piece(13, get(at.tokens)[...], grad_self[0])
    weight_piece(14, get(at.tokens)[...], grad_self[1])
    folded_piece(15, get(at.self_mix), grad_out[...].reshape(rows_all, grad_out.shape[2]))
    move_on(plans[3])
    vec_next(0)

    def token_block(index):
        return (
            product_nt(grad_queries[...], rows_of(get(at.self_query), wide, index))
            + product_nt(grad_self[0], rows_of(get(at.self_key), wide, index))
            + product_nt(grad_self[1], rows_of(get(at.self_value), wide, index))
        )

    token_total = []
    token_steps = sum_quarter_steps(
        place, token_block, near, far, *column_buffers[1], token_total, sent
    )
    next(token_steps)
    next(memory_steps)
    own_columns = pl.ds(pl.multiple_of(place * wide, wide), wide)
    step = 12
    for turn, start in enumerate(range(0, len(plans[4]), step)):
        move_on(plans[4][start : start + step])
        if turn == 0:
            run(token_steps)
            token_share[...] = token_total[0] + quarters[1][:, :, own_columns].reshape(
                rows_all, wide
            ).astype(jnp.float32)
        if turn == 1:
            run(memory_steps)
            memory_share[...] = memory_total[0]
        vec_next(turn + 1)
    for turn in range(-(-len(plans[4]) // step) + 1, len(vec_peers)):
        vec_next(turn)
    for copy in sent:
        copy.wait_send()
    finish(moved)


def layer_back(values, plain, number, table=None, narrow=None, moves=()):
    total = lax.axis_size("dp")
    bits = (total - 1).bit_length()
    rest = list(range(2, bits))
    orders = [[1, 0] + rest if piece in CROSSWISE else [0, 1] + rest for piece in range(PIECES)]
    given = list(values) + list(plain)
    in_specs = [ANY] * len(values) + [VMEM] * len(plain)
    rows, width = values.tokens.shape
    span = values.memory.shape[0]
    part = values.self_query.shape[1]
    quarter = rows // QUARTERS
    stages = bits + 2
    vecs = (6, width)
    out_shape = [
        jax.ShapeDtypeStruct((PIECES, width, part), jnp.bfloat16),
        jax.ShapeDtypeStruct(vecs, jnp.float32),
        jax.ShapeDtypeStruct((rows, part), jnp.float32),
        jax.ShapeDtypeStruct((span, part), jnp.float32),
    ]
    out_specs = [VMEM] * 4
    scratch = [pltpu.VMEM(value.shape, value.dtype) for value in values]
    scratch += [
        DMA((LOADS,)),
        pltpu.VMEM((PIECES, width, part), jnp.bfloat16),
        pltpu.VMEM((PIECES, width - (width >> bits), part), jnp.bfloat16),
        pltpu.VMEM((stages,) + vecs, jnp.float32),
        pltpu.VMEM((stages,) + vecs, jnp.float32),
        DMA((2, PIECES, bits)),
        DMA((2, PIECES, bits)),
        DMA((2, stages)),
    ]
    scratch += exchange_scratch(quarter, width) * 2
    scratch += [pltpu.VMEM((QUARTERS, quarter, width), jnp.bfloat16)] * 2
    scratch += exchange_scratch(span, part)[2:] + exchange_scratch(rows, part)[2:]
    scratch += [
        pltpu.VMEM((rows, values.feed_up.shape[1]), jnp.bfloat16),
        pltpu.VMEM((rows, part), jnp.bfloat16),
        pltpu.VMEM((rows, part), jnp.bfloat16),
        pltpu.VMEM((2, span, part), jnp.bfloat16),
        pltpu.VMEM((2, rows, part), jnp.bfloat16),
    ]
    aliases = {}
    if moves:
        aliases = {len(given) + 1: len(out_shape)}
        given += [table, narrow]
        in_specs += [ANY] * 2
        out_shape.append(jax.ShapeDtypeStruct(narrow.shape, narrow.dtype))
        out_specs.append(ANY)
        scratch.append(DMA((2, len(moves))))
    return pl.pallas_call(
        functools.partial(layer_back_kernel, total, orders, plans_of(bits), tuple(moves)),
        out_shape=out_shape,
        in_specs=in_specs,
        out_specs=out_specs,
        scratch_shapes=scratch,
        input_output_aliases=aliases,
        compiler_params=pltpu.CompilerParams(
            collective_id=number, has_side_effects=True, vmem_limit_bytes=62 * 2**20
        ),
    )(*given)


def unfold(matrix, height):
    return jnp.concatenate(
        [matrix[start : start + height] for start in range(0, matrix.shape[0], height)], axis=1
    )


def shift_pairs(total, step):
    return [(index, (index + step) % total) for index in range(total)]


def spread_rows(table):
    total = lax.axis_size("dp")
    place = lax.axis_index("dp")
    width = table.shape[1]
    part = table.shape[0] // total
    whole = jnp.zeros((part, width * total), table.dtype)
    for step in range(total):
        block = lax.dynamic_slice_in_dim(table, (place + step) % total * part, part, 0)
        if step:
            block = lax.ppermute(block, "dp", shift_pairs(total, step))
        whole = lax.dynamic_update_slice_in_dim(
            whole, block, (place - step) % total * width, 1
        )
    return whole


def return_rows(rows, height):
    total = lax.axis_size("dp")
    place = lax.axis_index("dp")
    part = rows.shape[0]
    width = rows.shape[1] // total
    whole = jnp.zeros((height, width), rows.dtype)
    for step in range(total):
        block = lax.dynamic_slice_in_dim(rows, (place + step) % total * width, width, 1)
        if step:
            block = lax.ppermute(block, "dp", shift_pairs(total, step))
        whole = lax.dynamic_update_slice_in_dim(
            whole, block, (place - step) % total * part, 0
        )
    return whole


def layer_apart(
    tokens, memory, segment_ids, ids, offset, words, self_query, self_key, self_value, self_out,
    cross_query, cross_key, cross_value, cross_out, feed_up, feed_down, gain_self, shift_self,
    gain_cross, shift_cross, gain_feed, shift_feed,
):
    row_len = segment_ids.shape[1]
    places = jnp.arange(row_len, dtype=jnp.int32)
    owners = jnp.arange(memory.shape[0], dtype=jnp.int32) // MEM
    self_mask = (segment_ids[0][:, None] == segment_ids[0][None, :]) & (
        places[None, :] <= places[:, None]
    )
    cross_mask = segment_ids[0][:, None] == owners[None, :]
    quarter = tokens.shape[0] // QUARTERS
    inputs = lax.dynamic_slice_in_dim(tokens, lax.axis_index("mp") * quarter, quarter, 0)
    query_self = product(tokens, self_query).astype(jnp.bfloat16)
    key_self = product(tokens, self_key).astype(jnp.bfloat16)
    value_self = product(tokens, self_value).astype(jnp.bfloat16)
    self_mix, self_totals = attend_forward(query_self, key_self, value_self, self_mask)
    first_low, first_norm, rows_self, ids_all = mix_norm(
        self_mix, self_out, inputs, gain_self, shift_self, 0, ids
    )
    query_cross = product(first_low, cross_query).astype(jnp.bfloat16)
    key_cross = product(memory, cross_key).astype(jnp.bfloat16)
    value_cross = product(memory, cross_value).astype(jnp.bfloat16)
    cross_mix, cross_totals = attend_forward(query_cross, key_cross, value_cross, cross_mask)
    second_low, second_norm, rows_cross = mix_norm(
        cross_mix, cross_out, first_norm, gain_cross, shift_cross, 1
    )
    feed_pre = product(second_low, feed_up)
    feed_act, gelu_pull = jax.vjp(gelu_exact, feed_pre)
    gelu_slope = gelu_pull(jnp.ones_like(feed_pre))[0]
    feed_act = feed_act.astype(jnp.bfloat16)
    answers = ids_all[:, ids.shape[0] // 3 : 2 * (ids.shape[0] // 3)].reshape(-1, 1, row_len)
    states, rows_feed, logits, totals = feed_norm(
        feed_act, feed_down, second_norm, gain_feed, shift_feed, answers - offset, 2, words
    )
    gelu_slope = jnp.concatenate(
        jnp.split(gelu_slope, gelu_slope.shape[1] // self_query.shape[1], axis=1), axis=0
    ).reshape((2,) + self_query.shape)
    kept = Kept(
        query_self, key_self, value_self, self_totals, self_mix, first_low, rows_self, key_cross,
        value_cross, query_cross, cross_totals, cross_mix, second_low, rows_cross, feed_act,
        gelu_slope, rows_feed, words, states,
    )
    return kept, logits, totals, ids_all


def local(
    tokens,
    memory,
    segment_ids,
    answer_ids,
    loss_mask,
    doc_scores,
    slot_place,
    self_query,
    self_key,
    self_value,
    self_out,
    cross_query,
    cross_key,
    cross_value,
    cross_out,
    feed_up,
    feed_down,
    gain_self,
    shift_self,
    gain_cross,
    shift_cross,
    gain_feed,
    shift_feed,
    embedding,
):
    row_count, row_len = segment_ids.shape
    total = lax.axis_size("dp")
    direct = total == 8 and embedding.shape[1] % 128 == 0
    vocab_local = embedding.shape[0]
    part = vocab_local // total
    offset = lax.axis_index("mp") * vocab_local + lax.axis_index("dp") * part
    norms = (gain_self, shift_self, gain_cross, shift_cross, gain_feed, shift_feed)
    if direct:
        kept, logits, totals, ids_all = layer_forward(
            Given(
                tokens, self_query, self_key, self_value, self_out, memory, cross_key,
                cross_value, cross_query, cross_out, feed_up, feed_down,
            ),
            Small(
                answer_ids.reshape(1, -1), loss_mask.reshape(1, -1),
                segment_ids.reshape(1, -1), segment_ids.reshape(-1, 1),
                *(vector.reshape(1, -1) for vector in norms),
            ),
            embedding,
            0,
        )
        words = kept.words
    else:
        words = spread_rows(embedding)
        kept, logits, totals, ids_all = layer_apart(
            tokens, memory, segment_ids,
            jnp.concatenate([segment_ids, answer_ids, loss_mask], axis=0), offset, words, self_query, self_key, self_value,
            self_out, cross_query, cross_key, cross_value, cross_out, feed_up, feed_down, *norms,
        )
    segments_all, answers_all, kept_all = (
        ids_all[:, kind * row_count : (kind + 1) * row_count].reshape(-1, row_len)
        for kind in range(3)
    )
    log_total = totals[0] + jnp.log(totals[1])
    picked = totals[2]
    keeper = kept_all.astype(jnp.float32)
    token_logp = (picked - log_total) * keeper
    seg_hot = (
        segments_all[:, :, None] == jnp.arange(SEG_ROW, dtype=jnp.int32)[None, None, :]
    ).astype(jnp.float32)
    seg_sums = jnp.sum(seg_hot * token_logp[:, :, None], axis=1)
    counts = jnp.sum(seg_hot * keeper[:, :, None], axis=1)
    likely_all = (seg_sums / jnp.maximum(counts, 1.0)).reshape(-1)
    place_hot = (
        slot_place[:, None] == jnp.arange(likely_all.shape[0], dtype=jnp.int32)[None, :]
    ).astype(jnp.float32)

    def marginal(scores, likely):
        joint_score = jax.nn.log_softmax(scores, axis=1) + jnp.dot(
            place_hot, likely, precision=highest
        ).reshape(scores.shape)
        return -jnp.sum(jax.nn.logsumexp(joint_score, axis=1))

    loss, pullback = jax.vjp(marginal, doc_scores, likely_all)
    grad_scores, grad_likely = pullback(jnp.ones_like(loss))
    per_segment = grad_likely.reshape(counts.shape) / jnp.maximum(counts, 1.0)
    grad_logp = jnp.sum(seg_hot * per_segment[:, None, :], axis=2) * keeper
    if direct:
        head_values = (logits, words, kept.states, log_total, grad_logp, ids_all)
    else:
        targets = (answers_all - offset)[:, None, :]
        hot = (targets == jnp.arange(part, dtype=jnp.int32)[None, :, None]).astype(jnp.float32)
        grad_logits = (
            grad_logp[:, None, :] * (hot - jnp.exp(logits - log_total[:, None, :]))
        ).astype(jnp.bfloat16)
        parts = jnp.einsum(
            "rvt,vd->rtd", grad_logits, words, preferred_element_type=jnp.float32
        ).astype(jnp.bfloat16)
        head_values = (parts.reshape(kept.states.shape),)
        grad_words = jnp.einsum(
            "rvt,rtd->vd",
            grad_logits,
            kept.states.reshape(total, -1, kept.states.shape[3]),
            preferred_element_type=jnp.float32,
        ).astype(jnp.bfloat16)
    grad_branch, grad_res3, grad_vecs_feed, *made = head_back(
        head_values, kept.rows_feed, gain_feed, 3, (4, 1, 0) if direct else ()
    )
    grad_words, *narrow = made if direct else (grad_words,)
    values = Loaded(
        grad_out=grad_branch,
        feed_down=feed_down,
        gelu_slope=kept.gelu_slope,
        feed_up=feed_up,
        feed_act=kept.feed_act,
        second_low=kept.second_low.reshape(tokens.shape),
        cross_out=cross_out,
        cross_query=cross_query,
        query_cross=kept.query_cross,
        key_cross=kept.key_cross,
        value_cross=kept.value_cross,
        cross_totals=kept.cross_totals,
        cross_mix=kept.cross_mix,
        first_low=kept.first_low.reshape(tokens.shape),
        memory=memory,
        cross_key=cross_key,
        cross_value=cross_value,
        self_out=self_out,
        query_self=kept.query_self,
        key_self=kept.key_self,
        value_self=kept.value_self,
        self_totals=kept.self_totals,
        self_mix=kept.self_mix,
        tokens=tokens,
        self_query=self_query,
        self_key=self_key,
        self_value=self_value,
    )
    plain = Plain(
        grad_rows=grad_res3,
        rows_cross=kept.rows_cross,
        gain_cross=gain_cross.reshape(1, -1),
        rows_self=kept.rows_self,
        gain_self=gain_self.reshape(1, -1),
        grad_vecs=grad_vecs_feed,
        segment_row=segment_ids.reshape(1, -1),
        segment_column=segment_ids.reshape(-1, 1),
    )
    sums, grad_vecs, grad_tokens, memory_share, *narrow = layer_back(
        values, plain, 4, grad_words, *narrow, moves=(5, 6, 7, 2, 3) if direct else ()
    )
    grad_table = (
        narrow[0] if direct else return_rows(grad_words, vocab_local)
    ).astype(jnp.float32)
    sums = [part.astype(jnp.float32) for part in sums]
    sum_down = jnp.concatenate(sums[0:4], axis=1)
    sum_up = jnp.concatenate(sums[4:8], axis=1)
    sum_ck, sum_cv, sum_cq, sum_co, sum_sq, sum_sk, sum_sv, sum_so = sums[8:]
    sum_co, sum_so = (unfold(part, self_out.shape[0]) for part in (sum_co, sum_so))
    return (
        loss,
        grad_tokens,
        memory_share,
        sum_sq,
        sum_sk,
        sum_sv,
        sum_so,
        sum_cq,
        sum_ck,
        sum_cv,
        sum_co,
        sum_up,
        sum_down,
        *grad_vecs,
        grad_table,
        grad_scores,
    )


def solution(mesh):
    return jax.shard_map(
        local,
        mesh=mesh,
        in_specs=(
            P("dp", None),
            P("dp", None),
            P("dp", None),
            P("dp", None),
            P("dp", None),
            P(),
            P(),
            P(None, "mp"),
            P(None, "mp"),
            P(None, "mp"),
            P("mp", None),
            P(None, "mp"),
            P(None, "mp"),
            P(None, "mp"),
            P("mp", None),
            P(None, "mp"),
            P("mp", None),
            P(),
            P(),
            P(),
            P(),
            P(),
            P(),
            P("mp", "dp"),
        ),
        out_specs=(
            P(),
            P("dp", "mp"),
            P("dp", "mp"),
            P(None, "mp"),
            P(None, "mp"),
            P(None, "mp"),
            P("mp", None),
            P(None, "mp"),
            P(None, "mp"),
            P(None, "mp"),
            P("mp", None),
            P(None, "mp"),
            P("mp", None),
            P(),
            P(),
            P(),
            P(),
            P(),
            P(),
            P("mp", "dp"),
            P(),
        ),
        check_vma=False,
    )
```

```python
import functools
import typing

import jax
import jax.numpy as jnp
from jax import lax
from jax.experimental import pallas as pl
from jax.experimental.pallas import tpu as pltpu
from jax.sharding import PartitionSpec as P

HEAD_DIM = 64
SEG_ROW = 8
MEM = 128


masked_score = -1e30
norm_eps = 1e-05
highest = lax.Precision.HIGHEST


def product(left_side, right_side):
    return jnp.dot(left_side, right_side, preferred_element_type=jnp.float32)


def product_tn(left_side, right_side):
    return lax.dot_general(
        left_side, right_side, (((0,), (0,)), ((), ())), preferred_element_type=jnp.float32
    )


def product_nt(left_side, right_side):
    return lax.dot_general(
        left_side, right_side, (((1,), (1,)), ((), ())), preferred_element_type=jnp.float32
    )


def gelu_exact(inputs):
    return jax.nn.gelu(inputs, approximate=False)


def split_heads(matrix):
    return matrix.reshape(matrix.shape[0], matrix.shape[1] // HEAD_DIM, HEAD_DIM)


def attention_scores(queries, keys, allowed):
    scores = jnp.einsum(
        "qhd,khd->hqk", split_heads(queries), split_heads(keys), preferred_element_type=jnp.float32
    ) * HEAD_DIM ** (-0.5)
    return jnp.where(allowed[None], scores, masked_score)


def attend_forward(queries, keys, values, allowed):
    scores = attention_scores(queries, keys, allowed)
    largest = jnp.max(scores, axis=-1, keepdims=True)
    weights = jnp.exp(scores - largest)
    total = jnp.sum(weights, axis=-1, keepdims=True)
    probabilities = (weights / total).astype(jnp.bfloat16)
    mixed_out = jnp.einsum(
        "hqk,khd->qhd", probabilities, split_heads(values), preferred_element_type=jnp.float32
    )
    mixed_out = mixed_out.reshape(queries.shape).astype(jnp.bfloat16)
    return mixed_out, (largest + jnp.log(total))[..., 0]


MESH = pl.DeviceIdType.MESH
VMEM = pl.BlockSpec(memory_space=pltpu.VMEM)
ANY = pl.BlockSpec(memory_space=pl.ANY)
DMA = pltpu.SemaphoreType.DMA
QUARTERS = 4


def flip(index, mask):
    for bit in range(mask.bit_length()):
        if mask >> bit & 1:
            step = 1 << bit
            index = index + step * (1 - 2 * lax.rem(lax.div(index, step), 2))
    return index


def greet(peers):
    barrier = pltpu.get_barrier_semaphore()
    for peer in peers:
        pl.semaphore_signal(barrier, inc=1, device_id=peer, device_id_type=MESH)
    pl.semaphore_wait(barrier, len(peers))


def remote(source, target, send_sem, recv_sem, peer):
    copy = pltpu.make_async_remote_copy(
        src_ref=source,
        dst_ref=target,
        send_sem=send_sem,
        recv_sem=recv_sem,
        device_id=peer,
        device_id_type=MESH,
    )
    copy.start()
    return copy


def sum_quarter_steps(
    place, block_of, near, far, sib_send, sib_recv, far_send, far_recv, sems, outcome, sent
):
    copies = []
    sends, recvs = (
        slots if isinstance(slots, list) else [slots.at[0], slots.at[1]]
        for slots in (sib_send, sib_recv)
    )
    for slot, mask in enumerate((3, 1)):
        sends[slot][...] = block_of(flip(place, mask)).astype(jnp.bfloat16)
        copies.append(
            remote(sends[slot], recvs[slot], sems.at[0, slot], sems.at[1, slot], near)
        )
    distant = block_of(flip(place, 2))
    copies[0].wait_recv()
    far_send[...] = (distant + recvs[0][...].astype(jnp.float32)).astype(jnp.bfloat16)
    copies.append(remote(far_send, far_recv, sems.at[0, 2], sems.at[1, 2], far))
    sent += copies
    own = block_of(place)
    copies[1].wait_recv()
    yield
    copies[2].wait_recv()
    outcome.append(own + recvs[1][...].astype(jnp.float32) + far_recv[...].astype(jnp.float32))


def share_quarter_steps(place, quarters, near, far, sems, sent):
    here = quarters.at[place]
    to_far = remote(here, here, sems.at[0, 3], sems.at[1, 3], far)
    to_near = remote(here, here, sems.at[0, 4], sems.at[1, 4], near)
    yield
    to_far.wait_recv()
    there = quarters.at[flip(place, 2)]
    passed = remote(there, there, sems.at[0, 5], sems.at[1, 5], near)
    to_near.wait_recv()
    passed.wait_recv()
    sent += [to_far, to_near, passed]


def run(steps, between=None):
    for _ in steps:
        if between is not None:
            between()


def sum_quarter(place, block_of, near, far, *buffers):
    outcome, sent = [], []
    run(sum_quarter_steps(place, block_of, near, far, *buffers, outcome, sent))
    return outcome[0], sent


def share_quarter(place, quarters, near, far, sems):
    sent = []
    run(share_quarter_steps(place, quarters, near, far, sems, sent))
    return sent


def table_copies(masks, back, source, target, sems):
    block, place = lax.axis_index("dp"), lax.axis_index("mp")
    total = lax.axis_size("dp")
    part, width = (source if back else target).shape[0], (target if back else source).shape[1]
    copies = []
    for slot, mask in enumerate(masks):
        other = flip(block, mask)
        here = pl.ds(pl.multiple_of((block if back else other) * part, part), part)
        there = pl.ds(pl.multiple_of((other if back else block) * width, width), width)
        if back:
            start, end = source.at[:, there], target.at[here, :]
        else:
            start, end = source.at[here, :], target.at[:, there]
        if mask:
            copies.append(remote(start, end, sems.at[0, slot], sems.at[1, slot], (other, place)))
        else:
            copy = pltpu.make_async_copy(start, end, sems.at[0, slot])
            copy.start()
            copies.append(copy)
    return copies


def finish(copies):
    for copy in copies:
        copy.wait()


def split_refs(refs, *counts):
    groups, start = [], 0
    for count in counts:
        groups.append(list(refs[start : start + count]))
        start += count
    return groups


def norm_rows(rows, gain, shift):
    center = rows - jnp.mean(rows, axis=-1, keepdims=True)
    spread = jnp.mean(center * center, axis=-1, keepdims=True)
    return center * lax.rsqrt(spread + norm_eps) * gain + shift


def norm_rows_back(rows, gain, grad):
    center = rows - jnp.mean(rows, axis=-1, keepdims=True)
    scale = lax.rsqrt(jnp.mean(center * center, axis=-1, keepdims=True) + norm_eps)
    normed = center * scale
    inner = grad * gain
    grad_rows = scale * (
        inner
        - jnp.mean(inner, axis=-1, keepdims=True)
        - normed * jnp.mean(inner * normed, axis=-1, keepdims=True)
    )
    return (
        grad_rows,
        jnp.sum(grad * normed, axis=0, keepdims=True),
        jnp.sum(grad, axis=0, keepdims=True),
    )


def rows_of(ref, height, index):
    return ref[pl.ds(pl.multiple_of(index * height, height), height), :]


def exchange_scratch(height, width):
    return [
        pltpu.VMEM((2, height, width), jnp.bfloat16),
        pltpu.VMEM((2, height, width), jnp.bfloat16),
        pltpu.VMEM((height, width), jnp.bfloat16),
        pltpu.VMEM((height, width), jnp.bfloat16),
        DMA((2, 6)),
    ]


def mix_norm_kernel(total, with_ids, masks, chained, *refs):
    (left, weight, kept, gain, shift), ids, table, (quarters, normed, rows), ids_all, wide, refs = (
        split_refs(
            refs, 5, with_ids, (1 + chained) * bool(masks), 3, with_ids, bool(masks), len(refs)
        )
    )
    sib_send, sib_recv, far_send, far_recv, sems = refs[:5]
    refs = refs[5:]
    block, place = lax.axis_index("dp"), lax.axis_index("mp")
    near, far = (block, flip(place, 1)), (block, flip(place, 2))
    height = kept.shape[0]
    others = range(1, total) if with_ids else [mask for mask in masks if mask]
    greet([near, far] + [(flip(block, mask), place) for mask in others])
    copies = []
    if with_ids:
        ids_sems, ids_local = refs[:2]
        refs = refs[2:]
        own = pltpu.make_async_copy(ids[0], ids_all[0].at[block], ids_local)
        own.start()
        copies.append(own)
        for mask in range(1, total):
            copies.append(
                remote(
                    ids[0], ids_all[0].at[block], ids_sems.at[0, mask], ids_sems.at[1, mask],
                    (flip(block, mask), place),
                )
            )

    def block_of(index):
        return jnp.dot(
            rows_of(left, height, index), weight[...], preferred_element_type=jnp.float32
        )

    if masks:
        copies += table_copies(masks, False, table[0], wide[0], refs[0])
    branch, sent = sum_quarter(
        place, block_of, near, far, sib_send, sib_recv, far_send, far_recv, sems
    )
    outcome = kept[...].astype(jnp.float32) + branch
    rows[...] = outcome
    outcome = norm_rows(outcome, gain[...], shift[...])
    normed[...] = outcome
    quarters[place] = outcome.astype(jnp.bfloat16)
    sent += share_quarter(place, quarters, near, far, sems)
    finish(copies)
    for copy in sent:
        copy.wait_send()


def mix_norm(left, weight, kept, gain, shift, number, ids=None, table=None, wide=None, masks=()):
    height, width = kept.shape
    total = lax.axis_size("dp")
    quarter = jax.ShapeDtypeStruct((height, width), jnp.float32)
    out_shape = [
        jax.ShapeDtypeStruct((QUARTERS, height, width), jnp.bfloat16), quarter, quarter
    ]
    out_specs = [VMEM] * 3
    given = [left, weight, kept, gain.reshape(1, -1), shift.reshape(1, -1)]
    in_specs = [VMEM] * 5
    scratch = exchange_scratch(height, width)
    aliases = {}
    if ids is not None:
        given.append(ids)
        in_specs.append(VMEM)
        out_shape.append(jax.ShapeDtypeStruct((total,) + ids.shape, ids.dtype))
        out_specs.append(VMEM)
        scratch += [DMA((2, total)), DMA]
    if masks:
        given.append(table)
        in_specs.append(ANY)
        if wide is not None:
            aliases = {len(given): len(out_shape)}
            given.append(wide)
            in_specs.append(ANY)
        out_shape.append(
            jax.ShapeDtypeStruct((table.shape[0] // total, table.shape[1] * total), table.dtype)
        )
        out_specs.append(ANY)
        scratch.append(DMA((2, len(masks))))
    outcome = pl.pallas_call(
        functools.partial(
            mix_norm_kernel, total, int(ids is not None), tuple(masks), int(wide is not None)
        ),
        out_shape=out_shape,
        in_specs=in_specs,
        out_specs=out_specs,
        scratch_shapes=scratch,
        input_output_aliases=aliases,
        compiler_params=pltpu.CompilerParams(
            collective_id=number, has_side_effects=True, vmem_limit_bytes=48 * 2**20
        ),
    )(*given)
    return (outcome[0].reshape(-1, width),) + tuple(outcome[1:])


def chunk_of(rows):
    return max(size for size in range(16, min(rows, 400) + 1, 16) if rows % size == 0)


def feed_norm_kernel(total, early, *refs):
    (left, weight, kept, gain, shift, targets), words, (states, rows, logits, totals), wide, refs = (
        split_refs(refs, 6, 1 + 2 * bool(early), 4, bool(early), len(refs))
    )
    last = words[-1]
    low, sib_send, sib_recv, far_send, far_recv, sems, hops, own_sem = refs[:8]
    (held, staged, sends, recvs, held_sem, staged_sems, stage_sems), refs = refs[8:15], refs[15:]
    block, place = lax.axis_index("dp"), lax.axis_index("mp")
    near, far = (block, flip(place, 1)), (block, flip(place, 2))
    beside = (flip(block, 1), place)
    height = kept.shape[0]
    bits = (total - 1).bit_length()
    others = set(range(1, total) if early else range(2, total, 2))
    others |= {1 << bit for bit in range(bits)}
    greet([near, far] + [(flip(block, mask), place) for mask in sorted(others)])

    def block_of(index):
        return jnp.dot(
            rows_of(left, height, index), weight[...], preferred_element_type=jnp.float32
        )

    moved = []
    if early:
        moved = table_copies(early, False, words[0], wide[0], refs[0])
    branch, sent = sum_quarter(
        place, block_of, near, far, sib_send, sib_recv, far_send, far_recv, sems
    )
    outcome = kept[...] + branch
    rows[...] = outcome
    low[...] = norm_rows(outcome, gain[...], shift[...]).astype(jnp.bfloat16)
    own = pltpu.make_async_copy(low, states.at[block, place], own_sem)
    own.start()
    across = flip(place, 2)

    def hop(kind, mask, source, peer, row, column):
        copy = remote(
            source, states.at[row, column], hops.at[0, kind, mask], hops.at[1, kind, mask], peer
        )
        sent.append(copy)
        return copy

    first = {}

    def spread(masks):
        for mask in masks:
            first[mask] = hop(0, mask, low, (flip(block, mask), place), block, place)

    spread([2])
    nearest = len(sent) - 1
    over, ends = {}, {}

    def pass_on(mask):
        over[mask].wait_recv()
        row = flip(block, mask)
        ends[mask, 1] = hop(3, mask, states.at[row, across], near, row, across)

    def arrive(mask):
        row = flip(block, mask)
        if mask:
            first[mask].wait_recv()
        source = states.at[row, place] if mask else low
        if mask % 2 == 0:
            first[mask + 1] = hop(0, mask + 1, source, beside, row, place)
        over[mask] = hop(1, mask, source, far, row, place)
        ends[mask, 0] = hop(2, mask, source, near, row, place)

    part, width = held.shape
    chunk = chunk_of(part)
    span = QUARTERS * height
    writes = {}

    def make(mask):
        row, slot = flip(block, mask), mask % 2
        for side in (0, 1):
            ends[mask, side].wait_recv()
        if mask >= 2:
            writes[mask - 2].wait()
        block_states = states[row].reshape(span, width)
        target = targets[row]

        def body(turn, carry):
            top, amount, picked = carry
            start = pl.multiple_of(turn * chunk, chunk)
            scores = product_nt(held[pl.ds(start, chunk), :], block_states)
            staged[slot, pl.ds(start, chunk), :] = scores
            ahead = jnp.maximum(top, jnp.max(scores, axis=0, keepdims=True))
            ids = start + lax.broadcasted_iota(jnp.int32, (chunk, 1), 0)
            return (
                ahead,
                amount * jnp.exp(top - ahead)
                + jnp.sum(jnp.exp(scores - ahead), axis=0, keepdims=True),
                picked
                + jnp.sum(jnp.where(ids == target, scores, 0.0), axis=0, keepdims=True),
            )

        scores = product_nt(held[0:chunk, :], block_states)
        staged[slot, 0:chunk, :] = scores
        top = jnp.max(scores, axis=0, keepdims=True)
        ids = lax.broadcasted_iota(jnp.int32, (chunk, 1), 0)
        carry = (
            top,
            jnp.sum(jnp.exp(scores - top), axis=0, keepdims=True),
            jnp.sum(jnp.where(ids == target, scores, 0.0), axis=0, keepdims=True),
        )
        if part > chunk:
            carry = lax.fori_loop(1, part // chunk, body, carry)
        for index in range(3):
            sends[0, index, pl.ds(row, 1), :] = carry[index]
        writes[mask] = pltpu.make_async_copy(
            staged.at[slot], logits.at[row], staged_sems.at[slot]
        )
        writes[mask].start()

    lag = 3
    for step in range(total + lag):
        if step < total:
            arrive(step)
        if step == 0:
            del sent[nearest]
            first[2].wait_send()
            spread(range(4, total, 2))
        if 2 <= step < total + 2:
            pass_on(step - 2)
        if step == lag:
            finish(moved)
            load = pltpu.make_async_copy(wide[0] if early else words[0], held, held_sem)
            load.start()
            own.wait()
            load.wait()
            if early:
                spot = pl.ds(pl.multiple_of(flip(block, total - 1) * last.shape[1], 128), 128)
                load = pltpu.make_async_copy(last, held.at[:, spot], held_sem)
                load.start()
                load.wait()
        if step >= lag:
            make(step - lag)
    lead = max(total - 2, 0)
    for mask in range(lead, total):
        writes[mask].wait()

    peers = [(near, lax.rem(place, 2)), (far, lax.div(place, 2))]
    for bit in range(bits):
        step = 1 << bit
        peers.append(((flip(block, step), place), lax.rem(lax.div(block, step), 2)))
    for stage, (peer, side) in enumerate(peers):
        copy = remote(
            sends.at[stage], recvs.at[stage], stage_sems.at[0, stage], stage_sems.at[1, stage],
            peer,
        )
        copy.wait_recv()
        sent.append(copy)
        mine = [sends[stage, index] for index in range(3)]
        theirs = [recvs[stage, index] for index in range(3)]
        leading = side == 0
        soon = [jnp.where(leading, one, other) for one, other in zip(mine, theirs)]
        late_ones = [jnp.where(leading, other, one) for one, other in zip(mine, theirs)]
        top = jnp.maximum(soon[0], late_ones[0])
        values = [
            top,
            soon[1] * jnp.exp(soon[0] - top) + late_ones[1] * jnp.exp(late_ones[0] - top),
            soon[2] + late_ones[2],
        ]
        for index in range(3):
            if stage + 1 < len(peers):
                sends[stage + 1, index] = values[index]
            else:
                totals[index] = values[index]
    for copy in sent:
        copy.wait_send()


def feed_norm(
    left, weight, kept, gain, shift, targets, number, table, wide=None, last=None, early=()
):
    height, width = kept.shape
    total = lax.axis_size("dp")
    stages = 2 + (total - 1).bit_length()
    span = QUARTERS * height
    words = wide if early else table
    part = words.shape[0]
    given = [left, weight, kept, gain.reshape(1, -1), shift.reshape(1, -1), targets, table]
    in_specs = [VMEM] * 6 + [ANY]
    out_shape = [
        jax.ShapeDtypeStruct((total, QUARTERS, height, width), jnp.bfloat16),
        jax.ShapeDtypeStruct((height, width), jnp.float32),
        jax.ShapeDtypeStruct((total, part, span), jnp.float32),
        jax.ShapeDtypeStruct((3, total, span), jnp.float32),
    ]
    out_specs = [VMEM, VMEM, ANY, VMEM]
    scratch = [pltpu.VMEM((height, width), jnp.bfloat16)] + exchange_scratch(height, width)
    scratch += [
        DMA((2, 4, total)),
        DMA,
        pltpu.VMEM((part, width), jnp.bfloat16),
        pltpu.VMEM((2, part, span), jnp.float32),
        pltpu.VMEM((stages, 3, total, span), jnp.float32),
        pltpu.VMEM((stages, 3, total, span), jnp.float32),
        DMA,
        DMA((2,)),
        DMA((2, stages)),
    ]
    aliases = {}
    if early:
        given += [wide, last]
        in_specs += [ANY] * 2
        out_shape.append(jax.ShapeDtypeStruct(wide.shape, wide.dtype))
        out_specs.append(ANY)
        aliases = {7: 4}
        scratch.append(DMA((2, len(early))))
    outcome = pl.pallas_call(
        functools.partial(feed_norm_kernel, total, tuple(early)),
        out_shape=out_shape,
        in_specs=in_specs,
        out_specs=out_specs,
        scratch_shapes=scratch,
        input_output_aliases=aliases,
        compiler_params=pltpu.CompilerParams(
            collective_id=number, has_side_effects=True, vmem_limit_bytes=62 * 2**20
        ),
    )(*given)
    return tuple(outcome)


def head_back_kernel(total, masks, fused, *refs):
    (parts, rows, gain), more, (quarters, grad_rows, grad_vecs), table, narrow, refs = split_refs(
        refs, 3, 5 * fused, 3, fused, bool(masks), len(refs)
    )
    mine, sib_recv, far_recv, beside_recv, across_recv, end_recv, sems = refs[:7]
    sib_sems, far_sems, beside_sems, end_sems, load_sems = refs[7:12]
    refs = refs[12:]
    block, place = lax.axis_index("dp"), lax.axis_index("mp")
    near, far = (block, flip(place, 1)), (block, flip(place, 2))
    beside = (flip(block, 1), place)
    height = rows.shape[0]
    others = range(1, total) if masks else [1] + list(range(2, total, 2))
    greet([near, far] + [(flip(block, mask), place) for mask in others])
    moved = []
    aside = [1]
    order = [mask for mask in range(total - 1, -1, -1) if mask != 1]
    order.insert(1, 1)
    sent, loads, sib, across, over, ends = [], {}, {}, {}, {}, {}

    def to_near(mask, slot, source):
        sib[mask, slot] = remote(
            source,
            sib_recv.at[mask, slot],
            sib_sems.at[0, mask, slot],
            sib_sems.at[1, mask, slot],
            near,
        )
        sent.append(sib[mask, slot])

    if fused:
        words, states, log_totals, grad_logp, ids_all = more
        if masks:
            move_sems, refs = refs[0], refs[1:]
        logits, held, grads, acc, held_sems = refs
        part = words.shape[0]
        chunk = chunk_of(part)
        span = grads.shape[2]

        def load(step):
            slot = step % 2
            loads[step] = pltpu.make_async_copy(
                parts.at[flip(block, order[step])], logits.at[slot], load_sems.at[slot, 0]
            )
            loads[step].start()

        def load_states(step):
            slot = step % 2
            loads[step, None] = pltpu.make_async_copy(
                states.at[flip(block, order[step])], held.at[slot], held_sems.at[slot]
            )
            loads[step, None].start()

        load(0)
        load_states(0)
    else:
        for mask in order:
            row = flip(block, mask)
            for turn in range(QUARTERS):
                if turn % 2 == 0:
                    loads[mask, turn] = pltpu.make_async_copy(
                        parts.at[row, flip(place, turn)],
                        mine.at[mask, 1 - turn // 2],
                        load_sems.at[mask, turn // 2],
                    )
                    loads[mask, turn].start()
                else:
                    to_near(mask, (3 - turn) // 2, parts.at[row, flip(place, turn)])

    def make(step):
        mask = order[step]
        if not fused:
            for turn in (0, 2):
                loads[mask, turn].wait()
            return
        if step + 1 < len(order):
            load(step + 1)
        loads[step].wait()
        row, slot = flip(block, mask), step % 2
        target = ids_all[row, 1:2] - (place * total + block) * part
        log_total, scale = log_totals[pl.ds(row, 1), :], grad_logp[pl.ds(row, 1), :]

        def body(turn, carry):
            start = pl.multiple_of(turn * chunk, chunk)
            ids = start + lax.broadcasted_iota(jnp.int32, (chunk, 1), 0)
            hot = (ids == target).astype(jnp.float32)
            chances = jnp.exp(logits[slot, pl.ds(start, chunk), :] - log_total)
            grads[step, pl.ds(start, chunk), :] = (scale * (hot - chances)).astype(jnp.bfloat16)
            return carry

        lax.fori_loop(0, part // chunk, body, 0)
        mine[mask] = (
            product_tn(grads[step], words[...]).astype(jnp.bfloat16).reshape(mine.shape[1:])
        )
        for slot, turn in enumerate((3, 1)):
            to_near(mask, slot, mine.at[mask, flip(place, turn)])

    def make_rows(step):
        if step + 1 < len(order):
            load_states(step + 1)
        loads[step, None].wait()
        block_states = held[step % 2].reshape(span, rows.shape[1])

        def body(turn, carry):
            here = pl.ds(pl.multiple_of(turn * chunk, chunk), chunk)
            value = dot_nn(grads[step, here, :], block_states)
            if step:
                value = value + acc[here, :]
            if step + 1 < len(order):
                acc[here, :] = value
            else:
                table[0][here, :] = value.astype(jnp.bfloat16)
            return carry

        lax.fori_loop(0, part // chunk, body, 0)

    own = (flip(place, 2), place) if fused else (0, 1)

    def join(mask, slot, *others):
        value = mine[mask, own[slot]].astype(jnp.float32)
        for other in others:
            value = value + other.astype(jnp.float32)
        return value

    def send_beside(mask, slot, target, sem_row):
        index = mask // 2
        copy = remote(
            mine.at[mask, own[slot]],
            target.at[index],
            beside_sems.at[0, sem_row, index],
            beside_sems.at[1, sem_row, index],
            beside,
        )
        sent.append(copy)
        return copy

    def to_far(mask):
        for slot in (0, 1):
            sib[mask, slot].wait_recv()
        terms = [sib_recv[mask, 0]]
        if mask + 1 in aside:
            across[mask + 1].wait_recv()
            terms.append(across_recv[mask // 2])
        mine[mask, own[0]] = join(mask, 0, *terms).astype(jnp.bfloat16)
        if mask in aside:
            mine[mask, own[1]] = join(mask, 1, sib_recv[mask, 1]).astype(jnp.bfloat16)
            across[mask] = send_beside(mask, 0, across_recv, 0)
            over[mask] = send_beside(mask, 1, beside_recv, 1)
            return
        across[mask] = remote(
            mine.at[mask, own[0]], far_recv.at[mask], far_sems.at[0, mask], far_sems.at[1, mask], far
        )
        sent.append(across[mask])

    def to_beside(mask):
        if mask in aside:
            return
        across[mask].wait_recv()
        mine[mask, own[1]] = join(mask, 1, sib_recv[mask, 1], far_recv[mask]).astype(jnp.bfloat16)
        over[mask] = send_beside(mask, 1, beside_recv, 1)

    def to_end(mask):
        across[mask].wait_recv()
        over[mask + 1].wait_recv()
        value = join(mask, 1, sib_recv[mask, 1], far_recv[mask], beside_recv[mask // 2])
        if mask == 0:
            return value
        mine[mask, own[1]] = value.astype(jnp.bfloat16)
        ends[mask] = remote(
            mine.at[mask, own[1]],
            end_recv.at[mask // 2],
            end_sems.at[0, mask // 2],
            end_sems.at[1, mask // 2],
            (flip(block, mask), place),
        )
        sent.append(ends[mask])
        return None

    outcome = None
    count = len(order)
    make(0)
    for step in range(count + 2):
        if step + 1 < count:
            make(step + 1)
        if step < count:
            to_far(order[step])
        if step >= 2:
            mask = order[step - 2]
            if mask % 2:
                to_beside(mask)
            else:
                outcome = to_end(mask)
        if fused and 1 <= step <= count:
            make_rows(step - 1)
            if masks and step == count:
                moved = table_copies(masks, True, table[0], narrow[0], move_sems)
    for mask in range(total - 2, 0, -2):
        ends[mask].wait_recv()
        outcome = outcome + end_recv[mask // 2].astype(jnp.float32)
    outcome, grad_gain, grad_shift = norm_rows_back(rows[...], gain[...], outcome)
    grad_rows[...] = outcome
    grad_vecs[0:1] = grad_gain
    grad_vecs[1:2] = grad_shift
    quarters[place] = outcome.astype(jnp.bfloat16)
    sent += share_quarter(place, quarters, near, far, sems)
    for copy in sent:
        copy.wait_send()
    finish(moved)


def head_back(values, rows, gain, number, masks=()):
    height, width = rows.shape
    total = lax.axis_size("dp")
    half = total // 2
    block = (height, width)
    fused = len(values) > 1
    out_shape = [
        jax.ShapeDtypeStruct((QUARTERS,) + block, jnp.bfloat16),
        jax.ShapeDtypeStruct(block, jnp.float32),
        jax.ShapeDtypeStruct((2, width), jnp.float32),
    ]
    out_specs = [VMEM] * 3
    scratch = [
        pltpu.VMEM((total, QUARTERS if fused else 2) + block, jnp.bfloat16),
        pltpu.VMEM((total, 2) + block, jnp.bfloat16),
        pltpu.VMEM((total,) + block, jnp.bfloat16),
        pltpu.VMEM((half,) + block, jnp.bfloat16),
        pltpu.VMEM((half,) + block, jnp.bfloat16),
        pltpu.VMEM((half,) + block, jnp.bfloat16),
        DMA((2, 6)),
        DMA((2, total, 2)),
        DMA((2, total)),
        DMA((2, 2, half)),
        DMA((2, half)),
        DMA((total, 2)),
    ]
    given = [values[0], rows, gain.reshape(1, -1)]
    in_specs = [ANY, VMEM, VMEM]
    if fused:
        words, states = values[1:3]
        part, span = values[0].shape[1:]
        given += list(values[1:])
        in_specs += [VMEM, ANY, VMEM, VMEM, VMEM]
        out_shape.append(jax.ShapeDtypeStruct(words.shape, jnp.bfloat16))
        out_specs.append(VMEM)
        if masks:
            narrow = (part * total, width // total)
            out_shape.append(jax.ShapeDtypeStruct(narrow, jnp.bfloat16))
            out_specs.append(ANY)
            scratch.append(DMA((2, len(masks))))
        scratch += [
            pltpu.VMEM((2, part, span), jnp.float32),
            pltpu.VMEM((2, QUARTERS) + block, jnp.bfloat16),
            pltpu.VMEM((total, part, span), jnp.bfloat16),
            pltpu.VMEM((part, width), jnp.float32),
            DMA((2,)),
        ]
    outcome = pl.pallas_call(
        functools.partial(head_back_kernel, total, tuple(masks), int(fused)),
        out_shape=out_shape,
        in_specs=in_specs,
        out_specs=out_specs,
        scratch_shapes=scratch,
        compiler_params=pltpu.CompilerParams(
            collective_id=number, has_side_effects=True, vmem_limit_bytes=63 * 2**20
        ),
    )(*given)
    return (outcome[0].reshape(-1, width),) + tuple(outcome[1:])


def dot_nn(left, right):
    return jnp.dot(left, right, preferred_element_type=jnp.float32)


def attend_back(queries, keys, values, grads, totals, allowed_at, acc_keys, acc_values, grad_queries,
                grad_keys, grad_values):
    span, width = keys.shape
    rows = queries.shape[0]
    step = min(256, rows)
    pair = 2 * HEAD_DIM
    lanes = lax.broadcasted_iota(jnp.int32, (1, pair), 1)
    sides = [(lanes // HEAD_DIM == side).astype(jnp.bfloat16) for side in range(2)]
    acc_keys[0:span] = jnp.zeros((span, width), jnp.float32)
    acc_values[0:span] = jnp.zeros((span, width), jnp.float32)

    def body(turn, carry):
        here = pl.ds(pl.multiple_of(turn * step, step), step)
        allowed = allowed_at(here)
        for start in range(0, width, pair):
            group = slice(start, start + pair)
            key, value = keys[:, group], values[:, group]
            query, grad = queries[here, group], grads[here, group]
            grad_query = jnp.zeros((step, pair), jnp.float32)
            for side in range(2):
                head = start // HEAD_DIM + side
                query_head, grad_head = query * sides[side], grad * sides[side]
                scores = product_nt(key, query_head) * HEAD_DIM ** (-0.5)
                scores = jnp.where(allowed, scores, masked_score)
                weights = jnp.exp(scores - totals[head : head + 1, here])
                grad_weights = product_nt(value, grad_head)
                row_dot = jnp.sum(grad_weights * weights, axis=0, keepdims=True)
                grad_scores = (weights * (grad_weights - row_dot)).astype(jnp.bfloat16)
                acc_values[0:span, group] += dot_nn(weights.astype(jnp.bfloat16), grad_head)
                acc_keys[0:span, group] += dot_nn(grad_scores, query_head)
                grad_query += product_tn(grad_scores, key * sides[side])
            grad_queries[here, group] = (grad_query * HEAD_DIM ** (-0.5)).astype(jnp.bfloat16)
        return carry

    lax.fori_loop(0, rows // step, body, 0)
    grad_keys[...] = (acc_keys[0:span] * HEAD_DIM ** (-0.5)).astype(jnp.bfloat16)
    grad_values[...] = acc_values[0:span].astype(jnp.bfloat16)


def attend(queries, keys, values, allowed_at, mixed, totals):
    rows, width = queries.shape
    step = min(256, rows)
    pair = 2 * HEAD_DIM
    lanes = lax.broadcasted_iota(jnp.int32, (1, pair), 1)
    sides = [(lanes // HEAD_DIM == side).astype(jnp.bfloat16) for side in range(2)]

    def body(turn, carry):
        here = pl.ds(pl.multiple_of(turn * step, step), step)
        allowed = allowed_at(here)
        for start in range(0, width, pair):
            group = slice(start, start + pair)
            key, value, query = keys[:, group], values[:, group], queries[here, group]
            mix = jnp.zeros((step, pair), jnp.float32)
            for side in range(2):
                head = start // HEAD_DIM + side
                scores = product_nt(key, query * sides[side]) * HEAD_DIM ** (-0.5)
                scores = jnp.where(allowed, scores, masked_score)
                largest = jnp.max(scores, axis=0, keepdims=True)
                weights = jnp.exp(scores - largest)
                amount = jnp.sum(weights, axis=0, keepdims=True)
                chances = (weights * (1.0 / amount)).astype(jnp.bfloat16)
                mix += product_tn(chances, value * sides[side])
                totals[head : head + 1, here] = largest + jnp.log(amount)
            mixed[here, group] = mix.astype(jnp.bfloat16)
        return carry

    lax.fori_loop(0, rows // step, body, 0)


class Given(typing.NamedTuple):
    tokens: typing.Any
    self_query: typing.Any
    self_key: typing.Any
    self_value: typing.Any
    self_out: typing.Any
    memory: typing.Any
    cross_key: typing.Any
    cross_value: typing.Any
    cross_query: typing.Any
    cross_out: typing.Any
    feed_up: typing.Any
    feed_down: typing.Any


class Small(typing.NamedTuple):
    answers: typing.Any
    counted: typing.Any
    segment_row: typing.Any
    segment_column: typing.Any
    gain_self: typing.Any
    shift_self: typing.Any
    gain_cross: typing.Any
    shift_cross: typing.Any
    gain_feed: typing.Any
    shift_feed: typing.Any


class Kept(typing.NamedTuple):
    query_self: typing.Any
    key_self: typing.Any
    value_self: typing.Any
    self_totals: typing.Any
    self_mix: typing.Any
    first_low: typing.Any
    rows_self: typing.Any
    key_cross: typing.Any
    value_cross: typing.Any
    query_cross: typing.Any
    cross_totals: typing.Any
    cross_mix: typing.Any
    second_low: typing.Any
    rows_cross: typing.Any
    feed_act: typing.Any
    gelu_slope: typing.Any
    rows_feed: typing.Any
    words: typing.Any
    states: typing.Any


def layer_kernel(total, *refs):
    count, made = len(Given._fields), len(Kept._fields)
    sources, small, table, targets, (logits, totals, ids_all), held, kept, refs = split_refs(
        refs, count, len(Small._fields), 1, made, 3, count, made, len(refs)
    )
    load_sems, keep_sems, ids_sems, ids_local, move_sems = refs[:5]
    buffers, refs = [refs[5:10], refs[10:15], refs[15:20]], refs[20:]
    normed, hops, staged, sends, recvs, staged_sems, stage_sems, ids = refs
    small, kept = Small(*small), Kept(*kept)
    block, place = lax.axis_index("dp"), lax.axis_index("mp")
    near, far = (block, flip(place, 1)), (block, flip(place, 2))
    beside = (flip(block, 1), place)
    bits = (total - 1).bit_length()
    loads = [
        pltpu.make_async_copy(source, target, load_sems.at[index])
        for index, (source, target) in enumerate(zip(sources, held))
    ]
    for copy in loads:
        copy.start()
    loaded = set()

    def get(index):
        if index not in loaded:
            loaded.add(index)
            loads[index].wait()
        return held[index]

    at = Given(*range(count))
    places = Kept(*range(made))
    saves = [
        pltpu.make_async_copy(source, target, keep_sems.at[index])
        for index, (source, target) in enumerate(zip(kept, targets))
    ]

    def save(*indices):
        for index in indices:
            saves[index].start()

    for index, source in enumerate((small.segment_row, small.answers, small.counted)):
        ids[index : index + 1] = source[...]
    greet([near, far] + [(flip(block, mask), place) for mask in range(1, total)])
    moved = table_copies((4, 5, 6, 7, 1, 2, 3, 0), False, table[0], kept.words, move_sems)
    ids_copies = [pltpu.make_async_copy(ids, ids_all.at[block], ids_local)]
    ids_copies[0].start()
    for mask in range(1, total):
        ids_copies.append(
            remote(
                ids, ids_all.at[block], ids_sems.at[0, mask], ids_sems.at[1, mask],
                (flip(block, mask), place),
            )
        )
    sent = []
    tokens = get(at.tokens)
    span, width = tokens.shape
    height = span // QUARTERS
    for weight, outcome, index in (
        (at.self_query, kept.query_self, places.query_self),
        (at.self_key, kept.key_self, places.key_self),
        (at.self_value, kept.value_self, places.value_self),
    ):
        outcome[...] = dot_nn(tokens[...], get(weight)[...]).astype(jnp.bfloat16)
        save(index)
    key_place = lax.broadcasted_iota(jnp.int32, (span, 1), 0)

    def allowed_self(here):
        query_place = here.start + lax.broadcasted_iota(jnp.int32, (1, here.size), 1)
        return (small.segment_column[...] == small.segment_row[:, here]) & (
            key_place <= query_place
        )

    attend(
        kept.query_self, kept.key_self, kept.value_self, allowed_self, kept.self_mix,
        kept.self_totals,
    )
    save(places.self_totals, places.self_mix)

    def join(turn, left, weight, residual, rows, fill):
        outcome = []
        run(
            sum_quarter_steps(
                place,
                lambda index: dot_nn(rows_of(left, height, index), weight[...]),
                near, far, *buffers[turn], outcome, sent,
            ),
            fill,
        )
        rows[...] = residual + outcome[0]

    def share(turn, quarters, fill):
        run(share_quarter_steps(place, quarters, near, far, buffers[turn][4], sent), fill)

    def make_keys():
        kept.key_cross[...] = dot_nn(get(at.memory)[...], get(at.cross_key)[...]).astype(
            jnp.bfloat16
        )

    def make_values():
        kept.value_cross[...] = dot_nn(get(at.memory)[...], get(at.cross_value)[...]).astype(
            jnp.bfloat16
        )

    join(
        0, kept.self_mix, get(at.self_out),
        rows_of(tokens, height, place).astype(jnp.float32), kept.rows_self, make_keys,
    )
    normed[...] = norm_rows(kept.rows_self[...], small.gain_self[...], small.shift_self[...])
    kept.first_low[place] = normed[...].astype(jnp.bfloat16)
    share(0, kept.first_low, make_values)
    save(places.key_cross, places.value_cross, places.rows_self, places.first_low)

    kept.query_cross[...] = dot_nn(
        kept.first_low[...].reshape(span, width), get(at.cross_query)[...]
    ).astype(jnp.bfloat16)
    owners = lax.broadcasted_iota(jnp.int32, (kept.key_cross.shape[0], 1), 0) // MEM
    attend(
        kept.query_cross, kept.key_cross, kept.value_cross,
        lambda here: owners == small.segment_row[:, here], kept.cross_mix, kept.cross_totals,
    )
    save(places.query_cross, places.cross_totals, places.cross_mix)
    join(1, kept.cross_mix, get(at.cross_out), normed[...], kept.rows_cross, None)
    normed[...] = norm_rows(kept.rows_cross[...], small.gain_cross[...], small.shift_cross[...])
    kept.second_low[place] = normed[...].astype(jnp.bfloat16)
    share(1, kept.second_low, None)
    save(places.rows_cross, places.second_low)

    get(at.feed_up)
    wide = kept.gelu_slope.shape[2]
    depth = kept.gelu_slope.shape[1]
    second = kept.second_low[...].reshape(span, width)
    for turn in range(kept.feed_act.shape[1] // wide):
        columns = slice(turn * wide, (turn + 1) * wide)
        pre = dot_nn(second, get(at.feed_up)[:, columns])
        chance = 0.5 + 0.5 * lax.erf(pre * 0.5**0.5)
        kept.feed_act[:, columns] = (pre * chance).astype(jnp.bfloat16)
        start = turn * span
        kept.gelu_slope[start // depth, start % depth : start % depth + span] = (
            chance + pre * jnp.exp(-0.5 * pre * pre) * (0.5 / jnp.pi) ** 0.5
        )
    save(places.feed_act, places.gelu_slope)
    join(2, kept.feed_act, get(at.feed_down), normed[...], kept.rows_feed, None)
    save(places.rows_feed)
    states = kept.states
    low = states.at[block, place]
    low[...] = norm_rows(
        kept.rows_feed[...], small.gain_feed[...], small.shift_feed[...]
    ).astype(jnp.bfloat16)
    across = flip(place, 2)

    def hop(kind, mask, peer, row, column):
        here = states.at[row, column]
        copy = remote(here, here, hops.at[0, kind, mask], hops.at[1, kind, mask], peer)
        sent.append(copy)
        return copy

    first, over, ends = {}, {}, {}

    def spread(masks):
        for mask in masks:
            first[mask] = hop(0, mask, (flip(block, mask), place), block, place)

    def pass_on(mask):
        over[mask].wait_recv()
        ends[mask, 1] = hop(3, mask, near, flip(block, mask), across)

    def arrive(mask):
        row = flip(block, mask)
        if mask:
            first[mask].wait_recv()
        if mask % 2 == 0:
            first[mask + 1] = hop(0, mask + 1, beside, row, place)
        over[mask] = hop(1, mask, far, row, place)
        ends[mask, 0] = hop(2, mask, near, row, place)

    words = kept.words
    part = words.shape[0]
    chunk = chunk_of(part)
    offset = (place * total + block) * part
    writes = {}

    def make(mask):
        row, slot = flip(block, mask), mask % 2
        for side in (0, 1):
            ends[mask, side].wait_recv()
        if mask >= 2:
            writes[mask - 2].wait()
        block_states = states[row].reshape(span, width)
        target = ids_all[row, 1:2] - offset

        def chunk_at(start):
            scores = product_nt(words[pl.ds(start, chunk), :], block_states)
            staged[slot, pl.ds(start, chunk), :] = scores
            ids = start + lax.broadcasted_iota(jnp.int32, (chunk, 1), 0)
            return (
                scores,
                jnp.max(scores, axis=0, keepdims=True),
                jnp.sum(jnp.where(ids == target, scores, 0.0), axis=0, keepdims=True),
            )

        def body(turn, carry):
            top, amount, picked = carry
            scores, ahead, more = chunk_at(pl.multiple_of(turn * chunk, chunk))
            ahead = jnp.maximum(top, ahead)
            return (
                ahead,
                amount * jnp.exp(top - ahead)
                + jnp.sum(jnp.exp(scores - ahead), axis=0, keepdims=True),
                picked + more,
            )

        scores, top, picked = chunk_at(0)
        carry = (top, jnp.sum(jnp.exp(scores - top), axis=0, keepdims=True), picked)
        carry = lax.fori_loop(1, part // chunk, body, carry)
        for index in range(3):
            sends[0, index, pl.ds(row, 1), :] = carry[index]
        writes[mask] = pltpu.make_async_copy(
            staged.at[slot], logits.at[row], staged_sems.at[slot]
        )
        writes[mask].start()

    spread([2])
    nearest = len(sent) - 1
    lag = 2
    for step in range(total + lag):
        if step < total:
            arrive(step)
        if step == 0:
            del sent[nearest]
            first[2].wait_send()
            spread(range(4, total, 2))
        if 2 <= step < total + 2:
            pass_on(step - 2)
        if step == lag:
            finish(ids_copies)
            finish(moved)
            save(places.words)
        if step >= lag:
            make(step - lag)
    save(places.states)

    peers = [(near, lax.rem(place, 2)), (far, lax.div(place, 2))]
    for bit in range(bits):
        step = 1 << bit
        peers.append(((flip(block, step), place), lax.rem(lax.div(block, step), 2)))
    for stage, (peer, side) in enumerate(peers):
        copy = remote(
            sends.at[stage], recvs.at[stage], stage_sems.at[0, stage], stage_sems.at[1, stage],
            peer,
        )
        copy.wait_recv()
        sent.append(copy)
        mine = [sends[stage, index] for index in range(3)]
        theirs = [recvs[stage, index] for index in range(3)]
        leading = side == 0
        soon = [jnp.where(leading, one, other) for one, other in zip(mine, theirs)]
        later = [jnp.where(leading, other, one) for one, other in zip(mine, theirs)]
        top = jnp.maximum(soon[0], later[0])
        values = [
            top,
            soon[1] * jnp.exp(soon[0] - top) + later[1] * jnp.exp(later[0] - top),
            soon[2] + later[2],
        ]
        for index in range(3):
            if stage + 1 < len(peers):
                sends[stage + 1, index] = values[index]
            else:
                totals[index] = values[index]
    for mask in range(total - 2, total):
        writes[mask].wait()
    for copy in sent:
        copy.wait_send()
    for copy in saves:
        copy.wait()


def layer_forward(given, small, table, number):
    total = lax.axis_size("dp")
    rows, width = given.tokens.shape
    span = given.memory.shape[0]
    part = given.self_query.shape[1]
    hidden = given.feed_up.shape[1]
    height = rows // QUARTERS
    words = table.shape[0] // total
    stages = 2 + (total - 1).bit_length()
    heads = part // HEAD_DIM

    def low(*shape):
        return jax.ShapeDtypeStruct(shape, jnp.bfloat16)

    def full(*shape):
        return jax.ShapeDtypeStruct(shape, jnp.float32)

    kept = Kept(
        query_self=low(rows, part),
        key_self=low(rows, part),
        value_self=low(rows, part),
        self_totals=full(heads, rows),
        self_mix=low(rows, part),
        first_low=low(QUARTERS, height, width),
        rows_self=full(height, width),
        key_cross=low(span, part),
        value_cross=low(span, part),
        query_cross=low(rows, part),
        cross_totals=full(heads, rows),
        cross_mix=low(rows, part),
        second_low=low(QUARTERS, height, width),
        rows_cross=full(height, width),
        feed_act=low(rows, hidden),
        gelu_slope=full(rows * hidden // (width * part), width, part),
        rows_feed=full(height, width),
        words=low(words, width),
        states=low(total, QUARTERS, height, width),
    )
    out_shape = list(kept) + [
        full(total, words, rows),
        full(3, total, rows),
        jax.ShapeDtypeStruct((total, 3, rows), jnp.int32),
    ]
    outcome = pl.pallas_call(
        functools.partial(layer_kernel, total),
        out_shape=out_shape,
        in_specs=[ANY] * len(given) + [VMEM] * len(small) + [ANY],
        out_specs=[ANY] * len(kept) + [ANY, VMEM, VMEM],
        scratch_shapes=[pltpu.VMEM(value.shape, value.dtype) for value in given]
        + [pltpu.VMEM(value.shape, value.dtype) for value in kept]
        + [DMA((len(given),)), DMA((len(kept),)), DMA((2, total)), DMA, DMA((2, total))]
        + exchange_scratch(height, width) * 3
        + [
            pltpu.VMEM((height, width), jnp.float32),
            DMA((2, 4, total)),
            pltpu.VMEM((2, words, rows), jnp.float32),
            pltpu.VMEM((stages, 3, total, rows), jnp.float32),
            pltpu.VMEM((stages, 3, total, rows), jnp.float32),
            DMA((2,)),
            DMA((2, stages)),
            pltpu.VMEM((3, rows), jnp.int32),
        ],
        compiler_params=pltpu.CompilerParams(
            collective_id=number, has_side_effects=True, vmem_limit_bytes=62 * 2**20
        ),
    )(*given, *small, table)
    return (Kept(*outcome[: len(kept)]),) + tuple(outcome[len(kept) :])


class Loaded(typing.NamedTuple):
    grad_out: typing.Any
    feed_down: typing.Any
    gelu_slope: typing.Any
    feed_up: typing.Any
    feed_act: typing.Any
    second_low: typing.Any
    cross_out: typing.Any
    cross_query: typing.Any
    query_cross: typing.Any
    key_cross: typing.Any
    value_cross: typing.Any
    cross_totals: typing.Any
    cross_mix: typing.Any
    first_low: typing.Any
    memory: typing.Any
    cross_key: typing.Any
    cross_value: typing.Any
    self_out: typing.Any
    query_self: typing.Any
    key_self: typing.Any
    value_self: typing.Any
    self_totals: typing.Any
    self_mix: typing.Any
    tokens: typing.Any
    self_query: typing.Any
    self_key: typing.Any
    self_value: typing.Any


class Plain(typing.NamedTuple):
    grad_rows: typing.Any
    rows_cross: typing.Any
    gain_cross: typing.Any
    rows_self: typing.Any
    gain_self: typing.Any
    grad_vecs: typing.Any
    segment_row: typing.Any
    segment_column: typing.Any


LOADS = len(Loaded._fields)
PIECES = 16
CROSSWISE = (8, 11)
PLANS = (
    (
        0, 6,
    ),
    (
        1, 7, 12, 18, 48,
    ),
    (
        2, 24, 8, 13, 30, 66,
    ),
    (
        3, 19, 25, 36,
    ),
    (
        9, 42, 14, 31, 54, 4, 20, 60, 26, 37, 49, 10, 67, 43, 15, 72, 32, 55, 21, 61, 78, 27,
        16, 38, 84, 50, 68, 73, 90, 44, 22, 33, 5, 56, 62, 79, 11, 28, 39, 17, 85, 51, 23, 69,
        91, 74, 29, 34, 45, 52, 57, 70, 40, 63, 80, 35, 46, 86, 92, 41, 75, 53, 47, 58, 71, 59,
        64, 81, 76, 87, 65, 93, 82, 88, 77, 94, 83, 89, 95,
    ),
)


def plans_of(bits):
    turns = 2 * bits
    if turns == 6:
        return [[divmod(code, turns) for code in plan] for plan in PLANS]
    feed, rest = range(0, 8), range(8, PIECES)
    plans = [
        [(piece, 0) for piece in feed],
        [(piece, 1) for piece in feed],
        [],
        [(piece, 0) for piece in range(8, 12)],
    ]
    plans.append([(piece, 0) for piece in range(12, PIECES)])
    plans[4] += [(piece, 1) for piece in rest]
    plans[4] += [(piece, turn) for turn in range(2, turns) for piece in range(PIECES)]
    return plans


def layer_back_kernel(total, orders, plans, moves, *refs):
    given_hbm, plain, table, outs, narrow, held, refs = split_refs(
        refs, LOADS, len(Plain._fields), 2 * bool(moves), 4, bool(moves), LOADS, len(refs)
    )
    outcome, vec_sums, token_share, memory_share = outs
    load_sems, refs = refs[0], refs[1:]
    (pieces, recv, vec_send, vec_recv, sum_sems, gather_sems, vec_sems), refs = refs[:7], refs[7:]
    norm_buffers = [refs[0:5], refs[5:10]]
    quarters, refs = refs[10:12], refs[12:]
    rows_all = quarters[0].shape[0] * quarters[0].shape[1]
    down, up = held[1], held[3]
    part = pieces.shape[2]
    column_buffers = [
        [
            [weight.at[0:size, turn * part : (turn + 1) * part] for turn in pair]
            for pair in ((0, 1), (2, 3))
        ]
        + refs[start : start + 3]
        for weight, size, start in ((down, pieces.shape[1], 0), (up, rows_all, 3))
    ]
    refs = refs[6:]
    grad_pre, grad_mix, grad_queries, grad_cross, grad_self = refs[:5]
    move_sems = refs[5:]
    loads = [
        pltpu.make_async_copy(source, target, load_sems.at[index])
        for index, (source, target) in enumerate(zip(given_hbm, held))
    ]
    for copy in loads:
        copy.start()
    loaded = set()

    def get(index):
        if index not in loaded:
            loaded.add(index)
            loads[index].wait()
        return held[index]

    at = Loaded(*range(LOADS))
    simple = Plain(*plain)
    block, place = lax.axis_index("dp"), lax.axis_index("mp")
    near, far = (block, flip(place, 1)), (block, flip(place, 2))
    bits = (total - 1).bit_length()
    over = [(flip(block, 1 << bit), place) for bit in range(bits)]
    sides = [lax.rem(lax.div(block, 1 << bit), 2) for bit in range(bits)]
    others = range(1, total) if moves else [1 << bit for bit in range(bits)]
    greet([near, far] + [(flip(block, mask), place) for mask in others])
    sent, moved = [], []
    if moves:
        moved = table_copies(moves, True, table[0], narrow[0], move_sems[0])

    height = pieces.shape[1]
    unit = height >> bits
    kept = [[0] for _ in range(PIECES)]
    copies = {}

    def offset(stage):
        return height - 2 * (height >> (stage + 1))

    def send_sum(piece, stage):
        side, rows = sides[orders[piece][stage]], height >> (stage + 1)
        kept[piece].append(kept[piece][stage] + side * rows)
        if stage:
            source, start = recv, offset(stage - 1) + (1 - side) * rows
        else:
            source, start = pieces, (1 - side) * rows
        copies[piece, stage] = remote(
            source.at[piece, pl.ds(pl.multiple_of(start, unit), rows), :],
            recv.at[piece, pl.ds(offset(stage), rows), :],
            sum_sems.at[0, piece, stage],
            sum_sems.at[1, piece, stage],
            over[orders[piece][stage]],
        )
        sent.append(copies[piece, stage])

    def take_sum(piece, stage):
        side, rows = sides[orders[piece][stage]], height >> (stage + 1)
        copies[piece, stage].wait_recv()
        if stage:
            source, start = recv, offset(stage - 1) + side * rows
        else:
            source, start = pieces, side * rows
        mine = source[piece, pl.ds(pl.multiple_of(start, unit), rows), :]
        there = pl.ds(offset(stage), rows)
        value = (
            mine.astype(jnp.float32) + recv[piece, there, :].astype(jnp.float32)
        ).astype(jnp.bfloat16)
        if stage + 1 < bits:
            recv[piece, there, :] = value
            send_sum(piece, stage + 1)
        else:
            start = kept[piece][bits]
            outcome[piece, pl.ds(pl.multiple_of(start, unit), rows), :] = value
            send_whole(piece, stage)

    def send_whole(piece, stage):
        rows = height >> (stage + 1)
        start = pl.multiple_of(kept[piece][stage + 1], unit)
        here = outcome.at[piece, pl.ds(start, rows), :]
        copies[piece, stage, True] = remote(
            here, here, gather_sems.at[0, piece, stage], gather_sems.at[1, piece, stage],
            over[orders[piece][stage]],
        )
        sent.append(copies[piece, stage, True])

    def move_on(plan):
        for piece, turn in plan:
            if turn < bits:
                take_sum(piece, turn)
                continue
            stage = 2 * bits - 1 - turn
            copies[piece, stage, True].wait_recv()
            if stage:
                send_whole(piece, stage - 1)

    def weight_piece(piece, left, right):
        pieces[piece] = product_tn(left, right).astype(jnp.bfloat16)
        send_sum(piece, 0)

    def folded_piece(piece, left, right):
        part = left.shape[1]
        for turn in range(height // part):
            columns = slice(turn * part, (turn + 1) * part)
            pieces[piece, columns, :] = product_tn(left[...], right[:, columns]).astype(
                jnp.bfloat16
            )
        send_sum(piece, 0)

    tasks = []

    def work(amount):
        for task in tasks[:amount]:
            task()
        del tasks[:amount]

    def norm_back(turn, block_of, kept_rows, rows, gain, first_amount):
        outcome_list = []
        run(
            sum_quarter_steps(
                place, block_of, near, far, *norm_buffers[turn], outcome_list, sent
            ),
            lambda: work(first_amount),
        )
        grad, grad_gain, grad_shift = norm_rows_back(
            rows[...], gain[...], kept_rows + outcome_list[0]
        )
        quarters[turn][place] = grad.astype(jnp.bfloat16)
        run(
            share_quarter_steps(place, quarters[turn], near, far, norm_buffers[turn][4], sent),
            lambda: work(len(tasks)),
        )
        return grad, grad_gain, grad_shift

    grad_out = get(at.grad_out)
    grad_act = product_nt(grad_out[...], get(at.feed_down)[...])
    slope = get(at.gelu_slope)
    acc_keys, acc_values = slope.at[0], slope.at[1]
    wide = pieces.shape[2]
    for turn in range(grad_pre.shape[1] // wide):
        columns = slice(turn * wide, (turn + 1) * wide)
        start = turn * rows_all
        grad_pre[:, columns] = (
            slope[start // height, start % height : start % height + rows_all]
            * grad_act[:, columns]
        ).astype(jnp.bfloat16)
    for index in (at.feed_up, at.feed_act, at.second_low):
        get(index)
    for turn in range(4):
        columns = slice(turn * wide, (turn + 1) * wide)
        tasks.append(
            functools.partial(
                lambda turn, columns: weight_piece(
                    turn, get(at.feed_act)[...], grad_out[:, columns]
                ),
                turn, columns,
            )
        )
    for turn in range(4):
        columns = slice(turn * wide, (turn + 1) * wide)
        tasks.append(
            functools.partial(
                lambda turn, columns: weight_piece(
                    4 + turn, get(at.second_low)[...], grad_pre[:, columns]
                ),
                turn, columns,
            )
        )
    quarter = rows_all // QUARTERS
    grad_second, *vecs_cross = norm_back(
        0,
        lambda index: product_nt(rows_of(grad_pre, quarter, index), get(at.feed_up)[...]),
        simple.grad_rows[...], simple.rows_cross, simple.gain_cross, 4,
    )

    grad_out = quarters[0]
    for index in range(QUARTERS):
        grad_mix[index * quarter : (index + 1) * quarter] = product_nt(
            grad_out[index], get(at.cross_out)[...]
        ).astype(jnp.bfloat16)
    for index in (at.query_cross, at.key_cross, at.value_cross, at.cross_totals):
        get(index)
    span = get(at.key_cross).shape[0]
    owners = lax.broadcasted_iota(jnp.int32, (span, 1), 0) // MEM
    attend_back(
        get(at.query_cross), get(at.key_cross), get(at.value_cross), grad_mix, get(at.cross_totals),
        lambda here: owners == simple.segment_row[:, here],
        acc_keys, acc_values, grad_queries, grad_cross.at[0], grad_cross.at[1],
    )
    move_on(plans[0])
    for index in (at.cross_query, at.cross_mix, at.first_low, at.memory, at.cross_key, at.cross_value):
        get(index)
    for kind in range(2):
        tasks.append(
            functools.partial(
                lambda kind: weight_piece(8 + kind, get(at.memory)[...], grad_cross[kind]), kind
            )
        )
    tasks.append(lambda: weight_piece(10, get(at.first_low)[...], grad_queries[...]))
    tasks.append(
        lambda: folded_piece(
            11, get(at.cross_mix), grad_out[...].reshape(rows_all, grad_out.shape[2])
        )
    )

    def memory_block(index):
        return product_nt(
            grad_cross[0], rows_of(get(at.cross_key), wide, index)
        ) + product_nt(grad_cross[1], rows_of(get(at.cross_value), wide, index))

    memory_total = []
    memory_steps = sum_quarter_steps(
        place, memory_block, near, far, *column_buffers[0], memory_total, sent
    )
    grad_first, *vecs_self = norm_back(
        1,
        lambda index: product_nt(rows_of(grad_queries, quarter, index), get(at.cross_query)[...]),
        grad_second, simple.rows_self, simple.gain_self, 3,
    )
    vec_peers = [near, far] + over

    def vec_start(stage, value):
        vec_send[stage] = value
        copies[None, stage] = remote(
            vec_send.at[stage], vec_recv.at[stage], vec_sems.at[0, stage], vec_sems.at[1, stage],
            vec_peers[stage],
        )
        sent.append(copies[None, stage])

    def vec_next(stage):
        if stage >= len(vec_peers):
            return
        copies[None, stage].wait_recv()
        value = vec_send[stage] + vec_recv[stage]
        if stage + 1 < len(vec_peers):
            vec_start(stage + 1, value)
        else:
            vec_sums[...] = value

    vec_start(
        0, jnp.concatenate(vecs_self + vecs_cross + [simple.grad_vecs[...]], axis=0)
    )

    grad_out = quarters[1]
    move_on(plans[1])
    for index in range(QUARTERS):
        grad_mix[index * quarter : (index + 1) * quarter] = product_nt(
            grad_out[index], get(at.self_out)[...]
        ).astype(jnp.bfloat16)
    for index in (at.query_self, at.key_self, at.value_self, at.self_totals):
        get(index)
    key_place = lax.broadcasted_iota(jnp.int32, (rows_all, 1), 0)

    def allowed_self(here):
        query_place = here.start + lax.broadcasted_iota(jnp.int32, (1, here.size), 1)
        return (simple.segment_column[...] == simple.segment_row[:, here]) & (
            key_place <= query_place
        )

    attend_back(
        get(at.query_self), get(at.key_self), get(at.value_self), grad_mix, get(at.self_totals),
        allowed_self, acc_keys, acc_values, grad_queries, grad_self.at[0], grad_self.at[1],
    )
    for index in (at.tokens, at.self_mix, at.self_query, at.self_key, at.self_value):
        get(index)
    move_on(plans[2])
    weight_piece(12, get(at.tokens)[...], grad_queries[...])
    weight_piece(13, get(at.tokens)[...], grad_self[0])
    weight_piece(14, get(at.tokens)[...], grad_self[1])
    folded_piece(15, get(at.self_mix), grad_out[...].reshape(rows_all, grad_out.shape[2]))
    move_on(plans[3])
    vec_next(0)

    def token_block(index):
        return (
            product_nt(grad_queries[...], rows_of(get(at.self_query), wide, index))
            + product_nt(grad_self[0], rows_of(get(at.self_key), wide, index))
            + product_nt(grad_self[1], rows_of(get(at.self_value), wide, index))
        )

    token_total = []
    token_steps = sum_quarter_steps(
        place, token_block, near, far, *column_buffers[1], token_total, sent
    )
    next(token_steps)
    next(memory_steps)
    own_columns = pl.ds(pl.multiple_of(place * wide, wide), wide)
    step = 12
    for turn, start in enumerate(range(0, len(plans[4]), step)):
        move_on(plans[4][start : start + step])
        if turn == 0:
            run(token_steps)
            token_share[...] = token_total[0] + quarters[1][:, :, own_columns].reshape(
                rows_all, wide
            ).astype(jnp.float32)
        if turn == 1:
            run(memory_steps)
            memory_share[...] = memory_total[0]
        vec_next(turn + 1)
    for turn in range(-(-len(plans[4]) // step) + 1, len(vec_peers)):
        vec_next(turn)
    for copy in sent:
        copy.wait_send()
    finish(moved)


def layer_back(values, plain, number, table=None, narrow=None, moves=()):
    total = lax.axis_size("dp")
    bits = (total - 1).bit_length()
    rest = list(range(2, bits))
    orders = [[1, 0] + rest if piece in CROSSWISE else [0, 1] + rest for piece in range(PIECES)]
    given = list(values) + list(plain)
    in_specs = [ANY] * len(values) + [VMEM] * len(plain)
    rows, width = values.tokens.shape
    span = values.memory.shape[0]
    part = values.self_query.shape[1]
    quarter = rows // QUARTERS
    stages = bits + 2
    vecs = (6, width)
    out_shape = [
        jax.ShapeDtypeStruct((PIECES, width, part), jnp.bfloat16),
        jax.ShapeDtypeStruct(vecs, jnp.float32),
        jax.ShapeDtypeStruct((rows, part), jnp.float32),
        jax.ShapeDtypeStruct((span, part), jnp.float32),
    ]
    out_specs = [VMEM] * 4
    scratch = [pltpu.VMEM(value.shape, value.dtype) for value in values]
    scratch += [
        DMA((LOADS,)),
        pltpu.VMEM((PIECES, width, part), jnp.bfloat16),
        pltpu.VMEM((PIECES, width - (width >> bits), part), jnp.bfloat16),
        pltpu.VMEM((stages,) + vecs, jnp.float32),
        pltpu.VMEM((stages,) + vecs, jnp.float32),
        DMA((2, PIECES, bits)),
        DMA((2, PIECES, bits)),
        DMA((2, stages)),
    ]
    scratch += exchange_scratch(quarter, width) * 2
    scratch += [pltpu.VMEM((QUARTERS, quarter, width), jnp.bfloat16)] * 2
    scratch += exchange_scratch(span, part)[2:] + exchange_scratch(rows, part)[2:]
    scratch += [
        pltpu.VMEM((rows, values.feed_up.shape[1]), jnp.bfloat16),
        pltpu.VMEM((rows, part), jnp.bfloat16),
        pltpu.VMEM((rows, part), jnp.bfloat16),
        pltpu.VMEM((2, span, part), jnp.bfloat16),
        pltpu.VMEM((2, rows, part), jnp.bfloat16),
    ]
    aliases = {}
    if moves:
        aliases = {len(given) + 1: len(out_shape)}
        given += [table, narrow]
        in_specs += [ANY] * 2
        out_shape.append(jax.ShapeDtypeStruct(narrow.shape, narrow.dtype))
        out_specs.append(ANY)
        scratch.append(DMA((2, len(moves))))
    return pl.pallas_call(
        functools.partial(layer_back_kernel, total, orders, plans_of(bits), tuple(moves)),
        out_shape=out_shape,
        in_specs=in_specs,
        out_specs=out_specs,
        scratch_shapes=scratch,
        input_output_aliases=aliases,
        compiler_params=pltpu.CompilerParams(
            collective_id=number, has_side_effects=True, vmem_limit_bytes=62 * 2**20
        ),
    )(*given)


def unfold(matrix, height):
    return jnp.concatenate(
        [matrix[start : start + height] for start in range(0, matrix.shape[0], height)], axis=1
    )


def shift_pairs(total, step):
    return [(index, (index + step) % total) for index in range(total)]


def spread_rows(table):
    total = lax.axis_size("dp")
    place = lax.axis_index("dp")
    width = table.shape[1]
    part = table.shape[0] // total
    whole = jnp.zeros((part, width * total), table.dtype)
    for step in range(total):
        block = lax.dynamic_slice_in_dim(table, (place + step) % total * part, part, 0)
        if step:
            block = lax.ppermute(block, "dp", shift_pairs(total, step))
        whole = lax.dynamic_update_slice_in_dim(
            whole, block, (place - step) % total * width, 1
        )
    return whole


def return_rows(rows, height):
    total = lax.axis_size("dp")
    place = lax.axis_index("dp")
    part = rows.shape[0]
    width = rows.shape[1] // total
    whole = jnp.zeros((height, width), rows.dtype)
    for step in range(total):
        block = lax.dynamic_slice_in_dim(rows, (place + step) % total * width, width, 1)
        if step:
            block = lax.ppermute(block, "dp", shift_pairs(total, step))
        whole = lax.dynamic_update_slice_in_dim(
            whole, block, (place - step) % total * part, 0
        )
    return whole


def layer_apart(
    tokens, memory, segment_ids, ids, offset, words, self_query, self_key, self_value, self_out,
    cross_query, cross_key, cross_value, cross_out, feed_up, feed_down, gain_self, shift_self,
    gain_cross, shift_cross, gain_feed, shift_feed,
):
    row_len = segment_ids.shape[1]
    places = jnp.arange(row_len, dtype=jnp.int32)
    owners = jnp.arange(memory.shape[0], dtype=jnp.int32) // MEM
    self_mask = (segment_ids[0][:, None] == segment_ids[0][None, :]) & (
        places[None, :] <= places[:, None]
    )
    cross_mask = segment_ids[0][:, None] == owners[None, :]
    quarter = tokens.shape[0] // QUARTERS
    inputs = lax.dynamic_slice_in_dim(tokens, lax.axis_index("mp") * quarter, quarter, 0)
    query_self = product(tokens, self_query).astype(jnp.bfloat16)
    key_self = product(tokens, self_key).astype(jnp.bfloat16)
    value_self = product(tokens, self_value).astype(jnp.bfloat16)
    self_mix, self_totals = attend_forward(query_self, key_self, value_self, self_mask)
    first_low, first_norm, rows_self, ids_all = mix_norm(
        self_mix, self_out, inputs, gain_self, shift_self, 0, ids
    )
    query_cross = product(first_low, cross_query).astype(jnp.bfloat16)
    key_cross = product(memory, cross_key).astype(jnp.bfloat16)
    value_cross = product(memory, cross_value).astype(jnp.bfloat16)
    cross_mix, cross_totals = attend_forward(query_cross, key_cross, value_cross, cross_mask)
    second_low, second_norm, rows_cross = mix_norm(
        cross_mix, cross_out, first_norm, gain_cross, shift_cross, 1
    )
    feed_pre = product(second_low, feed_up)
    feed_act, gelu_pull = jax.vjp(gelu_exact, feed_pre)
    gelu_slope = gelu_pull(jnp.ones_like(feed_pre))[0]
    feed_act = feed_act.astype(jnp.bfloat16)
    answers = ids_all[:, ids.shape[0] // 3 : 2 * (ids.shape[0] // 3)].reshape(-1, 1, row_len)
    states, rows_feed, logits, totals = feed_norm(
        feed_act, feed_down, second_norm, gain_feed, shift_feed, answers - offset, 2, words
    )
    gelu_slope = jnp.concatenate(
        jnp.split(gelu_slope, gelu_slope.shape[1] // self_query.shape[1], axis=1), axis=0
    ).reshape((2,) + self_query.shape)
    kept = Kept(
        query_self, key_self, value_self, self_totals, self_mix, first_low, rows_self, key_cross,
        value_cross, query_cross, cross_totals, cross_mix, second_low, rows_cross, feed_act,
        gelu_slope, rows_feed, words, states,
    )
    return kept, logits, totals, ids_all


def local(
    tokens,
    memory,
    segment_ids,
    answer_ids,
    loss_mask,
    doc_scores,
    slot_place,
    self_query,
    self_key,
    self_value,
    self_out,
    cross_query,
    cross_key,
    cross_value,
    cross_out,
    feed_up,
    feed_down,
    gain_self,
    shift_self,
    gain_cross,
    shift_cross,
    gain_feed,
    shift_feed,
    embedding,
):
    row_count, row_len = segment_ids.shape
    total = lax.axis_size("dp")
    direct = total == 8 and embedding.shape[1] % 128 == 0
    vocab_local = embedding.shape[0]
    part = vocab_local // total
    offset = lax.axis_index("mp") * vocab_local + lax.axis_index("dp") * part
    norms = (gain_self, shift_self, gain_cross, shift_cross, gain_feed, shift_feed)
    if direct:
        kept, logits, totals, ids_all = layer_forward(
            Given(
                tokens, self_query, self_key, self_value, self_out, memory, cross_key,
                cross_value, cross_query, cross_out, feed_up, feed_down,
            ),
            Small(
                answer_ids.reshape(1, -1), loss_mask.reshape(1, -1),
                segment_ids.reshape(1, -1), segment_ids.reshape(-1, 1),
                *(vector.reshape(1, -1) for vector in norms),
            ),
            embedding,
            0,
        )
        words = kept.words
    else:
        words = spread_rows(embedding)
        kept, logits, totals, ids_all = layer_apart(
            tokens, memory, segment_ids,
            jnp.concatenate([segment_ids, answer_ids, loss_mask], axis=0), offset, words, self_query, self_key, self_value,
            self_out, cross_query, cross_key, cross_value, cross_out, feed_up, feed_down, *norms,
        )
    segments_all, answers_all, kept_all = (
        ids_all[:, kind * row_count : (kind + 1) * row_count].reshape(-1, row_len)
        for kind in range(3)
    )
    log_total = totals[0] + jnp.log(totals[1])
    picked = totals[2]
    keeper = kept_all.astype(jnp.float32)
    token_logp = (picked - log_total) * keeper
    seg_hot = (
        segments_all[:, :, None] == jnp.arange(SEG_ROW, dtype=jnp.int32)[None, None, :]
    ).astype(jnp.float32)
    seg_sums = jnp.sum(seg_hot * token_logp[:, :, None], axis=1)
    counts = jnp.sum(seg_hot * keeper[:, :, None], axis=1)
    likely_all = (seg_sums / jnp.maximum(counts, 1.0)).reshape(-1)
    place_hot = (
        slot_place[:, None] == jnp.arange(likely_all.shape[0], dtype=jnp.int32)[None, :]
    ).astype(jnp.float32)

    def marginal(scores, likely):
        joint_score = jax.nn.log_softmax(scores, axis=1) + jnp.dot(
            place_hot, likely, precision=highest
        ).reshape(scores.shape)
        return -jnp.sum(jax.nn.logsumexp(joint_score, axis=1))

    loss, pullback = jax.vjp(marginal, doc_scores, likely_all)
    grad_scores, grad_likely = pullback(jnp.ones_like(loss))
    per_segment = grad_likely.reshape(counts.shape) / jnp.maximum(counts, 1.0)
    grad_logp = jnp.sum(seg_hot * per_segment[:, None, :], axis=2) * keeper
    if direct:
        head_values = (logits, words, kept.states, log_total, grad_logp, ids_all)
    else:
        targets = (answers_all - offset)[:, None, :]
        hot = (targets == jnp.arange(part, dtype=jnp.int32)[None, :, None]).astype(jnp.float32)
        grad_logits = (
            grad_logp[:, None, :] * (hot - jnp.exp(logits - log_total[:, None, :]))
        ).astype(jnp.bfloat16)
        parts = jnp.einsum(
            "rvt,vd->rtd", grad_logits, words, preferred_element_type=jnp.float32
        ).astype(jnp.bfloat16)
        head_values = (parts.reshape(kept.states.shape),)
        grad_words = jnp.einsum(
            "rvt,rtd->vd",
            grad_logits,
            kept.states.reshape(total, -1, kept.states.shape[3]),
            preferred_element_type=jnp.float32,
        ).astype(jnp.bfloat16)
    grad_branch, grad_res3, grad_vecs_feed, *made = head_back(
        head_values, kept.rows_feed, gain_feed, 3, (4, 1, 0) if direct else ()
    )
    grad_words, *narrow = made if direct else (grad_words,)
    values = Loaded(
        grad_out=grad_branch,
        feed_down=feed_down,
        gelu_slope=kept.gelu_slope,
        feed_up=feed_up,
        feed_act=kept.feed_act,
        second_low=kept.second_low.reshape(tokens.shape),
        cross_out=cross_out,
        cross_query=cross_query,
        query_cross=kept.query_cross,
        key_cross=kept.key_cross,
        value_cross=kept.value_cross,
        cross_totals=kept.cross_totals,
        cross_mix=kept.cross_mix,
        first_low=kept.first_low.reshape(tokens.shape),
        memory=memory,
        cross_key=cross_key,
        cross_value=cross_value,
        self_out=self_out,
        query_self=kept.query_self,
        key_self=kept.key_self,
        value_self=kept.value_self,
        self_totals=kept.self_totals,
        self_mix=kept.self_mix,
        tokens=tokens,
        self_query=self_query,
        self_key=self_key,
        self_value=self_value,
    )
    plain = Plain(
        grad_rows=grad_res3,
        rows_cross=kept.rows_cross,
        gain_cross=gain_cross.reshape(1, -1),
        rows_self=kept.rows_self,
        gain_self=gain_self.reshape(1, -1),
        grad_vecs=grad_vecs_feed,
        segment_row=segment_ids.reshape(1, -1),
        segment_column=segment_ids.reshape(-1, 1),
    )
    sums, grad_vecs, grad_tokens, memory_share, *narrow = layer_back(
        values, plain, 4, grad_words, *narrow, moves=(5, 6, 7, 2, 3) if direct else ()
    )
    grad_table = (
        narrow[0] if direct else return_rows(grad_words, vocab_local)
    ).astype(jnp.float32)
    sums = [part.astype(jnp.float32) for part in sums]
    sum_down = jnp.concatenate(sums[0:4], axis=1)
    sum_up = jnp.concatenate(sums[4:8], axis=1)
    sum_ck, sum_cv, sum_cq, sum_co, sum_sq, sum_sk, sum_sv, sum_so = sums[8:]
    sum_co, sum_so = (unfold(part, self_out.shape[0]) for part in (sum_co, sum_so))
    return (
        loss,
        grad_tokens,
        memory_share,
        sum_sq,
        sum_sk,
        sum_sv,
        sum_so,
        sum_cq,
        sum_ck,
        sum_cv,
        sum_co,
        sum_up,
        sum_down,
        *grad_vecs,
        grad_table,
        grad_scores,
    )


def solution(mesh):
    return jax.shard_map(
        local,
        mesh=mesh,
        in_specs=(
            P("dp", None),
            P("dp", None),
            P("dp", None),
            P("dp", None),
            P("dp", None),
            P(),
            P(),
            P(None, "mp"),
            P(None, "mp"),
            P(None, "mp"),
            P("mp", None),
            P(None, "mp"),
            P(None, "mp"),
            P(None, "mp"),
            P("mp", None),
            P(None, "mp"),
            P("mp", None),
            P(),
            P(),
            P(),
            P(),
            P(),
            P(),
            P("mp", "dp"),
        ),
        out_specs=(
            P(),
            P("dp", "mp"),
            P("dp", "mp"),
            P(None, "mp"),
            P(None, "mp"),
            P(None, "mp"),
            P("mp", None),
            P(None, "mp"),
            P(None, "mp"),
            P(None, "mp"),
            P("mp", None),
            P(None, "mp"),
            P("mp", None),
            P(),
            P(),
            P(),
            P(),
            P(),
            P(),
            P("mp", "dp"),
            P(),
        ),
        check_vma=False,
    )
```
